32 devices in a mesh: gx: 8 (over z, y), ta: 4 (over x, core).
Axes of the slice: x: 2, y: 2, z: 4, core: 2. Of those that a mesh axis runs over, the one named last changes fastest.
Arguments:
- features: bfloat16 [1, 128, 16, 8, 4096], P(None, 'gx', 'ta'), may hold values from -6 to 6
- cotangent: bfloat16 [1, 128, 16, 8, 4096], P(None, 'gx', 'ta'), may hold values from -6 to 6
- spec_weight: float32 [32, 16, 8, 8, 1024], P(None, None, None, None, ('gx', 'ta')), may hold values from -2 to 2
- point_weight: bfloat16 [8, 8], replicated, may hold values from -2 to 2
- bias_vector: float32 [8], replicated, may hold values from -1 to 1
Outputs:
- output: bfloat16 [1, 128, 16, 8, 4096], P(None, 'gx', 'ta')
- grad_field: bfloat16 [1, 128, 16, 8, 4096], P(None, 'gx', 'ta')
- grad_spec: float32 [32, 16, 8, 8, 1024], P(None, None, None, None, ('gx', 'ta'))
- grad_point: float32 [8, 8], replicated
- grad_bias: float32 [8], replicated
The draws below stay inside these ranges and needn't reach their ends.
All inputs are finite; a program needn't handle non-finite values.
Results may differ from the reference program's by a relative error of at most 0.014.
Values may be sent and summed in bfloat16 or wider, within the bound.
No kernel may reach another device: no remote copies, remote signals or barrier semaphores. Data moves between devices by JAX's collectives and lax.ppermute only.
A program may use at most 320 MiB of HBM per device.

```python
import math
import jax
import jax.numpy as jnp
from jax import lax

NX = 128
NY = 128
NZ = 32
NT = 16
C = 8
MX = 16
MY = 16
MZ = 16
MT = 8
BATCH = 1
KX = 32
KT = 16
KQ = 1024


def block_scale(rng, extent, pieces, low, high):
    factor_of = 1.0
    for axis_at, blocks in pieces:
        steps = jax.random.uniform(jax.random.fold_in(jax.random.fold_in(rng, 6), axis_at), (blocks,), jnp.float32, low / len(pieces), high / len(pieces))
        factor_of = factor_of * jnp.repeat(jnp.exp(steps), extent[axis_at] // blocks).reshape((-1,) + (1,) * (len(extent) - 1 - axis_at))
    return factor_of


def scatter_about(key, shape, deviation, reach, split=(), dtype=jnp.bfloat16):
    drawn = jax.random.normal(key, shape, jnp.float32) * deviation
    if len(split) > 0:
        drawn = block_scale(key, shape, split, -0.22, 0.18) * drawn
    return jnp.clip(drawn, min=-reach, max=reach).astype(dtype)


def setup_inputs(seed: int = 0) -> dict:
    keys = jax.random.split(jax.random.key(seed), 6)
    return {
        "features": scatter_about(keys[0], (BATCH, NX, NT, C, NY * NZ), 1.0, 6.0, ((1, 8), (2, 4))),
        "cotangent": scatter_about(keys[1], (BATCH, NX, NT, C, NY * NZ), 1.0, 6.0, ((1, 8), (2, 4))),
        "spec_weight": scatter_about(keys[2], (KX, KT, C, C, KQ), C ** -0.5, 2.0, ((4, 32),), jnp.float32),
        "point_weight": scatter_about(keys[3], (C, C), C ** -0.5, 2.0),
        "bias_vector": jnp.clip(jax.random.uniform(keys[4], (C,), jnp.float32, -1.0, 1.0), -1.0, 1.0),
    }


def basis(length, modes):
    frequency = jnp.concatenate([jnp.arange(modes + 1), jnp.arange(1, modes)]).astype(jnp.int32)
    samples_at = jnp.arange(length).astype(jnp.int32)
    phases = 2.0 * math.pi / length * (frequency[:, None] * samples_at[None, :] % length).astype(jnp.float32)
    cosine_row = jnp.arange(2 * modes) <= modes
    waves = jnp.where(cosine_row[:, None], jnp.cos(phases), jnp.sin(phases))
    at_edge = cosine_row & ((frequency == 0) | (2 * frequency == length))
    scales = jnp.where(at_edge, math.sqrt(1.0 / length), math.sqrt(2.0 / length)).astype(jnp.float32)
    return waves * scales[:, None]

def analyse_yz(spatial, by_table, bz_table):
    leading = spatial.shape[:-1]
    blocked = spatial.reshape(leading + (by_table.shape[1], bz_table.shape[1])).astype(jnp.float32)
    halfway = jnp.einsum('ky,...yz->...kz', by_table.astype(jnp.float32), blocked, precision=lax.Precision.HIGHEST)
    finished = jnp.einsum('lz,...kz->...kl', bz_table.astype(jnp.float32), halfway, precision=lax.Precision.HIGHEST)
    return finished.reshape(leading + (-1,))

def build_yz(modes_in, by_table, bz_table):
    leading = modes_in.shape[:-1]
    blocked = modes_in.reshape(leading + (by_table.shape[0], bz_table.shape[0])).astype(jnp.float32)
    halfway = jnp.einsum('lz,...kl->...kz', bz_table.astype(jnp.float32), blocked, precision=lax.Precision.HIGHEST)
    finished = jnp.einsum('ky,...kz->...yz', by_table.astype(jnp.float32), halfway, precision=lax.Precision.HIGHEST)
    return finished.reshape(leading + (-1,))

def analyse_xt(spread, bx_table, bt_table):
    values = spread.astype(jnp.float32)
    halfway = jnp.einsum('kx,bxtcq->bktcq', bx_table, values, precision=lax.Precision.HIGHEST)
    return jnp.einsum('lt,bktcq->bklcq', bt_table, halfway, precision=lax.Precision.HIGHEST)

def synthesise_xt(modes_in, bx_table, bt_table):
    halfway = jnp.einsum('lt,bklcq->bktcq', bt_table, modes_in, precision=lax.Precision.HIGHEST)
    return jnp.einsum('kx,bktcq->bxtcq', bx_table, halfway, precision=lax.Precision.HIGHEST)

def gelu_value(values):
    return 0.5 * values * (1.0 + jax.scipy.special.erf(values * 0.7071067811865476))

def gelu_slope(values):
    return 0.5 * (1.0 + jax.scipy.special.erf(values * 0.7071067811865476)) + values * jnp.exp(-0.5 * values * values) * 0.3989422804014327

def reference(features, cotangent, spec_weight, point_weight, bias_vector):
    by_table = basis(NY, MY).astype(jnp.bfloat16)
    bz_table = basis(NZ, MZ).astype(jnp.bfloat16)
    bx_table = basis(NX, MX)
    bt_table = basis(NT, MT)
    norm_scale = float(BATCH * NX * NT * NY * NZ) ** (-0.5)
    weight_wide = point_weight.astype(jnp.float32)
    positions = jnp.arange(NX).astype(jnp.int32)

    def take(array, position):
        return lax.dynamic_index_in_dim(array, position, 1, keepdims=False)

    def first_pass(position):
        return analyse_yz(take(features, position), by_table, bz_table).astype(jnp.bfloat16)
    yz_in = jnp.moveaxis(lax.map(first_pass, positions), 0, 1)
    spectrum = analyse_xt(yz_in, bx_table, bt_table)
    mixed = jnp.einsum('bklip,kliop->bklop', spectrum, spec_weight, precision=lax.Precision.HIGHEST)
    xt_out = synthesise_xt(mixed, bx_table, bt_table).astype(jnp.bfloat16)

    def second_pass(position):
        spatial = build_yz(take(xt_out, position), by_table, bz_table)
        own = take(features, position).astype(jnp.float32)
        pre = spatial + jnp.einsum('oi,btip->btop', weight_wide, own) + bias_vector[:, None]
        result = gelu_value(pre).astype(jnp.bfloat16)
        grad_pre = (take(cotangent, position).astype(jnp.float32) * gelu_slope(pre)).astype(jnp.bfloat16)
        grad_wide = grad_pre.astype(jnp.float32)
        point_part = jnp.einsum('btop,btip->oi', grad_wide, own)
        bias_part = lax.optimization_barrier(jnp.sum(grad_wide, axis=(0, 1, 3)))
        yz_grad = analyse_yz(grad_pre, by_table, bz_table).astype(jnp.bfloat16)
        return (result, grad_pre, point_part, bias_part, yz_grad)
    results, grad_pres, point_parts, bias_parts, yz_grads = lax.map(second_pass, positions)
    grad_point = lax.optimization_barrier(jnp.sum(point_parts, axis=0)) * norm_scale
    grad_bias = lax.optimization_barrier(jnp.sum(bias_parts, axis=0)) * norm_scale
    grad_modes = analyse_xt(jnp.moveaxis(yz_grads, 0, 1), bx_table, bt_table)
    grad_spec = jnp.einsum('bklip,bklop->kliop', spectrum, grad_modes, precision=lax.Precision.HIGHEST)
    grad_in_modes = jnp.einsum('kliop,bklop->bklip', spec_weight, grad_modes, precision=lax.Precision.HIGHEST)
    xt_grad = synthesise_xt(grad_in_modes, bx_table, bt_table).astype(jnp.bfloat16)

    def third_pass(position):
        spatial = build_yz(take(xt_grad, position), by_table, bz_table)
        grad_pre = grad_pres[position].astype(jnp.float32)
        return (spatial + jnp.einsum('oi,btop->btip', weight_wide, grad_pre)).astype(jnp.bfloat16)
    grad_field = jnp.moveaxis(lax.map(third_pass, positions), 0, 1)
    return (jnp.moveaxis(results, 0, 1), grad_field, grad_spec, grad_point, grad_bias)
```

```python
import functools
import math

import jax
import jax.numpy as jnp
import ml_dtypes
import numpy as np
from jax import lax
from jax.experimental import pallas as pl
from jax.experimental.pallas import tpu as pltpu
from jax.sharding import PartitionSpec as P

NX = 128
NY = 128
NZ = 32
NT = 16
MX = 16
MY = 16
MZ = 16
MT = 8
BATCH = 1
KX = 32
KT = 16
CHANS = 8
CELLS = NY * NZ
KQ = 1024
LANES = 128
F32 = jnp.float32
BF16 = jnp.bfloat16


def basis(length, modes):
    frequency = np.concatenate([np.arange(modes + 1), np.arange(1, modes)])
    samples_at = np.arange(length)
    phases = (2.0 * math.pi / length) * (frequency[:, None] * samples_at[None, :] % length)
    cosine_row = np.arange(2 * modes) <= modes
    waves = np.where(cosine_row[:, None], np.cos(phases), np.sin(phases))
    at_edge = cosine_row & ((frequency == 0) | (2 * frequency == length))
    scales = np.where(at_edge, math.sqrt(1.0 / length), math.sqrt(2.0 / length))
    return (waves * scales[:, None]).astype(np.float32)


def narrow(table):
    return np.asarray(table, np.float32).astype(ml_dtypes.bfloat16)


def vmem_params(mebibytes):
    return pltpu.CompilerParams(vmem_limit_bytes=mebibytes * 1024 * 1024)


def matmul(left, right):
    return jnp.dot(left, right, preferred_element_type=F32)


def swap_groups(tiles):
    rows = tiles[0].shape[0]
    lane = lax.broadcasted_iota(jnp.int32, (rows, LANES), 1)
    low_half = lane < 64
    even = (lane // 32) % 2 == 0
    first, second, third, fourth = tiles
    b0 = jnp.where(low_half, first, pltpu.roll(third, 64, 1))
    b2 = jnp.where(low_half, pltpu.roll(first, 64, 1), third)
    b1 = jnp.where(low_half, second, pltpu.roll(fourth, 64, 1))
    b3 = jnp.where(low_half, pltpu.roll(second, 64, 1), fourth)
    return (
        jnp.where(even, b0, pltpu.roll(b1, 32, 1)),
        jnp.where(even, pltpu.roll(b0, 96, 1), b1),
        jnp.where(even, b2, pltpu.roll(b3, 32, 1)),
        jnp.where(even, pltpu.roll(b2, 96, 1), b3),
    )


def pack_modes(modes, packed_ref, xl, tl):
    width = modes.shape[1]
    split = modes.reshape(xl, tl, CHANS, width)
    for tile in range(width // LANES):
        at = slice(tile * LANES, (tile + 1) * LANES)
        tiles = [split[:, step, :, at].reshape(xl * CHANS, LANES) for step in range(tl)]
        for owner, block in enumerate(swap_groups(tiles)):
            packed_ref[tile * tl + owner] = block.astype(BF16)


def unpack_modes(packed_ref, wide_ref, xl, tl):
    for tile in range(KQ // LANES):
        tiles = [packed_ref[tile * tl + owner].astype(F32) for owner in range(tl)]
        for step, block in enumerate(swap_groups(tiles)):
            wide_ref[:, step, :, tile * LANES : (tile + 1) * LANES] = block.reshape(
                xl, CHANS, LANES
            )


def analyse_kernel(xl, tl, field_ref, table_ref, packed_ref):
    pack_modes(matmul(field_ref[...], table_ref[...]), packed_ref, xl, tl)


def analyse(field, table, xl, tl, devices):
    rows = field.shape[0]
    steps = 4
    width = KQ // steps
    return pl.pallas_call(
        functools.partial(analyse_kernel, xl, tl),
        grid=(steps,),
        in_specs=[
            pl.BlockSpec((rows, CELLS), lambda n: (0, 0)),
            pl.BlockSpec((CELLS, width), lambda n: (0, n)),
        ],
        out_specs=pl.BlockSpec((devices // steps, LANES, LANES), lambda n: (n, 0, 0)),
        out_shape=jax.ShapeDtypeStruct((devices, LANES, LANES), BF16),
        compiler_params=vmem_params(48),
        cost_estimate=pl.CostEstimate(
            flops=2 * rows * CELLS * KQ, bytes_accessed=13 << 20, transcendentals=0
        ),
        name="analyse",
    )(field, table)


def weight_kernel(weight_ref, packed_ref):
    for kx in range(weight_ref.shape[0]):
        for group in range(KT // 4):
            parts = [weight_ref[kx, 4 * group + k] for k in range(4)]
            packed_ref[kx, :, :, group * LANES : (group + 1) * LANES] = jnp.concatenate(
                parts, axis=-1
            )


def pack_weight(weight):
    per = 4
    own = weight.shape[4]
    return pl.pallas_call(
        weight_kernel,
        grid=(KX // per,),
        in_specs=[pl.BlockSpec((per, KT, CHANS, CHANS, own), lambda n: (n, 0, 0, 0, 0))],
        out_specs=pl.BlockSpec((per, CHANS, CHANS, KT * own), lambda n: (n, 0, 0, 0)),
        out_shape=jax.ShapeDtypeStruct((KX, CHANS, CHANS, KT * own), F32),
        compiler_params=vmem_params(24),
        cost_estimate=pl.CostEstimate(flops=1 << 20, bytes_accessed=20 << 20, transcendentals=0),
        name="pack_weight",
    )(weight)


def to_modes(spread_ref, x_table_ref, t_table_ref):
    gx, ta = spread_ref.shape[:2]
    beside = jnp.concatenate(
        [spread_ref[:, at].reshape(gx * LANES, LANES) for at in range(ta)], axis=1
    )
    half = matmul(x_table_ref[...], beside).astype(BF16)
    return matmul(half, t_table_ref[...])


def from_modes(modes, x_table_ref, t_table_ref, spread_ref):
    gx, ta = spread_ref.shape[:2]
    half = matmul(modes.astype(BF16), t_table_ref[...]).astype(BF16)
    full = matmul(x_table_ref[...], half).astype(BF16)
    for at in range(ta):
        spread_ref[:, at] = full[:, at * LANES : (at + 1) * LANES].reshape(gx, LANES, LANES)


def mix_kernel(
    spread_ref, weight_ref, x_in_ref, t_in_ref, x_out_ref, t_out_ref, spectrum_ref, back_ref, mixed
):
    spectrum_ref[...] = to_modes(spread_ref, x_in_ref, t_in_ref)
    for kx in range(KX):
        rows = slice(kx * CHANS, (kx + 1) * CHANS)
        own = spectrum_ref[rows, :]
        total = own[0:1, :] * weight_ref[kx, 0]
        for i in range(1, CHANS):
            total = total + own[i : i + 1, :] * weight_ref[kx, i]
        mixed[rows, :] = total
    from_modes(mixed[...], x_out_ref, t_out_ref, back_ref)


def mix_back_kernel(
    spread_ref, weight_ref, x_in_ref, t_in_ref, x_out_ref, t_out_ref, grad_ref, back_ref, mixed
):
    grad_ref[...] = to_modes(spread_ref, x_in_ref, t_in_ref)
    for kx in range(KX):
        rows = slice(kx * CHANS, (kx + 1) * CHANS)
        own = grad_ref[rows, :]
        sums = [
            jnp.sum(own * weight_ref[kx, i], axis=0, keepdims=True) for i in range(CHANS)
        ]
        mixed[rows, :] = jnp.concatenate(sums, axis=0)
    from_modes(mixed[...], x_out_ref, t_out_ref, back_ref)


def mix(kernel, spread, weight, tables, name):
    modes = (KX * CHANS, weight.shape[3])
    return pl.pallas_call(
        kernel,
        out_shape=(
            jax.ShapeDtypeStruct(modes, F32),
            jax.ShapeDtypeStruct(spread.shape, BF16),
        ),
        in_specs=[pl.BlockSpec(memory_space=pltpu.VMEM)] * 6,
        out_specs=[pl.BlockSpec(memory_space=pltpu.VMEM)] * 2,
        scratch_shapes=[pltpu.VMEM(modes, F32)],
        compiler_params=vmem_params(32),
        cost_estimate=pl.CostEstimate(flops=1 << 30, bytes_accessed=9 << 20, transcendentals=0),
        name=name,
    )(spread, weight, *tables)


def outer_kernel(spectrum_ref, grad_ref, result_ref):
    own = result_ref.shape[4]
    for kx in range(result_ref.shape[0]):
        rows = slice(kx * CHANS, (kx + 1) * CHANS)
        for group in range(KT // 4):
            at = slice(group * LANES, (group + 1) * LANES)
            inputs = spectrum_ref[rows, at]
            grads = grad_ref[rows, at]
            for i in range(CHANS):
                product = inputs[i : i + 1, :] * grads
                for k in range(4):
                    result_ref[kx, 4 * group + k, i] = product[:, k * own : (k + 1) * own]


def outer(spectrum, grad, own):
    per = 4
    width = KT * own
    return pl.pallas_call(
        outer_kernel,
        grid=(KX // per,),
        in_specs=[pl.BlockSpec((per * CHANS, width), lambda n: (n, 0))] * 2,
        out_specs=pl.BlockSpec((per, KT, CHANS, CHANS, own), lambda n: (n, 0, 0, 0, 0)),
        out_shape=jax.ShapeDtypeStruct((KX, KT, CHANS, CHANS, own), F32),
        compiler_params=vmem_params(24),
        cost_estimate=pl.CostEstimate(flops=1 << 20, bytes_accessed=17 << 20, transcendentals=0),
        name="outer",
    )(spectrum, grad)


def normal_parts(values):
    t = 1.0 / (1.0 + 0.2316419 * jnp.abs(values))
    density = jnp.exp(-0.5 * values * values) * 0.3989422804014327
    series = 1.330274429 * t - 1.821255978
    series = series * t + 1.781477937
    series = series * t - 0.356563782
    series = series * t + 0.319381530
    tail = density * (series * t)
    return jnp.where(values >= 0.0, 1.0 - tail, tail), density


def middle_kernel(
    xl,
    tl,
    packed_ref,
    field_ref,
    cotangent_ref,
    build_ref,
    analyse_ref,
    mixer_ref,
    bias_ref,
    output_ref,
    grad_ref,
    sent_ref,
    sums_ref,
    wide,
    modes,
    pre,
    total,
    gram,
    row_sums,
):
    step = pl.program_id(0)
    rows = field_ref.shape[0]
    half = mixer_ref.shape[0]

    @pl.when(step == 0)
    def _():
        unpack_modes(packed_ref, wide, xl, tl)
        modes[...] = wide[...].reshape(rows, KQ).astype(BF16)
        total[...] = jnp.zeros_like(total)
        gram[...] = jnp.zeros_like(gram)
        row_sums[...] = jnp.zeros_like(row_sums)

    pre[...] = matmul(modes[...], build_ref[...])
    for at in range(rows // half):
        part = slice(at * half, (at + 1) * half)
        pre[part, :] += matmul(mixer_ref[...], field_ref[part, :])

    chunk = 16

    def pointwise(index, carry):
        part = pl.ds(pl.multiple_of(index * chunk, chunk), chunk)
        values = pre[part, :] + bias_ref[part, 0:1]
        integral, density = normal_parts(values)
        output_ref[part, :] = (values * integral).astype(BF16)
        slope = integral + values * density
        grad = (cotangent_ref[part, :].astype(F32) * slope).astype(BF16)
        grad_ref[part, :] = grad
        wide_grad = grad.astype(F32)
        sums = row_sums[part, :]
        for tile in range(wide_grad.shape[1] // LANES):
            sums = sums + wide_grad[:, tile * LANES : (tile + 1) * LANES]
        row_sums[part, :] = sums
        return carry

    lax.fori_loop(0, rows // chunk, pointwise, 0)

    total[...] += matmul(grad_ref[...], analyse_ref[...])
    for at in range(rows // half):
        part = slice(at * half, (at + 1) * half)
        gram[...] += lax.dot_general(
            grad_ref[part, :],
            field_ref[part, :],
            (((1,), (1,)), ((), ())),
            preferred_element_type=F32,
        )

    @pl.when(step == pl.num_programs(0) - 1)
    def _():
        pack_modes(total[...], sent_ref, xl, tl)
        row = lax.broadcasted_iota(jnp.int32, (half, half), 0)
        column = lax.broadcasted_iota(jnp.int32, (half, half), 1)
        same = jnp.where(row // CHANS == column // CHANS, gram[...], 0.0)
        folded = jnp.sum(same.reshape(half // CHANS, CHANS, half), axis=0)
        source = lax.broadcasted_iota(jnp.int32, (half, LANES), 0)
        target = lax.broadcasted_iota(jnp.int32, (half, LANES), 1)
        select = jnp.where(source % CHANS == target, 1.0, 0.0)
        point = jnp.dot(
            folded, select, precision=lax.Precision.HIGHEST, preferred_element_type=F32
        )
        bias = jnp.sum(
            jnp.sum(row_sums[...].reshape(rows // CHANS, CHANS, LANES), axis=0),
            axis=1,
            keepdims=True,
        )
        lane = lax.broadcasted_iota(jnp.int32, (CHANS, LANES), 1)
        sums_ref[...] = jnp.where(lane == CHANS, bias, point)


def middle(packed, field, cotangent, build_table, analyse_table, mixer, bias, xl, tl):
    rows = field.shape[0]
    width = 512
    steps = CELLS // width
    half = mixer.shape[0]
    whole = lambda *shape: pl.BlockSpec(shape, lambda n: (0,) * len(shape))
    tile = pl.BlockSpec((rows, width), lambda n: (0, n))
    return pl.pallas_call(
        functools.partial(middle_kernel, xl, tl),
        grid=(steps,),
        in_specs=[
            whole(*packed.shape),
            tile,
            tile,
            pl.BlockSpec((KQ, width), lambda n: (0, n)),
            pl.BlockSpec((width, KQ), lambda n: (n, 0)),
            whole(half, half),
            whole(rows, LANES),
        ],
        out_specs=[tile, tile, whole(*packed.shape), whole(CHANS, LANES)],
        out_shape=(
            jax.ShapeDtypeStruct((rows, CELLS), BF16),
            jax.ShapeDtypeStruct((rows, CELLS), BF16),
            jax.ShapeDtypeStruct(packed.shape, BF16),
            jax.ShapeDtypeStruct((CHANS, LANES), F32),
        ),
        scratch_shapes=[
            pltpu.VMEM((xl, tl, CHANS, KQ), F32),
            pltpu.VMEM((rows, KQ), BF16),
            pltpu.VMEM((rows, width), F32),
            pltpu.VMEM((rows, KQ), F32),
            pltpu.VMEM((half, half), F32),
            pltpu.VMEM((rows, LANES), F32),
        ],
        compiler_params=vmem_params(48),
        cost_estimate=pl.CostEstimate(
            flops=5 * rows * CELLS * KQ, bytes_accessed=34 << 20, transcendentals=rows * CELLS
        ),
        name="middle",
    )(packed, field, cotangent, build_table, analyse_table, mixer, bias)


def last_kernel(xl, tl, packed_ref, grad_ref, build_ref, mixer_ref, field_ref, wide, modes):
    rows = grad_ref.shape[0]
    half = mixer_ref.shape[0]

    @pl.when(pl.program_id(0) == 0)
    def _():
        unpack_modes(packed_ref, wide, xl, tl)
        modes[...] = wide[...].reshape(rows, KQ).astype(BF16)

    for at in range(rows // half):
        part = slice(at * half, (at + 1) * half)
        field_ref[part, :] = (
            matmul(modes[part, :], build_ref[...]) + matmul(mixer_ref[...], grad_ref[part, :])
        ).astype(BF16)


def last(packed, grad, build_table, mixer, xl, tl):
    rows = grad.shape[0]
    width = 512
    half = mixer.shape[0]
    tile = pl.BlockSpec((rows, width), lambda n: (0, n))
    return pl.pallas_call(
        functools.partial(last_kernel, xl, tl),
        grid=(CELLS // width,),
        in_specs=[
            pl.BlockSpec(packed.shape, lambda n: (0, 0, 0)),
            tile,
            pl.BlockSpec((KQ, width), lambda n: (0, n)),
            pl.BlockSpec((half, half), lambda n: (0, 0)),
        ],
        out_specs=tile,
        out_shape=jax.ShapeDtypeStruct((rows, CELLS), BF16),
        scratch_shapes=[
            pltpu.VMEM((xl, tl, CHANS, KQ), F32),
            pltpu.VMEM((rows, KQ), BF16),
        ],
        compiler_params=vmem_params(32),
        cost_estimate=pl.CostEstimate(
            flops=2 * rows * CELLS * KQ, bytes_accessed=18 << 20, transcendentals=0
        ),
        name="last",
    )(packed, grad, build_table, mixer)


def swap(blocks):
    return lax.all_to_all(blocks, ("gx", "ta"), split_axis=0, concat_axis=0, tiled=True)


def fast_body(gx, ta, features, cotangent, spec_weight, point_weight, bias_vector):
    _, xl, tl, _, cells = features.shape
    own = spec_weight.shape[4]
    devices = gx * ta
    rows = xl * tl * CHANS
    yz = np.kron(
        narrow(basis(NY, MY)).astype(np.float32), narrow(basis(NZ, MZ)).astype(np.float32)
    )
    build_table = jnp.asarray(narrow(yz))
    analyse_table = jnp.asarray(narrow(yz.T))
    x_wide = np.kron(basis(NX, MX), np.eye(CHANS))
    t_wide = np.kron(basis(NT, MT), np.eye(own))
    x_in, x_out = jnp.asarray(narrow(x_wide)), jnp.asarray(narrow(x_wide.T))
    t_in, t_out = jnp.asarray(narrow(t_wide.T)), jnp.asarray(narrow(t_wide))
    tables = (x_in, t_in, x_out, t_out)
    norm_scale = float(BATCH * NX * NT * NY * NZ) ** (-0.5)

    field = features.reshape(rows, cells)
    packed_weight = pack_weight(spec_weight)
    group = rows // 2
    eye = jnp.asarray(np.eye(group // CHANS), BF16)
    mixer = jnp.kron(eye, point_weight)
    mixer_back = jnp.kron(eye, point_weight.T)
    bias = jnp.broadcast_to(jnp.tile(bias_vector, xl * tl)[:, None], (rows, LANES))

    spread_shape = (gx, ta, LANES, LANES)
    spread_in = swap(analyse(field, analyse_table, xl, tl, devices)).reshape(spread_shape)
    spectrum, mixed = mix(mix_kernel, spread_in, packed_weight, tables, "mix")
    returned = swap(mixed.reshape(devices, LANES, LANES))
    output, grad_pre, sent, sums = middle(
        returned,
        field,
        cotangent.reshape(rows, cells),
        build_table,
        analyse_table,
        mixer,
        bias,
        xl,
        tl,
    )
    gathered = lax.all_gather(sums, ("gx", "ta"))
    spread_grad = swap(sent).reshape(spread_shape)
    grad_modes, mixed_back = mix(mix_back_kernel, spread_grad, packed_weight, tables, "mix_back")
    grad_back = swap(mixed_back.reshape(devices, LANES, LANES))
    grad_spec = outer(spectrum, grad_modes, own)
    grad_field = last(grad_back, grad_pre, build_table, mixer_back, xl, tl)
    summed = jnp.sum(gathered, axis=0) * norm_scale
    return (
        output.reshape(features.shape),
        grad_field.reshape(features.shape),
        grad_spec,
        summed[:, :CHANS],
        summed[:, CHANS],
    )


def analyse_yz(spatial, yz_table):
    return jnp.einsum(
        "qp,bxtcp->bxtcq", yz_table, spatial.astype(F32), precision=lax.Precision.HIGHEST
    )


def build_yz(modes_in, yz_table):
    return jnp.einsum(
        "qp,bxtcq->bxtcp", yz_table, modes_in.astype(F32), precision=lax.Precision.HIGHEST
    )


def analyse_xt(spread, table):
    sizes = spread.shape
    flattened = spread.reshape(sizes[0], sizes[1] * sizes[2], sizes[3] * sizes[4]).astype(F32)
    spectral = jnp.einsum("mp,bpr->bmr", table, flattened, precision=lax.Precision.HIGHEST)
    return spectral.reshape(sizes[0], KX, KT, sizes[3], sizes[4])


def synthesise_xt(modes_in, table):
    sizes = modes_in.shape
    flattened = modes_in.reshape(sizes[0], sizes[1] * sizes[2], sizes[3] * sizes[4])
    spatial = jnp.einsum("mp,bmr->bpr", table, flattened, precision=lax.Precision.HIGHEST)
    return spatial.reshape(sizes[0], NX, NT, sizes[3], sizes[4])


def to_owners(modes_in):
    first = lax.all_to_all(modes_in, "gx", split_axis=4, concat_axis=1, tiled=True)
    return lax.all_to_all(first, "ta", split_axis=4, concat_axis=2, tiled=True)


def to_cells(spread, shape):
    first = lax.all_to_all(
        spread[:, :, :, :, None, None, :], "gx", split_axis=1, concat_axis=4, tiled=True
    )
    second = lax.all_to_all(first, "ta", split_axis=2, concat_axis=5, tiled=True)
    return second.reshape(shape[:4] + (-1,))


def general_body(features, cotangent, spec_weight, point_weight, bias_vector):
    shape = features.shape
    yz_table = jnp.asarray(
        np.kron(narrow(basis(NY, MY)).astype(np.float32), narrow(basis(NZ, MZ)).astype(np.float32))
    )
    xt_table = jnp.asarray(np.kron(basis(NX, MX), basis(NT, MT)))
    norm_scale = float(BATCH * NX * NT * NY * NZ) ** (-0.5)
    highest = lax.Precision.HIGHEST
    spectrum = analyse_xt(to_owners(analyse_yz(features, yz_table).astype(BF16)), xt_table)
    mixed = jnp.einsum("bklip,kliop->bklop", spectrum, spec_weight, precision=highest)
    returned = to_cells(synthesise_xt(mixed, xt_table).astype(BF16), shape)
    pointwise = jnp.einsum("oi,bxtip->bxtop", point_weight, features, preferred_element_type=F32)
    pre = build_yz(returned, yz_table) + pointwise + bias_vector[:, None]
    integral = 0.5 * (1.0 + jax.scipy.special.erf(pre * 0.7071067811865476))
    output = (pre * integral).astype(BF16)
    slope = integral + pre * jnp.exp(-0.5 * pre * pre) * 0.3989422804014327
    grad_pre = (cotangent.astype(F32) * slope).astype(BF16)
    local_point = jnp.einsum("bxtop,bxtip->oi", grad_pre, features, preferred_element_type=F32)
    local_bias = jnp.sum(grad_pre.astype(F32), axis=(0, 1, 2, 4))
    total_point, total_bias = lax.psum((local_point, local_bias), ("gx", "ta"))
    grad_modes = analyse_xt(to_owners(analyse_yz(grad_pre, yz_table).astype(BF16)), xt_table)
    grad_spec = jnp.einsum("bklip,bklop->kliop", spectrum, grad_modes, precision=highest)
    grad_in = jnp.einsum("kliop,bklop->bklip", spec_weight, grad_modes, precision=highest)
    grad_back = to_cells(synthesise_xt(grad_in, xt_table).astype(BF16), shape)
    point_term = jnp.einsum("oi,bxtop->bxtip", point_weight, grad_pre, preferred_element_type=F32)
    grad_field = (build_yz(grad_back, yz_table) + point_term).astype(BF16)
    return (output, grad_field, grad_spec, total_point * norm_scale, total_bias * norm_scale)


def solution(mesh):
    split_field = P(None, "gx", "ta", None, None)
    split_weight = P(None, None, None, None, ("gx", "ta"))
    in_specs = (split_field, split_field, split_weight, P(), P())
    out_specs = (split_field, split_field, split_weight, P(), P())
    gx, ta = mesh.shape["gx"], mesh.shape["ta"]
    own, xl, tl = KQ // (gx * ta), NX // gx, NT // ta
    if own == 32 and xl * CHANS == LANES and tl == 4:
        body = functools.partial(fast_body, gx, ta)
    else:
        body = general_body
    return jax.shard_map(body, mesh=mesh, in_specs=in_specs, out_specs=out_specs, check_vma=False)
```

```python
import functools
import math

import jax
import jax.numpy as jnp
import ml_dtypes
import numpy as np
from jax import lax
from jax.experimental import pallas as pl
from jax.experimental.pallas import tpu as pltpu
from jax.sharding import PartitionSpec as P

NX = 128
NY = 128
NZ = 32
NT = 16
MX = 16
MY = 16
MZ = 16
MT = 8
BATCH = 1
KX = 32
KT = 16
CHANS = 8
CELLS = NY * NZ
KQ = 1024
LANES = 128
PARTS = 2
LOG2_E = math.log2(math.e)
DENSITY = 1.0 / math.sqrt(2.0 * math.pi)
F32 = jnp.float32
BF16 = jnp.bfloat16


def basis(length, modes):
    frequency = np.concatenate([np.arange(modes + 1), np.arange(1, modes)])
    samples_at = np.arange(length)
    phases = (2.0 * math.pi / length) * (frequency[:, None] * samples_at[None, :] % length)
    cosine_row = np.arange(2 * modes) <= modes
    waves = np.where(cosine_row[:, None], np.cos(phases), np.sin(phases))
    at_edge = cosine_row & ((frequency == 0) | (2 * frequency == length))
    scales = np.where(at_edge, math.sqrt(1.0 / length), math.sqrt(2.0 / length))
    return (waves * scales[:, None]).astype(np.float32)


def narrow(table):
    return np.asarray(table, np.float32).astype(ml_dtypes.bfloat16)


def vmem_params(mebibytes):
    return pltpu.CompilerParams(vmem_limit_bytes=mebibytes * 1024 * 1024)


def matmul(left, right):
    return jnp.dot(left, right, preferred_element_type=F32)


def swap_groups(tiles):
    rows = tiles[0].shape[0]
    lane = lax.broadcasted_iota(jnp.int32, (rows, LANES), 1)
    low_half = lane < 64
    even = (lane // 32) % 2 == 0
    first, second, third, fourth = tiles
    b0 = jnp.where(low_half, first, pltpu.roll(third, 64, 1))
    b2 = jnp.where(low_half, pltpu.roll(first, 64, 1), third)
    b1 = jnp.where(low_half, second, pltpu.roll(fourth, 64, 1))
    b3 = jnp.where(low_half, pltpu.roll(second, 64, 1), fourth)
    return (
        jnp.where(even, b0, pltpu.roll(b1, 32, 1)),
        jnp.where(even, pltpu.roll(b0, 96, 1), b1),
        jnp.where(even, b2, pltpu.roll(b3, 32, 1)),
        jnp.where(even, pltpu.roll(b2, 96, 1), b3),
    )


def pack_modes(modes, packed_ref, xl, tl):
    width = modes.shape[1]
    split = modes.reshape(xl, tl, CHANS, width)
    for tile in range(width // LANES):
        at = slice(tile * LANES, (tile + 1) * LANES)
        tiles = [split[:, step, :, at].reshape(xl * CHANS, LANES) for step in range(tl)]
        for owner, block in enumerate(swap_groups(tiles)):
            packed_ref[tile * tl + owner] = block.astype(BF16)


def unpack_modes(packed_ref, wide_ref, xl, tl):
    for tile in range(KQ // LANES):
        tiles = [packed_ref[tile * tl + owner].astype(F32) for owner in range(tl)]
        for step, block in enumerate(swap_groups(tiles)):
            wide_ref[:, step, :, tile * LANES : (tile + 1) * LANES] = block.reshape(
                xl, CHANS, LANES
            )


def analyse_kernel(xl, tl, field_ref, table_ref, packed_ref):
    pack_modes(matmul(field_ref[...], table_ref[...]), packed_ref, xl, tl)


def analyse(field, table, part, xl, tl, devices):
    rows = xl * tl * CHANS
    steps = 4
    width = KQ // steps
    return pl.pallas_call(
        functools.partial(analyse_kernel, xl, tl),
        grid=(steps,),
        in_specs=[
            pl.BlockSpec((rows, CELLS), lambda n: (part, 0)),
            pl.BlockSpec((CELLS, width), lambda n: (0, n)),
        ],
        out_specs=pl.BlockSpec((devices // steps, xl * CHANS, LANES), lambda n: (n, 0, 0)),
        out_shape=jax.ShapeDtypeStruct((devices, xl * CHANS, LANES), BF16),
        compiler_params=vmem_params(56),
        cost_estimate=pl.CostEstimate(
            flops=2 * rows * CELLS * KQ, bytes_accessed=10 << 20, transcendentals=0
        ),
        name="analyse",
    )(field, table)


def weight_kernel(weight_ref, packed_ref):
    for kx in range(weight_ref.shape[0]):
        for group in range(KT // 4):
            parts = [weight_ref[kx, 4 * group + k] for k in range(4)]
            packed_ref[kx, :, :, group * LANES : (group + 1) * LANES] = jnp.concatenate(
                parts, axis=-1
            )


def pack_weight(weight):
    per = 4
    own = weight.shape[4]
    return pl.pallas_call(
        weight_kernel,
        grid=(KX // per,),
        in_specs=[pl.BlockSpec((per, KT, CHANS, CHANS, own), lambda n: (n, 0, 0, 0, 0))],
        out_specs=pl.BlockSpec((per, CHANS, CHANS, KT * own), lambda n: (n, 0, 0, 0)),
        out_shape=jax.ShapeDtypeStruct((KX, CHANS, CHANS, KT * own), F32),
        compiler_params=vmem_params(56),
        cost_estimate=pl.CostEstimate(flops=1 << 20, bytes_accessed=20 << 20, transcendentals=0),
        name="pack_weight",
    )(weight)


def to_modes(spread_refs, x_table_refs, t_table_ref):
    total = 0.0
    for spread_ref, x_table_ref in zip(spread_refs, x_table_refs):
        gx, ta, rows, _ = spread_ref.shape
        beside = jnp.concatenate(
            [spread_ref[:, at].reshape(gx * rows, LANES) for at in range(ta)], axis=1
        )
        total = total + matmul(x_table_ref[...], beside)
    return matmul(total.astype(BF16), t_table_ref[...])


def from_modes(modes, x_table_ref, t_table_ref, held_ref):
    gx, ta, rows, _ = held_ref.shape[1:]
    half = matmul(modes.astype(BF16), t_table_ref[...]).astype(BF16)
    for part in range(PARTS):
        full = matmul(x_table_ref[part], half).astype(BF16)
        for at in range(ta):
            held_ref[part, :, at] = full[:, at * LANES : (at + 1) * LANES].reshape(gx, rows, LANES)


def mix_kernel(
    backward,
    spread_a_ref,
    spread_b_ref,
    weight_ref,
    x_in_ref,
    t_in_ref,
    x_out_ref,
    t_out_ref,
    modes_ref,
    back_a_ref,
    back_b_ref,
    weight,
    modes,
    mixed,
    held,
    weight_sem,
    modes_sem,
    back_sems,
):
    fetch = pltpu.make_async_copy(weight_ref, weight, weight_sem)
    fetch.start()
    modes[...] = to_modes(
        (spread_a_ref, spread_b_ref), (x_in_ref.at[0], x_in_ref.at[1]), t_in_ref
    )
    keep = pltpu.make_async_copy(modes, modes_ref, modes_sem)
    keep.start()
    fetch.wait()
    for kx in range(KX):
        rows = slice(kx * CHANS, (kx + 1) * CHANS)
        own = modes[rows, :]
        if backward:
            sums = [jnp.sum(own * weight[kx, i], axis=0, keepdims=True) for i in range(CHANS)]
            mixed[rows, :] = jnp.concatenate(sums, axis=0)
        else:
            total = own[0:1, :] * weight[kx, 0]
            for i in range(1, CHANS):
                total = total + own[i : i + 1, :] * weight[kx, i]
            mixed[rows, :] = total
    from_modes(mixed[...], x_out_ref, t_out_ref, held)
    sends = [
        pltpu.make_async_copy(held.at[part], ref, back_sems.at[part])
        for part, ref in enumerate((back_a_ref, back_b_ref))
    ]
    for send in sends:
        send.start()
    for send in sends:
        send.wait()
    keep.wait()


def mix(spreads, weight, tables, backward):
    modes = (KX * CHANS, weight.shape[3])
    shape = spreads[0].shape
    anywhere = pl.BlockSpec(memory_space=pl.ANY)
    on_chip = pl.BlockSpec(memory_space=pltpu.VMEM)
    return pl.pallas_call(
        functools.partial(mix_kernel, backward),
        out_shape=(
            jax.ShapeDtypeStruct(modes, F32),
            jax.ShapeDtypeStruct(shape, BF16),
            jax.ShapeDtypeStruct(shape, BF16),
        ),
        in_specs=[on_chip] * 2 + [anywhere] + [on_chip] * 4,
        out_specs=[anywhere] * 3,
        scratch_shapes=[
            pltpu.VMEM(weight.shape, F32),
            pltpu.VMEM(modes, F32),
            pltpu.VMEM(modes, F32),
            pltpu.VMEM((PARTS,) + shape, BF16),
            pltpu.SemaphoreType.DMA,
            pltpu.SemaphoreType.DMA,
            pltpu.SemaphoreType.DMA((PARTS,)),
        ],
        compiler_params=vmem_params(32),
        cost_estimate=pl.CostEstimate(flops=1 << 30, bytes_accessed=9 << 20, transcendentals=0),
        name="mix_back" if backward else "mix",
    )(*spreads, weight, *tables)


def outer_kernel(spectrum_ref, grad_ref, result_ref):
    own = result_ref.shape[4]
    for kx in range(result_ref.shape[0]):
        rows = slice(kx * CHANS, (kx + 1) * CHANS)
        for group in range(KT // 4):
            at = slice(group * LANES, (group + 1) * LANES)
            inputs = spectrum_ref[rows, at]
            grads = grad_ref[rows, at]
            for i in range(CHANS):
                product = inputs[i : i + 1, :] * grads
                for k in range(4):
                    result_ref[kx, 4 * group + k, i] = product[:, k * own : (k + 1) * own]


def outer(spectrum, grad, own):
    per = 4
    width = KT * own
    return pl.pallas_call(
        outer_kernel,
        grid=(KX // per,),
        in_specs=[pl.BlockSpec((per * CHANS, width), lambda n: (n, 0))] * 2,
        out_specs=pl.BlockSpec((per, KT, CHANS, CHANS, own), lambda n: (n, 0, 0, 0, 0)),
        out_shape=jax.ShapeDtypeStruct((KX, KT, CHANS, CHANS, own), F32),
        compiler_params=vmem_params(56),
        cost_estimate=pl.CostEstimate(flops=1 << 20, bytes_accessed=17 << 20, transcendentals=0),
        name="outer",
    )(spectrum, grad)


def normal_parts(values):
    scaled = 1.0 + 0.2316419 * jnp.abs(values)
    guess = pl.reciprocal(scaled, approx=True)
    t = guess * (2.0 - scaled * guess)
    decay = jnp.exp2(values * values * (-0.5 * LOG2_E))
    series = (1.330274429 * DENSITY) * t - 1.821255978 * DENSITY
    series = series * t + 1.781477937 * DENSITY
    series = series * t - 0.356563782 * DENSITY
    series = series * t + 0.319381530 * DENSITY
    tail = decay * (series * t)
    return jnp.where(values >= 0.0, 1.0 - tail, tail), decay


def middle_kernel(
    xl,
    tl,
    packed_ref,
    field_ref,
    cotangent_ref,
    build_ref,
    analyse_ref,
    mixer_ref,
    bias_ref,
    sums_in_ref,
    _,
    output_ref,
    grad_ref,
    sent_ref,
    sums_ref,
    wide,
    modes,
    total,
    gram,
    row_sums,
):
    step = pl.program_id(0)
    rows, width = field_ref.shape
    tile = 256
    chunk = 32

    @pl.when(step == 0)
    def _():
        unpack_modes(packed_ref, wide, xl, tl)
        modes[...] = wide[...].reshape(rows, KQ).astype(BF16)
        total[...] = jnp.zeros_like(total)
        gram[...] = jnp.zeros_like(gram)
        row_sums[...] = jnp.zeros_like(row_sums)

    def build(at):
        return matmul(modes[...], build_ref[:, at]) + matmul(mixer_ref[...], field_ref[:, at])

    def pointwise(pre, at):
        for first in range(0, rows, chunk):
            part = slice(first, first + chunk)
            bias = bias_ref[part, :]
            values = pre[part, :] + jnp.concatenate([bias] * (tile // LANES), axis=1)
            integral, decay = normal_parts(values)
            output_ref[part, at] = (values * integral).astype(BF16)
            slope = integral + (values * DENSITY) * decay
            grad = (cotangent_ref[part, at].astype(F32) * slope).astype(BF16)
            grad_ref[part, at] = grad
            wide_grad = grad.astype(F32)
            sums = row_sums[part, :]
            for lanes in range(0, tile, LANES):
                sums = sums + wide_grad[:, lanes : lanes + LANES]
            row_sums[part, :] = sums

    def gather(at):
        total[...] += matmul(grad_ref[:, at], analyse_ref[at, :])
        gram[...] += lax.dot_general(
            grad_ref[:, at],
            field_ref[:, at],
            (((1,), (1,)), ((), ())),
            preferred_element_type=F32,
        )

    tiles = [slice(first, first + tile) for first in range(0, width, tile)]
    ready = build(tiles[0])
    for index, at in enumerate(tiles):
        pre = ready
        if index + 1 < len(tiles):
            ready = build(tiles[index + 1])
        pointwise(pre, at)
        if index % 2 == 1:
            gather(slice(tiles[index - 1].start, at.stop))

    @pl.when(step == pl.num_programs(0) - 1)
    def _():
        pack_modes(total[...], sent_ref, xl, tl)
        row = lax.broadcasted_iota(jnp.int32, (rows, rows), 0)
        column = lax.broadcasted_iota(jnp.int32, (rows, rows), 1)
        same = jnp.where(row // CHANS == column // CHANS, gram[...], 0.0)
        folded = jnp.sum(same.reshape(rows // CHANS, CHANS, rows), axis=0)
        source = lax.broadcasted_iota(jnp.int32, (rows, LANES), 0)
        target = lax.broadcasted_iota(jnp.int32, (rows, LANES), 1)
        select = jnp.where(source % CHANS == target, 1.0, 0.0)
        point = jnp.dot(
            folded, select, precision=lax.Precision.HIGHEST, preferred_element_type=F32
        )
        bias = jnp.sum(
            jnp.sum(row_sums[...].reshape(rows // CHANS, CHANS, LANES), axis=0),
            axis=1,
            keepdims=True,
        )
        lane = lax.broadcasted_iota(jnp.int32, (CHANS, LANES), 1)
        sums_ref[...] = sums_in_ref[...] + jnp.where(lane == CHANS, bias, point)


def middle(packed, field, cotangent, tables, mixer, bias, sums, output, part, xl, tl):
    build_table, analyse_table = tables
    rows = xl * tl * CHANS
    width = 512
    whole = lambda *shape: pl.BlockSpec(shape, lambda n: (0,) * len(shape))
    tile = pl.BlockSpec((rows, width), lambda n: (part, n))
    kernel = functools.partial(middle_kernel, xl, tl)
    operands = (packed, field, cotangent, build_table, analyse_table, mixer, bias, sums)
    specs = [
        whole(*packed.shape),
        tile,
        tile,
        pl.BlockSpec((KQ, width), lambda n: (0, n)),
        pl.BlockSpec((width, KQ), lambda n: (n, 0)),
        whole(rows, rows),
        whole(rows, LANES),
        whole(CHANS, LANES),
    ]
    aliases = {}
    if output is None:
        inner = kernel
        kernel = lambda *refs: inner(*refs[:8], None, *refs[8:])
    else:
        aliases = {len(operands): 0}
        operands += (output,)
        specs.append(pl.BlockSpec(memory_space=pl.ANY))
    return pl.pallas_call(
        kernel,
        grid=(CELLS // width,),
        in_specs=specs,
        out_specs=[
            tile,
            pl.BlockSpec((rows, width), lambda n: (0, n)),
            whole(*packed.shape),
            whole(CHANS, LANES),
        ],
        out_shape=(
            jax.ShapeDtypeStruct(field.shape, BF16),
            jax.ShapeDtypeStruct((rows, CELLS), BF16),
            jax.ShapeDtypeStruct(packed.shape, BF16),
            jax.ShapeDtypeStruct((CHANS, LANES), F32),
        ),
        scratch_shapes=[
            pltpu.VMEM((xl, tl, CHANS, KQ), F32),
            pltpu.VMEM((rows, KQ), BF16),
            pltpu.VMEM((rows, KQ), F32),
            pltpu.VMEM((rows, rows), F32),
            pltpu.VMEM((rows, LANES), F32),
        ],
        input_output_aliases=aliases,
        compiler_params=vmem_params(56),
        cost_estimate=pl.CostEstimate(
            flops=5 * rows * CELLS * KQ, bytes_accessed=26 << 20, transcendentals=rows * CELLS
        ),
        name="middle",
    )(*operands)


def last_kernel(xl, tl, packed_ref, grad_ref, build_ref, mixer_ref, _, field_ref, wide, modes):
    rows = grad_ref.shape[0]

    @pl.when(pl.program_id(0) == 0)
    def _():
        unpack_modes(packed_ref, wide, xl, tl)
        modes[...] = wide[...].reshape(rows, KQ).astype(BF16)

    field_ref[...] = (
        matmul(modes[...], build_ref[...]) + matmul(mixer_ref[...], grad_ref[...])
    ).astype(BF16)


def last(packed, grad, build_table, mixer, result, part, xl, tl):
    rows = grad.shape[0]
    width = 512
    kernel = functools.partial(last_kernel, xl, tl)
    operands = (packed, grad, build_table, mixer)
    specs = [
        pl.BlockSpec(packed.shape, lambda n: (0, 0, 0)),
        pl.BlockSpec((rows, width), lambda n: (0, n)),
        pl.BlockSpec((KQ, width), lambda n: (0, n)),
        pl.BlockSpec((rows, rows), lambda n: (0, 0)),
    ]
    aliases = {}
    if result is None:
        inner = kernel
        kernel = lambda *refs: inner(*refs[:4], None, *refs[4:])
    else:
        aliases = {len(operands): 0}
        operands += (result,)
        specs.append(pl.BlockSpec(memory_space=pl.ANY))
    return pl.pallas_call(
        kernel,
        grid=(CELLS // width,),
        in_specs=specs,
        out_specs=pl.BlockSpec((rows, width), lambda n: (part, n)),
        out_shape=jax.ShapeDtypeStruct((rows * PARTS, CELLS), BF16),
        scratch_shapes=[
            pltpu.VMEM((xl, tl, CHANS, KQ), F32),
            pltpu.VMEM((rows, KQ), BF16),
        ],
        input_output_aliases=aliases,
        compiler_params=vmem_params(56),
        cost_estimate=pl.CostEstimate(
            flops=2 * rows * CELLS * KQ, bytes_accessed=12 << 20, transcendentals=0
        ),
        name="last",
    )(*operands)


def swap(blocks):
    return lax.all_to_all(blocks, ("gx", "ta"), split_axis=0, concat_axis=0, tiled=True)


def sum_everywhere(values, devices):
    step = 1
    while step < devices:
        pairs = [(at, at ^ step) for at in range(devices)]
        values = values + lax.ppermute(values, ("gx", "ta"), pairs)
        step *= 2
    return values


def fast_body(gx, ta, features, cotangent, spec_weight, point_weight, bias_vector):
    _, xl_all, tl, _, cells = features.shape
    own = spec_weight.shape[4]
    devices = gx * ta
    xl = xl_all // PARTS
    rows = xl * tl * CHANS
    yz = np.kron(
        narrow(basis(NY, MY)).astype(np.float32), narrow(basis(NZ, MZ)).astype(np.float32)
    )
    build_table = jnp.asarray(narrow(yz))
    analyse_table = jnp.asarray(narrow(yz.T))
    x_split = basis(NX, MX).reshape(KX, gx, PARTS, xl)
    x_wide = [
        np.kron(x_split[:, :, part].reshape(KX, gx * xl), np.eye(CHANS)) for part in range(PARTS)
    ]
    t_wide = np.kron(basis(NT, MT), np.eye(own))
    x_in = jnp.asarray(narrow(np.stack(x_wide)))
    x_out = jnp.asarray(narrow(np.stack([table.T for table in x_wide])))
    t_in, t_out = jnp.asarray(narrow(t_wide.T)), jnp.asarray(narrow(t_wide))
    tables = (x_in, t_in, x_out, t_out)
    norm_scale = float(BATCH * NX * NT * NY * NZ) ** (-0.5)

    field = features.reshape(PARTS * rows, cells)
    cot = cotangent.reshape(PARTS * rows, cells)
    pick = np.tile(np.eye(CHANS, dtype=np.float32), (rows // CHANS, 1))
    same = np.kron(np.eye(rows // CHANS, dtype=np.float32), np.ones((CHANS, CHANS), np.float32))
    picked = jnp.asarray(narrow(pick))
    spread_point = matmul(matmul(picked, point_weight).astype(BF16), picked.T)
    spread_back = matmul(matmul(picked, point_weight.T).astype(BF16), picked.T)
    mixer = (spread_point * jnp.asarray(same)).astype(BF16)
    mixer_back = (spread_back * jnp.asarray(same)).astype(BF16)
    bias = jnp.dot(
        jnp.asarray(pick),
        jnp.broadcast_to(bias_vector[:, None], (CHANS, LANES)),
        precision=lax.Precision.HIGHEST,
    )
    spread_shape = (gx, ta, xl * CHANS, LANES)
    block_shape = (devices, xl * CHANS, LANES)

    packed_weight = pack_weight(spec_weight)
    spread_in = [
        swap(analyse(field, analyse_table, part, xl, tl, devices)).reshape(spread_shape)
        for part in range(PARTS)
    ]
    spectrum, *mixed = mix(spread_in, packed_weight, tables, False)
    output, sums = None, jnp.zeros((CHANS, LANES), F32)
    grads, spread_grad = [], []
    for part in range(PARTS):
        returned = swap(mixed[part].reshape(block_shape))
        output, grad, sent, sums = middle(
            returned,
            field,
            cot,
            (build_table, analyse_table),
            mixer,
            bias,
            sums,
            output,
            part,
            xl,
            tl,
        )
        grads.append(grad)
        spread_grad.append(swap(sent).reshape(spread_shape))
    summed = sum_everywhere(sums, devices) * norm_scale
    grad_modes, *mixed_back = mix(spread_grad, packed_weight, tables, True)
    grad_field = None
    for part in range(PARTS):
        grad_back = swap(mixed_back[part].reshape(block_shape))
        grad_field = last(
            grad_back, grads[part], build_table, mixer_back, grad_field, part, xl, tl
        )
    grad_spec = outer(spectrum, grad_modes, own)
    return (
        output.reshape(features.shape),
        grad_field.reshape(features.shape),
        grad_spec,
        summed[:, :CHANS],
        summed[:, CHANS],
    )


def analyse_yz(spatial, yz_table):
    return jnp.einsum(
        "qp,bxtcp->bxtcq", yz_table, spatial.astype(F32), precision=lax.Precision.HIGHEST
    )


def build_yz(modes_in, yz_table):
    return jnp.einsum(
        "qp,bxtcq->bxtcp", yz_table, modes_in.astype(F32), precision=lax.Precision.HIGHEST
    )


def analyse_xt(spread, table):
    sizes = spread.shape
    flattened = spread.reshape(sizes[0], sizes[1] * sizes[2], sizes[3] * sizes[4]).astype(F32)
    spectral = jnp.einsum("mp,bpr->bmr", table, flattened, precision=lax.Precision.HIGHEST)
    return spectral.reshape(sizes[0], KX, KT, sizes[3], sizes[4])


def synthesise_xt(modes_in, table):
    sizes = modes_in.shape
    flattened = modes_in.reshape(sizes[0], sizes[1] * sizes[2], sizes[3] * sizes[4])
    spatial = jnp.einsum("mp,bmr->bpr", table, flattened, precision=lax.Precision.HIGHEST)
    return spatial.reshape(sizes[0], NX, NT, sizes[3], sizes[4])


def to_owners(modes_in):
    first = lax.all_to_all(modes_in, "gx", split_axis=4, concat_axis=1, tiled=True)
    return lax.all_to_all(first, "ta", split_axis=4, concat_axis=2, tiled=True)


def to_cells(spread, shape):
    first = lax.all_to_all(
        spread[:, :, :, :, None, None, :], "gx", split_axis=1, concat_axis=4, tiled=True
    )
    second = lax.all_to_all(first, "ta", split_axis=2, concat_axis=5, tiled=True)
    return second.reshape(shape[:4] + (-1,))


def general_body(features, cotangent, spec_weight, point_weight, bias_vector):
    shape = features.shape
    yz_table = jnp.asarray(
        np.kron(narrow(basis(NY, MY)).astype(np.float32), narrow(basis(NZ, MZ)).astype(np.float32))
    )
    xt_table = jnp.asarray(np.kron(basis(NX, MX), basis(NT, MT)))
    norm_scale = float(BATCH * NX * NT * NY * NZ) ** (-0.5)
    highest = lax.Precision.HIGHEST
    spectrum = analyse_xt(to_owners(analyse_yz(features, yz_table).astype(BF16)), xt_table)
    mixed = jnp.einsum("bklip,kliop->bklop", spectrum, spec_weight, precision=highest)
    returned = to_cells(synthesise_xt(mixed, xt_table).astype(BF16), shape)
    pointwise = jnp.einsum("oi,bxtip->bxtop", point_weight, features, preferred_element_type=F32)
    pre = build_yz(returned, yz_table) + pointwise + bias_vector[:, None]
    integral = 0.5 * (1.0 + jax.scipy.special.erf(pre * 0.7071067811865476))
    output = (pre * integral).astype(BF16)
    slope = integral + pre * jnp.exp(-0.5 * pre * pre) * 0.3989422804014327
    grad_pre = (cotangent.astype(F32) * slope).astype(BF16)
    local_point = jnp.einsum("bxtop,bxtip->oi", grad_pre, features, preferred_element_type=F32)
    local_bias = jnp.sum(grad_pre.astype(F32), axis=(0, 1, 2, 4))
    total_point, total_bias = lax.psum((local_point, local_bias), ("gx", "ta"))
    grad_modes = analyse_xt(to_owners(analyse_yz(grad_pre, yz_table).astype(BF16)), xt_table)
    grad_spec = jnp.einsum("bklip,bklop->kliop", spectrum, grad_modes, precision=highest)
    grad_in = jnp.einsum("kliop,bklop->bklip", spec_weight, grad_modes, precision=highest)
    grad_back = to_cells(synthesise_xt(grad_in, xt_table).astype(BF16), shape)
    point_term = jnp.einsum("oi,bxtop->bxtip", point_weight, grad_pre, preferred_element_type=F32)
    grad_field = (build_yz(grad_back, yz_table) + point_term).astype(BF16)
    return (output, grad_field, grad_spec, total_point * norm_scale, total_bias * norm_scale)


def solution(mesh):
    split_field = P(None, "gx", "ta", None, None)
    split_weight = P(None, None, None, None, ("gx", "ta"))
    in_specs = (split_field, split_field, split_weight, P(), P())
    out_specs = (split_field, split_field, split_weight, P(), P())
    gx, ta = mesh.shape["gx"], mesh.shape["ta"]
    own, xl, tl = KQ // (gx * ta), NX // gx, NT // ta
    if own == 32 and xl * CHANS == LANES and tl == 4:
        body = functools.partial(fast_body, gx, ta)
    else:
        body = general_body
    return jax.shard_map(body, mesh=mesh, in_specs=in_specs, out_specs=out_specs, check_vma=False)
```

```python
import functools
import math

import jax
import jax.numpy as jnp
import ml_dtypes
import numpy as np
from jax import lax
from jax.experimental import pallas as pl
from jax.experimental.pallas import tpu as pltpu
from jax.sharding import PartitionSpec as P

NX = 128
NY = 128
NZ = 32
NT = 16
MX = 16
MY = 16
MZ = 16
MT = 8
BATCH = 1
KX = 32
KT = 16
CHANS = 8
CELLS = NY * NZ
KQ = 1024
LANES = 128
PARTS = 2
WIDTH = 512
LOG2_E = math.log2(math.e)
DENSITY = 1.0 / math.sqrt(2.0 * math.pi)
F32 = jnp.float32
BF16 = jnp.bfloat16


def basis(length, modes):
    frequency = np.concatenate([np.arange(modes + 1), np.arange(1, modes)])
    samples_at = np.arange(length)
    phases = (2.0 * math.pi / length) * (frequency[:, None] * samples_at[None, :] % length)
    cosine_row = np.arange(2 * modes) <= modes
    waves = np.where(cosine_row[:, None], np.cos(phases), np.sin(phases))
    at_edge = cosine_row & ((frequency == 0) | (2 * frequency == length))
    scales = np.where(at_edge, math.sqrt(1.0 / length), math.sqrt(2.0 / length))
    return (waves * scales[:, None]).astype(np.float32)


def narrow(table):
    return np.asarray(table, np.float32).astype(ml_dtypes.bfloat16)


def vmem_params(mebibytes):
    return pltpu.CompilerParams(vmem_limit_bytes=mebibytes * 1024 * 1024)


def matmul(left, right):
    return jnp.dot(left, right, preferred_element_type=F32)


def matmul_turned(left, right):
    return lax.dot_general(
        left, right, (((1,), (1,)), ((), ())), preferred_element_type=F32
    )


def swap_groups(tiles):
    rows = tiles[0].shape[0]
    lane = lax.broadcasted_iota(jnp.int32, (rows, LANES), 1)
    low_half = lane < 64
    even = (lane // 32) % 2 == 0
    first, second, third, fourth = tiles
    b0 = jnp.where(low_half, first, pltpu.roll(third, 64, 1))
    b2 = jnp.where(low_half, pltpu.roll(first, 64, 1), third)
    b1 = jnp.where(low_half, second, pltpu.roll(fourth, 64, 1))
    b3 = jnp.where(low_half, pltpu.roll(second, 64, 1), fourth)
    return (
        jnp.where(even, b0, pltpu.roll(b1, 32, 1)),
        jnp.where(even, pltpu.roll(b0, 96, 1), b1),
        jnp.where(even, b2, pltpu.roll(b3, 32, 1)),
        jnp.where(even, pltpu.roll(b2, 96, 1), b3),
    )


def pack_modes(modes_ref, packed_ref, xl, tl):
    for tile in range(KQ // LANES):
        modes = modes_ref[tile * LANES : (tile + 1) * LANES, :].T
        split = modes.reshape(xl, tl, CHANS, LANES)
        tiles = [split[:, step].reshape(xl * CHANS, LANES) for step in range(tl)]
        for owner, block in enumerate(swap_groups(tiles)):
            packed_ref[tile * tl + owner] = block.astype(BF16)


def unpack_modes(packed_ref, wide_ref, xl, tl):
    for tile in range(KQ // LANES):
        tiles = [packed_ref[tile * tl + owner].astype(F32) for owner in range(tl)]
        for step, block in enumerate(swap_groups(tiles)):
            wide_ref[:, step, :, tile * LANES : (tile + 1) * LANES] = block.reshape(
                xl, CHANS, LANES
            )


def analyse_kernel(xl, tl, field_ref, table_ref, packed_ref, total):
    step = pl.program_id(0)
    part = 0.0
    for at in range(table_ref.shape[0]):
        part = part + matmul_turned(
            table_ref[at], field_ref[:, at * WIDTH : (at + 1) * WIDTH]
        )

    @pl.when(step == 0)
    def _():
        total[...] = part

    @pl.when(step > 0)
    def _():
        total[...] += part

    @pl.when(step == pl.num_programs(0) - 1)
    def _():
        pack_modes(total, packed_ref, xl, tl)


def analyse(field, table, xl, tl, devices):
    rows = xl * tl * CHANS
    per = 2
    return pl.pallas_call(
        functools.partial(analyse_kernel, xl, tl),
        grid=(CELLS // (per * WIDTH),),
        in_specs=[
            pl.BlockSpec((rows, per * WIDTH), lambda n: (0, n)),
            pl.BlockSpec((per, KQ, WIDTH), lambda n: (n, 0, 0)),
        ],
        out_specs=pl.BlockSpec((devices, xl * CHANS, LANES), lambda n: (0, 0, 0)),
        out_shape=jax.ShapeDtypeStruct((devices, xl * CHANS, LANES), BF16),
        scratch_shapes=[pltpu.VMEM((KQ, rows), F32)],
        compiler_params=vmem_params(56),
        cost_estimate=pl.CostEstimate(
            flops=2 * rows * CELLS * KQ, bytes_accessed=13 << 20, transcendentals=0
        ),
        name="analyse",
    )(field, table)


def weight_kernel(weight_ref, packed_ref):
    for kx in range(weight_ref.shape[0]):
        for group in range(KT // 4):
            parts = [weight_ref[kx, 4 * group + k] for k in range(4)]
            packed_ref[kx, :, :, group * LANES : (group + 1) * LANES] = jnp.concatenate(
                parts, axis=-1
            )


def pack_weight(weight):
    per = 4
    own = weight.shape[4]
    return pl.pallas_call(
        weight_kernel,
        grid=(KX // per,),
        in_specs=[pl.BlockSpec((per, KT, CHANS, CHANS, own), lambda n: (n, 0, 0, 0, 0))],
        out_specs=pl.BlockSpec((per, CHANS, CHANS, KT * own), lambda n: (n, 0, 0, 0)),
        out_shape=jax.ShapeDtypeStruct((KX, CHANS, CHANS, KT * own), F32),
        compiler_params=vmem_params(56),
        cost_estimate=pl.CostEstimate(flops=1 << 20, bytes_accessed=20 << 20, transcendentals=0),
        name="pack_weight",
    )(weight)


def to_modes(spread_refs, x_table_ref, t_table_ref):
    total = 0.0
    for part, spread_ref in enumerate(spread_refs):
        gx, ta, rows, _ = spread_ref.shape
        beside = jnp.concatenate(
            [spread_ref[:, at].reshape(gx * rows, LANES) for at in range(ta)], axis=1
        )
        total = total + matmul(x_table_ref[part], beside)
    return matmul(total.astype(BF16), t_table_ref[...])


def from_modes(modes, x_table_ref, t_table_ref, held_ref):
    parts, gx, ta, rows, _ = held_ref.shape
    half = matmul(modes.astype(BF16), t_table_ref[...]).astype(BF16)
    for part in range(parts):
        full = matmul(x_table_ref[part], half).astype(BF16)
        for at in range(ta):
            held_ref[part, :, at] = full[:, at * LANES : (at + 1) * LANES].reshape(gx, rows, LANES)


def mix_kernel(
    backward,
    weight_ref,
    _,
    x_in_ref,
    t_in_ref,
    x_out_ref,
    t_out_ref,
    *refs,
):
    ins, outs = x_in_ref.shape[0], x_out_ref.shape[0]
    spread_refs, modes_ref, back_refs = refs[:ins], refs[ins], refs[ins + 1 : ins + 1 + outs]
    weight, modes, mixed, held, weight_sem, modes_sem, back_sems = refs[ins + 1 + outs :]
    fetch = pltpu.make_async_copy(weight_ref, weight, weight_sem)
    fetch.start()
    modes[...] = to_modes(spread_refs, x_in_ref, t_in_ref)
    keep = pltpu.make_async_copy(modes, modes_ref, modes_sem)
    keep.start()
    fetch.wait()
    for kx in range(KX):
        rows = slice(kx * CHANS, (kx + 1) * CHANS)
        own = modes[rows, :]
        if backward:
            sums = [jnp.sum(own * weight[kx, i], axis=0, keepdims=True) for i in range(CHANS)]
            mixed[rows, :] = jnp.concatenate(sums, axis=0)
        else:
            total = own[0:1, :] * weight[kx, 0]
            for i in range(1, CHANS):
                total = total + own[i : i + 1, :] * weight[kx, i]
            mixed[rows, :] = total
    from_modes(mixed[...], x_out_ref, t_out_ref, held)
    sends = [
        pltpu.make_async_copy(held.at[part], ref, back_sems.at[part])
        for part, ref in enumerate(back_refs)
    ]
    for send in sends:
        send.start()
    for send in sends:
        send.wait()
    keep.wait()


def mix(spreads, weight, after, tables, backward):
    modes = (KX * CHANS, weight.shape[3])
    gx, ta, _, lanes = spreads[0].shape
    outs = tables[2].shape[0]
    back = (gx, ta, tables[2].shape[1] // gx, lanes)
    anywhere = pl.BlockSpec(memory_space=pl.ANY)
    on_chip = pl.BlockSpec(memory_space=pltpu.VMEM)
    return pl.pallas_call(
        functools.partial(mix_kernel, backward),
        out_shape=[jax.ShapeDtypeStruct(modes, F32)] + [jax.ShapeDtypeStruct(back, BF16)] * outs,
        in_specs=[anywhere] * 2 + [on_chip] * (4 + len(spreads)),
        out_specs=[anywhere] * (1 + outs),
        scratch_shapes=[
            pltpu.VMEM(weight.shape, F32),
            pltpu.VMEM(modes, F32),
            pltpu.VMEM(modes, F32),
            pltpu.VMEM((outs,) + back, BF16),
            pltpu.SemaphoreType.DMA,
            pltpu.SemaphoreType.DMA,
            pltpu.SemaphoreType.DMA((outs,)),
        ],
        compiler_params=vmem_params(52),
        cost_estimate=pl.CostEstimate(flops=1 << 30, bytes_accessed=9 << 20, transcendentals=0),
        name="mix_back" if backward else "mix",
    )(weight, after, *tables, *spreads)


def outer_kernel(spectrum_ref, grad_ref, result_ref):
    own = result_ref.shape[4]
    for kx in range(result_ref.shape[0]):
        rows = slice(kx * CHANS, (kx + 1) * CHANS)
        for group in range(KT // 4):
            at = slice(group * LANES, (group + 1) * LANES)
            inputs = spectrum_ref[rows, at]
            grads = grad_ref[rows, at]
            for i in range(CHANS):
                product = inputs[i : i + 1, :] * grads
                for k in range(4):
                    result_ref[kx, 4 * group + k, i] = product[:, k * own : (k + 1) * own]


def outer(spectrum, grad, own):
    per = 4
    width = KT * own
    return pl.pallas_call(
        outer_kernel,
        grid=(KX // per,),
        in_specs=[pl.BlockSpec((per * CHANS, width), lambda n: (n, 0))] * 2,
        out_specs=pl.BlockSpec((per, KT, CHANS, CHANS, own), lambda n: (n, 0, 0, 0, 0)),
        out_shape=jax.ShapeDtypeStruct((KX, KT, CHANS, CHANS, own), F32),
        compiler_params=vmem_params(56),
        cost_estimate=pl.CostEstimate(flops=1 << 20, bytes_accessed=17 << 20, transcendentals=0),
        name="outer",
    )(spectrum, grad)


def normal_parts(values):
    scaled = 1.0 + 0.2316419 * jnp.abs(values)
    guess = pl.reciprocal(scaled, approx=True)
    t = guess * (2.0 - scaled * guess)
    decay = jnp.exp2(values * values * (-0.5 * LOG2_E))
    series = (1.330274429 * DENSITY) * t - 1.821255978 * DENSITY
    series = series * t + 1.781477937 * DENSITY
    series = series * t - 0.356563782 * DENSITY
    series = series * t + 0.319381530 * DENSITY
    tail = decay * (series * t)
    return jnp.where(values >= 0.0, 1.0 - tail, tail), decay


def middle_kernel(
    xl,
    tl,
    packed_ref,
    field_ref,
    cotangent_ref,
    table_ref,
    mixer_ref,
    bias_ref,
    sums_in_ref,
    _,
    output_ref,
    grad_ref,
    sent_ref,
    sums_ref,
    wide,
    modes,
    total,
    row_sums,
):
    step = pl.program_id(0)
    rows, width = field_ref.shape
    tile = 256
    chunk = 32

    @pl.when(step == 0)
    def _():
        unpack_modes(packed_ref, wide, xl, tl)
        modes[...] = wide[...].reshape(rows, KQ).astype(BF16)
        total[...] = jnp.zeros_like(total)
        row_sums[...] = jnp.zeros_like(row_sums)

    def build(at):
        return matmul(modes[...], table_ref[0, :, at]) + matmul(mixer_ref[...], field_ref[:, at])

    def pointwise(pre, at):
        for first in range(0, rows, chunk):
            part = slice(first, first + chunk)
            bias = bias_ref[part, :]
            values = pre[part, :] + jnp.concatenate([bias] * (tile // LANES), axis=1)
            integral, decay = normal_parts(values)
            output_ref[part, at] = (values * integral).astype(BF16)
            slope = integral + (values * DENSITY) * decay
            grad = (cotangent_ref[part, at].astype(F32) * slope).astype(BF16)
            grad_ref[part, at] = grad
            wide_grad = grad.astype(F32)
            sums = row_sums[part, :]
            for lanes in range(0, tile, LANES):
                sums = sums + wide_grad[:, lanes : lanes + LANES]
            row_sums[part, :] = sums

    def gather(at):
        passing = jnp.concatenate([table_ref[0, :, at], field_ref[:, at]], axis=0)
        total[...] += matmul_turned(passing, grad_ref[:, at])

    tiles = [slice(first, first + tile) for first in range(0, width, tile)]
    ready = build(tiles[0])
    for index, at in enumerate(tiles):
        pre = ready
        if index + 1 < len(tiles):
            ready = build(tiles[index + 1])
        pointwise(pre, at)
        if index % 2 == 1:
            gather(slice(tiles[index - 1].start, at.stop))

    @pl.when(step == pl.num_programs(0) - 1)
    def _():
        pack_modes(total, sent_ref, xl, tl)
        row = lax.broadcasted_iota(jnp.int32, (rows, rows), 0)
        column = lax.broadcasted_iota(jnp.int32, (rows, rows), 1)
        same = jnp.where(row // CHANS == column // CHANS, total[KQ:, :].T, 0.0)
        folded = jnp.sum(same.reshape(rows // CHANS, CHANS, rows), axis=0)
        source = lax.broadcasted_iota(jnp.int32, (rows, LANES), 0)
        target = lax.broadcasted_iota(jnp.int32, (rows, LANES), 1)
        select = jnp.where(source % CHANS == target, 1.0, 0.0)
        point = jnp.dot(
            folded, select, precision=lax.Precision.HIGHEST, preferred_element_type=F32
        )
        bias = jnp.sum(
            jnp.sum(row_sums[...].reshape(rows // CHANS, CHANS, LANES), axis=0),
            axis=1,
            keepdims=True,
        )
        lane = lax.broadcasted_iota(jnp.int32, (CHANS, LANES), 1)
        sums_ref[...] = sums_in_ref[...] + jnp.where(lane == CHANS, bias, point)


def middle(packed, field, cotangent, table, mixer, bias, sums, output, part, xl, tl):
    rows = xl * tl * CHANS
    width = WIDTH
    whole = lambda *shape: pl.BlockSpec(shape, lambda n: (0,) * len(shape))
    tile = pl.BlockSpec((rows, width), lambda n: (part, n))
    kernel = functools.partial(middle_kernel, xl, tl)
    operands = (packed, field, cotangent, table, mixer, bias, sums)
    specs = [
        whole(*packed.shape),
        tile,
        tile,
        pl.BlockSpec((1, KQ, width), lambda n: (n, 0, 0)),
        whole(rows, rows),
        whole(rows, LANES),
        whole(CHANS, LANES),
    ]
    aliases = {}
    if output is None:
        inner = kernel
        kernel = lambda *refs: inner(*refs[:7], None, *refs[7:])
    else:
        aliases = {len(operands): 0}
        operands += (output,)
        specs.append(pl.BlockSpec(memory_space=pl.ANY))
    return pl.pallas_call(
        kernel,
        grid=(CELLS // width,),
        in_specs=specs,
        out_specs=[
            tile,
            pl.BlockSpec((rows, width), lambda n: (0, n)),
            whole(*packed.shape),
            whole(CHANS, LANES),
        ],
        out_shape=(
            jax.ShapeDtypeStruct(field.shape, BF16),
            jax.ShapeDtypeStruct((rows, CELLS), BF16),
            jax.ShapeDtypeStruct(packed.shape, BF16),
            jax.ShapeDtypeStruct((CHANS, LANES), F32),
        ),
        scratch_shapes=[
            pltpu.VMEM((xl, tl, CHANS, KQ), F32),
            pltpu.VMEM((rows, KQ), BF16),
            pltpu.VMEM((KQ + rows, rows), F32),
            pltpu.VMEM((rows, LANES), F32),
        ],
        input_output_aliases=aliases,
        compiler_params=vmem_params(56),
        cost_estimate=pl.CostEstimate(
            flops=5 * rows * CELLS * KQ, bytes_accessed=26 << 20, transcendentals=rows * CELLS
        ),
        name="middle",
    )(*operands)


def last_kernel(xl, tl, packed_ref, table_ref, mixer_ref, *refs):
    grad_refs, (field_ref, wide, modes) = refs[:PARTS], refs[PARTS:]

    @pl.when(pl.program_id(0) == 0)
    def _():
        unpack_modes(packed_ref, wide, xl, tl)
        modes[...] = wide[...].reshape(modes.shape).astype(BF16)

    spatial = matmul(modes[...], table_ref[0])
    point = [matmul(mixer_ref[...], grad_ref[...]) for grad_ref in grad_refs]
    field_ref[...] = (spatial + jnp.concatenate(point, axis=0)).astype(BF16)


def last(packed, grads, table, mixer, xl, tl):
    rows = xl * tl * CHANS
    part = rows // PARTS
    return pl.pallas_call(
        functools.partial(last_kernel, xl, tl),
        grid=(CELLS // WIDTH,),
        in_specs=[
            pl.BlockSpec(packed.shape, lambda n: (0, 0, 0)),
            pl.BlockSpec((1, KQ, WIDTH), lambda n: (n, 0, 0)),
            pl.BlockSpec((part, part), lambda n: (0, 0)),
        ]
        + [pl.BlockSpec((part, WIDTH), lambda n: (0, n))] * PARTS,
        out_specs=pl.BlockSpec((rows, WIDTH), lambda n: (0, n)),
        out_shape=jax.ShapeDtypeStruct((rows, CELLS), BF16),
        scratch_shapes=[
            pltpu.VMEM((xl, tl, CHANS, KQ), F32),
            pltpu.VMEM((rows, KQ), BF16),
        ],
        compiler_params=vmem_params(56),
        cost_estimate=pl.CostEstimate(
            flops=2 * rows * CELLS * KQ, bytes_accessed=18 << 20, transcendentals=0
        ),
        name="last",
    )(packed, table, mixer, *grads)


def swap(blocks):
    return lax.all_to_all(blocks, ("gx", "ta"), split_axis=0, concat_axis=0, tiled=True)


def sum_everywhere(values, devices):
    step = 1
    while step < devices:
        pairs = [(at, at ^ step) for at in range(devices)]
        values = values + lax.ppermute(values, ("gx", "ta"), pairs)
        step *= 2
    return values


def fast_body(gx, ta, features, cotangent, spec_weight, point_weight, bias_vector):
    _, xl_all, tl, _, cells = features.shape
    own = spec_weight.shape[4]
    devices = gx * ta
    xl = xl_all // PARTS
    rows = xl * tl * CHANS
    yz = np.kron(
        narrow(basis(NY, MY)).astype(np.float32), narrow(basis(NZ, MZ)).astype(np.float32)
    )
    blocks = yz.reshape(KQ, CELLS // WIDTH, WIDTH).transpose(1, 0, 2)
    table = jnp.asarray(narrow(blocks))
    x_whole = basis(NX, MX).reshape(KX, gx, 1, xl_all)
    x_split = basis(NX, MX).reshape(KX, gx, PARTS, xl)
    x_tables = [
        np.stack(
            [
                np.kron(split[:, :, part].reshape(KX, -1), np.eye(CHANS))
                for part in range(split.shape[2])
            ]
        )
        for split in (x_whole, x_split)
    ]
    x_in = [jnp.asarray(narrow(x_table)) for x_table in x_tables]
    x_out = [jnp.asarray(narrow(x_table.transpose(0, 2, 1))) for x_table in x_tables]
    t_wide = np.kron(basis(NT, MT), np.eye(own))
    t_in, t_out = jnp.asarray(narrow(t_wide.T)), jnp.asarray(narrow(t_wide))
    norm_scale = float(BATCH * NX * NT * NY * NZ) ** (-0.5)

    field = features.reshape(PARTS * rows, cells)
    cot = cotangent.reshape(PARTS * rows, cells)
    pick = np.tile(np.eye(CHANS, dtype=np.float32), (rows // CHANS, 1))
    same = np.kron(np.eye(rows // CHANS, dtype=np.float32), np.ones((CHANS, CHANS), np.float32))
    picked = jnp.asarray(narrow(pick))
    spread_point = matmul(matmul(picked, point_weight).astype(BF16), picked.T)
    spread_back = matmul(matmul(picked, point_weight.T).astype(BF16), picked.T)
    mixer = (spread_point * jnp.asarray(same)).astype(BF16)
    mixer_back = (spread_back * jnp.asarray(same)).astype(BF16)
    bias = jnp.dot(
        jnp.asarray(pick),
        jnp.broadcast_to(bias_vector[:, None], (CHANS, LANES)),
        precision=lax.Precision.HIGHEST,
    )
    part_shape = (gx, ta, xl * CHANS, LANES)
    whole_shape = (gx, ta, xl_all * CHANS, LANES)
    packed_weight = pack_weight(spec_weight)
    sums = jnp.zeros((CHANS, LANES), F32)

    spread_in = swap(analyse(field, table, xl_all, tl, devices)).reshape(whole_shape)
    spectrum, *mixed = mix(
        [spread_in], packed_weight, sums, (x_in[0], t_in, x_out[1], t_out), False
    )
    output = None
    grads, spread_grad = [], []
    for part in range(PARTS):
        returned = swap(mixed[part].reshape(devices, xl * CHANS, LANES))
        output, grad, sent, sums = middle(
            returned, field, cot, table, mixer, bias, sums, output, part, xl, tl
        )
        grads.append(grad)
        spread_grad.append(swap(sent).reshape(part_shape))
    summed = sum_everywhere(sums, devices)
    grad_modes, mixed_back = mix(
        spread_grad, packed_weight, summed, (x_in[1], t_in, x_out[0], t_out), True
    )
    grad_back = swap(mixed_back.reshape(devices, xl_all * CHANS, LANES))
    grad_spec = outer(spectrum, grad_modes, own)
    grad_field = last(grad_back, grads, table, mixer_back, xl_all, tl)
    summed = summed * norm_scale
    return (
        output.reshape(features.shape),
        grad_field.reshape(features.shape),
        grad_spec,
        summed[:, :CHANS],
        summed[:, CHANS],
    )


def analyse_yz(spatial, yz_table):
    return jnp.einsum(
        "qp,bxtcp->bxtcq", yz_table, spatial.astype(F32), precision=lax.Precision.HIGHEST
    )


def build_yz(modes_in, yz_table):
    return jnp.einsum(
        "qp,bxtcq->bxtcp", yz_table, modes_in.astype(F32), precision=lax.Precision.HIGHEST
    )


def analyse_xt(spread, table):
    sizes = spread.shape
    flattened = spread.reshape(sizes[0], sizes[1] * sizes[2], sizes[3] * sizes[4]).astype(F32)
    spectral = jnp.einsum("mp,bpr->bmr", table, flattened, precision=lax.Precision.HIGHEST)
    return spectral.reshape(sizes[0], KX, KT, sizes[3], sizes[4])


def synthesise_xt(modes_in, table):
    sizes = modes_in.shape
    flattened = modes_in.reshape(sizes[0], sizes[1] * sizes[2], sizes[3] * sizes[4])
    spatial = jnp.einsum("mp,bmr->bpr", table, flattened, precision=lax.Precision.HIGHEST)
    return spatial.reshape(sizes[0], NX, NT, sizes[3], sizes[4])


def to_owners(modes_in):
    first = lax.all_to_all(modes_in, "gx", split_axis=4, concat_axis=1, tiled=True)
    return lax.all_to_all(first, "ta", split_axis=4, concat_axis=2, tiled=True)


def to_cells(spread, shape):
    first = lax.all_to_all(
        spread[:, :, :, :, None, None, :], "gx", split_axis=1, concat_axis=4, tiled=True
    )
    second = lax.all_to_all(first, "ta", split_axis=2, concat_axis=5, tiled=True)
    return second.reshape(shape[:4] + (-1,))


def general_body(features, cotangent, spec_weight, point_weight, bias_vector):
    shape = features.shape
    yz_table = jnp.asarray(
        np.kron(narrow(basis(NY, MY)).astype(np.float32), narrow(basis(NZ, MZ)).astype(np.float32))
    )
    xt_table = jnp.asarray(np.kron(basis(NX, MX), basis(NT, MT)))
    norm_scale = float(BATCH * NX * NT * NY * NZ) ** (-0.5)
    highest = lax.Precision.HIGHEST
    spectrum = analyse_xt(to_owners(analyse_yz(features, yz_table).astype(BF16)), xt_table)
    mixed = jnp.einsum("bklip,kliop->bklop", spectrum, spec_weight, precision=highest)
    returned = to_cells(synthesise_xt(mixed, xt_table).astype(BF16), shape)
    pointwise = jnp.einsum("oi,bxtip->bxtop", point_weight, features, preferred_element_type=F32)
    pre = build_yz(returned, yz_table) + pointwise + bias_vector[:, None]
    integral = 0.5 * (1.0 + jax.scipy.special.erf(pre * 0.7071067811865476))
    output = (pre * integral).astype(BF16)
    slope = integral + pre * jnp.exp(-0.5 * pre * pre) * 0.3989422804014327
    grad_pre = (cotangent.astype(F32) * slope).astype(BF16)
    local_point = jnp.einsum("bxtop,bxtip->oi", grad_pre, features, preferred_element_type=F32)
    local_bias = jnp.sum(grad_pre.astype(F32), axis=(0, 1, 2, 4))
    total_point, total_bias = lax.psum((local_point, local_bias), ("gx", "ta"))
    grad_modes = analyse_xt(to_owners(analyse_yz(grad_pre, yz_table).astype(BF16)), xt_table)
    grad_spec = jnp.einsum("bklip,bklop->kliop", spectrum, grad_modes, precision=highest)
    grad_in = jnp.einsum("kliop,bklop->bklip", spec_weight, grad_modes, precision=highest)
    grad_back = to_cells(synthesise_xt(grad_in, xt_table).astype(BF16), shape)
    point_term = jnp.einsum("oi,bxtop->bxtip", point_weight, grad_pre, preferred_element_type=F32)
    grad_field = (build_yz(grad_back, yz_table) + point_term).astype(BF16)
    return (output, grad_field, grad_spec, total_point * norm_scale, total_bias * norm_scale)


def solution(mesh):
    split_field = P(None, "gx", "ta", None, None)
    split_weight = P(None, None, None, None, ("gx", "ta"))
    in_specs = (split_field, split_field, split_weight, P(), P())
    out_specs = (split_field, split_field, split_weight, P(), P())
    gx, ta = mesh.shape["gx"], mesh.shape["ta"]
    own, xl, tl = KQ // (gx * ta), NX // gx, NT // ta
    if own == 32 and xl * CHANS == LANES and tl == 4:
        body = functools.partial(fast_body, gx, ta)
    else:
        body = general_body
    return jax.shard_map(body, mesh=mesh, in_specs=in_specs, out_specs=out_specs, check_vma=False)
```

```python
import functools
import math

import jax
import jax.numpy as jnp
import ml_dtypes
import numpy as np
from jax import lax
from jax.experimental import pallas as pl
from jax.experimental.pallas import tpu as pltpu
from jax.sharding import PartitionSpec as P

NX = 128
NY = 128
NZ = 32
NT = 16
MX = 16
MY = 16
MZ = 16
MT = 8
BATCH = 1
KX = 32
KT = 16
CHANS = 8
CELLS = NY * NZ
KQ = 1024
LANES = 128
PARTS = 2
WIDTH = 512
LOG2_E = math.log2(math.e)
DENSITY = 1.0 / math.sqrt(2.0 * math.pi)
F32 = jnp.float32
BF16 = jnp.bfloat16


def basis(length, modes):
    frequency = np.concatenate([np.arange(modes + 1), np.arange(1, modes)])
    samples_at = np.arange(length)
    phases = (2.0 * math.pi / length) * (frequency[:, None] * samples_at[None, :] % length)
    cosine_row = np.arange(2 * modes) <= modes
    waves = np.where(cosine_row[:, None], np.cos(phases), np.sin(phases))
    at_edge = cosine_row & ((frequency == 0) | (2 * frequency == length))
    scales = np.where(at_edge, math.sqrt(1.0 / length), math.sqrt(2.0 / length))
    return (waves * scales[:, None]).astype(np.float32)


def narrow(table):
    return np.asarray(table, np.float32).astype(ml_dtypes.bfloat16)


def vmem_params(mebibytes):
    return pltpu.CompilerParams(vmem_limit_bytes=mebibytes * 1024 * 1024)


def matmul(left, right):
    return jnp.dot(left, right, preferred_element_type=F32)


def matmul_turned(left, right):
    return lax.dot_general(
        left, right, (((1,), (1,)), ((), ())), preferred_element_type=F32
    )


def swap_groups(tiles):
    rows = tiles[0].shape[0]
    lane = lax.broadcasted_iota(jnp.int32, (rows, LANES), 1)
    low_half = lane < 64
    even = (lane // 32) % 2 == 0
    first, second, third, fourth = tiles
    b0 = jnp.where(low_half, first, pltpu.roll(third, 64, 1))
    b2 = jnp.where(low_half, pltpu.roll(first, 64, 1), third)
    b1 = jnp.where(low_half, second, pltpu.roll(fourth, 64, 1))
    b3 = jnp.where(low_half, pltpu.roll(second, 64, 1), fourth)
    return (
        jnp.where(even, b0, pltpu.roll(b1, 32, 1)),
        jnp.where(even, pltpu.roll(b0, 96, 1), b1),
        jnp.where(even, b2, pltpu.roll(b3, 32, 1)),
        jnp.where(even, pltpu.roll(b2, 96, 1), b3),
    )


def pack_modes(modes_ref, held_ref, packed_ref, sems, xl, tl):
    sends = []
    for tile in range(KQ // LANES):
        modes = modes_ref[tile * LANES : (tile + 1) * LANES, :].T
        split = modes.reshape(xl, tl, CHANS, LANES)
        tiles = [split[:, step].reshape(xl * CHANS, LANES) for step in range(tl)]
        owners = slice(tile * tl, (tile + 1) * tl)
        held_ref[owners] = jnp.stack([block.astype(BF16) for block in swap_groups(tiles)])
        send = pltpu.make_async_copy(held_ref.at[owners], packed_ref.at[owners], sems.at[tile])
        send.start()
        sends.append(send)
    for send in sends:
        send.wait()


def unpack_modes(packed_ref, wide_ref, xl, tl):
    for tile in range(KQ // LANES):
        tiles = [packed_ref[tile * tl + owner].astype(F32) for owner in range(tl)]
        for step, block in enumerate(swap_groups(tiles)):
            wide_ref[:, step, :, tile * LANES : (tile + 1) * LANES] = block.reshape(
                xl, CHANS, LANES
            )


def analyse_kernel(
    xl, tl, field_ref, table_ref, packed_ref, field, table, total, held, field_sems, table_sems, sems
):
    chunks = table.shape[0]
    ahead = 4
    fetches = []
    for at in range(chunks):
        lanes = slice(at * WIDTH, (at + 1) * WIDTH)
        fetches.append(
            (
                pltpu.make_async_copy(field_ref.at[:, lanes], field.at[at], field_sems.at[at]),
                pltpu.make_async_copy(table_ref.at[at], table.at[at], table_sems.at[at]),
            )
        )

    def start(at):
        for fetch in fetches[at]:
            fetch.start()

    for at in range(ahead):
        start(at)
    for at in range(0, chunks, 2):
        for now in (at, at + 1):
            for fetch in fetches[now]:
                fetch.wait()
            if now + ahead < chunks:
                start(now + ahead)
        part = matmul_turned(
            jnp.concatenate([table[at], table[at + 1]], axis=1),
            jnp.concatenate([field[at], field[at + 1]], axis=1),
        )
        total[...] = part if at == 0 else total[...] + part
    pack_modes(total, held, packed_ref, sems, xl, tl)


def analyse(field, table, xl, tl, devices):
    rows = xl * tl * CHANS
    chunks = CELLS // WIDTH
    packed = (devices, xl * CHANS, LANES)
    return pl.pallas_call(
        functools.partial(analyse_kernel, xl, tl),
        in_specs=[pl.BlockSpec(memory_space=pltpu.HBM)] * 2,
        out_specs=pl.BlockSpec(memory_space=pl.ANY),
        out_shape=jax.ShapeDtypeStruct(packed, BF16),
        scratch_shapes=[
            pltpu.VMEM((chunks, rows, WIDTH), BF16),
            pltpu.VMEM((chunks, KQ, WIDTH), BF16),
            pltpu.VMEM((KQ, rows), F32),
            pltpu.VMEM(packed, BF16),
            pltpu.SemaphoreType.DMA((chunks,)),
            pltpu.SemaphoreType.DMA((chunks,)),
            pltpu.SemaphoreType.DMA((KQ // LANES,)),
        ],
        compiler_params=vmem_params(44),
        cost_estimate=pl.CostEstimate(
            flops=2 * rows * CELLS * KQ, bytes_accessed=13 << 20, transcendentals=0
        ),
        name="analyse",
    )(field, table)


def weight_kernel(weight_ref, packed_ref):
    for kx in range(weight_ref.shape[0]):
        for group in range(KT // 4):
            parts = [weight_ref[kx, 4 * group + k] for k in range(4)]
            packed_ref[kx, :, :, group * LANES : (group + 1) * LANES] = jnp.concatenate(
                parts, axis=-1
            )


def pack_weight(weight):
    per = 4
    own = weight.shape[4]
    return pl.pallas_call(
        weight_kernel,
        grid=(KX // per,),
        in_specs=[pl.BlockSpec((per, KT, CHANS, CHANS, own), lambda n: (n, 0, 0, 0, 0))],
        out_specs=pl.BlockSpec((per, CHANS, CHANS, KT * own), lambda n: (n, 0, 0, 0)),
        out_shape=jax.ShapeDtypeStruct((KX, CHANS, CHANS, KT * own), F32),
        compiler_params=vmem_params(44),
        cost_estimate=pl.CostEstimate(flops=1 << 20, bytes_accessed=20 << 20, transcendentals=0),
        name="pack_weight",
    )(weight)


def to_modes(spread_refs, x_table_ref, t_table_ref):
    total = 0.0
    for part, spread_ref in enumerate(spread_refs):
        gx, ta, rows, _ = spread_ref.shape
        beside = jnp.concatenate(
            [spread_ref[:, at].reshape(gx * rows, LANES) for at in range(ta)], axis=1
        )
        total = total + matmul(x_table_ref[part], beside)
    return matmul(total.astype(BF16), t_table_ref[...])


def from_modes(modes, x_table_ref, t_table_ref, held_ref):
    parts, gx, ta, rows, _ = held_ref.shape
    half = matmul(modes.astype(BF16), t_table_ref[...]).astype(BF16)
    for part in range(parts):
        full = matmul(x_table_ref[part], half).astype(BF16)
        for at in range(ta):
            held_ref[part, :, at] = full[:, at * LANES : (at + 1) * LANES].reshape(gx, rows, LANES)


def mix_kernel(
    backward,
    weight_ref,
    _,
    x_in_ref,
    t_in_ref,
    x_out_ref,
    t_out_ref,
    *refs,
):
    ins, outs = x_in_ref.shape[0], x_out_ref.shape[0]
    spread_refs, modes_ref, back_refs = refs[:ins], refs[ins], refs[ins + 1 : ins + 1 + outs]
    weight, modes, mixed, held, x_in, t_in, x_out, t_out, sems, weight_sems, back_sems = refs[
        ins + 1 + outs :
    ]
    pieces = weight_sems.shape[0]
    per = KX // pieces
    sources = (x_in_ref, t_in_ref, t_out_ref, x_out_ref)
    tables = [
        pltpu.make_async_copy(source, target, sems.at[at])
        for at, (source, target) in enumerate(zip(sources, (x_in, t_in, t_out, x_out)))
    ]
    fetches = []
    for at in range(pieces):
        part = slice(at * per, (at + 1) * per)
        fetches.append(
            pltpu.make_async_copy(weight_ref.at[part], weight.at[part], weight_sems.at[at])
        )
    for copy in tables[:2] + fetches + tables[2:]:
        copy.start()
    tables[0].wait()
    tables[1].wait()
    modes[...] = to_modes(spread_refs, x_in, t_in)
    keep = pltpu.make_async_copy(modes, modes_ref, sems.at[4])
    keep.start()
    for fetch in fetches:
        fetch.wait()
    for kx in range(KX):
        rows = slice(kx * CHANS, (kx + 1) * CHANS)
        own = modes[rows, :]
        if backward:
            sums = [jnp.sum(own * weight[kx, i], axis=0, keepdims=True) for i in range(CHANS)]
            mixed[rows, :] = jnp.concatenate(sums, axis=0)
        else:
            total = own[0:1, :] * weight[kx, 0]
            for i in range(1, CHANS):
                total = total + own[i : i + 1, :] * weight[kx, i]
            mixed[rows, :] = total
    tables[2].wait()
    tables[3].wait()
    from_modes(mixed[...], x_out, t_out, held)
    sends = [
        pltpu.make_async_copy(held.at[part], ref, back_sems.at[part])
        for part, ref in enumerate(back_refs)
    ]
    for send in sends:
        send.start()
    for send in sends:
        send.wait()
    keep.wait()


def mix(spreads, weight, after, tables, backward):
    modes = (KX * CHANS, weight.shape[3])
    gx, ta, _, lanes = spreads[0].shape
    outs = tables[2].shape[0]
    back = (gx, ta, tables[2].shape[1] // gx, lanes)
    anywhere = pl.BlockSpec(memory_space=pl.ANY)
    on_chip = pl.BlockSpec(memory_space=pltpu.VMEM)
    apart = pl.BlockSpec(memory_space=pltpu.HBM)
    return pl.pallas_call(
        functools.partial(mix_kernel, backward),
        out_shape=[jax.ShapeDtypeStruct(modes, F32)] + [jax.ShapeDtypeStruct(back, BF16)] * outs,
        in_specs=[apart] + [anywhere] + [apart] * 4 + [on_chip] * len(spreads),
        out_specs=[apart] + [anywhere] * outs,
        scratch_shapes=[
            pltpu.VMEM(weight.shape, F32),
            pltpu.VMEM(modes, F32),
            pltpu.VMEM(modes, F32),
            pltpu.VMEM((outs,) + back, BF16),
            *[pltpu.VMEM(table.shape, BF16) for table in tables],
            pltpu.SemaphoreType.DMA((5,)),
            pltpu.SemaphoreType.DMA((8,)),
            pltpu.SemaphoreType.DMA((outs,)),
        ],
        compiler_params=vmem_params(40),
        cost_estimate=pl.CostEstimate(flops=1 << 30, bytes_accessed=9 << 20, transcendentals=0),
        name="mix_back" if backward else "mix",
    )(weight, after, *tables, *spreads)


def outer_kernel(spectrum_ref, grad_ref, result_ref):
    own = result_ref.shape[4]
    for kx in range(result_ref.shape[0]):
        rows = slice(kx * CHANS, (kx + 1) * CHANS)
        for group in range(KT // 4):
            at = slice(group * LANES, (group + 1) * LANES)
            inputs = spectrum_ref[rows, at]
            grads = grad_ref[rows, at]
            for i in range(CHANS):
                product = inputs[i : i + 1, :] * grads
                for k in range(4):
                    result_ref[kx, 4 * group + k, i] = product[:, k * own : (k + 1) * own]


def outer(spectrum, grad, own):
    per = 4
    width = KT * own
    return pl.pallas_call(
        outer_kernel,
        grid=(KX // per,),
        in_specs=[pl.BlockSpec((per * CHANS, width), lambda n: (n, 0))] * 2,
        out_specs=pl.BlockSpec((per, KT, CHANS, CHANS, own), lambda n: (n, 0, 0, 0, 0)),
        out_shape=jax.ShapeDtypeStruct((KX, KT, CHANS, CHANS, own), F32),
        compiler_params=vmem_params(44),
        cost_estimate=pl.CostEstimate(flops=1 << 20, bytes_accessed=17 << 20, transcendentals=0),
        name="outer",
    )(spectrum, grad)


def normal_parts(values):
    scaled = 1.0 + 0.2316419 * jnp.abs(values)
    guess = pl.reciprocal(scaled, approx=True)
    t = guess * (2.0 - scaled * guess)
    decay = jnp.exp2(values * values * (-0.5 * LOG2_E))
    series = (1.330274429 * DENSITY) * t - 1.821255978 * DENSITY
    series = series * t + 1.781477937 * DENSITY
    series = series * t - 0.356563782 * DENSITY
    series = series * t + 0.319381530 * DENSITY
    tail = decay * (series * t)
    return jnp.where(values >= 0.0, 1.0 - tail, tail), decay


def middle_kernel(
    xl,
    tl,
    packed_ref,
    field_ref,
    cotangent_ref,
    table_ref,
    mixer_ref,
    bias_ref,
    sums_in_ref,
    _,
    output_ref,
    grad_ref,
    sent_ref,
    sums_ref,
    wide,
    modes,
    total,
    table,
    held,
    table_sems,
    sems,
):
    step = pl.program_id(0)
    rows, width = field_ref.shape
    tile = 256
    chunk = 32
    chunks = table.shape[0]
    ahead = 3
    ones = 16

    def fetch(at):
        return pltpu.make_async_copy(table_ref.at[at], table.at[at], table_sems.at[at])

    @pl.when(step == 0)
    def _():
        for at in range(ahead):
            fetch(at).start()
        unpack_modes(packed_ref, wide, xl, tl)
        modes[...] = wide[...].reshape(rows, KQ).astype(BF16)
        total[...] = jnp.zeros_like(total)

    @pl.when(step + ahead < chunks)
    def _():
        fetch(step + ahead).start()

    fetch(step).wait()

    passing = jnp.concatenate(
        [table[step], field_ref[...], jnp.ones((ones, width), BF16)], axis=0
    )
    cotangent = cotangent_ref[...]
    biases = jnp.concatenate([bias_ref[...]] * (tile // LANES), axis=1)
    pre = [
        matmul(modes[...], table[step, :, at : at + tile])
        + matmul(mixer_ref[...], field_ref[:, at : at + tile])
        for at in range(0, width, tile)
    ]
    results, grads = [], []
    for index, at in enumerate(range(0, width, tile)):
        results.append([])
        grads.append([])
        for first in range(0, rows, chunk):
            part = slice(first, first + chunk)
            values = pre[index][part] + biases[part]
            integral, decay = normal_parts(values)
            results[-1].append((values * integral).astype(BF16))
            slope = integral + (values * DENSITY) * decay
            wide_cotangent = cotangent[part, at : at + tile].astype(F32)
            grads[-1].append((wide_cotangent * slope).astype(BF16))
    grad = jnp.concatenate([jnp.concatenate(column, axis=0) for column in grads], axis=1)
    output_ref[...] = jnp.concatenate(
        [jnp.concatenate(column, axis=0) for column in results], axis=1
    )
    grad_ref[...] = grad
    total[...] += matmul_turned(passing, grad)

    @pl.when(step == pl.num_programs(0) - 1)
    def _():
        pack_modes(total, held, sent_ref, sems, xl, tl)
        row = lax.broadcasted_iota(jnp.int32, (rows, rows), 0)
        column = lax.broadcasted_iota(jnp.int32, (rows, rows), 1)
        gram = total[KQ : KQ + rows, :].T
        bias = total[KQ + rows : KQ + rows + CHANS, :]
        same = jnp.where(row // CHANS == column // CHANS, gram, 0.0)
        folded = jnp.sum(same.reshape(rows // CHANS, CHANS, rows), axis=0)
        source = lax.broadcasted_iota(jnp.int32, (rows, LANES), 0)
        target = lax.broadcasted_iota(jnp.int32, (rows, LANES), 1)
        select = jnp.where(source % CHANS == target, 1.0, 0.0)
        chan = lax.broadcasted_iota(jnp.int32, (CHANS, rows), 0)
        place = lax.broadcasted_iota(jnp.int32, (CHANS, rows), 1)
        own_bias = jnp.sum(
            jnp.where(place % CHANS == chan, bias, 0.0), axis=1, keepdims=True
        )
        point = jnp.dot(
            folded, select, precision=lax.Precision.HIGHEST, preferred_element_type=F32
        )
        lane = lax.broadcasted_iota(jnp.int32, (CHANS, LANES), 1)
        sums_ref[...] = sums_in_ref[...] + jnp.where(lane == CHANS, own_bias, point)


def middle(packed, field, cotangent, table, mixer, bias, sums, output, part, xl, tl):
    rows = xl * tl * CHANS
    width = WIDTH
    chunks = CELLS // width
    whole = lambda *shape: pl.BlockSpec(shape, lambda n: (0,) * len(shape))
    tile = pl.BlockSpec((rows, width), lambda n: (part, n))
    kernel = functools.partial(middle_kernel, xl, tl)
    operands = (packed, field, cotangent, table, mixer, bias, sums)
    specs = [
        pl.BlockSpec(memory_space=pltpu.VMEM),
        tile,
        tile,
        pl.BlockSpec(memory_space=pltpu.HBM),
        whole(rows, rows),
        whole(rows, LANES),
        whole(CHANS, LANES),
    ]
    aliases = {}
    if output is None:
        inner = kernel
        kernel = lambda *refs: inner(*refs[:7], None, *refs[7:])
    else:
        aliases = {len(operands): 0}
        operands += (output,)
        specs.append(pl.BlockSpec(memory_space=pltpu.HBM))
    return pl.pallas_call(
        kernel,
        grid=(chunks,),
        in_specs=specs,
        out_specs=[
            tile,
            pl.BlockSpec((rows, width), lambda n: (0, n)),
            pl.BlockSpec(memory_space=pl.ANY),
            whole(CHANS, LANES),
        ],
        out_shape=(
            jax.ShapeDtypeStruct(field.shape, BF16),
            jax.ShapeDtypeStruct((rows, CELLS), BF16),
            jax.ShapeDtypeStruct(packed.shape, BF16),
            jax.ShapeDtypeStruct((CHANS, LANES), F32),
        ),
        scratch_shapes=[
            pltpu.VMEM((xl, tl, CHANS, KQ), F32),
            pltpu.VMEM((rows, KQ), BF16),
            pltpu.VMEM((KQ + rows + 16, rows), F32),
            pltpu.VMEM((chunks, KQ, width), BF16),
            pltpu.VMEM(packed.shape, BF16),
            pltpu.SemaphoreType.DMA((chunks,)),
            pltpu.SemaphoreType.DMA((KQ // LANES,)),
        ],
        input_output_aliases=aliases,
        compiler_params=vmem_params(44),
        cost_estimate=pl.CostEstimate(
            flops=5 * rows * CELLS * KQ, bytes_accessed=18 << 20, transcendentals=rows * CELLS
        ),
        name="middle",
    )(*operands)


def last_kernel(
    xl,
    tl,
    packed_ref,
    mixer_ref,
    table_ref,
    *refs,
):
    grad_refs, field_ref = refs[:PARTS], refs[PARTS]
    wide, modes, table, grads, field, table_sems, grad_sems, field_sems = refs[PARTS + 1 :]
    chunks = table.shape[0]
    ahead = 4
    fetches, sends = [], []
    for at in range(chunks):
        lanes = slice(at * WIDTH, (at + 1) * WIDTH)
        fetches.append([pltpu.make_async_copy(table_ref.at[at], table.at[at], table_sems.at[at])])
        for part, grad_ref in enumerate(grad_refs):
            fetches[at].append(
                pltpu.make_async_copy(
                    grad_ref.at[:, lanes], grads.at[at, part], grad_sems.at[at, part]
                )
            )
        sends.append(
            pltpu.make_async_copy(field.at[at], field_ref.at[:, lanes], field_sems.at[at])
        )

    def start(at):
        for fetch in fetches[at]:
            fetch.start()

    for at in range(ahead):
        start(at)
    unpack_modes(packed_ref, wide, xl, tl)
    modes[...] = wide[...].reshape(modes.shape).astype(BF16)
    for at in range(chunks):
        for fetch in fetches[at]:
            fetch.wait()
        if at + ahead < chunks:
            start(at + ahead)
        point = [matmul(mixer_ref[...], grads[at, part]) for part in range(PARTS)]
        field[at] = (
            matmul(modes[...], table[at]) + jnp.concatenate(point, axis=0)
        ).astype(BF16)
        sends[at].start()
    for send in sends:
        send.wait()


def last(packed, grads, table, mixer, xl, tl):
    rows = xl * tl * CHANS
    part = rows // PARTS
    chunks = CELLS // WIDTH
    apart = pl.BlockSpec(memory_space=pltpu.HBM)
    on_chip = pl.BlockSpec(memory_space=pltpu.VMEM)
    return pl.pallas_call(
        functools.partial(last_kernel, xl, tl),
        in_specs=[on_chip] * 2 + [apart] * (1 + PARTS),
        out_specs=apart,
        out_shape=jax.ShapeDtypeStruct((rows, CELLS), BF16),
        scratch_shapes=[
            pltpu.VMEM((xl, tl, CHANS, KQ), F32),
            pltpu.VMEM((rows, KQ), BF16),
            pltpu.VMEM((chunks, KQ, WIDTH), BF16),
            pltpu.VMEM((chunks, PARTS, part, WIDTH), BF16),
            pltpu.VMEM((chunks, rows, WIDTH), BF16),
            pltpu.SemaphoreType.DMA((chunks,)),
            pltpu.SemaphoreType.DMA((chunks, PARTS)),
            pltpu.SemaphoreType.DMA((chunks,)),
        ],
        compiler_params=vmem_params(44),
        cost_estimate=pl.CostEstimate(
            flops=2 * rows * CELLS * KQ, bytes_accessed=18 << 20, transcendentals=0
        ),
        name="last",
    )(packed, mixer, table, *grads)


def swap(blocks):
    return lax.all_to_all(blocks, ("gx", "ta"), split_axis=0, concat_axis=0, tiled=True)


def sum_everywhere(values, devices):
    step = 1
    while step < devices:
        pairs = [(at, at ^ step) for at in range(devices)]
        values = values + lax.ppermute(values, ("gx", "ta"), pairs)
        step *= 2
    return values


def fast_body(gx, ta, features, cotangent, spec_weight, point_weight, bias_vector):
    _, xl_all, tl, _, cells = features.shape
    own = spec_weight.shape[4]
    devices = gx * ta
    xl = xl_all // PARTS
    rows = xl * tl * CHANS
    yz = np.kron(
        narrow(basis(NY, MY)).astype(np.float32), narrow(basis(NZ, MZ)).astype(np.float32)
    )
    blocks = yz.reshape(KQ, CELLS // WIDTH, WIDTH).transpose(1, 0, 2)
    table = jnp.asarray(narrow(blocks))
    x_whole = basis(NX, MX).reshape(KX, gx, 1, xl_all)
    x_split = basis(NX, MX).reshape(KX, gx, PARTS, xl)
    x_tables = [
        np.stack(
            [
                np.kron(split[:, :, part].reshape(KX, -1), np.eye(CHANS))
                for part in range(split.shape[2])
            ]
        )
        for split in (x_whole, x_split)
    ]
    x_in = [jnp.asarray(narrow(x_table)) for x_table in x_tables]
    x_out = [jnp.asarray(narrow(x_table.transpose(0, 2, 1))) for x_table in x_tables]
    t_wide = np.kron(basis(NT, MT), np.eye(own))
    t_in, t_out = jnp.asarray(narrow(t_wide.T)), jnp.asarray(narrow(t_wide))
    norm_scale = float(BATCH * NX * NT * NY * NZ) ** (-0.5)

    field = features.reshape(PARTS * rows, cells)
    cot = cotangent.reshape(PARTS * rows, cells)
    pick = np.tile(np.eye(CHANS, dtype=np.float32), (rows // CHANS, 1))
    same = np.kron(np.eye(rows // CHANS, dtype=np.float32), np.ones((CHANS, CHANS), np.float32))
    picked = jnp.asarray(narrow(pick))
    spread_point = matmul(matmul(picked, point_weight).astype(BF16), picked.T)
    spread_back = matmul(matmul(picked, point_weight.T).astype(BF16), picked.T)
    mixer = (spread_point * jnp.asarray(same)).astype(BF16)
    mixer_back = (spread_back * jnp.asarray(same)).astype(BF16)
    bias = jnp.dot(
        jnp.asarray(pick),
        jnp.broadcast_to(bias_vector[:, None], (CHANS, LANES)),
        precision=lax.Precision.HIGHEST,
    )
    part_shape = (gx, ta, xl * CHANS, LANES)
    whole_shape = (gx, ta, xl_all * CHANS, LANES)
    packed_weight = pack_weight(spec_weight)
    sums = jnp.zeros((CHANS, LANES), F32)

    spread_in = swap(analyse(field, table, xl_all, tl, devices)).reshape(whole_shape)
    spectrum, *mixed = mix(
        [spread_in], packed_weight, sums, (x_in[0], t_in, x_out[1], t_out), False
    )
    output = None
    grads, spread_grad = [], []
    for part in range(PARTS):
        returned = swap(mixed[part].reshape(devices, xl * CHANS, LANES))
        output, grad, sent, sums = middle(
            returned, field, cot, table, mixer, bias, sums, output, part, xl, tl
        )
        grads.append(grad)
        spread_grad.append(swap(sent).reshape(part_shape))
    summed = sum_everywhere(sums, devices)
    grad_modes, mixed_back = mix(
        spread_grad, packed_weight, summed, (x_in[1], t_in, x_out[0], t_out), True
    )
    grad_back = swap(mixed_back.reshape(devices, xl_all * CHANS, LANES))
    grad_spec = outer(spectrum, grad_modes, own)
    grad_field = last(grad_back, grads, table, mixer_back, xl_all, tl)
    summed = summed * norm_scale
    return (
        output.reshape(features.shape),
        grad_field.reshape(features.shape),
        grad_spec,
        summed[:, :CHANS],
        summed[:, CHANS],
    )


def analyse_yz(spatial, yz_table):
    return jnp.einsum(
        "qp,bxtcp->bxtcq", yz_table, spatial.astype(F32), precision=lax.Precision.HIGHEST
    )


def build_yz(modes_in, yz_table):
    return jnp.einsum(
        "qp,bxtcq->bxtcp", yz_table, modes_in.astype(F32), precision=lax.Precision.HIGHEST
    )


def analyse_xt(spread, table):
    sizes = spread.shape
    flattened = spread.reshape(sizes[0], sizes[1] * sizes[2], sizes[3] * sizes[4]).astype(F32)
    spectral = jnp.einsum("mp,bpr->bmr", table, flattened, precision=lax.Precision.HIGHEST)
    return spectral.reshape(sizes[0], KX, KT, sizes[3], sizes[4])


def synthesise_xt(modes_in, table):
    sizes = modes_in.shape
    flattened = modes_in.reshape(sizes[0], sizes[1] * sizes[2], sizes[3] * sizes[4])
    spatial = jnp.einsum("mp,bmr->bpr", table, flattened, precision=lax.Precision.HIGHEST)
    return spatial.reshape(sizes[0], NX, NT, sizes[3], sizes[4])


def to_owners(modes_in):
    first = lax.all_to_all(modes_in, "gx", split_axis=4, concat_axis=1, tiled=True)
    return lax.all_to_all(first, "ta", split_axis=4, concat_axis=2, tiled=True)


def to_cells(spread, shape):
    first = lax.all_to_all(
        spread[:, :, :, :, None, None, :], "gx", split_axis=1, concat_axis=4, tiled=True
    )
    second = lax.all_to_all(first, "ta", split_axis=2, concat_axis=5, tiled=True)
    return second.reshape(shape[:4] + (-1,))


def general_body(features, cotangent, spec_weight, point_weight, bias_vector):
    shape = features.shape
    yz_table = jnp.asarray(
        np.kron(narrow(basis(NY, MY)).astype(np.float32), narrow(basis(NZ, MZ)).astype(np.float32))
    )
    xt_table = jnp.asarray(np.kron(basis(NX, MX), basis(NT, MT)))
    norm_scale = float(BATCH * NX * NT * NY * NZ) ** (-0.5)
    highest = lax.Precision.HIGHEST
    spectrum = analyse_xt(to_owners(analyse_yz(features, yz_table).astype(BF16)), xt_table)
    mixed = jnp.einsum("bklip,kliop->bklop", spectrum, spec_weight, precision=highest)
    returned = to_cells(synthesise_xt(mixed, xt_table).astype(BF16), shape)
    pointwise = jnp.einsum("oi,bxtip->bxtop", point_weight, features, preferred_element_type=F32)
    pre = build_yz(returned, yz_table) + pointwise + bias_vector[:, None]
    integral = 0.5 * (1.0 + jax.scipy.special.erf(pre * 0.7071067811865476))
    output = (pre * integral).astype(BF16)
    slope = integral + pre * jnp.exp(-0.5 * pre * pre) * 0.3989422804014327
    grad_pre = (cotangent.astype(F32) * slope).astype(BF16)
    local_point = jnp.einsum("bxtop,bxtip->oi", grad_pre, features, preferred_element_type=F32)
    local_bias = jnp.sum(grad_pre.astype(F32), axis=(0, 1, 2, 4))
    total_point, total_bias = lax.psum((local_point, local_bias), ("gx", "ta"))
    grad_modes = analyse_xt(to_owners(analyse_yz(grad_pre, yz_table).astype(BF16)), xt_table)
    grad_spec = jnp.einsum("bklip,bklop->kliop", spectrum, grad_modes, precision=highest)
    grad_in = jnp.einsum("kliop,bklop->bklip", spec_weight, grad_modes, precision=highest)
    grad_back = to_cells(synthesise_xt(grad_in, xt_table).astype(BF16), shape)
    point_term = jnp.einsum("oi,bxtop->bxtip", point_weight, grad_pre, preferred_element_type=F32)
    grad_field = (build_yz(grad_back, yz_table) + point_term).astype(BF16)
    return (output, grad_field, grad_spec, total_point * norm_scale, total_bias * norm_scale)


def solution(mesh):
    split_field = P(None, "gx", "ta", None, None)
    split_weight = P(None, None, None, None, ("gx", "ta"))
    in_specs = (split_field, split_field, split_weight, P(), P())
    out_specs = (split_field, split_field, split_weight, P(), P())
    gx, ta = mesh.shape["gx"], mesh.shape["ta"]
    own, xl, tl = KQ // (gx * ta), NX // gx, NT // ta
    if own == 32 and xl * CHANS == LANES and tl == 4:
        body = functools.partial(fast_body, gx, ta)
    else:
        body = general_body
    return jax.shard_map(body, mesh=mesh, in_specs=in_specs, out_specs=out_specs, check_vma=False)
```

```python
import functools
import math

import jax
import jax.numpy as jnp
import ml_dtypes
import numpy as np
from jax import lax
from jax.experimental import pallas as pl
from jax.experimental.pallas import tpu as pltpu
from jax.sharding import PartitionSpec as P

NX = 128
NY = 128
NZ = 32
NT = 16
MX = 16
MY = 16
MZ = 16
MT = 8
BATCH = 1
KX = 32
KT = 16
CHANS = 8
CELLS = NY * NZ
KQ = 1024
LANES = 128
PARTS = 2
WIDTH = 512
LOG2_E = math.log2(math.e)
DENSITY = 1.0 / math.sqrt(2.0 * math.pi)
F32 = jnp.float32
BF16 = jnp.bfloat16


def basis(length, modes):
    frequency = np.concatenate([np.arange(modes + 1), np.arange(1, modes)])
    samples_at = np.arange(length)
    phases = (2.0 * math.pi / length) * (frequency[:, None] * samples_at[None, :] % length)
    cosine_row = np.arange(2 * modes) <= modes
    waves = np.where(cosine_row[:, None], np.cos(phases), np.sin(phases))
    at_edge = cosine_row & ((frequency == 0) | (2 * frequency == length))
    scales = np.where(at_edge, math.sqrt(1.0 / length), math.sqrt(2.0 / length))
    return (waves * scales[:, None]).astype(np.float32)


def narrow(table):
    return np.asarray(table, np.float32).astype(ml_dtypes.bfloat16)


def vmem_params(mebibytes):
    return pltpu.CompilerParams(vmem_limit_bytes=mebibytes * 1024 * 1024)


def matmul(left, right):
    return jnp.dot(left, right, preferred_element_type=F32)


def matmul_turned(left, right):
    return lax.dot_general(
        left, right, (((1,), (1,)), ((), ())), preferred_element_type=F32
    )


def swap_groups(tiles):
    rows = tiles[0].shape[0]
    lane = lax.broadcasted_iota(jnp.int32, (rows, LANES), 1)
    low_half = lane < 64
    even = (lane // 32) % 2 == 0
    first, second, third, fourth = tiles
    b0 = jnp.where(low_half, first, pltpu.roll(third, 64, 1))
    b2 = jnp.where(low_half, pltpu.roll(first, 64, 1), third)
    b1 = jnp.where(low_half, second, pltpu.roll(fourth, 64, 1))
    b3 = jnp.where(low_half, pltpu.roll(second, 64, 1), fourth)
    return (
        jnp.where(even, b0, pltpu.roll(b1, 32, 1)),
        jnp.where(even, pltpu.roll(b0, 96, 1), b1),
        jnp.where(even, b2, pltpu.roll(b3, 32, 1)),
        jnp.where(even, pltpu.roll(b2, 96, 1), b3),
    )


def pack_modes(modes_ref, held_ref, packed_ref, sems, xl, tl):
    sends = []
    for tile in range(KQ // LANES):
        modes = modes_ref[tile * LANES : (tile + 1) * LANES, :].T
        split = modes.reshape(xl, tl, CHANS, LANES)
        tiles = [split[:, step].reshape(xl * CHANS, LANES) for step in range(tl)]
        owners = slice(tile * tl, (tile + 1) * tl)
        held_ref[owners] = jnp.stack([block.astype(BF16) for block in swap_groups(tiles)])
        send = pltpu.make_async_copy(held_ref.at[owners], packed_ref.at[owners], sems.at[tile])
        send.start()
        sends.append(send)
    for send in sends:
        send.wait()


def unpack_modes(packed_ref, wide_ref, xl, tl):
    for tile in range(KQ // LANES):
        tiles = [packed_ref[tile * tl + owner].astype(F32) for owner in range(tl)]
        for step, block in enumerate(swap_groups(tiles)):
            wide_ref[:, step, :, tile * LANES : (tile + 1) * LANES] = block.reshape(
                xl, CHANS, LANES
            )


def analyse_kernel(
    xl, tl, field_ref, table_ref, packed_ref, field, table, total, held, field_sems, table_sems, sems
):
    chunks = table.shape[0]
    ahead = 4
    fetches = []
    for at in range(chunks):
        lanes = slice(at * WIDTH, (at + 1) * WIDTH)
        fetches.append(
            (
                pltpu.make_async_copy(field_ref.at[:, lanes], field.at[at], field_sems.at[at]),
                pltpu.make_async_copy(table_ref.at[at], table.at[at], table_sems.at[at]),
            )
        )

    def start(at):
        for fetch in fetches[at]:
            fetch.start()

    for at in range(ahead):
        start(at)
    for at in range(0, chunks, 2):
        for now in (at, at + 1):
            for fetch in fetches[now]:
                fetch.wait()
            if now + ahead < chunks:
                start(now + ahead)
        part = matmul_turned(
            jnp.concatenate([table[at], table[at + 1]], axis=1),
            jnp.concatenate([field[at], field[at + 1]], axis=1),
        )
        total[...] = part if at == 0 else total[...] + part
    pack_modes(total, held, packed_ref, sems, xl, tl)


def analyse(field, table, xl, tl, devices):
    rows = xl * tl * CHANS
    chunks = CELLS // WIDTH
    packed = (devices, xl * CHANS, LANES)
    return pl.pallas_call(
        functools.partial(analyse_kernel, xl, tl),
        in_specs=[pl.BlockSpec(memory_space=pltpu.HBM)] * 2,
        out_specs=pl.BlockSpec(memory_space=pl.ANY),
        out_shape=jax.ShapeDtypeStruct(packed, BF16),
        scratch_shapes=[
            pltpu.VMEM((chunks, rows, WIDTH), BF16),
            pltpu.VMEM((chunks, KQ, WIDTH), BF16),
            pltpu.VMEM((KQ, rows), F32),
            pltpu.VMEM(packed, BF16),
            pltpu.SemaphoreType.DMA((chunks,)),
            pltpu.SemaphoreType.DMA((chunks,)),
            pltpu.SemaphoreType.DMA((KQ // LANES,)),
        ],
        compiler_params=vmem_params(60),
        cost_estimate=pl.CostEstimate(
            flops=2 * rows * CELLS * KQ, bytes_accessed=13 << 20, transcendentals=0
        ),
        name="analyse",
    )(field, table)


def weight_kernel(weight_ref, packed_ref):
    for kx in range(weight_ref.shape[0]):
        for group in range(KT // 4):
            parts = [weight_ref[kx, 4 * group + k] for k in range(4)]
            packed_ref[kx, :, :, group * LANES : (group + 1) * LANES] = jnp.concatenate(
                parts, axis=-1
            )


def pack_weight(weight):
    per = 4
    own = weight.shape[4]
    return pl.pallas_call(
        weight_kernel,
        grid=(KX // per,),
        in_specs=[pl.BlockSpec((per, KT, CHANS, CHANS, own), lambda n: (n, 0, 0, 0, 0))],
        out_specs=pl.BlockSpec((per, CHANS, CHANS, KT * own), lambda n: (n, 0, 0, 0)),
        out_shape=jax.ShapeDtypeStruct((KX, CHANS, CHANS, KT * own), F32),
        compiler_params=vmem_params(60),
        cost_estimate=pl.CostEstimate(flops=1 << 20, bytes_accessed=20 << 20, transcendentals=0),
        name="pack_weight",
    )(weight)


def to_modes(spread_refs, x_table_ref, t_table_ref):
    total = 0.0
    for part, spread_ref in enumerate(spread_refs):
        gx, ta, rows, _ = spread_ref.shape
        beside = jnp.concatenate(
            [spread_ref[:, at].reshape(gx * rows, LANES) for at in range(ta)], axis=1
        )
        total = total + matmul(x_table_ref[part], beside)
    return matmul(total.astype(BF16), t_table_ref[...])


def from_modes(modes, x_table_ref, t_table_ref, held_ref):
    parts, gx, ta, rows, _ = held_ref.shape
    half = matmul(modes.astype(BF16), t_table_ref[...]).astype(BF16)
    for part in range(parts):
        full = matmul(x_table_ref[part], half).astype(BF16)
        for at in range(ta):
            held_ref[part, :, at] = full[:, at * LANES : (at + 1) * LANES].reshape(gx, rows, LANES)


def mix_kernel(
    backward,
    weight_ref,
    _,
    x_in_ref,
    t_in_ref,
    x_out_ref,
    t_out_ref,
    *refs,
):
    ins, outs = x_in_ref.shape[0], x_out_ref.shape[0]
    spread_refs, modes_ref, back_refs = refs[:ins], refs[ins], refs[ins + 1 : ins + 1 + outs]
    scratch = refs[ins + 1 + outs :]
    weight, modes, mixed, held, x_in, t_in, x_out, t_out = scratch[:8]
    spreads, (sems, weight_sems, spread_sems, back_sems) = scratch[8:-4], scratch[-4:]
    arrivals = [
        pltpu.make_async_copy(source, target, spread_sems.at[at])
        for at, (source, target) in enumerate(zip(spread_refs, spreads))
    ]
    pieces = weight_sems.shape[0]
    per = KX // pieces
    sources = (x_in_ref, t_in_ref, t_out_ref, x_out_ref)
    tables = [
        pltpu.make_async_copy(source, target, sems.at[at])
        for at, (source, target) in enumerate(zip(sources, (x_in, t_in, t_out, x_out)))
    ]
    fetches = []
    for at in range(pieces):
        part = slice(at * per, (at + 1) * per)
        fetches.append(
            pltpu.make_async_copy(weight_ref.at[part], weight.at[part], weight_sems.at[at])
        )
    for copy in arrivals + tables[:2] + fetches + tables[2:]:
        copy.start()
    for copy in arrivals + tables[:2]:
        copy.wait()
    modes[...] = to_modes(spreads, x_in, t_in)
    keep = pltpu.make_async_copy(modes, modes_ref, sems.at[4])
    keep.start()
    for fetch in fetches:
        fetch.wait()
    for kx in range(KX):
        rows = slice(kx * CHANS, (kx + 1) * CHANS)
        own = modes[rows, :]
        if backward:
            sums = [jnp.sum(own * weight[kx, i], axis=0, keepdims=True) for i in range(CHANS)]
            mixed[rows, :] = jnp.concatenate(sums, axis=0)
        else:
            total = own[0:1, :] * weight[kx, 0]
            for i in range(1, CHANS):
                total = total + own[i : i + 1, :] * weight[kx, i]
            mixed[rows, :] = total
    tables[2].wait()
    tables[3].wait()
    from_modes(mixed[...], x_out, t_out, held)
    sends = [
        pltpu.make_async_copy(held.at[part], ref, back_sems.at[part])
        for part, ref in enumerate(back_refs)
    ]
    for send in sends:
        send.start()
    for send in sends:
        send.wait()
    keep.wait()


def mix(spreads, weight, after, tables, backward):
    modes = (KX * CHANS, weight.shape[3])
    gx, ta, _, lanes = spreads[0].shape
    outs = tables[2].shape[0]
    back = (gx, ta, tables[2].shape[1] // gx, lanes)
    anywhere = pl.BlockSpec(memory_space=pl.ANY)
    apart = pl.BlockSpec(memory_space=pltpu.HBM)
    return pl.pallas_call(
        functools.partial(mix_kernel, backward),
        out_shape=[jax.ShapeDtypeStruct(modes, F32)] + [jax.ShapeDtypeStruct(back, BF16)] * outs,
        in_specs=[apart] + [anywhere] + [apart] * 4 + [anywhere] * len(spreads),
        out_specs=[apart] + [anywhere] * outs,
        scratch_shapes=[
            pltpu.VMEM(weight.shape, F32),
            pltpu.VMEM(modes, F32),
            pltpu.VMEM(modes, F32),
            pltpu.VMEM((outs,) + back, BF16),
            *[pltpu.VMEM(table.shape, BF16) for table in tables],
            *[pltpu.VMEM(spread.shape, BF16) for spread in spreads],
            pltpu.SemaphoreType.DMA((5,)),
            pltpu.SemaphoreType.DMA((8,)),
            pltpu.SemaphoreType.DMA((len(spreads),)),
            pltpu.SemaphoreType.DMA((outs,)),
        ],
        compiler_params=vmem_params(60),
        cost_estimate=pl.CostEstimate(flops=1 << 30, bytes_accessed=9 << 20, transcendentals=0),
        name="mix_back" if backward else "mix",
    )(weight, after, *tables, *spreads)


def outer_kernel(spectrum_ref, grad_ref, result_ref):
    own = result_ref.shape[4]
    for kx in range(result_ref.shape[0]):
        rows = slice(kx * CHANS, (kx + 1) * CHANS)
        for group in range(KT // 4):
            at = slice(group * LANES, (group + 1) * LANES)
            inputs = spectrum_ref[rows, at]
            grads = grad_ref[rows, at]
            for i in range(CHANS):
                product = inputs[i : i + 1, :] * grads
                for k in range(4):
                    result_ref[kx, 4 * group + k, i] = product[:, k * own : (k + 1) * own]


def outer(spectrum, grad, own):
    per = 4
    width = KT * own
    return pl.pallas_call(
        outer_kernel,
        grid=(KX // per,),
        in_specs=[pl.BlockSpec((per * CHANS, width), lambda n: (n, 0))] * 2,
        out_specs=pl.BlockSpec((per, KT, CHANS, CHANS, own), lambda n: (n, 0, 0, 0, 0)),
        out_shape=jax.ShapeDtypeStruct((KX, KT, CHANS, CHANS, own), F32),
        compiler_params=vmem_params(60),
        cost_estimate=pl.CostEstimate(flops=1 << 20, bytes_accessed=17 << 20, transcendentals=0),
        name="outer",
    )(spectrum, grad)


def normal_parts(values):
    scaled = 1.0 + 0.2316419 * jnp.abs(values)
    guess = pl.reciprocal(scaled, approx=True)
    t = guess * (2.0 - scaled * guess)
    decay = jnp.exp2(values * values * (-0.5 * LOG2_E))
    series = (1.330274429 * DENSITY) * t - 1.821255978 * DENSITY
    series = series * t + 1.781477937 * DENSITY
    series = series * t - 0.356563782 * DENSITY
    series = series * t + 0.319381530 * DENSITY
    tail = decay * (series * t)
    return jnp.where(values >= 0.0, 1.0 - tail, tail), decay


def point_kernel(mixer_ref, bias_ref, *refs):
    field_refs, mixed_ref = refs[:PARTS], refs[PARTS]
    rows, width = field_refs[0].shape
    bias = jnp.concatenate([bias_ref[...]] * (width // LANES), axis=1)
    for part, field_ref in enumerate(field_refs):
        mixed = matmul(mixer_ref[...], field_ref[...]) + bias
        mixed_ref[part * rows : (part + 1) * rows, :] = mixed.astype(mixed_ref.dtype)


def point(fields, parts, mixer, bias, dtype, name):
    rows = mixer.shape[0]
    tiles = [pl.BlockSpec((rows, WIDTH), lambda n, part=part: (part, n)) for part in parts]
    return pl.pallas_call(
        point_kernel,
        grid=(CELLS // WIDTH,),
        in_specs=[
            pl.BlockSpec((rows, rows), lambda n: (0, 0)),
            pl.BlockSpec((rows, LANES), lambda n: (0, 0)),
        ]
        + tiles,
        out_specs=pl.BlockSpec((PARTS * rows, WIDTH), lambda n: (0, n)),
        out_shape=jax.ShapeDtypeStruct((PARTS * rows, CELLS), dtype),
        compiler_params=vmem_params(60),
        cost_estimate=pl.CostEstimate(
            flops=2 * PARTS * rows * CELLS * rows, bytes_accessed=12 << 20, transcendentals=0
        ),
        name=name,
    )(mixer, bias, *fields)


def middle_kernel(
    xl,
    tl,
    packed_ref,
    field_ref,
    cotangent_ref,
    mixed_ref,
    table_ref,
    sums_in_ref,
    _,
    output_ref,
    grad_ref,
    sent_ref,
    sums_ref,
    wide,
    modes,
    total,
    held,
    sems,
):
    step = pl.program_id(0)
    rows, width = field_ref.shape
    tile = 256
    chunk = 32
    ones = 16

    @pl.when(step == 0)
    def _():
        unpack_modes(packed_ref, wide, xl, tl)
        modes[...] = wide[...].reshape(rows, KQ).astype(BF16)
        total[...] = jnp.zeros_like(total)

    def build(at):
        return matmul(modes[...], table_ref[0, :, at])

    def pointwise(pre, at):
        for first in range(0, rows, chunk):
            part = slice(first, first + chunk)
            values = pre[part, :] + mixed_ref[part, at]
            integral, decay = normal_parts(values)
            output_ref[part, at] = (values * integral).astype(BF16)
            slope = integral + (values * DENSITY) * decay
            grad_ref[part, at] = (cotangent_ref[part, at].astype(F32) * slope).astype(BF16)

    tiles = [slice(first, first + tile) for first in range(0, width, tile)]
    ready = build(tiles[0])
    for index, at in enumerate(tiles):
        pre = ready
        if index + 1 < len(tiles):
            ready = build(tiles[index + 1])
        pointwise(pre, at)
    passing = jnp.concatenate(
        [table_ref[0], field_ref[...], jnp.ones((ones, width), BF16)], axis=0
    )
    total[...] += matmul_turned(passing, grad_ref[...])

    @pl.when(step == pl.num_programs(0) - 1)
    def _():
        pack_modes(total, held, sent_ref, sems, xl, tl)
        row = lax.broadcasted_iota(jnp.int32, (rows, rows), 0)
        column = lax.broadcasted_iota(jnp.int32, (rows, rows), 1)
        gram = total[KQ : KQ + rows, :].T
        bias = total[KQ + rows : KQ + rows + CHANS, :]
        same = jnp.where(row // CHANS == column // CHANS, gram, 0.0)
        folded = jnp.sum(same.reshape(rows // CHANS, CHANS, rows), axis=0)
        source = lax.broadcasted_iota(jnp.int32, (rows, LANES), 0)
        target = lax.broadcasted_iota(jnp.int32, (rows, LANES), 1)
        select = jnp.where(source % CHANS == target, 1.0, 0.0)
        chan = lax.broadcasted_iota(jnp.int32, (CHANS, rows), 0)
        place = lax.broadcasted_iota(jnp.int32, (CHANS, rows), 1)
        own_bias = jnp.sum(
            jnp.where(place % CHANS == chan, bias, 0.0), axis=1, keepdims=True
        )
        sums = jnp.dot(
            folded, select, precision=lax.Precision.HIGHEST, preferred_element_type=F32
        )
        lane = lax.broadcasted_iota(jnp.int32, (CHANS, LANES), 1)
        sums_ref[...] = sums_in_ref[...] + jnp.where(lane == CHANS, own_bias, sums)


def middle(packed, field, cotangent, mixed, table, sums, output, part, xl, tl):
    rows = xl * tl * CHANS
    width = WIDTH
    chunks = CELLS // width
    whole = lambda *shape: pl.BlockSpec(shape, lambda n: (0,) * len(shape))
    tile = pl.BlockSpec((rows, width), lambda n: (part, n))
    kernel = functools.partial(middle_kernel, xl, tl)
    operands = (packed, field, cotangent, mixed, table, sums)
    specs = [
        whole(*packed.shape),
        tile,
        tile,
        tile,
        pl.BlockSpec((1, KQ, width), lambda n: (n, 0, 0)),
        whole(CHANS, LANES),
    ]
    aliases = {}
    if output is None:
        inner = kernel
        kernel = lambda *refs: inner(*refs[:6], None, *refs[6:])
    else:
        aliases = {len(operands): 0}
        operands += (output,)
        specs.append(pl.BlockSpec(memory_space=pltpu.HBM))
    return pl.pallas_call(
        kernel,
        grid=(chunks,),
        in_specs=specs,
        out_specs=[
            tile,
            pl.BlockSpec((rows, width), lambda n: (0, n)),
            pl.BlockSpec(memory_space=pl.ANY),
            whole(CHANS, LANES),
        ],
        out_shape=(
            jax.ShapeDtypeStruct(field.shape, BF16),
            jax.ShapeDtypeStruct((rows, CELLS), BF16),
            jax.ShapeDtypeStruct(packed.shape, BF16),
            jax.ShapeDtypeStruct((CHANS, LANES), F32),
        ),
        scratch_shapes=[
            pltpu.VMEM((xl, tl, CHANS, KQ), F32),
            pltpu.VMEM((rows, KQ), BF16),
            pltpu.VMEM((KQ + rows + 16, rows), F32),
            pltpu.VMEM(packed.shape, BF16),
            pltpu.SemaphoreType.DMA((KQ // LANES,)),
        ],
        input_output_aliases=aliases,
        compiler_params=vmem_params(60),
        cost_estimate=pl.CostEstimate(
            flops=5 * rows * CELLS * KQ, bytes_accessed=18 << 20, transcendentals=rows * CELLS
        ),
        name="middle",
    )(*operands)


def last_kernel(xl, tl, packed_ref, table_ref, mixed_ref, field_ref, *scratch):
    packed, wide, modes, table, mixed, field, packed_sem, table_sems, mixed_sems, field_sems = (
        scratch
    )
    chunks = table.shape[0]
    ahead = 4
    fetches, sends = [], []
    for at in range(chunks):
        lanes = slice(at * WIDTH, (at + 1) * WIDTH)
        fetches.append(
            (
                pltpu.make_async_copy(table_ref.at[at], table.at[at], table_sems.at[at]),
                pltpu.make_async_copy(mixed_ref.at[:, lanes], mixed.at[at], mixed_sems.at[at]),
            )
        )
        sends.append(
            pltpu.make_async_copy(field.at[at], field_ref.at[:, lanes], field_sems.at[at])
        )

    def start(at):
        for fetch in fetches[at]:
            fetch.start()

    own = pltpu.make_async_copy(packed_ref, packed, packed_sem)
    own.start()
    for at in range(ahead):
        start(at)
    own.wait()
    unpack_modes(packed, wide, xl, tl)
    modes[...] = wide[...].reshape(modes.shape).astype(BF16)
    for at in range(chunks):
        for fetch in fetches[at]:
            fetch.wait()
        if at + ahead < chunks:
            start(at + ahead)
        field[at] = (matmul(modes[...], table[at]) + mixed[at].astype(F32)).astype(BF16)
        sends[at].start()
    for send in sends:
        send.wait()


def last(packed, mixed, table, xl, tl):
    rows = xl * tl * CHANS
    chunks = CELLS // WIDTH
    return pl.pallas_call(
        functools.partial(last_kernel, xl, tl),
        in_specs=[pl.BlockSpec(memory_space=pl.ANY)] + [pl.BlockSpec(memory_space=pltpu.HBM)] * 2,
        out_specs=pl.BlockSpec(memory_space=pltpu.HBM),
        out_shape=jax.ShapeDtypeStruct((rows, CELLS), BF16),
        scratch_shapes=[
            pltpu.VMEM(packed.shape, BF16),
            pltpu.VMEM((xl, tl, CHANS, KQ), F32),
            pltpu.VMEM((rows, KQ), BF16),
            pltpu.VMEM((chunks, KQ, WIDTH), BF16),
            pltpu.VMEM((chunks, rows, WIDTH), BF16),
            pltpu.VMEM((chunks, rows, WIDTH), BF16),
            pltpu.SemaphoreType.DMA,
            pltpu.SemaphoreType.DMA((chunks,)),
            pltpu.SemaphoreType.DMA((chunks,)),
            pltpu.SemaphoreType.DMA((chunks,)),
        ],
        compiler_params=vmem_params(60),
        cost_estimate=pl.CostEstimate(
            flops=2 * rows * CELLS * KQ, bytes_accessed=18 << 20, transcendentals=0
        ),
        name="last",
    )(packed, table, mixed)


def swap(blocks):
    return lax.all_to_all(blocks, ("gx", "ta"), split_axis=0, concat_axis=0, tiled=True)


def sum_everywhere(values, devices):
    step = 1
    while step < devices:
        pairs = [(at, at ^ step) for at in range(devices)]
        values = values + lax.ppermute(values, ("gx", "ta"), pairs)
        step *= 2
    return values


def fast_body(gx, ta, features, cotangent, spec_weight, point_weight, bias_vector):
    _, xl_all, tl, _, cells = features.shape
    own = spec_weight.shape[4]
    devices = gx * ta
    xl = xl_all // PARTS
    rows = xl * tl * CHANS
    yz = np.kron(
        narrow(basis(NY, MY)).astype(np.float32), narrow(basis(NZ, MZ)).astype(np.float32)
    )
    blocks = yz.reshape(KQ, CELLS // WIDTH, WIDTH).transpose(1, 0, 2)
    table = jnp.asarray(narrow(blocks))
    x_whole = basis(NX, MX).reshape(KX, gx, 1, xl_all)
    x_split = basis(NX, MX).reshape(KX, gx, PARTS, xl)
    x_tables = [
        np.stack(
            [
                np.kron(split[:, :, part].reshape(KX, -1), np.eye(CHANS))
                for part in range(split.shape[2])
            ]
        )
        for split in (x_whole, x_split)
    ]
    x_in = [jnp.asarray(narrow(x_table)) for x_table in x_tables]
    x_out = [jnp.asarray(narrow(x_table.transpose(0, 2, 1))) for x_table in x_tables]
    t_wide = np.kron(basis(NT, MT), np.eye(own))
    t_in, t_out = jnp.asarray(narrow(t_wide.T)), jnp.asarray(narrow(t_wide))
    norm_scale = float(BATCH * NX * NT * NY * NZ) ** (-0.5)

    field = features.reshape(PARTS * rows, cells)
    cot = cotangent.reshape(PARTS * rows, cells)
    pick = np.tile(np.eye(CHANS, dtype=np.float32), (rows // CHANS, 1))
    same = np.kron(np.eye(rows // CHANS, dtype=np.float32), np.ones((CHANS, CHANS), np.float32))
    picked = jnp.asarray(narrow(pick))
    spread_point = matmul(matmul(picked, point_weight).astype(BF16), picked.T)
    spread_back = matmul(matmul(picked, point_weight.T).astype(BF16), picked.T)
    mixer = (spread_point * jnp.asarray(same)).astype(BF16)
    mixer_back = (spread_back * jnp.asarray(same)).astype(BF16)
    bias = jnp.dot(
        jnp.asarray(pick),
        jnp.broadcast_to(bias_vector[:, None], (CHANS, LANES)),
        precision=lax.Precision.HIGHEST,
    )
    part_shape = (gx, ta, xl * CHANS, LANES)
    whole_shape = (gx, ta, xl_all * CHANS, LANES)
    packed_weight = pack_weight(spec_weight)
    sums = jnp.zeros((CHANS, LANES), F32)

    spread_in = swap(analyse(field, table, xl_all, tl, devices)).reshape(whole_shape)
    spectrum, *mixed = mix(
        [spread_in], packed_weight, sums, (x_in[0], t_in, x_out[1], t_out), False
    )
    halves = range(PARTS)
    mixed_field = point([field] * PARTS, halves, mixer, bias, F32, "point")
    output = None
    grads, spread_grad = [], []
    for part in range(PARTS):
        returned = swap(mixed[part].reshape(devices, xl * CHANS, LANES))
        output, grad, sent, sums = middle(
            returned, field, cot, mixed_field, table, sums, output, part, xl, tl
        )
        grads.append(grad)
        spread_grad.append(swap(sent).reshape(part_shape))
    summed = sum_everywhere(sums, devices)
    grad_modes, mixed_back = mix(
        spread_grad, packed_weight, summed, (x_in[1], t_in, x_out[0], t_out), True
    )
    grad_back = swap(mixed_back.reshape(devices, xl_all * CHANS, LANES))
    grad_spec = outer(spectrum, grad_modes, own)
    mixed_grad = point(grads, [0] * PARTS, mixer_back, jnp.zeros_like(bias), BF16, "point_back")
    grad_field = last(grad_back, mixed_grad, table, xl_all, tl)
    summed = summed * norm_scale
    return (
        output.reshape(features.shape),
        grad_field.reshape(features.shape),
        grad_spec,
        summed[:, :CHANS],
        summed[:, CHANS],
    )


def analyse_yz(spatial, yz_table):
    return jnp.einsum(
        "qp,bxtcp->bxtcq", yz_table, spatial.astype(F32), precision=lax.Precision.HIGHEST
    )


def build_yz(modes_in, yz_table):
    return jnp.einsum(
        "qp,bxtcq->bxtcp", yz_table, modes_in.astype(F32), precision=lax.Precision.HIGHEST
    )


def analyse_xt(spread, table):
    sizes = spread.shape
    flattened = spread.reshape(sizes[0], sizes[1] * sizes[2], sizes[3] * sizes[4]).astype(F32)
    spectral = jnp.einsum("mp,bpr->bmr", table, flattened, precision=lax.Precision.HIGHEST)
    return spectral.reshape(sizes[0], KX, KT, sizes[3], sizes[4])


def synthesise_xt(modes_in, table):
    sizes = modes_in.shape
    flattened = modes_in.reshape(sizes[0], sizes[1] * sizes[2], sizes[3] * sizes[4])
    spatial = jnp.einsum("mp,bmr->bpr", table, flattened, precision=lax.Precision.HIGHEST)
    return spatial.reshape(sizes[0], NX, NT, sizes[3], sizes[4])


def to_owners(modes_in):
    first = lax.all_to_all(modes_in, "gx", split_axis=4, concat_axis=1, tiled=True)
    return lax.all_to_all(first, "ta", split_axis=4, concat_axis=2, tiled=True)


def to_cells(spread, shape):
    first = lax.all_to_all(
        spread[:, :, :, :, None, None, :], "gx", split_axis=1, concat_axis=4, tiled=True
    )
    second = lax.all_to_all(first, "ta", split_axis=2, concat_axis=5, tiled=True)
    return second.reshape(shape[:4] + (-1,))


def general_body(features, cotangent, spec_weight, point_weight, bias_vector):
    shape = features.shape
    yz_table = jnp.asarray(
        np.kron(narrow(basis(NY, MY)).astype(np.float32), narrow(basis(NZ, MZ)).astype(np.float32))
    )
    xt_table = jnp.asarray(np.kron(basis(NX, MX), basis(NT, MT)))
    norm_scale = float(BATCH * NX * NT * NY * NZ) ** (-0.5)
    highest = lax.Precision.HIGHEST
    spectrum = analyse_xt(to_owners(analyse_yz(features, yz_table).astype(BF16)), xt_table)
    mixed = jnp.einsum("bklip,kliop->bklop", spectrum, spec_weight, precision=highest)
    returned = to_cells(synthesise_xt(mixed, xt_table).astype(BF16), shape)
    pointwise = jnp.einsum("oi,bxtip->bxtop", point_weight, features, preferred_element_type=F32)
    pre = build_yz(returned, yz_table) + pointwise + bias_vector[:, None]
    integral = 0.5 * (1.0 + jax.scipy.special.erf(pre * 0.7071067811865476))
    output = (pre * integral).astype(BF16)
    slope = integral + pre * jnp.exp(-0.5 * pre * pre) * 0.3989422804014327
    grad_pre = (cotangent.astype(F32) * slope).astype(BF16)
    local_point = jnp.einsum("bxtop,bxtip->oi", grad_pre, features, preferred_element_type=F32)
    local_bias = jnp.sum(grad_pre.astype(F32), axis=(0, 1, 2, 4))
    total_point, total_bias = lax.psum((local_point, local_bias), ("gx", "ta"))
    grad_modes = analyse_xt(to_owners(analyse_yz(grad_pre, yz_table).astype(BF16)), xt_table)
    grad_spec = jnp.einsum("bklip,bklop->kliop", spectrum, grad_modes, precision=highest)
    grad_in = jnp.einsum("kliop,bklop->bklip", spec_weight, grad_modes, precision=highest)
    grad_back = to_cells(synthesise_xt(grad_in, xt_table).astype(BF16), shape)
    point_term = jnp.einsum("oi,bxtop->bxtip", point_weight, grad_pre, preferred_element_type=F32)
    grad_field = (build_yz(grad_back, yz_table) + point_term).astype(BF16)
    return (output, grad_field, grad_spec, total_point * norm_scale, total_bias * norm_scale)


def solution(mesh):
    split_field = P(None, "gx", "ta", None, None)
    split_weight = P(None, None, None, None, ("gx", "ta"))
    in_specs = (split_field, split_field, split_weight, P(), P())
    out_specs = (split_field, split_field, split_weight, P(), P())
    gx, ta = mesh.shape["gx"], mesh.shape["ta"]
    own, xl, tl = KQ // (gx * ta), NX // gx, NT // ta
    if own == 32 and xl * CHANS == LANES and tl == 4:
        body = functools.partial(fast_body, gx, ta)
    else:
        body = general_body
    return jax.shard_map(body, mesh=mesh, in_specs=in_specs, out_specs=out_specs, check_vma=False)
```

```python
import functools
import math

import jax
import jax.numpy as jnp
import ml_dtypes
import numpy as np
from jax import lax
from jax.experimental import pallas as pl
from jax.experimental.pallas import tpu as pltpu
from jax.sharding import PartitionSpec as P

NX = 128
NY = 128
NZ = 32
NT = 16
MX = 16
MY = 16
MZ = 16
MT = 8
BATCH = 1
KX = 32
KT = 16
CHANS = 8
CELLS = NY * NZ
KQ = 1024
LANES = 128
PARTS = 2
WIDTH = 512
DENSITY = 1.0 / math.sqrt(2.0 * math.pi)
F32 = jnp.float32
BF16 = jnp.bfloat16


def basis(length, modes):
    frequency = np.concatenate([np.arange(modes + 1), np.arange(1, modes)])
    samples_at = np.arange(length)
    phases = (2.0 * math.pi / length) * (frequency[:, None] * samples_at[None, :] % length)
    cosine_row = np.arange(2 * modes) <= modes
    waves = np.where(cosine_row[:, None], np.cos(phases), np.sin(phases))
    at_edge = cosine_row & ((frequency == 0) | (2 * frequency == length))
    scales = np.where(at_edge, math.sqrt(1.0 / length), math.sqrt(2.0 / length))
    return (waves * scales[:, None]).astype(np.float32)


def narrow(table):
    return np.asarray(table, np.float32).astype(ml_dtypes.bfloat16)


def vmem_params(mebibytes):
    return pltpu.CompilerParams(vmem_limit_bytes=mebibytes * 1024 * 1024)


def matmul(left, right):
    return jnp.dot(left, right, preferred_element_type=F32)


def matmul_turned(left, right):
    return lax.dot_general(
        left, right, (((1,), (1,)), ((), ())), preferred_element_type=F32
    )


def swap_groups(tiles):
    rows = tiles[0].shape[0]
    lane = lax.broadcasted_iota(jnp.int32, (rows, LANES), 1)
    low_half = lane < 64
    even = (lane // 32) % 2 == 0
    first, second, third, fourth = tiles
    b0 = jnp.where(low_half, first, pltpu.roll(third, 64, 1))
    b2 = jnp.where(low_half, pltpu.roll(first, 64, 1), third)
    b1 = jnp.where(low_half, second, pltpu.roll(fourth, 64, 1))
    b3 = jnp.where(low_half, pltpu.roll(second, 64, 1), fourth)
    return (
        jnp.where(even, b0, pltpu.roll(b1, 32, 1)),
        jnp.where(even, pltpu.roll(b0, 96, 1), b1),
        jnp.where(even, b2, pltpu.roll(b3, 32, 1)),
        jnp.where(even, pltpu.roll(b2, 96, 1), b3),
    )


def pack_modes(modes_ref, held_ref, packed_ref, sems, xl, tl):
    sends = []
    for tile in range(KQ // LANES):
        modes = modes_ref[tile * LANES : (tile + 1) * LANES, :].T
        split = modes.reshape(xl, tl, CHANS, LANES)
        tiles = [split[:, step].reshape(xl * CHANS, LANES) for step in range(tl)]
        owners = slice(tile * tl, (tile + 1) * tl)
        held_ref[owners] = jnp.stack([block.astype(BF16) for block in swap_groups(tiles)])
        send = pltpu.make_async_copy(held_ref.at[owners], packed_ref.at[owners], sems.at[tile])
        send.start()
        sends.append(send)
    for send in sends:
        send.wait()


def unpack_modes(packed_ref, wide_ref, xl, tl):
    for tile in range(KQ // LANES):
        tiles = [packed_ref[tile * tl + owner].astype(F32) for owner in range(tl)]
        for step, block in enumerate(swap_groups(tiles)):
            wide_ref[:, step, :, tile * LANES : (tile + 1) * LANES] = block.reshape(
                xl, CHANS, LANES
            )


def analyse_kernel(
    xl, tl, field_ref, table_ref, packed_ref, field, table, total, held, field_sems, table_sems, sems
):
    chunks = table.shape[0]
    ahead = 4
    fetches = []
    for at in range(chunks):
        lanes = slice(at * WIDTH, (at + 1) * WIDTH)
        fetches.append(
            (
                pltpu.make_async_copy(field_ref.at[:, lanes], field.at[at], field_sems.at[at]),
                pltpu.make_async_copy(table_ref.at[at], table.at[at], table_sems.at[at]),
            )
        )

    def start(at):
        for fetch in fetches[at]:
            fetch.start()

    for at in range(ahead):
        start(at)
    for at in range(0, chunks, 2):
        for now in (at, at + 1):
            for fetch in fetches[now]:
                fetch.wait()
            if now + ahead < chunks:
                start(now + ahead)
        part = matmul_turned(
            jnp.concatenate([table[at], table[at + 1]], axis=1),
            jnp.concatenate([field[at], field[at + 1]], axis=1),
        )
        total[...] = part if at == 0 else total[...] + part
    pack_modes(total, held, packed_ref, sems, xl, tl)


def analyse(field, table, xl, tl, devices):
    rows = xl * tl * CHANS
    chunks = CELLS // WIDTH
    packed = (devices, xl * CHANS, LANES)
    return pl.pallas_call(
        functools.partial(analyse_kernel, xl, tl),
        in_specs=[pl.BlockSpec(memory_space=pltpu.HBM)] * 2,
        out_specs=pl.BlockSpec(memory_space=pl.ANY),
        out_shape=jax.ShapeDtypeStruct(packed, BF16),
        scratch_shapes=[
            pltpu.VMEM((chunks, rows, WIDTH), BF16),
            pltpu.VMEM((chunks, KQ, WIDTH), BF16),
            pltpu.VMEM((KQ, rows), F32),
            pltpu.VMEM(packed, BF16),
            pltpu.SemaphoreType.DMA((chunks,)),
            pltpu.SemaphoreType.DMA((chunks,)),
            pltpu.SemaphoreType.DMA((KQ // LANES,)),
        ],
        compiler_params=vmem_params(60),
        cost_estimate=pl.CostEstimate(
            flops=2 * rows * CELLS * KQ, bytes_accessed=13 << 20, transcendentals=0
        ),
        name="analyse",
    )(field, table)


def weight_kernel(weight_ref, packed_ref):
    for kx in range(weight_ref.shape[0]):
        for group in range(KT // 4):
            parts = [weight_ref[kx, 4 * group + k] for k in range(4)]
            joined = jnp.concatenate(parts, axis=-1).reshape(CHANS * CHANS, LANES)
            packed_ref[kx, :, group * LANES : (group + 1) * LANES] = joined.astype(BF16)


def pack_weight(weight):
    per = 4
    own = weight.shape[4]
    return pl.pallas_call(
        weight_kernel,
        grid=(KX // per,),
        in_specs=[pl.BlockSpec((per, KT, CHANS, CHANS, own), lambda n: (n, 0, 0, 0, 0))],
        out_specs=pl.BlockSpec((per, CHANS * CHANS, KT * own), lambda n: (n, 0, 0)),
        out_shape=jax.ShapeDtypeStruct((KX, CHANS * CHANS, KT * own), BF16),
        compiler_params=vmem_params(60),
        cost_estimate=pl.CostEstimate(flops=1 << 20, bytes_accessed=20 << 20, transcendentals=0),
        name="pack_weight",
    )(weight)


def to_modes(spread_refs, x_table_ref, t_table_ref):
    total = 0.0
    for part, spread_ref in enumerate(spread_refs):
        gx, ta, rows, _ = spread_ref.shape
        beside = jnp.concatenate(
            [spread_ref[:, at].reshape(gx * rows, LANES) for at in range(ta)], axis=1
        )
        total = total + matmul(x_table_ref[part], beside)
    return matmul(total.astype(BF16), t_table_ref[...])


def from_modes(modes, x_table_ref, t_table_ref, held_ref):
    parts, gx, ta, rows, _ = held_ref.shape
    half = matmul(modes.astype(BF16), t_table_ref[...]).astype(BF16)
    for part in range(parts):
        full = matmul(x_table_ref[part], half).astype(BF16)
        for at in range(ta):
            held_ref[part, :, at] = full[:, at * LANES : (at + 1) * LANES].reshape(gx, rows, LANES)


def mix_kernel(
    backward,
    afters,
    weight_ref,
    *refs,
):
    x_in_ref, t_in_ref, x_out_ref, t_out_ref = refs[afters : afters + 4]
    refs = refs[afters + 4 :]
    ins, outs = x_in_ref.shape[0], x_out_ref.shape[0]
    spread_refs, modes_ref, back_refs = refs[:ins], refs[ins], refs[ins + 1 : ins + 1 + outs]
    scratch = refs[ins + 1 + outs :]
    weight, modes, mixed, held, x_in, t_in, x_out, t_out = scratch[:8]
    spreads, (sems, weight_sems, spread_sems, back_sems) = scratch[8:-4], scratch[-4:]
    arrivals = [
        pltpu.make_async_copy(source, target, spread_sems.at[at])
        for at, (source, target) in enumerate(zip(spread_refs, spreads))
    ]
    pieces = weight_sems.shape[0]
    per = KX // pieces
    sources = (x_in_ref, t_in_ref, t_out_ref, x_out_ref)
    tables = [
        pltpu.make_async_copy(source, target, sems.at[at])
        for at, (source, target) in enumerate(zip(sources, (x_in, t_in, t_out, x_out)))
    ]
    fetches = []
    for at in range(pieces):
        part = slice(at * per, (at + 1) * per)
        fetches.append(
            pltpu.make_async_copy(weight_ref.at[part], weight.at[part], weight_sems.at[at])
        )
    for copy in arrivals + tables[:2] + fetches + tables[2:]:
        copy.start()
    for copy in arrivals + tables[:2]:
        copy.wait()
    modes[...] = to_modes(spreads, x_in, t_in)
    keep = pltpu.make_async_copy(modes, modes_ref, sems.at[4])
    keep.start()
    for fetch in fetches:
        fetch.wait()
    for kx in range(KX):
        rows = slice(kx * CHANS, (kx + 1) * CHANS)
        own = modes[rows, :]
        weights = weight[kx].astype(F32).reshape(CHANS, CHANS, own.shape[1])
        if backward:
            sums = [jnp.sum(own * weights[i], axis=0, keepdims=True) for i in range(CHANS)]
            mixed[rows, :] = jnp.concatenate(sums, axis=0)
        else:
            total = own[0:1, :] * weights[0]
            for i in range(1, CHANS):
                total = total + own[i : i + 1, :] * weights[i]
            mixed[rows, :] = total
    tables[2].wait()
    tables[3].wait()
    from_modes(mixed[...], x_out, t_out, held)
    sends = [
        pltpu.make_async_copy(held.at[part], ref, back_sems.at[part])
        for part, ref in enumerate(back_refs)
    ]
    for send in sends:
        send.start()
    for send in sends:
        send.wait()
    keep.wait()


def mix(spreads, weight, after, tables, backward):
    modes = (KX * CHANS, weight.shape[2])
    gx, ta, _, lanes = spreads[0].shape
    outs = tables[2].shape[0]
    back = (gx, ta, tables[2].shape[1] // gx, lanes)
    anywhere = pl.BlockSpec(memory_space=pl.ANY)
    apart = pl.BlockSpec(memory_space=pltpu.HBM)
    return pl.pallas_call(
        functools.partial(mix_kernel, backward, len(after)),
        out_shape=[jax.ShapeDtypeStruct(modes, F32)] + [jax.ShapeDtypeStruct(back, BF16)] * outs,
        in_specs=[apart] + [anywhere] * len(after) + [apart] * 4 + [anywhere] * len(spreads),
        out_specs=[apart] + [anywhere] * outs,
        scratch_shapes=[
            pltpu.VMEM(weight.shape, BF16),
            pltpu.VMEM(modes, F32),
            pltpu.VMEM(modes, F32),
            pltpu.VMEM((outs,) + back, BF16),
            *[pltpu.VMEM(table.shape, BF16) for table in tables],
            *[pltpu.VMEM(spread.shape, BF16) for spread in spreads],
            pltpu.SemaphoreType.DMA((5,)),
            pltpu.SemaphoreType.DMA((8,)),
            pltpu.SemaphoreType.DMA((len(spreads),)),
            pltpu.SemaphoreType.DMA((outs,)),
        ],
        compiler_params=vmem_params(60),
        cost_estimate=pl.CostEstimate(flops=1 << 30, bytes_accessed=9 << 20, transcendentals=0),
        name="mix_back" if backward else "mix",
    )(weight, *after, *tables, *spreads)


def outer_kernel(spectrum_ref, grad_ref, result_ref):
    own = result_ref.shape[4]
    for kx in range(result_ref.shape[0]):
        rows = slice(kx * CHANS, (kx + 1) * CHANS)
        for group in range(KT // 4):
            at = slice(group * LANES, (group + 1) * LANES)
            inputs = spectrum_ref[rows, at]
            grads = grad_ref[rows, at]
            for i in range(CHANS):
                product = inputs[i : i + 1, :] * grads
                for k in range(4):
                    result_ref[kx, 4 * group + k, i] = product[:, k * own : (k + 1) * own]


def outer(spectrum, grad, own):
    per = 4
    width = KT * own
    return pl.pallas_call(
        outer_kernel,
        grid=(KX // per,),
        in_specs=[pl.BlockSpec((per * CHANS, width), lambda n: (n, 0))] * 2,
        out_specs=pl.BlockSpec((per, KT, CHANS, CHANS, own), lambda n: (n, 0, 0, 0, 0)),
        out_shape=jax.ShapeDtypeStruct((KX, KT, CHANS, CHANS, own), F32),
        compiler_params=vmem_params(60),
        cost_estimate=pl.CostEstimate(flops=1 << 20, bytes_accessed=17 << 20, transcendentals=0),
        name="outer",
    )(spectrum, grad)


def normal_parts(values):
    scaled = 1.0 + 0.2316419 * jnp.abs(values)
    guess = pl.reciprocal(scaled, approx=True)
    t = guess * (2.0 - scaled * guess)
    decay = jnp.exp(values * values * -0.5)
    series = (1.330274429 * DENSITY) * t - 1.821255978 * DENSITY
    series = series * t + 1.781477937 * DENSITY
    series = series * t - 0.356563782 * DENSITY
    series = series * t + 0.319381530 * DENSITY
    tail = decay * (series * t)
    return jnp.where(values >= 0.0, 1.0 - tail, tail), decay


def middle_kernel(
    xl,
    tl,
    packed_ref,
    field_ref,
    cotangent_ref,
    table_ref,
    mixer_ref,
    bias_ref,
    sums_in_ref,
    _,
    output_ref,
    grad_ref,
    sent_ref,
    sums_ref,
    wide,
    modes,
    total,
    held,
    sems,
):
    step = pl.program_id(0)
    rows, width = field_ref.shape
    tile = 256
    chunk = 32
    ones = 16

    @pl.when(step == 0)
    def _():
        unpack_modes(packed_ref, wide, xl, tl)
        modes[...] = wide[...].reshape(rows, KQ).astype(BF16)
        total[...] = jnp.zeros_like(total)

    blocks = table_ref.shape[0]

    def build(at):
        block, first = divmod(at.start, WIDTH)
        spatial = matmul(modes[...], table_ref[block, :, first : first + tile])
        return spatial + matmul(mixer_ref[...], field_ref[:, at])

    def pointwise(pre, at):
        for first in range(0, rows, chunk):
            part = slice(first, first + chunk)
            values = pre[part, :] + jnp.concatenate([bias_ref[part, :]] * (tile // LANES), axis=1)
            integral, decay = normal_parts(values)
            output_ref[part, at] = (values * integral).astype(BF16)
            slope = integral + (values * DENSITY) * decay
            grad = (cotangent_ref[part, at].astype(F32) * slope).astype(BF16)
            grad_ref[at.start // WIDTH, part, at.start % WIDTH : at.start % WIDTH + tile] = grad

    tiles = [slice(first, first + tile) for first in range(0, width, tile)]
    ready = build(tiles[0])
    for index, at in enumerate(tiles):
        pre = ready
        if index + 1 < len(tiles):
            ready = build(tiles[index + 1])
        pointwise(pre, at)
    passing = jnp.concatenate([table_ref[at] for at in range(blocks)], axis=1)
    passing = jnp.concatenate([passing, field_ref[...], jnp.ones((ones, width), BF16)], axis=0)
    grads = jnp.concatenate([grad_ref[at] for at in range(blocks)], axis=1)
    total[...] += matmul_turned(passing, grads)

    @pl.when(step == pl.num_programs(0) - 1)
    def _():
        pack_modes(total, held, sent_ref, sems, xl, tl)
        row = lax.broadcasted_iota(jnp.int32, (rows, rows), 0)
        column = lax.broadcasted_iota(jnp.int32, (rows, rows), 1)
        gram = total[KQ : KQ + rows, :].T
        bias = total[KQ + rows : KQ + rows + CHANS, :]
        same = jnp.where(row // CHANS == column // CHANS, gram, 0.0)
        folded = jnp.sum(same.reshape(rows // CHANS, CHANS, rows), axis=0)
        source = lax.broadcasted_iota(jnp.int32, (rows, LANES), 0)
        target = lax.broadcasted_iota(jnp.int32, (rows, LANES), 1)
        select = jnp.where(source % CHANS == target, 1.0, 0.0)
        chan = lax.broadcasted_iota(jnp.int32, (CHANS, rows), 0)
        place = lax.broadcasted_iota(jnp.int32, (CHANS, rows), 1)
        own_bias = jnp.sum(
            jnp.where(place % CHANS == chan, bias, 0.0), axis=1, keepdims=True
        )
        sums = jnp.dot(
            folded, select, precision=lax.Precision.HIGHEST, preferred_element_type=F32
        )
        lane = lax.broadcasted_iota(jnp.int32, (CHANS, LANES), 1)
        sums_ref[...] = sums_in_ref[...] + jnp.where(lane == CHANS, own_bias, sums)


def middle(packed, field, cotangent, table, mixer, bias, sums, output, part, xl, tl):
    rows = xl * tl * CHANS
    per = 2
    chunks = CELLS // WIDTH
    whole = lambda *shape: pl.BlockSpec(shape, lambda n: (0,) * len(shape))
    tile = pl.BlockSpec((rows, per * WIDTH), lambda n: (part, n))
    kernel = functools.partial(middle_kernel, xl, tl)
    operands = (packed, field, cotangent, table, mixer, bias, sums)
    specs = [
        whole(*packed.shape),
        tile,
        tile,
        pl.BlockSpec((per, KQ, WIDTH), lambda n: (n, 0, 0)),
        whole(rows, rows),
        whole(rows, LANES),
        whole(CHANS, LANES),
    ]
    aliases = {}
    if output is None:
        inner = kernel
        kernel = lambda *refs: inner(*refs[:7], None, *refs[7:])
    else:
        aliases = {len(operands): 0}
        operands += (output,)
        specs.append(pl.BlockSpec(memory_space=pltpu.HBM))
    return pl.pallas_call(
        kernel,
        grid=(chunks // per,),
        in_specs=specs,
        out_specs=[
            tile,
            pl.BlockSpec((per, rows, WIDTH), lambda n: (n, 0, 0)),
            pl.BlockSpec(memory_space=pl.ANY),
            whole(CHANS, LANES),
        ],
        out_shape=(
            jax.ShapeDtypeStruct(field.shape, BF16),
            jax.ShapeDtypeStruct((chunks, rows, WIDTH), BF16),
            jax.ShapeDtypeStruct(packed.shape, BF16),
            jax.ShapeDtypeStruct((CHANS, LANES), F32),
        ),
        scratch_shapes=[
            pltpu.VMEM((xl, tl, CHANS, KQ), F32),
            pltpu.VMEM((rows, KQ), BF16),
            pltpu.VMEM((KQ + rows + 16, rows), F32),
            pltpu.VMEM(packed.shape, BF16),
            pltpu.SemaphoreType.DMA((KQ // LANES,)),
        ],
        input_output_aliases=aliases,
        compiler_params=vmem_params(60),
        cost_estimate=pl.CostEstimate(
            flops=5 * rows * CELLS * KQ, bytes_accessed=18 << 20, transcendentals=rows * CELLS
        ),
        name="middle",
    )(*operands)


def last_kernel(xl, tl, mixer_ref, packed_ref, table_ref, *refs):
    grad_refs, field_ref = refs[:PARTS], refs[PARTS]
    scratch = refs[PARTS + 1 :]
    packed, wide, modes, table, grads, field, packed_sem, table_sems, grad_sems, field_sems = (
        scratch
    )
    chunks = table.shape[0]
    ahead = 4
    fetches, sends = [], []
    for at in range(chunks):
        lanes = slice(at * WIDTH, (at + 1) * WIDTH)
        fetches.append([pltpu.make_async_copy(table_ref.at[at], table.at[at], table_sems.at[at])])
        for part, grad_ref in enumerate(grad_refs):
            fetches[at].append(
                pltpu.make_async_copy(
                    grad_ref.at[at], grads.at[at, part], grad_sems.at[at, part]
                )
            )
        sends.append(
            pltpu.make_async_copy(field.at[at], field_ref.at[:, lanes], field_sems.at[at])
        )

    def start(at):
        for fetch in fetches[at]:
            fetch.start()

    own = pltpu.make_async_copy(packed_ref, packed, packed_sem)
    own.start()
    for at in range(ahead):
        start(at)
    own.wait()
    unpack_modes(packed, wide, xl, tl)
    modes[...] = wide[...].reshape(modes.shape).astype(BF16)
    for at in range(chunks):
        for fetch in fetches[at]:
            fetch.wait()
        if at + ahead < chunks:
            start(at + ahead)
        point = [matmul(mixer_ref[...], grads[at, part]) for part in range(PARTS)]
        field[at] = (
            matmul(modes[...], table[at]) + jnp.concatenate(point, axis=0)
        ).astype(BF16)
        sends[at].start()
    for send in sends:
        send.wait()


def last(packed, grads, table, mixer, xl, tl):
    rows = xl * tl * CHANS
    part = rows // PARTS
    chunks = CELLS // WIDTH
    apart = pl.BlockSpec(memory_space=pltpu.HBM)
    return pl.pallas_call(
        functools.partial(last_kernel, xl, tl),
        in_specs=[
            pl.BlockSpec(memory_space=pltpu.VMEM),
            pl.BlockSpec(memory_space=pl.ANY),
        ]
        + [apart] * (1 + PARTS),
        out_specs=apart,
        out_shape=jax.ShapeDtypeStruct((rows, CELLS), BF16),
        scratch_shapes=[
            pltpu.VMEM(packed.shape, BF16),
            pltpu.VMEM((xl, tl, CHANS, KQ), F32),
            pltpu.VMEM((rows, KQ), BF16),
            pltpu.VMEM((chunks, KQ, WIDTH), BF16),
            pltpu.VMEM((chunks, PARTS, part, WIDTH), BF16),
            pltpu.VMEM((chunks, rows, WIDTH), BF16),
            pltpu.SemaphoreType.DMA,
            pltpu.SemaphoreType.DMA((chunks,)),
            pltpu.SemaphoreType.DMA((chunks, PARTS)),
            pltpu.SemaphoreType.DMA((chunks,)),
        ],
        compiler_params=vmem_params(60),
        cost_estimate=pl.CostEstimate(
            flops=2 * rows * CELLS * KQ, bytes_accessed=18 << 20, transcendentals=0
        ),
        name="last",
    )(mixer, packed, table, *grads)


def swap(blocks):
    return lax.all_to_all(blocks, ("gx", "ta"), split_axis=0, concat_axis=0, tiled=True)


def sum_pairs(values, devices, step, end):
    while step < end:
        pairs = [(at, at ^ step) for at in range(devices)]
        values = values + lax.ppermute(values, ("gx", "ta"), pairs)
        step *= 2
    return values


def fast_body(gx, ta, features, cotangent, spec_weight, point_weight, bias_vector):
    _, xl_all, tl, _, cells = features.shape
    own = spec_weight.shape[4]
    devices = gx * ta
    xl = xl_all // PARTS
    rows = xl * tl * CHANS
    yz = np.kron(
        narrow(basis(NY, MY)).astype(np.float32), narrow(basis(NZ, MZ)).astype(np.float32)
    )
    blocks = yz.reshape(KQ, CELLS // WIDTH, WIDTH).transpose(1, 0, 2)
    table = jnp.asarray(narrow(blocks))
    x_whole = basis(NX, MX).reshape(KX, gx, 1, xl_all)
    x_split = basis(NX, MX).reshape(KX, gx, PARTS, xl)
    x_tables = [
        np.stack(
            [
                np.kron(split[:, :, part].reshape(KX, -1), np.eye(CHANS))
                for part in range(split.shape[2])
            ]
        )
        for split in (x_whole, x_split)
    ]
    x_in = [jnp.asarray(narrow(x_table)) for x_table in x_tables]
    x_out = [jnp.asarray(narrow(x_table.transpose(0, 2, 1))) for x_table in x_tables]
    t_wide = np.kron(basis(NT, MT), np.eye(own))
    t_in, t_out = jnp.asarray(narrow(t_wide.T)), jnp.asarray(narrow(t_wide))
    norm_scale = float(BATCH * NX * NT * NY * NZ) ** (-0.5)

    field = features.reshape(PARTS * rows, cells)
    cot = cotangent.reshape(PARTS * rows, cells)
    pick = np.tile(np.eye(CHANS, dtype=np.float32), (rows // CHANS, 1))
    same = np.kron(np.eye(rows // CHANS, dtype=np.float32), np.ones((CHANS, CHANS), np.float32))
    picked = jnp.asarray(narrow(pick))
    spread_point = matmul(matmul(picked, point_weight).astype(BF16), picked.T)
    spread_back = matmul(matmul(picked, point_weight.T).astype(BF16), picked.T)
    mixer = (spread_point * jnp.asarray(same)).astype(BF16)
    mixer_back = (spread_back * jnp.asarray(same)).astype(BF16)
    bias = jnp.dot(
        jnp.asarray(pick),
        jnp.broadcast_to(bias_vector[:, None], (CHANS, LANES)),
        precision=lax.Precision.HIGHEST,
    )
    part_shape = (gx, ta, xl * CHANS, LANES)
    whole_shape = (gx, ta, xl_all * CHANS, LANES)
    packed_weight = pack_weight(spec_weight)
    sums = jnp.zeros((CHANS, LANES), F32)

    spread_in = swap(analyse(field, table, xl_all, tl, devices)).reshape(whole_shape)
    spectrum, *mixed = mix(
        [spread_in], packed_weight, (mixer, mixer_back, bias), (x_in[0], t_in, x_out[1], t_out), False
    )
    output = None
    grads, spread_grad = [], []
    for part in range(PARTS):
        returned = swap(mixed[part].reshape(devices, xl * CHANS, LANES))
        output, grad, sent, sums = middle(
            returned, field, cot, table, mixer, bias, sums, output, part, xl, tl
        )
        grads.append(grad)
        spread_grad.append(swap(sent).reshape(part_shape))
    partly = sum_pairs(sums, devices, 1, 8)
    grad_modes, mixed_back = mix(
        spread_grad, packed_weight, (partly,), (x_in[1], t_in, x_out[0], t_out), True
    )
    grad_back = swap(mixed_back.reshape(devices, xl_all * CHANS, LANES))
    grad_spec = outer(spectrum, grad_modes, own)
    grad_field = last(grad_back, grads, table, mixer_back, xl_all, tl)
    summed = sum_pairs(partly, devices, 8, devices) * norm_scale
    return (
        output.reshape(features.shape),
        grad_field.reshape(features.shape),
        grad_spec,
        summed[:, :CHANS],
        summed[:, CHANS],
    )


def analyse_yz(spatial, yz_table):
    return jnp.einsum(
        "qp,bxtcp->bxtcq", yz_table, spatial.astype(F32), precision=lax.Precision.HIGHEST
    )


def build_yz(modes_in, yz_table):
    return jnp.einsum(
        "qp,bxtcq->bxtcp", yz_table, modes_in.astype(F32), precision=lax.Precision.HIGHEST
    )


def analyse_xt(spread, table):
    sizes = spread.shape
    flattened = spread.reshape(sizes[0], sizes[1] * sizes[2], sizes[3] * sizes[4]).astype(F32)
    spectral = jnp.einsum("mp,bpr->bmr", table, flattened, precision=lax.Precision.HIGHEST)
    return spectral.reshape(sizes[0], KX, KT, sizes[3], sizes[4])


def synthesise_xt(modes_in, table):
    sizes = modes_in.shape
    flattened = modes_in.reshape(sizes[0], sizes[1] * sizes[2], sizes[3] * sizes[4])
    spatial = jnp.einsum("mp,bmr->bpr", table, flattened, precision=lax.Precision.HIGHEST)
    return spatial.reshape(sizes[0], NX, NT, sizes[3], sizes[4])


def to_owners(modes_in):
    first = lax.all_to_all(modes_in, "gx", split_axis=4, concat_axis=1, tiled=True)
    return lax.all_to_all(first, "ta", split_axis=4, concat_axis=2, tiled=True)


def to_cells(spread, shape):
    first = lax.all_to_all(
        spread[:, :, :, :, None, None, :], "gx", split_axis=1, concat_axis=4, tiled=True
    )
    second = lax.all_to_all(first, "ta", split_axis=2, concat_axis=5, tiled=True)
    return second.reshape(shape[:4] + (-1,))


def general_body(features, cotangent, spec_weight, point_weight, bias_vector):
    shape = features.shape
    yz_table = jnp.asarray(
        np.kron(narrow(basis(NY, MY)).astype(np.float32), narrow(basis(NZ, MZ)).astype(np.float32))
    )
    xt_table = jnp.asarray(np.kron(basis(NX, MX), basis(NT, MT)))
    norm_scale = float(BATCH * NX * NT * NY * NZ) ** (-0.5)
    highest = lax.Precision.HIGHEST
    spectrum = analyse_xt(to_owners(analyse_yz(features, yz_table).astype(BF16)), xt_table)
    mixed = jnp.einsum("bklip,kliop->bklop", spectrum, spec_weight, precision=highest)
    returned = to_cells(synthesise_xt(mixed, xt_table).astype(BF16), shape)
    pointwise = jnp.einsum("oi,bxtip->bxtop", point_weight, features, preferred_element_type=F32)
    pre = build_yz(returned, yz_table) + pointwise + bias_vector[:, None]
    integral = 0.5 * (1.0 + jax.scipy.special.erf(pre * 0.7071067811865476))
    output = (pre * integral).astype(BF16)
    slope = integral + pre * jnp.exp(-0.5 * pre * pre) * 0.3989422804014327
    grad_pre = (cotangent.astype(F32) * slope).astype(BF16)
    local_point = jnp.einsum("bxtop,bxtip->oi", grad_pre, features, preferred_element_type=F32)
    local_bias = jnp.sum(grad_pre.astype(F32), axis=(0, 1, 2, 4))
    total_point, total_bias = lax.psum((local_point, local_bias), ("gx", "ta"))
    grad_modes = analyse_xt(to_owners(analyse_yz(grad_pre, yz_table).astype(BF16)), xt_table)
    grad_spec = jnp.einsum("bklip,bklop->kliop", spectrum, grad_modes, precision=highest)
    grad_in = jnp.einsum("kliop,bklop->bklip", spec_weight, grad_modes, precision=highest)
    grad_back = to_cells(synthesise_xt(grad_in, xt_table).astype(BF16), shape)
    point_term = jnp.einsum("oi,bxtop->bxtip", point_weight, grad_pre, preferred_element_type=F32)
    grad_field = (build_yz(grad_back, yz_table) + point_term).astype(BF16)
    return (output, grad_field, grad_spec, total_point * norm_scale, total_bias * norm_scale)


def solution(mesh):
    split_field = P(None, "gx", "ta", None, None)
    split_weight = P(None, None, None, None, ("gx", "ta"))
    in_specs = (split_field, split_field, split_weight, P(), P())
    out_specs = (split_field, split_field, split_weight, P(), P())
    gx, ta = mesh.shape["gx"], mesh.shape["ta"]
    own, xl, tl = KQ // (gx * ta), NX // gx, NT // ta
    if own == 32 and xl * CHANS == LANES and tl == 4:
        body = functools.partial(fast_body, gx, ta)
    else:
        body = general_body
    return jax.shard_map(body, mesh=mesh, in_specs=in_specs, out_specs=out_specs, check_vma=False)
```

```python
import functools
import math

import jax
import jax.numpy as jnp
import ml_dtypes
import numpy as np
from jax import lax
from jax.experimental import pallas as pl
from jax.experimental.pallas import tpu as pltpu
from jax.sharding import PartitionSpec as P

NX = 128
NY = 128
NZ = 32
NT = 16
MX = 16
MY = 16
MZ = 16
MT = 8
BATCH = 1
KX = 32
KT = 16
CHANS = 8
CELLS = NY * NZ
KQ = 1024
LANES = 128
PARTS = 2
WIDTH = 512
DENSITY = 1.0 / math.sqrt(2.0 * math.pi)
F32 = jnp.float32
BF16 = jnp.bfloat16


def basis(length, modes):
    frequency = np.concatenate([np.arange(modes + 1), np.arange(1, modes)])
    samples_at = np.arange(length)
    phases = (2.0 * math.pi / length) * (frequency[:, None] * samples_at[None, :] % length)
    cosine_row = np.arange(2 * modes) <= modes
    waves = np.where(cosine_row[:, None], np.cos(phases), np.sin(phases))
    at_edge = cosine_row & ((frequency == 0) | (2 * frequency == length))
    scales = np.where(at_edge, math.sqrt(1.0 / length), math.sqrt(2.0 / length))
    return (waves * scales[:, None]).astype(np.float32)


def narrow(table):
    return np.asarray(table, np.float32).astype(ml_dtypes.bfloat16)


def vmem_params(mebibytes):
    return pltpu.CompilerParams(vmem_limit_bytes=mebibytes * 1024 * 1024)


def matmul(left, right):
    return jnp.dot(left, right, preferred_element_type=F32)


def matmul_turned(left, right):
    return lax.dot_general(
        left, right, (((1,), (1,)), ((), ())), preferred_element_type=F32
    )


def swap_groups(tiles):
    rows = tiles[0].shape[0]
    lane = lax.broadcasted_iota(jnp.int32, (rows, LANES), 1)
    low_half = lane < 64
    even = (lane // 32) % 2 == 0
    first, second, third, fourth = tiles
    b0 = jnp.where(low_half, first, pltpu.roll(third, 64, 1))
    b2 = jnp.where(low_half, pltpu.roll(first, 64, 1), third)
    b1 = jnp.where(low_half, second, pltpu.roll(fourth, 64, 1))
    b3 = jnp.where(low_half, pltpu.roll(second, 64, 1), fourth)
    return (
        jnp.where(even, b0, pltpu.roll(b1, 32, 1)),
        jnp.where(even, pltpu.roll(b0, 96, 1), b1),
        jnp.where(even, b2, pltpu.roll(b3, 32, 1)),
        jnp.where(even, pltpu.roll(b2, 96, 1), b3),
    )


def pack_modes(modes_ref, held_ref, packed_ref, sems, xl, tl):
    sends = []
    for tile in range(KQ // LANES):
        modes = modes_ref[tile * LANES : (tile + 1) * LANES, :].T
        split = modes.reshape(xl, tl, CHANS, LANES)
        tiles = [split[:, step].reshape(xl * CHANS, LANES) for step in range(tl)]
        owners = slice(tile * tl, (tile + 1) * tl)
        held_ref[owners] = jnp.stack([block.astype(BF16) for block in swap_groups(tiles)])
        send = pltpu.make_async_copy(held_ref.at[owners], packed_ref.at[owners], sems.at[tile])
        send.start()
        sends.append(send)
    for send in sends:
        send.wait()


def unpack_modes(packed_ref, wide_ref, xl, tl):
    for tile in range(KQ // LANES):
        tiles = [packed_ref[tile * tl + owner].astype(F32) for owner in range(tl)]
        for step, block in enumerate(swap_groups(tiles)):
            wide_ref[:, step, :, tile * LANES : (tile + 1) * LANES] = block.reshape(
                xl, CHANS, LANES
            )


def analyse_kernel(
    xl, tl, field_ref, table_ref, packed_ref, field, table, total, held, field_sems, table_sems, sems
):
    chunks = table.shape[0]
    ahead = 4
    fetches = []
    for at in range(chunks):
        lanes = slice(at * WIDTH, (at + 1) * WIDTH)
        fetches.append(
            (
                pltpu.make_async_copy(field_ref.at[:, lanes], field.at[at], field_sems.at[at]),
                pltpu.make_async_copy(table_ref.at[at], table.at[at], table_sems.at[at]),
            )
        )

    def start(at):
        for fetch in fetches[at]:
            fetch.start()

    for at in range(ahead):
        start(at)
    for at in range(0, chunks, 2):
        for now in (at, at + 1):
            for fetch in fetches[now]:
                fetch.wait()
            if now + ahead < chunks:
                start(now + ahead)
        part = matmul_turned(
            jnp.concatenate([table[at], table[at + 1]], axis=1),
            jnp.concatenate([field[at], field[at + 1]], axis=1),
        )
        total[...] = part if at == 0 else total[...] + part
    pack_modes(total, held, packed_ref, sems, xl, tl)


def analyse(field, table, xl, tl, devices):
    rows = xl * tl * CHANS
    chunks = CELLS // WIDTH
    packed = (devices, xl * CHANS, LANES)
    return pl.pallas_call(
        functools.partial(analyse_kernel, xl, tl),
        in_specs=[pl.BlockSpec(memory_space=pltpu.HBM)] * 2,
        out_specs=pl.BlockSpec(memory_space=pl.ANY),
        out_shape=jax.ShapeDtypeStruct(packed, BF16),
        scratch_shapes=[
            pltpu.VMEM((chunks, rows, WIDTH), BF16),
            pltpu.VMEM((chunks, KQ, WIDTH), BF16),
            pltpu.VMEM((KQ, rows), F32),
            pltpu.VMEM(packed, BF16),
            pltpu.SemaphoreType.DMA((chunks,)),
            pltpu.SemaphoreType.DMA((chunks,)),
            pltpu.SemaphoreType.DMA((KQ // LANES,)),
        ],
        compiler_params=vmem_params(60),
        cost_estimate=pl.CostEstimate(
            flops=2 * rows * CELLS * KQ, bytes_accessed=13 << 20, transcendentals=0
        ),
        name="analyse",
    )(field, table)


def weight_kernel(weight_ref, packed_ref):
    for kx in range(weight_ref.shape[0]):
        for group in range(KT // 4):
            parts = [weight_ref[kx, 4 * group + k] for k in range(4)]
            joined = jnp.concatenate(parts, axis=-1).reshape(CHANS * CHANS, LANES)
            packed_ref[kx, :, group * LANES : (group + 1) * LANES] = joined.astype(BF16)


def pack_weight(weight):
    per = 4
    own = weight.shape[4]
    return pl.pallas_call(
        weight_kernel,
        grid=(KX // per,),
        in_specs=[pl.BlockSpec((per, KT, CHANS, CHANS, own), lambda n: (n, 0, 0, 0, 0))],
        out_specs=pl.BlockSpec((per, CHANS * CHANS, KT * own), lambda n: (n, 0, 0)),
        out_shape=jax.ShapeDtypeStruct((KX, CHANS * CHANS, KT * own), BF16),
        compiler_params=vmem_params(60),
        cost_estimate=pl.CostEstimate(flops=1 << 20, bytes_accessed=20 << 20, transcendentals=0),
        name="pack_weight",
    )(weight)


def to_modes(spread_refs, x_table_ref, t_table_ref):
    total = 0.0
    for part, spread_ref in enumerate(spread_refs):
        gx, ta, rows, _ = spread_ref.shape
        beside = jnp.concatenate(
            [spread_ref[:, at].reshape(gx * rows, LANES) for at in range(ta)], axis=1
        )
        total = total + matmul(x_table_ref[part], beside)
    return matmul(total.astype(BF16), t_table_ref[...])


def from_modes(modes, x_table_ref, t_table_ref, held_ref, back_refs, sems):
    parts, gx, ta, rows, _ = held_ref.shape
    half = matmul(modes.astype(BF16), t_table_ref[...]).astype(BF16)
    pieces = sems.shape[1]
    per = gx // pieces
    sends = []
    for part in range(parts):
        for piece in range(pieces):
            table = x_table_ref[part, piece * per * rows : (piece + 1) * per * rows, :]
            full = matmul(table, half).astype(BF16)
            owners = slice(piece * per, (piece + 1) * per)
            for at in range(ta):
                held_ref[part, owners, at] = full[:, at * LANES : (at + 1) * LANES].reshape(
                    per, rows, LANES
                )
            send = pltpu.make_async_copy(
                held_ref.at[part, owners], back_refs[part].at[owners], sems.at[part, piece]
            )
            send.start()
            sends.append(send)
    for send in sends:
        send.wait()


def mix_kernel(
    backward,
    afters,
    weight_ref,
    *refs,
):
    x_in_ref, t_in_ref, x_out_ref, t_out_ref = refs[afters : afters + 4]
    refs = refs[afters + 4 :]
    ins, outs = x_in_ref.shape[0], x_out_ref.shape[0]
    spread_refs, modes_ref, back_refs = refs[:ins], refs[ins], refs[ins + 1 : ins + 1 + outs]
    scratch = refs[ins + 1 + outs :]
    weight, modes, mixed, held, x_in, t_in, x_out, t_out = scratch[:8]
    spreads, (sems, weight_sems, spread_sems, back_sems) = scratch[8:-4], scratch[-4:]
    arrivals = [
        pltpu.make_async_copy(source, target, spread_sems.at[at])
        for at, (source, target) in enumerate(zip(spread_refs, spreads))
    ]
    pieces = weight_sems.shape[0]
    per = KX // pieces
    sources = (x_in_ref, t_in_ref, t_out_ref, x_out_ref)
    tables = [
        pltpu.make_async_copy(source, target, sems.at[at])
        for at, (source, target) in enumerate(zip(sources, (x_in, t_in, t_out, x_out)))
    ]
    fetches = []
    for at in range(pieces):
        part = slice(at * per, (at + 1) * per)
        fetches.append(
            pltpu.make_async_copy(weight_ref.at[part], weight.at[part], weight_sems.at[at])
        )
    for copy in arrivals + tables[:2] + fetches + tables[2:]:
        copy.start()
    for copy in arrivals + tables[:2]:
        copy.wait()
    modes[...] = to_modes(spreads, x_in, t_in)
    keep = pltpu.make_async_copy(modes, modes_ref, sems.at[4])
    keep.start()
    for fetch in fetches:
        fetch.wait()
    for kx in range(KX):
        rows = slice(kx * CHANS, (kx + 1) * CHANS)
        own = modes[rows, :]
        weights = weight[kx].astype(F32).reshape(CHANS, CHANS, own.shape[1])
        if backward:
            sums = [jnp.sum(own * weights[i], axis=0, keepdims=True) for i in range(CHANS)]
            mixed[rows, :] = jnp.concatenate(sums, axis=0)
        else:
            total = own[0:1, :] * weights[0]
            for i in range(1, CHANS):
                total = total + own[i : i + 1, :] * weights[i]
            mixed[rows, :] = total
    tables[2].wait()
    tables[3].wait()
    from_modes(mixed[...], x_out, t_out, held, back_refs, back_sems)
    keep.wait()


def mix(spreads, weight, after, tables, backward):
    modes = (KX * CHANS, weight.shape[2])
    gx, ta, _, lanes = spreads[0].shape
    outs = tables[2].shape[0]
    back = (gx, ta, tables[2].shape[1] // gx, lanes)
    anywhere = pl.BlockSpec(memory_space=pl.ANY)
    apart = pl.BlockSpec(memory_space=pltpu.HBM)
    return pl.pallas_call(
        functools.partial(mix_kernel, backward, len(after)),
        out_shape=[jax.ShapeDtypeStruct(modes, F32)] + [jax.ShapeDtypeStruct(back, BF16)] * outs,
        in_specs=[apart] + [anywhere] * len(after) + [apart] * 4 + [anywhere] * len(spreads),
        out_specs=[apart] + [anywhere] * outs,
        scratch_shapes=[
            pltpu.VMEM(weight.shape, BF16),
            pltpu.VMEM(modes, F32),
            pltpu.VMEM(modes, F32),
            pltpu.VMEM((outs,) + back, BF16),
            *[pltpu.VMEM(table.shape, BF16) for table in tables],
            *[pltpu.VMEM(spread.shape, BF16) for spread in spreads],
            pltpu.SemaphoreType.DMA((5,)),
            pltpu.SemaphoreType.DMA((8,)),
            pltpu.SemaphoreType.DMA((len(spreads),)),
            pltpu.SemaphoreType.DMA((outs, 4 // outs)),
        ],
        compiler_params=vmem_params(60),
        cost_estimate=pl.CostEstimate(flops=1 << 30, bytes_accessed=9 << 20, transcendentals=0),
        name="mix_back" if backward else "mix",
    )(weight, *after, *tables, *spreads)


def outer_kernel(spectrum_ref, grad_ref, result_ref):
    own = result_ref.shape[4]
    for kx in range(result_ref.shape[0]):
        rows = slice(kx * CHANS, (kx + 1) * CHANS)
        for group in range(KT // 4):
            at = slice(group * LANES, (group + 1) * LANES)
            inputs = spectrum_ref[rows, at]
            grads = grad_ref[rows, at]
            for i in range(CHANS):
                product = inputs[i : i + 1, :] * grads
                for k in range(4):
                    result_ref[kx, 4 * group + k, i] = product[:, k * own : (k + 1) * own]


def outer(spectrum, grad, own):
    per = 4
    width = KT * own
    return pl.pallas_call(
        outer_kernel,
        grid=(KX // per,),
        in_specs=[pl.BlockSpec((per * CHANS, width), lambda n: (n, 0))] * 2,
        out_specs=pl.BlockSpec((per, KT, CHANS, CHANS, own), lambda n: (n, 0, 0, 0, 0)),
        out_shape=jax.ShapeDtypeStruct((KX, KT, CHANS, CHANS, own), F32),
        compiler_params=vmem_params(60),
        cost_estimate=pl.CostEstimate(flops=1 << 20, bytes_accessed=17 << 20, transcendentals=0),
        name="outer",
    )(spectrum, grad)


def normal_parts(values):
    scaled = 1.0 + 0.2316419 * jnp.abs(values)
    guess = pl.reciprocal(scaled, approx=True)
    t = guess * (2.0 - scaled * guess)
    decay = jnp.exp(values * values * -0.5)
    series = (1.330274429 * DENSITY) * t - 1.821255978 * DENSITY
    series = series * t + 1.781477937 * DENSITY
    series = series * t - 0.356563782 * DENSITY
    series = series * t + 0.319381530 * DENSITY
    tail = decay * (series * t)
    return jnp.where(values >= 0.0, 1.0 - tail, tail), decay


def point_kernel(mixer_ref, *refs):
    grad_refs, mixed_ref = refs[:PARTS], refs[PARTS]
    rows = mixer_ref.shape[0]
    for at in range(mixed_ref.shape[0]):
        for part, grad_ref in enumerate(grad_refs):
            mixed = matmul(mixer_ref[...], grad_ref[at])
            mixed_ref[at, part * rows : (part + 1) * rows, :] = mixed.astype(BF16)


def point(grads, mixer):
    chunks, rows, _ = grads[0].shape
    per = 2
    return pl.pallas_call(
        point_kernel,
        grid=(chunks // per,),
        in_specs=[pl.BlockSpec((rows, rows), lambda n: (0, 0))]
        + [pl.BlockSpec((per, rows, WIDTH), lambda n: (n, 0, 0))] * PARTS,
        out_specs=pl.BlockSpec((per, PARTS * rows, WIDTH), lambda n: (n, 0, 0)),
        out_shape=jax.ShapeDtypeStruct((chunks, PARTS * rows, WIDTH), BF16),
        compiler_params=vmem_params(60),
        cost_estimate=pl.CostEstimate(
            flops=2 * PARTS * rows * CELLS * rows, bytes_accessed=8 << 20, transcendentals=0
        ),
        name="point",
    )(mixer, *grads)


def middle_kernel(
    xl,
    tl,
    packed_ref,
    field_ref,
    cotangent_ref,
    table_ref,
    mixer_ref,
    bias_ref,
    sums_in_ref,
    _,
    output_ref,
    grad_ref,
    sent_ref,
    sums_ref,
    wide,
    modes,
    total,
    held,
    sems,
):
    step = pl.program_id(0)
    rows, width = field_ref.shape
    tile = 256
    chunk = 32
    ones = 16

    @pl.when(step == 0)
    def _():
        unpack_modes(packed_ref, wide, xl, tl)
        modes[...] = wide[...].reshape(rows, KQ).astype(BF16)
        total[...] = jnp.zeros_like(total)

    blocks = table_ref.shape[0]

    def build(at):
        block, first = divmod(at.start, WIDTH)
        spatial = matmul(modes[...], table_ref[block, :, first : first + tile])
        return spatial + matmul(mixer_ref[...], field_ref[:, at])

    def pointwise(pre, at):
        for first in range(0, rows, chunk):
            part = slice(first, first + chunk)
            values = pre[part, :] + jnp.concatenate([bias_ref[part, :]] * (tile // LANES), axis=1)
            integral, decay = normal_parts(values)
            output_ref[part, at] = (values * integral).astype(BF16)
            slope = integral + (values * DENSITY) * decay
            grad = (cotangent_ref[part, at].astype(F32) * slope).astype(BF16)
            grad_ref[at.start // WIDTH, part, at.start % WIDTH : at.start % WIDTH + tile] = grad

    tiles = [slice(first, first + tile) for first in range(0, width, tile)]
    ready = build(tiles[0])
    for index, at in enumerate(tiles):
        pre = ready
        if index + 1 < len(tiles):
            ready = build(tiles[index + 1])
        pointwise(pre, at)
    passing = jnp.concatenate([table_ref[at] for at in range(blocks)], axis=1)
    passing = jnp.concatenate([passing, field_ref[...], jnp.ones((ones, width), BF16)], axis=0)
    grads = jnp.concatenate([grad_ref[at] for at in range(blocks)], axis=1)
    total[...] += matmul_turned(passing, grads)

    @pl.when(step == pl.num_programs(0) - 1)
    def _():
        pack_modes(total, held, sent_ref, sems, xl, tl)
        row = lax.broadcasted_iota(jnp.int32, (rows, rows), 0)
        column = lax.broadcasted_iota(jnp.int32, (rows, rows), 1)
        gram = total[KQ : KQ + rows, :].T
        bias = total[KQ + rows : KQ + rows + CHANS, :]
        same = jnp.where(row // CHANS == column // CHANS, gram, 0.0)
        folded = jnp.sum(same.reshape(rows // CHANS, CHANS, rows), axis=0)
        source = lax.broadcasted_iota(jnp.int32, (rows, LANES), 0)
        target = lax.broadcasted_iota(jnp.int32, (rows, LANES), 1)
        select = jnp.where(source % CHANS == target, 1.0, 0.0)
        chan = lax.broadcasted_iota(jnp.int32, (CHANS, rows), 0)
        place = lax.broadcasted_iota(jnp.int32, (CHANS, rows), 1)
        own_bias = jnp.sum(
            jnp.where(place % CHANS == chan, bias, 0.0), axis=1, keepdims=True
        )
        sums = jnp.dot(
            folded, select, precision=lax.Precision.HIGHEST, preferred_element_type=F32
        )
        lane = lax.broadcasted_iota(jnp.int32, (CHANS, LANES), 1)
        sums = jnp.where(lane == CHANS, own_bias, sums)
        sums_ref[...] = sums if sums_in_ref is None else sums_in_ref[...] + sums


def middle(packed, field, cotangent, table, mixer, bias, sums, output, part, xl, tl):
    rows = xl * tl * CHANS
    per = 2
    chunks = CELLS // WIDTH
    whole = lambda *shape: pl.BlockSpec(shape, lambda n: (0,) * len(shape))
    tile = pl.BlockSpec((rows, per * WIDTH), lambda n: (part, n))
    kernel = functools.partial(middle_kernel, xl, tl)
    operands = (packed, field, cotangent, table, mixer, bias)
    specs = [
        whole(*packed.shape),
        tile,
        tile,
        pl.BlockSpec((per, KQ, WIDTH), lambda n: (n, 0, 0)),
        whole(rows, rows),
        whole(rows, LANES),
    ]
    aliases = {}
    if output is None:
        inner = kernel
        kernel = lambda *refs: inner(*refs[:6], None, None, *refs[6:])
    else:
        operands += (sums, output)
        aliases = {len(operands) - 1: 0}
        specs += [whole(CHANS, LANES), pl.BlockSpec(memory_space=pltpu.HBM)]
    return pl.pallas_call(
        kernel,
        grid=(chunks // per,),
        in_specs=specs,
        out_specs=[
            tile,
            pl.BlockSpec((per, rows, WIDTH), lambda n: (n, 0, 0)),
            pl.BlockSpec(memory_space=pl.ANY),
            whole(CHANS, LANES),
        ],
        out_shape=(
            jax.ShapeDtypeStruct(field.shape, BF16),
            jax.ShapeDtypeStruct((chunks, rows, WIDTH), BF16),
            jax.ShapeDtypeStruct(packed.shape, BF16),
            jax.ShapeDtypeStruct((CHANS, LANES), F32),
        ),
        scratch_shapes=[
            pltpu.VMEM((xl, tl, CHANS, KQ), F32),
            pltpu.VMEM((rows, KQ), BF16),
            pltpu.VMEM((KQ + rows + 16, rows), F32),
            pltpu.VMEM(packed.shape, BF16),
            pltpu.SemaphoreType.DMA((KQ // LANES,)),
        ],
        input_output_aliases=aliases,
        compiler_params=vmem_params(60),
        cost_estimate=pl.CostEstimate(
            flops=5 * rows * CELLS * KQ, bytes_accessed=18 << 20, transcendentals=rows * CELLS
        ),
        name="middle",
    )(*operands)


def last_kernel(xl, tl, packed_ref, table_ref, mixed_ref, field_ref, *scratch):
    wide, modes, table, mixed, field, table_sems, mixed_sems, field_sems = scratch
    chunks = table.shape[0]
    ahead = 4
    fetches, sends = [], []
    for at in range(chunks):
        lanes = slice(at * WIDTH, (at + 1) * WIDTH)
        fetches.append(
            (
                pltpu.make_async_copy(table_ref.at[at], table.at[at], table_sems.at[at]),
                pltpu.make_async_copy(mixed_ref.at[at], mixed.at[at], mixed_sems.at[at]),
            )
        )
        sends.append(
            pltpu.make_async_copy(field.at[at], field_ref.at[:, lanes], field_sems.at[at])
        )

    def start(at):
        for fetch in fetches[at]:
            fetch.start()

    for at in range(ahead):
        start(at)
    unpack_modes(packed_ref, wide, xl, tl)
    modes[...] = wide[...].reshape(modes.shape).astype(BF16)
    for at in range(chunks):
        for fetch in fetches[at]:
            fetch.wait()
        if at + ahead < chunks:
            start(at + ahead)
        field[at] = (matmul(modes[...], table[at]) + mixed[at].astype(F32)).astype(BF16)
        sends[at].start()
    for send in sends:
        send.wait()


def last(packed, mixed, table, xl, tl):
    rows = xl * tl * CHANS
    chunks = CELLS // WIDTH
    apart = pl.BlockSpec(memory_space=pltpu.HBM)
    return pl.pallas_call(
        functools.partial(last_kernel, xl, tl),
        in_specs=[pl.BlockSpec(memory_space=pltpu.VMEM), apart, apart],
        out_specs=apart,
        out_shape=jax.ShapeDtypeStruct((rows, CELLS), BF16),
        scratch_shapes=[
            pltpu.VMEM((xl, tl, CHANS, KQ), F32),
            pltpu.VMEM((rows, KQ), BF16),
            pltpu.VMEM((chunks, KQ, WIDTH), BF16),
            pltpu.VMEM((chunks, rows, WIDTH), BF16),
            pltpu.VMEM((chunks, rows, WIDTH), BF16),
            pltpu.SemaphoreType.DMA((chunks,)),
            pltpu.SemaphoreType.DMA((chunks,)),
            pltpu.SemaphoreType.DMA((chunks,)),
        ],
        compiler_params=vmem_params(44),
        cost_estimate=pl.CostEstimate(
            flops=2 * rows * CELLS * KQ, bytes_accessed=18 << 20, transcendentals=0
        ),
        name="last",
    )(packed, table, mixed)


def swap(blocks):
    return lax.all_to_all(blocks, ("gx", "ta"), split_axis=0, concat_axis=0, tiled=True)


def sum_everywhere(values, devices):
    step = 1
    while step < devices:
        pairs = [(at, at ^ step) for at in range(devices)]
        values = values + lax.ppermute(values, ("gx", "ta"), pairs)
        step *= 2
    return values


def fast_body(gx, ta, features, cotangent, spec_weight, point_weight, bias_vector):
    _, xl_all, tl, _, cells = features.shape
    own = spec_weight.shape[4]
    devices = gx * ta
    xl = xl_all // PARTS
    rows = xl * tl * CHANS
    yz = np.kron(
        narrow(basis(NY, MY)).astype(np.float32), narrow(basis(NZ, MZ)).astype(np.float32)
    )
    blocks = yz.reshape(KQ, CELLS // WIDTH, WIDTH).transpose(1, 0, 2)
    table = jnp.asarray(narrow(blocks))
    x_whole = basis(NX, MX).reshape(KX, gx, 1, xl_all)
    x_split = basis(NX, MX).reshape(KX, gx, PARTS, xl)
    x_tables = [
        np.stack(
            [
                np.kron(split[:, :, part].reshape(KX, -1), np.eye(CHANS))
                for part in range(split.shape[2])
            ]
        )
        for split in (x_whole, x_split)
    ]
    x_in = [jnp.asarray(narrow(x_table)) for x_table in x_tables]
    x_out = [jnp.asarray(narrow(x_table.transpose(0, 2, 1))) for x_table in x_tables]
    t_wide = np.kron(basis(NT, MT), np.eye(own))
    t_in, t_out = jnp.asarray(narrow(t_wide.T)), jnp.asarray(narrow(t_wide))
    norm_scale = float(BATCH * NX * NT * NY * NZ) ** (-0.5)

    field = features.reshape(PARTS * rows, cells)
    cot = cotangent.reshape(PARTS * rows, cells)
    pick = np.tile(np.eye(CHANS, dtype=np.float32), (rows // CHANS, 1))
    same = np.kron(np.eye(rows // CHANS, dtype=np.float32), np.ones((CHANS, CHANS), np.float32))
    picked = jnp.asarray(narrow(pick))
    spread_point = matmul(matmul(picked, point_weight).astype(BF16), picked.T)
    spread_back = matmul(matmul(picked, point_weight.T).astype(BF16), picked.T)
    mixer = (spread_point * jnp.asarray(same)).astype(BF16)
    mixer_back = (spread_back * jnp.asarray(same)).astype(BF16)
    bias = jnp.dot(
        jnp.asarray(pick),
        jnp.broadcast_to(bias_vector[:, None], (CHANS, LANES)),
        precision=lax.Precision.HIGHEST,
    )
    part_shape = (gx, ta, xl * CHANS, LANES)
    whole_shape = (gx, ta, xl_all * CHANS, LANES)
    packed_weight = pack_weight(spec_weight)

    spread_in = swap(analyse(field, table, xl_all, tl, devices)).reshape(whole_shape)
    spectrum, *mixed = mix(
        [spread_in], packed_weight, (mixer, mixer_back, bias), (x_in[0], t_in, x_out[1], t_out), False
    )
    output, sums = None, None
    grads, spread_grad = [], []
    for part in range(PARTS):
        returned = swap(mixed[part].reshape(devices, xl * CHANS, LANES))
        output, grad, sent, sums = middle(
            returned, field, cot, table, mixer, bias, sums, output, part, xl, tl
        )
        grads.append(grad)
        spread_grad.append(swap(sent).reshape(part_shape))
    summed = sum_everywhere(sums, devices)
    grad_modes, mixed_back = mix(
        spread_grad, packed_weight, (summed,), (x_in[1], t_in, x_out[0], t_out), True
    )
    grad_back = swap(mixed_back.reshape(devices, xl_all * CHANS, LANES))
    grad_spec = outer(spectrum, grad_modes, own)
    grad_field = last(grad_back, point(grads, mixer_back), table, xl_all, tl)
    summed = summed * norm_scale
    return (
        output.reshape(features.shape),
        grad_field.reshape(features.shape),
        grad_spec,
        summed[:, :CHANS],
        summed[:, CHANS],
    )


def analyse_yz(spatial, yz_table):
    return jnp.einsum(
        "qp,bxtcp->bxtcq", yz_table, spatial.astype(F32), precision=lax.Precision.HIGHEST
    )


def build_yz(modes_in, yz_table):
    return jnp.einsum(
        "qp,bxtcq->bxtcp", yz_table, modes_in.astype(F32), precision=lax.Precision.HIGHEST
    )


def analyse_xt(spread, table):
    sizes = spread.shape
    flattened = spread.reshape(sizes[0], sizes[1] * sizes[2], sizes[3] * sizes[4]).astype(F32)
    spectral = jnp.einsum("mp,bpr->bmr", table, flattened, precision=lax.Precision.HIGHEST)
    return spectral.reshape(sizes[0], KX, KT, sizes[3], sizes[4])


def synthesise_xt(modes_in, table):
    sizes = modes_in.shape
    flattened = modes_in.reshape(sizes[0], sizes[1] * sizes[2], sizes[3] * sizes[4])
    spatial = jnp.einsum("mp,bmr->bpr", table, flattened, precision=lax.Precision.HIGHEST)
    return spatial.reshape(sizes[0], NX, NT, sizes[3], sizes[4])


def to_owners(modes_in):
    first = lax.all_to_all(modes_in, "gx", split_axis=4, concat_axis=1, tiled=True)
    return lax.all_to_all(first, "ta", split_axis=4, concat_axis=2, tiled=True)


def to_cells(spread, shape):
    first = lax.all_to_all(
        spread[:, :, :, :, None, None, :], "gx", split_axis=1, concat_axis=4, tiled=True
    )
    second = lax.all_to_all(first, "ta", split_axis=2, concat_axis=5, tiled=True)
    return second.reshape(shape[:4] + (-1,))


def general_body(features, cotangent, spec_weight, point_weight, bias_vector):
    shape = features.shape
    yz_table = jnp.asarray(
        np.kron(narrow(basis(NY, MY)).astype(np.float32), narrow(basis(NZ, MZ)).astype(np.float32))
    )
    xt_table = jnp.asarray(np.kron(basis(NX, MX), basis(NT, MT)))
    norm_scale = float(BATCH * NX * NT * NY * NZ) ** (-0.5)
    highest = lax.Precision.HIGHEST
    spectrum = analyse_xt(to_owners(analyse_yz(features, yz_table).astype(BF16)), xt_table)
    mixed = jnp.einsum("bklip,kliop->bklop", spectrum, spec_weight, precision=highest)
    returned = to_cells(synthesise_xt(mixed, xt_table).astype(BF16), shape)
    pointwise = jnp.einsum("oi,bxtip->bxtop", point_weight, features, preferred_element_type=F32)
    pre = build_yz(returned, yz_table) + pointwise + bias_vector[:, None]
    integral = 0.5 * (1.0 + jax.scipy.special.erf(pre * 0.7071067811865476))
    output = (pre * integral).astype(BF16)
    slope = integral + pre * jnp.exp(-0.5 * pre * pre) * 0.3989422804014327
    grad_pre = (cotangent.astype(F32) * slope).astype(BF16)
    local_point = jnp.einsum("bxtop,bxtip->oi", grad_pre, features, preferred_element_type=F32)
    local_bias = jnp.sum(grad_pre.astype(F32), axis=(0, 1, 2, 4))
    total_point, total_bias = lax.psum((local_point, local_bias), ("gx", "ta"))
    grad_modes = analyse_xt(to_owners(analyse_yz(grad_pre, yz_table).astype(BF16)), xt_table)
    grad_spec = jnp.einsum("bklip,bklop->kliop", spectrum, grad_modes, precision=highest)
    grad_in = jnp.einsum("kliop,bklop->bklip", spec_weight, grad_modes, precision=highest)
    grad_back = to_cells(synthesise_xt(grad_in, xt_table).astype(BF16), shape)
    point_term = jnp.einsum("oi,bxtop->bxtip", point_weight, grad_pre, preferred_element_type=F32)
    grad_field = (build_yz(grad_back, yz_table) + point_term).astype(BF16)
    return (output, grad_field, grad_spec, total_point * norm_scale, total_bias * norm_scale)


def solution(mesh):
    split_field = P(None, "gx", "ta", None, None)
    split_weight = P(None, None, None, None, ("gx", "ta"))
    in_specs = (split_field, split_field, split_weight, P(), P())
    out_specs = (split_field, split_field, split_weight, P(), P())
    gx, ta = mesh.shape["gx"], mesh.shape["ta"]
    own, xl, tl = KQ // (gx * ta), NX // gx, NT // ta
    if own == 32 and xl * CHANS == LANES and tl == 4:
        body = functools.partial(fast_body, gx, ta)
    else:
        body = general_body
    return jax.shard_map(body, mesh=mesh, in_specs=in_specs, out_specs=out_specs, check_vma=False)
```

```python
import functools
import math

import jax
import jax.numpy as jnp
import ml_dtypes
import numpy as np
from jax import lax
from jax.experimental import pallas as pl
from jax.experimental.pallas import tpu as pltpu
from jax.sharding import PartitionSpec as P

NX = 128
NY = 128
NZ = 32
NT = 16
MX = 16
MY = 16
MZ = 16
MT = 8
BATCH = 1
KX = 32
KT = 16
CHANS = 8
CELLS = NY * NZ
KQ = 1024
LANES = 128
PARTS = 2
WIDTH = 512
DENSITY = 1.0 / math.sqrt(2.0 * math.pi)
F32 = jnp.float32
BF16 = jnp.bfloat16


def basis(length, modes):
    frequency = np.concatenate([np.arange(modes + 1), np.arange(1, modes)])
    samples_at = np.arange(length)
    phases = (2.0 * math.pi / length) * (frequency[:, None] * samples_at[None, :] % length)
    cosine_row = np.arange(2 * modes) <= modes
    waves = np.where(cosine_row[:, None], np.cos(phases), np.sin(phases))
    at_edge = cosine_row & ((frequency == 0) | (2 * frequency == length))
    scales = np.where(at_edge, math.sqrt(1.0 / length), math.sqrt(2.0 / length))
    return (waves * scales[:, None]).astype(np.float32)


def narrow(table):
    return np.asarray(table, np.float32).astype(ml_dtypes.bfloat16)


def vmem_params(mebibytes):
    return pltpu.CompilerParams(vmem_limit_bytes=mebibytes * 1024 * 1024)


def matmul(left, right):
    return jnp.dot(left, right, preferred_element_type=F32)


def matmul_turned(left, right):
    return lax.dot_general(
        left, right, (((1,), (1,)), ((), ())), preferred_element_type=F32
    )


def swap_groups(tiles):
    rows = tiles[0].shape[0]
    lane = lax.broadcasted_iota(jnp.int32, (rows, LANES), 1)
    low_half = lane < 64
    even = (lane // 32) % 2 == 0
    first, second, third, fourth = tiles
    b0 = jnp.where(low_half, first, pltpu.roll(third, 64, 1))
    b2 = jnp.where(low_half, pltpu.roll(first, 64, 1), third)
    b1 = jnp.where(low_half, second, pltpu.roll(fourth, 64, 1))
    b3 = jnp.where(low_half, pltpu.roll(second, 64, 1), fourth)
    return (
        jnp.where(even, b0, pltpu.roll(b1, 32, 1)),
        jnp.where(even, pltpu.roll(b0, 96, 1), b1),
        jnp.where(even, b2, pltpu.roll(b3, 32, 1)),
        jnp.where(even, pltpu.roll(b2, 96, 1), b3),
    )


def pack_modes(modes_ref, held_ref, packed_ref, sems, xl, tl):
    sends = []
    for tile in range(KQ // LANES):
        modes = modes_ref[tile * LANES : (tile + 1) * LANES, :].T
        split = modes.reshape(xl, tl, CHANS, LANES)
        tiles = [split[:, step].reshape(xl * CHANS, LANES) for step in range(tl)]
        owners = slice(tile * tl, (tile + 1) * tl)
        held_ref[owners] = jnp.stack([block.astype(BF16) for block in swap_groups(tiles)])
        send = pltpu.make_async_copy(held_ref.at[owners], packed_ref.at[owners], sems.at[tile])
        send.start()
        sends.append(send)
    for send in sends:
        send.wait()


def unpack_modes(packed_ref, wide_ref, xl, tl):
    for tile in range(KQ // LANES):
        tiles = [packed_ref[tile * tl + owner].astype(F32) for owner in range(tl)]
        for step, block in enumerate(swap_groups(tiles)):
            wide_ref[:, step, :, tile * LANES : (tile + 1) * LANES] = block.reshape(
                xl, CHANS, LANES
            )


def analyse_kernel(
    xl, tl, field_ref, table_ref, packed_ref, field, table, total, held, field_sems, table_sems, sems
):
    chunks = table.shape[0]
    ahead = 4
    fetches = []
    for at in range(chunks):
        lanes = slice(at * WIDTH, (at + 1) * WIDTH)
        fetches.append(
            (
                pltpu.make_async_copy(field_ref.at[:, lanes], field.at[at], field_sems.at[at]),
                pltpu.make_async_copy(table_ref.at[at], table.at[at], table_sems.at[at]),
            )
        )

    def start(at):
        for fetch in fetches[at]:
            fetch.start()

    for at in range(ahead):
        start(at)
    for at in range(0, chunks, 2):
        for now in (at, at + 1):
            for fetch in fetches[now]:
                fetch.wait()
            if now + ahead < chunks:
                start(now + ahead)
        part = matmul_turned(
            jnp.concatenate([table[at], table[at + 1]], axis=1),
            jnp.concatenate([field[at], field[at + 1]], axis=1),
        )
        total[...] = part if at == 0 else total[...] + part
    pack_modes(total, held, packed_ref, sems, xl, tl)


def analyse(field, table, xl, tl, devices):
    rows = xl * tl * CHANS
    chunks = CELLS // WIDTH
    packed = (devices, xl * CHANS, LANES)
    return pl.pallas_call(
        functools.partial(analyse_kernel, xl, tl),
        in_specs=[pl.BlockSpec(memory_space=pltpu.HBM)] * 2,
        out_specs=pl.BlockSpec(memory_space=pl.ANY),
        out_shape=jax.ShapeDtypeStruct(packed, BF16),
        scratch_shapes=[
            pltpu.VMEM((chunks, rows, WIDTH), BF16),
            pltpu.VMEM((chunks, KQ, WIDTH), BF16),
            pltpu.VMEM((KQ, rows), F32),
            pltpu.VMEM(packed, BF16),
            pltpu.SemaphoreType.DMA((chunks,)),
            pltpu.SemaphoreType.DMA((chunks,)),
            pltpu.SemaphoreType.DMA((KQ // LANES,)),
        ],
        compiler_params=vmem_params(60),
        cost_estimate=pl.CostEstimate(
            flops=2 * rows * CELLS * KQ, bytes_accessed=13 << 20, transcendentals=0
        ),
        name="analyse",
    )(field, table)


def weight_kernel(weight_ref, packed_ref, later_ref):
    for kx in range(weight_ref.shape[0]):
        for group in range(KT // 4):
            parts = [weight_ref[kx, 4 * group + k] for k in range(4)]
            joined = jnp.concatenate(parts, axis=-1).reshape(CHANS * CHANS, LANES)
            packed_ref[kx, :, group * LANES : (group + 1) * LANES] = joined.astype(BF16)
            later_ref[kx, :, group * LANES : (group + 1) * LANES] = joined.astype(BF16)


def pack_weight(weight):
    per = 4
    own = weight.shape[4]
    return pl.pallas_call(
        weight_kernel,
        grid=(KX // per,),
        in_specs=[pl.BlockSpec((per, KT, CHANS, CHANS, own), lambda n: (n, 0, 0, 0, 0))],
        out_specs=[pl.BlockSpec((per, CHANS * CHANS, KT * own), lambda n: (n, 0, 0))] * 2,
        out_shape=[jax.ShapeDtypeStruct((KX, CHANS * CHANS, KT * own), BF16)] * 2,
        compiler_params=vmem_params(24),
        cost_estimate=pl.CostEstimate(flops=1 << 20, bytes_accessed=20 << 20, transcendentals=0),
        name="pack_weight",
    )(weight)


def to_modes(spread_refs, x_table_ref, t_table_ref):
    total = 0.0
    for part, spread_ref in enumerate(spread_refs):
        gx, ta, rows, _ = spread_ref.shape
        beside = jnp.concatenate(
            [spread_ref[:, at].reshape(gx * rows, LANES) for at in range(ta)], axis=1
        )
        total = total + matmul(x_table_ref[part], beside)
    return matmul(total.astype(BF16), t_table_ref[...])


def from_modes(modes, x_table_ref, t_table_ref, held_ref, back_refs, sems):
    parts, gx, ta, rows, _ = held_ref.shape
    half = matmul(modes.astype(BF16), t_table_ref[...]).astype(BF16)
    pieces = sems.shape[1]
    per = gx // pieces
    sends = []
    for part in range(parts):
        for piece in range(pieces):
            table = x_table_ref[part, piece * per * rows : (piece + 1) * per * rows, :]
            full = matmul(table, half).astype(BF16)
            owners = slice(piece * per, (piece + 1) * per)
            for at in range(ta):
                held_ref[part, owners, at] = full[:, at * LANES : (at + 1) * LANES].reshape(
                    per, rows, LANES
                )
            send = pltpu.make_async_copy(
                held_ref.at[part, owners], back_refs[part].at[owners], sems.at[part, piece]
            )
            send.start()
            sends.append(send)
    for send in sends:
        send.wait()


def mix_kernel(
    backward,
    afters,
    weight_ref,
    *refs,
):
    x_in_ref, t_in_ref, x_out_ref, t_out_ref = refs[afters : afters + 4]
    refs = refs[afters + 4 :]
    ins, outs = x_in_ref.shape[0], x_out_ref.shape[0]
    spread_refs, modes_ref, back_refs = refs[:ins], refs[ins], refs[ins + 1 : ins + 1 + outs]
    scratch = refs[ins + 1 + outs :]
    weight, modes, mixed, held, x_in, t_in, x_out, t_out = scratch[:8]
    spreads, (sems, weight_sems, spread_sems, back_sems) = scratch[8:-4], scratch[-4:]
    arrivals = [
        pltpu.make_async_copy(source, target, spread_sems.at[at])
        for at, (source, target) in enumerate(zip(spread_refs, spreads))
    ]
    pieces = weight_sems.shape[0]
    per = KX // pieces
    sources = (x_in_ref, t_in_ref, t_out_ref, x_out_ref)
    tables = [
        pltpu.make_async_copy(source, target, sems.at[at])
        for at, (source, target) in enumerate(zip(sources, (x_in, t_in, t_out, x_out)))
    ]
    fetches = []
    for at in range(pieces):
        part = slice(at * per, (at + 1) * per)
        fetches.append(
            pltpu.make_async_copy(weight_ref.at[part], weight.at[part], weight_sems.at[at])
        )
    for copy in arrivals + tables[:2] + fetches + tables[2:]:
        copy.start()
    for copy in arrivals + tables[:2]:
        copy.wait()
    modes[...] = to_modes(spreads, x_in, t_in)
    keep = pltpu.make_async_copy(modes, modes_ref, sems.at[4])
    keep.start()
    for fetch in fetches:
        fetch.wait()
    for kx in range(KX):
        rows = slice(kx * CHANS, (kx + 1) * CHANS)
        own = modes[rows, :]
        weights = weight[kx].astype(F32).reshape(CHANS, CHANS, own.shape[1])
        if backward:
            sums = [jnp.sum(own * weights[i], axis=0, keepdims=True) for i in range(CHANS)]
            mixed[rows, :] = jnp.concatenate(sums, axis=0)
        else:
            total = own[0:1, :] * weights[0]
            for i in range(1, CHANS):
                total = total + own[i : i + 1, :] * weights[i]
            mixed[rows, :] = total
    tables[2].wait()
    tables[3].wait()
    from_modes(mixed[...], x_out, t_out, held, back_refs, back_sems)
    keep.wait()


def mix(spreads, weight, after, tables, backward):
    modes = (KX * CHANS, weight.shape[2])
    gx, ta, _, lanes = spreads[0].shape
    outs = tables[2].shape[0]
    back = (gx, ta, tables[2].shape[1] // gx, lanes)
    anywhere = pl.BlockSpec(memory_space=pl.ANY)
    apart = pl.BlockSpec(memory_space=pltpu.HBM)
    return pl.pallas_call(
        functools.partial(mix_kernel, backward, len(after)),
        out_shape=[jax.ShapeDtypeStruct(modes, F32)] + [jax.ShapeDtypeStruct(back, BF16)] * outs,
        in_specs=[apart] + [anywhere] * len(after) + [apart] * 4 + [anywhere] * len(spreads),
        out_specs=[apart] + [anywhere] * outs,
        scratch_shapes=[
            pltpu.VMEM(weight.shape, BF16),
            pltpu.VMEM(modes, F32),
            pltpu.VMEM(modes, F32),
            pltpu.VMEM((outs,) + back, BF16),
            *[pltpu.VMEM(table.shape, BF16) for table in tables],
            *[pltpu.VMEM(spread.shape, BF16) for spread in spreads],
            pltpu.SemaphoreType.DMA((5,)),
            pltpu.SemaphoreType.DMA((8,)),
            pltpu.SemaphoreType.DMA((len(spreads),)),
            pltpu.SemaphoreType.DMA((outs, 4 // outs)),
        ],
        compiler_params=vmem_params(60 if backward else 40),
        cost_estimate=pl.CostEstimate(flops=1 << 30, bytes_accessed=9 << 20, transcendentals=0),
        name="mix_back" if backward else "mix",
    )(weight, *after, *tables, *spreads)


def outer_kernel(spectrum_ref, grad_ref, result_ref):
    own = result_ref.shape[4]
    for kx in range(result_ref.shape[0]):
        rows = slice(kx * CHANS, (kx + 1) * CHANS)
        for group in range(KT // 4):
            at = slice(group * LANES, (group + 1) * LANES)
            inputs = spectrum_ref[rows, at]
            grads = grad_ref[rows, at]
            for i in range(CHANS):
                product = inputs[i : i + 1, :] * grads
                for k in range(4):
                    result_ref[kx, 4 * group + k, i] = product[:, k * own : (k + 1) * own]


def outer(spectrum, grad, own):
    per = 4
    width = KT * own
    return pl.pallas_call(
        outer_kernel,
        grid=(KX // per,),
        in_specs=[pl.BlockSpec((per * CHANS, width), lambda n: (n, 0))] * 2,
        out_specs=pl.BlockSpec((per, KT, CHANS, CHANS, own), lambda n: (n, 0, 0, 0, 0)),
        out_shape=jax.ShapeDtypeStruct((KX, KT, CHANS, CHANS, own), F32),
        compiler_params=vmem_params(24),
        cost_estimate=pl.CostEstimate(flops=1 << 20, bytes_accessed=17 << 20, transcendentals=0),
        name="outer",
    )(spectrum, grad)


def normal_parts(values):
    scaled = 1.0 + 0.2316419 * jnp.abs(values)
    guess = pl.reciprocal(scaled, approx=True)
    t = guess * (2.0 - scaled * guess)
    decay = jnp.exp(values * values * -0.5)
    series = (1.330274429 * DENSITY) * t - 1.821255978 * DENSITY
    series = series * t + 1.781477937 * DENSITY
    series = series * t - 0.356563782 * DENSITY
    series = series * t + 0.319381530 * DENSITY
    tail = decay * (series * t)
    return jnp.where(values >= 0.0, 1.0 - tail, tail), decay


def point_kernel(mixer_ref, *refs):
    grad_refs, mixed_ref = refs[:PARTS], refs[PARTS]
    rows = mixer_ref.shape[0]
    for at in range(mixed_ref.shape[0]):
        for part, grad_ref in enumerate(grad_refs):
            mixed = matmul(mixer_ref[...], grad_ref[at])
            mixed_ref[at, part * rows : (part + 1) * rows, :] = mixed.astype(BF16)


def point(grads, mixer):
    chunks, rows, _ = grads[0].shape
    per = 2
    return pl.pallas_call(
        point_kernel,
        grid=(chunks // per,),
        in_specs=[pl.BlockSpec((rows, rows), lambda n: (0, 0))]
        + [pl.BlockSpec((per, rows, WIDTH), lambda n: (n, 0, 0))] * PARTS,
        out_specs=pl.BlockSpec((per, PARTS * rows, WIDTH), lambda n: (n, 0, 0)),
        out_shape=jax.ShapeDtypeStruct((chunks, PARTS * rows, WIDTH), BF16),
        compiler_params=vmem_params(24),
        cost_estimate=pl.CostEstimate(
            flops=2 * PARTS * rows * CELLS * rows, bytes_accessed=8 << 20, transcendentals=0
        ),
        name="point",
    )(mixer, *grads)


def middle_kernel(
    xl,
    tl,
    packed_ref,
    field_ref,
    cotangent_ref,
    table_ref,
    mixer_ref,
    bias_ref,
    sums_in_ref,
    _,
    output_ref,
    grad_ref,
    sent_ref,
    sums_ref,
    wide,
    modes,
    total,
    held,
    sems,
):
    step = pl.program_id(0)
    rows, width = field_ref.shape
    tile = 256
    chunk = 32
    ones = 16

    @pl.when(step == 0)
    def _():
        unpack_modes(packed_ref, wide, xl, tl)
        modes[...] = wide[...].reshape(rows, KQ).astype(BF16)
        total[...] = jnp.zeros_like(total)

    blocks = table_ref.shape[0]

    def build(at):
        block, first = divmod(at.start, WIDTH)
        spatial = matmul(modes[...], table_ref[block, :, first : first + tile])
        return spatial + matmul(mixer_ref[...], field_ref[:, at])

    def pointwise(pre, at):
        for first in range(0, rows, chunk):
            part = slice(first, first + chunk)
            values = pre[part, :] + jnp.concatenate([bias_ref[part, :]] * (tile // LANES), axis=1)
            integral, decay = normal_parts(values)
            output_ref[part, at] = (values * integral).astype(BF16)
            slope = integral + (values * DENSITY) * decay
            grad = (cotangent_ref[part, at].astype(F32) * slope).astype(BF16)
            grad_ref[at.start // WIDTH, part, at.start % WIDTH : at.start % WIDTH + tile] = grad

    tiles = [slice(first, first + tile) for first in range(0, width, tile)]
    ready = build(tiles[0])
    for index, at in enumerate(tiles):
        pre = ready
        if index + 1 < len(tiles):
            ready = build(tiles[index + 1])
        pointwise(pre, at)
    passing = jnp.concatenate([table_ref[at] for at in range(blocks)], axis=1)
    passing = jnp.concatenate([passing, field_ref[...], jnp.ones((ones, width), BF16)], axis=0)
    grads = jnp.concatenate([grad_ref[at] for at in range(blocks)], axis=1)
    total[...] += matmul_turned(passing, grads)

    @pl.when(step == pl.num_programs(0) - 1)
    def _():
        pack_modes(total, held, sent_ref, sems, xl, tl)
        row = lax.broadcasted_iota(jnp.int32, (rows, rows), 0)
        column = lax.broadcasted_iota(jnp.int32, (rows, rows), 1)
        gram = total[KQ : KQ + rows, :].T
        bias = total[KQ + rows : KQ + rows + CHANS, :]
        same = jnp.where(row // CHANS == column // CHANS, gram, 0.0)
        folded = jnp.sum(same.reshape(rows // CHANS, CHANS, rows), axis=0)
        source = lax.broadcasted_iota(jnp.int32, (rows, LANES), 0)
        target = lax.broadcasted_iota(jnp.int32, (rows, LANES), 1)
        select = jnp.where(source % CHANS == target, 1.0, 0.0)
        chan = lax.broadcasted_iota(jnp.int32, (CHANS, rows), 0)
        place = lax.broadcasted_iota(jnp.int32, (CHANS, rows), 1)
        own_bias = jnp.sum(
            jnp.where(place % CHANS == chan, bias, 0.0), axis=1, keepdims=True
        )
        sums = jnp.dot(
            folded, select, precision=lax.Precision.HIGHEST, preferred_element_type=F32
        )
        lane = lax.broadcasted_iota(jnp.int32, (CHANS, LANES), 1)
        sums = jnp.where(lane == CHANS, own_bias, sums)
        sums_ref[...] = sums if sums_in_ref is None else sums_in_ref[...] + sums


def middle(packed, field, cotangent, table, mixer, bias, sums, output, part, xl, tl):
    rows = xl * tl * CHANS
    per = 2
    chunks = CELLS // WIDTH
    whole = lambda *shape: pl.BlockSpec(shape, lambda n: (0,) * len(shape))
    tile = pl.BlockSpec((rows, per * WIDTH), lambda n: (part, n))
    kernel = functools.partial(middle_kernel, xl, tl)
    operands = (packed, field, cotangent, table, mixer, bias)
    specs = [
        whole(*packed.shape),
        tile,
        tile,
        pl.BlockSpec((per, KQ, WIDTH), lambda n: (n, 0, 0)),
        whole(rows, rows),
        whole(rows, LANES),
    ]
    aliases = {}
    if output is None:
        inner = kernel
        kernel = lambda *refs: inner(*refs[:6], None, None, *refs[6:])
    else:
        operands += (sums, output)
        aliases = {len(operands) - 1: 0}
        specs += [whole(CHANS, LANES), pl.BlockSpec(memory_space=pltpu.HBM)]
    return pl.pallas_call(
        kernel,
        grid=(chunks // per,),
        in_specs=specs,
        out_specs=[
            tile,
            pl.BlockSpec((per, rows, WIDTH), lambda n: (n, 0, 0)),
            pl.BlockSpec(memory_space=pl.ANY),
            whole(CHANS, LANES),
        ],
        out_shape=(
            jax.ShapeDtypeStruct(field.shape, BF16),
            jax.ShapeDtypeStruct((chunks, rows, WIDTH), BF16),
            jax.ShapeDtypeStruct(packed.shape, BF16),
            jax.ShapeDtypeStruct((CHANS, LANES), F32),
        ),
        scratch_shapes=[
            pltpu.VMEM((xl, tl, CHANS, KQ), F32),
            pltpu.VMEM((rows, KQ), BF16),
            pltpu.VMEM((KQ + rows + 16, rows), F32),
            pltpu.VMEM(packed.shape, BF16),
            pltpu.SemaphoreType.DMA((KQ // LANES,)),
        ],
        input_output_aliases=aliases,
        compiler_params=vmem_params(60),
        cost_estimate=pl.CostEstimate(
            flops=5 * rows * CELLS * KQ, bytes_accessed=18 << 20, transcendentals=rows * CELLS
        ),
        name="middle",
    )(*operands)


def last_kernel(xl, tl, packed_ref, table_ref, mixed_ref, field_ref, *scratch):
    wide, modes, table, mixed, field, table_sems, mixed_sems, field_sems = scratch
    chunks = table.shape[0]
    ahead = 4
    fetches, sends = [], []
    for at in range(chunks):
        lanes = slice(at * WIDTH, (at + 1) * WIDTH)
        fetches.append(
            (
                pltpu.make_async_copy(table_ref.at[at], table.at[at], table_sems.at[at]),
                pltpu.make_async_copy(mixed_ref.at[at], mixed.at[at], mixed_sems.at[at]),
            )
        )
        sends.append(
            pltpu.make_async_copy(field.at[at], field_ref.at[:, lanes], field_sems.at[at])
        )

    def start(at):
        for fetch in fetches[at]:
            fetch.start()

    for at in range(ahead):
        start(at)
    unpack_modes(packed_ref, wide, xl, tl)
    modes[...] = wide[...].reshape(modes.shape).astype(BF16)
    for at in range(chunks):
        for fetch in fetches[at]:
            fetch.wait()
        if at + ahead < chunks:
            start(at + ahead)
        field[at] = (matmul(modes[...], table[at]) + mixed[at].astype(F32)).astype(BF16)
        sends[at].start()
    for send in sends:
        send.wait()


def last(packed, mixed, table, xl, tl):
    rows = xl * tl * CHANS
    chunks = CELLS // WIDTH
    apart = pl.BlockSpec(memory_space=pltpu.HBM)
    return pl.pallas_call(
        functools.partial(last_kernel, xl, tl),
        in_specs=[pl.BlockSpec(memory_space=pltpu.VMEM), apart, apart],
        out_specs=apart,
        out_shape=jax.ShapeDtypeStruct((rows, CELLS), BF16),
        scratch_shapes=[
            pltpu.VMEM((xl, tl, CHANS, KQ), F32),
            pltpu.VMEM((rows, KQ), BF16),
            pltpu.VMEM((chunks, KQ, WIDTH), BF16),
            pltpu.VMEM((chunks, rows, WIDTH), BF16),
            pltpu.VMEM((chunks, rows, WIDTH), BF16),
            pltpu.SemaphoreType.DMA((chunks,)),
            pltpu.SemaphoreType.DMA((chunks,)),
            pltpu.SemaphoreType.DMA((chunks,)),
        ],
        compiler_params=vmem_params(44),
        cost_estimate=pl.CostEstimate(
            flops=2 * rows * CELLS * KQ, bytes_accessed=18 << 20, transcendentals=0
        ),
        name="last",
    )(packed, table, mixed)


def swap(blocks):
    return lax.all_to_all(blocks, ("gx", "ta"), split_axis=0, concat_axis=0, tiled=True)


def sum_everywhere(values, devices):
    step = 1
    while step < devices:
        others = 3 if 2 * step < devices else 1
        got = [
            lax.ppermute(values, ("gx", "ta"), [(at, at ^ (k * step)) for at in range(devices)])
            for k in range(1, others + 1)
        ]
        values = values + got[0]
        if others == 3:
            values = values + (got[1] + got[2])
        step *= others + 1
    return values


def fast_body(gx, ta, features, cotangent, spec_weight, point_weight, bias_vector):
    _, xl_all, tl, _, cells = features.shape
    own = spec_weight.shape[4]
    devices = gx * ta
    xl = xl_all // PARTS
    rows = xl * tl * CHANS
    yz = np.kron(
        narrow(basis(NY, MY)).astype(np.float32), narrow(basis(NZ, MZ)).astype(np.float32)
    )
    blocks = yz.reshape(KQ, CELLS // WIDTH, WIDTH).transpose(1, 0, 2)
    table = jnp.asarray(narrow(blocks))
    x_whole = basis(NX, MX).reshape(KX, gx, 1, xl_all)
    x_split = basis(NX, MX).reshape(KX, gx, PARTS, xl)
    x_tables = [
        np.stack(
            [
                np.kron(split[:, :, part].reshape(KX, -1), np.eye(CHANS))
                for part in range(split.shape[2])
            ]
        )
        for split in (x_whole, x_split)
    ]
    x_in = [jnp.asarray(narrow(x_table)) for x_table in x_tables]
    x_out = [jnp.asarray(narrow(x_table.transpose(0, 2, 1))) for x_table in x_tables]
    t_wide = np.kron(basis(NT, MT), np.eye(own))
    t_in, t_out = jnp.asarray(narrow(t_wide.T)), jnp.asarray(narrow(t_wide))
    norm_scale = float(BATCH * NX * NT * NY * NZ) ** (-0.5)

    field = features.reshape(PARTS * rows, cells)
    cot = cotangent.reshape(PARTS * rows, cells)
    pick = np.tile(np.eye(CHANS, dtype=np.float32), (rows // CHANS, 1))
    same = np.kron(np.eye(rows // CHANS, dtype=np.float32), np.ones((CHANS, CHANS), np.float32))
    picked = jnp.asarray(narrow(pick))
    spread_point = matmul(matmul(picked, point_weight).astype(BF16), picked.T)
    spread_back = matmul(matmul(picked, point_weight.T).astype(BF16), picked.T)
    mixer = (spread_point * jnp.asarray(same)).astype(BF16)
    mixer_back = (spread_back * jnp.asarray(same)).astype(BF16)
    bias = jnp.dot(
        jnp.asarray(pick),
        jnp.broadcast_to(bias_vector[:, None], (CHANS, LANES)),
        precision=lax.Precision.HIGHEST,
    )
    part_shape = (gx, ta, xl * CHANS, LANES)
    whole_shape = (gx, ta, xl_all * CHANS, LANES)
    packed_weight, later_weight = pack_weight(spec_weight)

    spread_in = swap(analyse(field, table, xl_all, tl, devices)).reshape(whole_shape)
    spectrum, *mixed = mix(
        [spread_in], packed_weight, (mixer, mixer_back, bias), (x_in[0], t_in, x_out[1], t_out), False
    )
    output, sums = None, None
    grads, spread_grad = [], []
    for part in range(PARTS):
        returned = swap(mixed[part].reshape(devices, xl * CHANS, LANES))
        output, grad, sent, sums = middle(
            returned, field, cot, table, mixer, bias, sums, output, part, xl, tl
        )
        grads.append(grad)
        spread_grad.append(swap(sent).reshape(part_shape))
    summed = sum_everywhere(sums, devices)
    grad_modes, mixed_back = mix(
        spread_grad, later_weight, (summed,), (x_in[1], t_in, x_out[0], t_out), True
    )
    grad_back = swap(mixed_back.reshape(devices, xl_all * CHANS, LANES))
    grad_spec = outer(spectrum, grad_modes, own)
    grad_field = last(grad_back, point(grads, mixer_back), table, xl_all, tl)
    summed = summed * norm_scale
    return (
        output.reshape(features.shape),
        grad_field.reshape(features.shape),
        grad_spec,
        summed[:, :CHANS],
        summed[:, CHANS],
    )


def analyse_yz(spatial, yz_table):
    return jnp.einsum(
        "qp,bxtcp->bxtcq", yz_table, spatial.astype(F32), precision=lax.Precision.HIGHEST
    )


def build_yz(modes_in, yz_table):
    return jnp.einsum(
        "qp,bxtcq->bxtcp", yz_table, modes_in.astype(F32), precision=lax.Precision.HIGHEST
    )


def analyse_xt(spread, table):
    sizes = spread.shape
    flattened = spread.reshape(sizes[0], sizes[1] * sizes[2], sizes[3] * sizes[4]).astype(F32)
    spectral = jnp.einsum("mp,bpr->bmr", table, flattened, precision=lax.Precision.HIGHEST)
    return spectral.reshape(sizes[0], KX, KT, sizes[3], sizes[4])


def synthesise_xt(modes_in, table):
    sizes = modes_in.shape
    flattened = modes_in.reshape(sizes[0], sizes[1] * sizes[2], sizes[3] * sizes[4])
    spatial = jnp.einsum("mp,bmr->bpr", table, flattened, precision=lax.Precision.HIGHEST)
    return spatial.reshape(sizes[0], NX, NT, sizes[3], sizes[4])


def to_owners(modes_in):
    first = lax.all_to_all(modes_in, "gx", split_axis=4, concat_axis=1, tiled=True)
    return lax.all_to_all(first, "ta", split_axis=4, concat_axis=2, tiled=True)


def to_cells(spread, shape):
    first = lax.all_to_all(
        spread[:, :, :, :, None, None, :], "gx", split_axis=1, concat_axis=4, tiled=True
    )
    second = lax.all_to_all(first, "ta", split_axis=2, concat_axis=5, tiled=True)
    return second.reshape(shape[:4] + (-1,))


def general_body(features, cotangent, spec_weight, point_weight, bias_vector):
    shape = features.shape
    yz_table = jnp.asarray(
        np.kron(narrow(basis(NY, MY)).astype(np.float32), narrow(basis(NZ, MZ)).astype(np.float32))
    )
    xt_table = jnp.asarray(np.kron(basis(NX, MX), basis(NT, MT)))
    norm_scale = float(BATCH * NX * NT * NY * NZ) ** (-0.5)
    highest = lax.Precision.HIGHEST
    spectrum = analyse_xt(to_owners(analyse_yz(features, yz_table).astype(BF16)), xt_table)
    mixed = jnp.einsum("bklip,kliop->bklop", spectrum, spec_weight, precision=highest)
    returned = to_cells(synthesise_xt(mixed, xt_table).astype(BF16), shape)
    pointwise = jnp.einsum("oi,bxtip->bxtop", point_weight, features, preferred_element_type=F32)
    pre = build_yz(returned, yz_table) + pointwise + bias_vector[:, None]
    integral = 0.5 * (1.0 + jax.scipy.special.erf(pre * 0.7071067811865476))
    output = (pre * integral).astype(BF16)
    slope = integral + pre * jnp.exp(-0.5 * pre * pre) * 0.3989422804014327
    grad_pre = (cotangent.astype(F32) * slope).astype(BF16)
    local_point = jnp.einsum("bxtop,bxtip->oi", grad_pre, features, preferred_element_type=F32)
    local_bias = jnp.sum(grad_pre.astype(F32), axis=(0, 1, 2, 4))
    total_point, total_bias = lax.psum((local_point, local_bias), ("gx", "ta"))
    grad_modes = analyse_xt(to_owners(analyse_yz(grad_pre, yz_table).astype(BF16)), xt_table)
    grad_spec = jnp.einsum("bklip,bklop->kliop", spectrum, grad_modes, precision=highest)
    grad_in = jnp.einsum("kliop,bklop->bklip", spec_weight, grad_modes, precision=highest)
    grad_back = to_cells(synthesise_xt(grad_in, xt_table).astype(BF16), shape)
    point_term = jnp.einsum("oi,bxtop->bxtip", point_weight, grad_pre, preferred_element_type=F32)
    grad_field = (build_yz(grad_back, yz_table) + point_term).astype(BF16)
    return (output, grad_field, grad_spec, total_point * norm_scale, total_bias * norm_scale)


def solution(mesh):
    split_field = P(None, "gx", "ta", None, None)
    split_weight = P(None, None, None, None, ("gx", "ta"))
    in_specs = (split_field, split_field, split_weight, P(), P())
    out_specs = (split_field, split_field, split_weight, P(), P())
    gx, ta = mesh.shape["gx"], mesh.shape["ta"]
    own, xl, tl = KQ // (gx * ta), NX // gx, NT // ta
    if own == 32 and xl * CHANS == LANES and tl == 4:
        body = functools.partial(fast_body, gx, ta)
    else:
        body = general_body
    return jax.shard_map(body, mesh=mesh, in_specs=in_specs, out_specs=out_specs, check_vma=False)
```

```python
import functools
import math

import jax
import jax.numpy as jnp
import ml_dtypes
import numpy as np
from jax import lax
from jax.experimental import pallas as pl
from jax.experimental.pallas import tpu as pltpu
from jax.sharding import PartitionSpec as P

NX = 128
NY = 128
NZ = 32
NT = 16
MX = 16
MY = 16
MZ = 16
MT = 8
BATCH = 1
KX = 32
KT = 16
CHANS = 8
CELLS = NY * NZ
KQ = 1024
LANES = 128
PARTS = 2
WIDTH = 512
DENSITY = 1.0 / math.sqrt(2.0 * math.pi)
F32 = jnp.float32
BF16 = jnp.bfloat16


def basis(length, modes):
    frequency = np.concatenate([np.arange(modes + 1), np.arange(1, modes)])
    samples_at = np.arange(length)
    phases = (2.0 * math.pi / length) * (frequency[:, None] * samples_at[None, :] % length)
    cosine_row = np.arange(2 * modes) <= modes
    waves = np.where(cosine_row[:, None], np.cos(phases), np.sin(phases))
    at_edge = cosine_row & ((frequency == 0) | (2 * frequency == length))
    scales = np.where(at_edge, math.sqrt(1.0 / length), math.sqrt(2.0 / length))
    return (waves * scales[:, None]).astype(np.float32)


def narrow(table):
    return np.asarray(table, np.float32).astype(ml_dtypes.bfloat16)


def vmem_params(mebibytes):
    return pltpu.CompilerParams(vmem_limit_bytes=mebibytes * 1024 * 1024)


def matmul(left, right):
    return jnp.dot(left, right, preferred_element_type=F32)


def matmul_turned(left, right):
    return lax.dot_general(
        left, right, (((1,), (1,)), ((), ())), preferred_element_type=F32
    )


def swap_groups(tiles):
    rows = tiles[0].shape[0]
    lane = lax.broadcasted_iota(jnp.int32, (rows, LANES), 1)
    low_half = lane < 64
    even = (lane // 32) % 2 == 0
    first, second, third, fourth = tiles
    b0 = jnp.where(low_half, first, pltpu.roll(third, 64, 1))
    b2 = jnp.where(low_half, pltpu.roll(first, 64, 1), third)
    b1 = jnp.where(low_half, second, pltpu.roll(fourth, 64, 1))
    b3 = jnp.where(low_half, pltpu.roll(second, 64, 1), fourth)
    return (
        jnp.where(even, b0, pltpu.roll(b1, 32, 1)),
        jnp.where(even, pltpu.roll(b0, 96, 1), b1),
        jnp.where(even, b2, pltpu.roll(b3, 32, 1)),
        jnp.where(even, pltpu.roll(b2, 96, 1), b3),
    )


def pack_modes(modes_ref, held_ref, packed_ref, sems, xl, tl):
    sends = []
    for tile in range(KQ // LANES):
        modes = modes_ref[tile * LANES : (tile + 1) * LANES, :].T
        split = modes.reshape(xl, tl, CHANS, LANES)
        tiles = [split[:, step].reshape(xl * CHANS, LANES) for step in range(tl)]
        owners = slice(tile * tl, (tile + 1) * tl)
        held_ref[owners] = jnp.stack([block.astype(BF16) for block in swap_groups(tiles)])
        send = pltpu.make_async_copy(held_ref.at[owners], packed_ref.at[owners], sems.at[tile])
        send.start()
        sends.append(send)
    for send in sends:
        send.wait()


def unpack_modes(packed_ref, wide_ref, xl, tl):
    for tile in range(KQ // LANES):
        tiles = [packed_ref[tile * tl + owner].astype(F32) for owner in range(tl)]
        for step, block in enumerate(swap_groups(tiles)):
            wide_ref[:, step, :, tile * LANES : (tile + 1) * LANES] = block.reshape(
                xl, CHANS, LANES
            )


def analyse_kernel(
    xl, tl, field_ref, table_ref, packed_ref, field, table, total, held, field_sems, table_sems, sems
):
    chunks = table.shape[0]
    ahead = 4
    fetches = []
    for at in range(chunks):
        lanes = slice(at * WIDTH, (at + 1) * WIDTH)
        fetches.append(
            (
                pltpu.make_async_copy(field_ref.at[:, lanes], field.at[at], field_sems.at[at]),
                pltpu.make_async_copy(table_ref.at[at], table.at[at], table_sems.at[at]),
            )
        )

    def start(at):
        for fetch in fetches[at]:
            fetch.start()

    for at in range(ahead):
        start(at)
    for at in range(0, chunks, 2):
        for now in (at, at + 1):
            for fetch in fetches[now]:
                fetch.wait()
            if now + ahead < chunks:
                start(now + ahead)
        part = matmul_turned(
            jnp.concatenate([table[at], table[at + 1]], axis=1),
            jnp.concatenate([field[at], field[at + 1]], axis=1),
        )
        total[...] = part if at == 0 else total[...] + part
    pack_modes(total, held, packed_ref, sems, xl, tl)


def analyse(field, table, xl, tl, devices):
    rows = xl * tl * CHANS
    chunks = CELLS // WIDTH
    packed = (devices, xl * CHANS, LANES)
    return pl.pallas_call(
        functools.partial(analyse_kernel, xl, tl),
        in_specs=[pl.BlockSpec(memory_space=pltpu.HBM)] * 2,
        out_specs=pl.BlockSpec(memory_space=pl.ANY),
        out_shape=jax.ShapeDtypeStruct(packed, BF16),
        scratch_shapes=[
            pltpu.VMEM((chunks, rows, WIDTH), BF16),
            pltpu.VMEM((chunks, KQ, WIDTH), BF16),
            pltpu.VMEM((KQ, rows), F32),
            pltpu.VMEM(packed, BF16),
            pltpu.SemaphoreType.DMA((chunks,)),
            pltpu.SemaphoreType.DMA((chunks,)),
            pltpu.SemaphoreType.DMA((KQ // LANES,)),
        ],
        compiler_params=vmem_params(60),
        cost_estimate=pl.CostEstimate(
            flops=2 * rows * CELLS * KQ, bytes_accessed=13 << 20, transcendentals=0
        ),
        name="analyse",
    )(field, table)


def weight_kernel(weight_ref, packed_ref):
    for kx in range(weight_ref.shape[0]):
        for group in range(KT // 4):
            parts = [weight_ref[kx, 4 * group + k] for k in range(4)]
            joined = jnp.concatenate(parts, axis=-1).reshape(CHANS * CHANS, LANES)
            packed_ref[kx, :, group * LANES : (group + 1) * LANES] = joined.astype(BF16)


def pack_weight(weight):
    per = 4
    own = weight.shape[4]
    return pl.pallas_call(
        weight_kernel,
        grid=(KX // per,),
        in_specs=[pl.BlockSpec((per, KT, CHANS, CHANS, own), lambda n: (n, 0, 0, 0, 0))],
        out_specs=pl.BlockSpec((per, CHANS * CHANS, KT * own), lambda n: (n, 0, 0)),
        out_shape=jax.ShapeDtypeStruct((KX, CHANS * CHANS, KT * own), BF16),
        compiler_params=vmem_params(60),
        cost_estimate=pl.CostEstimate(flops=1 << 20, bytes_accessed=20 << 20, transcendentals=0),
        name="pack_weight",
    )(weight)


def to_modes(spread_refs, x_table_ref, t_table_ref):
    total = 0.0
    for part, spread_ref in enumerate(spread_refs):
        gx, ta, rows, _ = spread_ref.shape
        beside = jnp.concatenate(
            [spread_ref[:, at].reshape(gx * rows, LANES) for at in range(ta)], axis=1
        )
        total = total + matmul(x_table_ref[part], beside)
    return matmul(total.astype(BF16), t_table_ref[...])


def from_modes(modes, x_table_ref, t_table_ref, held_ref, back_refs, sems):
    parts, gx, ta, rows, _ = held_ref.shape
    half = matmul(modes.astype(BF16), t_table_ref[...]).astype(BF16)
    pieces = sems.shape[1]
    per = gx // pieces
    sends = []
    for part in range(parts):
        for piece in range(pieces):
            table = x_table_ref[part, piece * per * rows : (piece + 1) * per * rows, :]
            full = matmul(table, half).astype(BF16)
            owners = slice(piece * per, (piece + 1) * per)
            for at in range(ta):
                held_ref[part, owners, at] = full[:, at * LANES : (at + 1) * LANES].reshape(
                    per, rows, LANES
                )
            send = pltpu.make_async_copy(
                held_ref.at[part, owners], back_refs[part].at[owners], sems.at[part, piece]
            )
            send.start()
            sends.append(send)
    for send in sends:
        send.wait()


def mix_kernel(
    backward,
    afters,
    weight_ref,
    *refs,
):
    x_in_ref, t_in_ref, x_out_ref, t_out_ref = refs[afters : afters + 4]
    refs = refs[afters + 4 :]
    ins, outs = x_in_ref.shape[0], x_out_ref.shape[0]
    spread_refs, modes_ref, back_refs = refs[:ins], refs[ins], refs[ins + 1 : ins + 1 + outs]
    scratch = refs[ins + 1 + outs :]
    weight, modes, mixed, held, x_in, t_in, x_out, t_out = scratch[:8]
    spreads, (sems, weight_sems, spread_sems, back_sems) = scratch[8:-4], scratch[-4:]
    arrivals = [
        pltpu.make_async_copy(source, target, spread_sems.at[at])
        for at, (source, target) in enumerate(zip(spread_refs, spreads))
    ]
    pieces = weight_sems.shape[0]
    per = KX // pieces
    sources = (x_in_ref, t_in_ref, t_out_ref, x_out_ref)
    tables = [
        pltpu.make_async_copy(source, target, sems.at[at])
        for at, (source, target) in enumerate(zip(sources, (x_in, t_in, t_out, x_out)))
    ]
    fetches = []
    for at in range(pieces):
        part = slice(at * per, (at + 1) * per)
        fetches.append(
            pltpu.make_async_copy(weight_ref.at[part], weight.at[part], weight_sems.at[at])
        )
    for copy in arrivals + tables[:2] + fetches + tables[2:]:
        copy.start()
    for copy in arrivals + tables[:2]:
        copy.wait()
    modes[...] = to_modes(spreads, x_in, t_in)
    keep = pltpu.make_async_copy(modes, modes_ref, sems.at[4])
    keep.start()
    for fetch in fetches:
        fetch.wait()
    for kx in range(KX):
        rows = slice(kx * CHANS, (kx + 1) * CHANS)
        own = modes[rows, :]
        weights = weight[kx].astype(F32).reshape(CHANS, CHANS, own.shape[1])
        if backward:
            sums = [jnp.sum(own * weights[i], axis=0, keepdims=True) for i in range(CHANS)]
            mixed[rows, :] = jnp.concatenate(sums, axis=0)
        else:
            total = own[0:1, :] * weights[0]
            for i in range(1, CHANS):
                total = total + own[i : i + 1, :] * weights[i]
            mixed[rows, :] = total
    tables[2].wait()
    tables[3].wait()
    from_modes(mixed[...], x_out, t_out, held, back_refs, back_sems)
    keep.wait()


def mix(spreads, weight, after, tables, backward):
    modes = (KX * CHANS, weight.shape[2])
    gx, ta, _, lanes = spreads[0].shape
    outs = tables[2].shape[0]
    back = (gx, ta, tables[2].shape[1] // gx, lanes)
    anywhere = pl.BlockSpec(memory_space=pl.ANY)
    apart = pl.BlockSpec(memory_space=pltpu.HBM)
    return pl.pallas_call(
        functools.partial(mix_kernel, backward, len(after)),
        out_shape=[jax.ShapeDtypeStruct(modes, F32)] + [jax.ShapeDtypeStruct(back, BF16)] * outs,
        in_specs=[apart] + [anywhere] * len(after) + [apart] * 4 + [anywhere] * len(spreads),
        out_specs=[apart] + [anywhere] * outs,
        scratch_shapes=[
            pltpu.VMEM(weight.shape, BF16),
            pltpu.VMEM(modes, F32),
            pltpu.VMEM(modes, F32),
            pltpu.VMEM((outs,) + back, BF16),
            *[pltpu.VMEM(table.shape, BF16) for table in tables],
            *[pltpu.VMEM(spread.shape, BF16) for spread in spreads],
            pltpu.SemaphoreType.DMA((5,)),
            pltpu.SemaphoreType.DMA((8,)),
            pltpu.SemaphoreType.DMA((len(spreads),)),
            pltpu.SemaphoreType.DMA((outs, 4 // outs)),
        ],
        compiler_params=vmem_params(60),
        cost_estimate=pl.CostEstimate(flops=1 << 30, bytes_accessed=9 << 20, transcendentals=0),
        name="mix_back" if backward else "mix",
    )(weight, *after, *tables, *spreads)


def outer_kernel(spectrum_ref, grad_ref, result_ref):
    own = result_ref.shape[4]
    for kx in range(result_ref.shape[0]):
        rows = slice(kx * CHANS, (kx + 1) * CHANS)
        for group in range(KT // 4):
            at = slice(group * LANES, (group + 1) * LANES)
            inputs = spectrum_ref[rows, at]
            grads = grad_ref[rows, at]
            for i in range(CHANS):
                product = inputs[i : i + 1, :] * grads
                for k in range(4):
                    result_ref[kx, 4 * group + k, i] = product[:, k * own : (k + 1) * own]


def outer(spectrum, grad, own):
    per = 4
    width = KT * own
    return pl.pallas_call(
        outer_kernel,
        grid=(KX // per,),
        in_specs=[pl.BlockSpec((per * CHANS, width), lambda n: (n, 0))] * 2,
        out_specs=pl.BlockSpec((per, KT, CHANS, CHANS, own), lambda n: (n, 0, 0, 0, 0)),
        out_shape=jax.ShapeDtypeStruct((KX, KT, CHANS, CHANS, own), F32),
        compiler_params=vmem_params(60),
        cost_estimate=pl.CostEstimate(flops=1 << 20, bytes_accessed=17 << 20, transcendentals=0),
        name="outer",
    )(spectrum, grad)


def normal_parts(values):
    scaled = 1.0 + 0.2316419 * jnp.abs(values)
    guess = pl.reciprocal(scaled, approx=True)
    t = guess * (2.0 - scaled * guess)
    decay = jnp.exp(values * values * -0.5)
    series = (1.330274429 * DENSITY) * t - 1.821255978 * DENSITY
    series = series * t + 1.781477937 * DENSITY
    series = series * t - 0.356563782 * DENSITY
    series = series * t + 0.319381530 * DENSITY
    tail = decay * (series * t)
    return jnp.where(values >= 0.0, 1.0 - tail, tail), decay


def point_field_kernel(mixer_ref, bias_ref, field_ref, mixed_ref):
    rows = mixer_ref.shape[0]
    bias = jnp.concatenate([bias_ref[...]] * (WIDTH // LANES), axis=1)
    for at in range(mixed_ref.shape[0]):
        for first in range(0, field_ref.shape[0], rows):
            part = slice(first, first + rows)
            field = field_ref[part, at * WIDTH : (at + 1) * WIDTH]
            mixed_ref[at, part, :] = (matmul(mixer_ref[...], field) + bias).astype(BF16)


def point_field(field, mixer, bias):
    rows = field.shape[0]
    group = mixer.shape[0]
    per = 2
    return pl.pallas_call(
        point_field_kernel,
        grid=(CELLS // (per * WIDTH),),
        in_specs=[
            pl.BlockSpec((group, group), lambda n: (0, 0)),
            pl.BlockSpec((group, LANES), lambda n: (0, 0)),
            pl.BlockSpec((rows, per * WIDTH), lambda n: (0, n)),
        ],
        out_specs=pl.BlockSpec((per, rows, WIDTH), lambda n: (n, 0, 0)),
        out_shape=jax.ShapeDtypeStruct((CELLS // WIDTH, rows, WIDTH), BF16),
        compiler_params=vmem_params(60),
        cost_estimate=pl.CostEstimate(
            flops=2 * rows * CELLS * group, bytes_accessed=8 << 20, transcendentals=0
        ),
        name="point_field",
    )(mixer, bias, field)


def point_grad_kernel(mixer_ref, grad_ref, mixed_ref):
    rows = mixer_ref.shape[0]
    for at in range(mixed_ref.shape[0]):
        for first in range(0, grad_ref.shape[1], rows):
            part = slice(first, first + rows)
            mixed_ref[at, part, :] = matmul(mixer_ref[...], grad_ref[at, part, :]).astype(BF16)


def point_grad(grad, mixer):
    chunks, rows, _ = grad.shape
    group = mixer.shape[0]
    per = 2
    blocks = pl.BlockSpec((per, rows, WIDTH), lambda n: (n, 0, 0))
    return pl.pallas_call(
        point_grad_kernel,
        grid=(chunks // per,),
        in_specs=[pl.BlockSpec((group, group), lambda n: (0, 0)), blocks],
        out_specs=blocks,
        out_shape=jax.ShapeDtypeStruct(grad.shape, BF16),
        compiler_params=vmem_params(60),
        cost_estimate=pl.CostEstimate(
            flops=2 * rows * CELLS * group, bytes_accessed=8 << 20, transcendentals=0
        ),
        name="point_grad",
    )(mixer, grad)


def sums_kernel(group, field_ref, grad_ref, sums_ref, total):
    step = pl.program_id(0)
    rows, width = field_ref.shape
    blocks = grad_ref.shape[0]
    ones = jnp.ones((16, width), BF16)
    part = 0.0
    for first in range(0, rows, group):
        at = slice(first, first + group)
        passing = jnp.concatenate([field_ref[at, :], ones], axis=0)
        grads = jnp.concatenate([grad_ref[block, at, :] for block in range(blocks)], axis=1)
        part = part + matmul_turned(passing, grads)

    @pl.when(step == 0)
    def _():
        total[...] = part

    @pl.when(step > 0)
    def _():
        total[...] += part

    @pl.when(step == pl.num_programs(0) - 1)
    def _():
        row = lax.broadcasted_iota(jnp.int32, (group, group), 0)
        column = lax.broadcasted_iota(jnp.int32, (group, group), 1)
        gram = total[:group, :].T
        bias = total[group : group + CHANS, :]
        same = jnp.where(row // CHANS == column // CHANS, gram, 0.0)
        folded = jnp.sum(same.reshape(group // CHANS, CHANS, group), axis=0)
        source = lax.broadcasted_iota(jnp.int32, (group, LANES), 0)
        target = lax.broadcasted_iota(jnp.int32, (group, LANES), 1)
        select = jnp.where(source % CHANS == target, 1.0, 0.0)
        chan = lax.broadcasted_iota(jnp.int32, (CHANS, group), 0)
        place = lax.broadcasted_iota(jnp.int32, (CHANS, group), 1)
        own_bias = jnp.sum(
            jnp.where(place % CHANS == chan, bias, 0.0), axis=1, keepdims=True
        )
        point = jnp.dot(
            folded, select, precision=lax.Precision.HIGHEST, preferred_element_type=F32
        )
        lane = lax.broadcasted_iota(jnp.int32, (CHANS, LANES), 1)
        sums_ref[...] = jnp.where(lane == CHANS, own_bias, point)


def own_sums(field, grad, group):
    chunks, rows, _ = grad.shape
    per = 2
    return pl.pallas_call(
        functools.partial(sums_kernel, group),
        grid=(chunks // per,),
        in_specs=[
            pl.BlockSpec((rows, per * WIDTH), lambda n: (0, n)),
            pl.BlockSpec((per, rows, WIDTH), lambda n: (n, 0, 0)),
        ],
        out_specs=pl.BlockSpec((CHANS, LANES), lambda n: (0, 0)),
        out_shape=jax.ShapeDtypeStruct((CHANS, LANES), F32),
        scratch_shapes=[pltpu.VMEM((group + 16, group), F32)],
        compiler_params=vmem_params(60),
        cost_estimate=pl.CostEstimate(
            flops=2 * rows * CELLS * group, bytes_accessed=8 << 20, transcendentals=0
        ),
        name="own_sums",
    )(field, grad)


def middle_kernel(
    xl,
    tl,
    packed_ref,
    cotangent_ref,
    mixed_ref,
    table_ref,
    output_ref,
    grad_ref,
    sent_ref,
    wide,
    modes,
    total,
    held,
    sems,
):
    step = pl.program_id(0)
    rows, width = cotangent_ref.shape
    tile = 256
    chunk = 32

    @pl.when(step == 0)
    def _():
        unpack_modes(packed_ref, wide, xl, tl)
        modes[...] = wide[...].reshape(rows, KQ).astype(BF16)
        total[...] = jnp.zeros_like(total)

    def build(at):
        return matmul(modes[...], table_ref[0, :, at])

    def pointwise(pre, at):
        for first in range(0, rows, chunk):
            part = slice(first, first + chunk)
            values = pre[part, :] + mixed_ref[0, part, at].astype(F32)
            integral, decay = normal_parts(values)
            output_ref[part, at] = (values * integral).astype(BF16)
            slope = integral + (values * DENSITY) * decay
            grad_ref[0, part, at] = (cotangent_ref[part, at].astype(F32) * slope).astype(BF16)

    tiles = [slice(first, first + tile) for first in range(0, width, tile)]
    ready = build(tiles[0])
    for index, at in enumerate(tiles):
        pre = ready
        if index + 1 < len(tiles):
            ready = build(tiles[index + 1])
        pointwise(pre, at)
    total[...] += matmul_turned(table_ref[0], grad_ref[0])

    @pl.when(step == pl.num_programs(0) - 1)
    def _():
        pack_modes(total, held, sent_ref, sems, xl, tl)


def middle(packed, cotangent, mixed, table, xl, tl):
    rows = xl * tl * CHANS
    chunks = CELLS // WIDTH
    tile = pl.BlockSpec((rows, WIDTH), lambda n: (0, n))
    block = pl.BlockSpec((1, rows, WIDTH), lambda n: (n, 0, 0))
    return pl.pallas_call(
        functools.partial(middle_kernel, xl, tl),
        grid=(chunks,),
        in_specs=[
            pl.BlockSpec(packed.shape, lambda n: (0, 0, 0)),
            tile,
            block,
            pl.BlockSpec((1, KQ, WIDTH), lambda n: (n, 0, 0)),
        ],
        out_specs=[tile, block, pl.BlockSpec(memory_space=pl.ANY)],
        out_shape=(
            jax.ShapeDtypeStruct((rows, CELLS), BF16),
            jax.ShapeDtypeStruct((chunks, rows, WIDTH), BF16),
            jax.ShapeDtypeStruct(packed.shape, BF16),
        ),
        scratch_shapes=[
            pltpu.VMEM((xl, tl, CHANS, KQ), F32),
            pltpu.VMEM((rows, KQ), BF16),
            pltpu.VMEM((KQ, rows), F32),
            pltpu.VMEM(packed.shape, BF16),
            pltpu.SemaphoreType.DMA((KQ // LANES,)),
        ],
        compiler_params=vmem_params(60),
        cost_estimate=pl.CostEstimate(
            flops=4 * rows * CELLS * KQ, bytes_accessed=26 << 20, transcendentals=rows * CELLS
        ),
        name="middle",
    )(packed, cotangent, mixed, table)


def last_kernel(xl, tl, packed_ref, table_ref, mixed_ref, field_ref, *scratch):
    wide, modes, table, mixed, field, table_sems, mixed_sems, field_sems = scratch
    chunks = table.shape[0]
    ahead = 4
    fetches, sends = [], []
    for at in range(chunks):
        lanes = slice(at * WIDTH, (at + 1) * WIDTH)
        fetches.append(
            (
                pltpu.make_async_copy(table_ref.at[at], table.at[at], table_sems.at[at]),
                pltpu.make_async_copy(mixed_ref.at[at], mixed.at[at], mixed_sems.at[at]),
            )
        )
        sends.append(
            pltpu.make_async_copy(field.at[at], field_ref.at[:, lanes], field_sems.at[at])
        )

    def start(at):
        for fetch in fetches[at]:
            fetch.start()

    for at in range(ahead):
        start(at)
    unpack_modes(packed_ref, wide, xl, tl)
    modes[...] = wide[...].reshape(modes.shape).astype(BF16)
    for at in range(chunks):
        for fetch in fetches[at]:
            fetch.wait()
        if at + ahead < chunks:
            start(at + ahead)
        field[at] = (matmul(modes[...], table[at]) + mixed[at].astype(F32)).astype(BF16)
        sends[at].start()
    for send in sends:
        send.wait()


def last(packed, mixed, table, xl, tl):
    rows = xl * tl * CHANS
    chunks = CELLS // WIDTH
    apart = pl.BlockSpec(memory_space=pltpu.HBM)
    return pl.pallas_call(
        functools.partial(last_kernel, xl, tl),
        in_specs=[pl.BlockSpec(memory_space=pltpu.VMEM), apart, apart],
        out_specs=apart,
        out_shape=jax.ShapeDtypeStruct((rows, CELLS), BF16),
        scratch_shapes=[
            pltpu.VMEM((xl, tl, CHANS, KQ), F32),
            pltpu.VMEM((rows, KQ), BF16),
            pltpu.VMEM((chunks, KQ, WIDTH), BF16),
            pltpu.VMEM((chunks, rows, WIDTH), BF16),
            pltpu.VMEM((chunks, rows, WIDTH), BF16),
            pltpu.SemaphoreType.DMA((chunks,)),
            pltpu.SemaphoreType.DMA((chunks,)),
            pltpu.SemaphoreType.DMA((chunks,)),
        ],
        compiler_params=vmem_params(44),
        cost_estimate=pl.CostEstimate(
            flops=2 * rows * CELLS * KQ, bytes_accessed=18 << 20, transcendentals=0
        ),
        name="last",
    )(packed, table, mixed)


def swap(blocks):
    return lax.all_to_all(blocks, ("gx", "ta"), split_axis=0, concat_axis=0, tiled=True)


def sum_everywhere(values, devices):
    step = 1
    while step < devices:
        pairs = [(at, at ^ step) for at in range(devices)]
        values = values + lax.ppermute(values, ("gx", "ta"), pairs)
        step *= 2
    return values


def fast_body(gx, ta, features, cotangent, spec_weight, point_weight, bias_vector):
    _, xl, tl, _, cells = features.shape
    own = spec_weight.shape[4]
    devices = gx * ta
    rows = xl * tl * CHANS
    group = rows // PARTS
    yz = np.kron(
        narrow(basis(NY, MY)).astype(np.float32), narrow(basis(NZ, MZ)).astype(np.float32)
    )
    blocks = yz.reshape(KQ, CELLS // WIDTH, WIDTH).transpose(1, 0, 2)
    table = jnp.asarray(narrow(blocks))
    x_wide = np.kron(basis(NX, MX), np.eye(CHANS))[None]
    x_in, x_out = jnp.asarray(narrow(x_wide)), jnp.asarray(narrow(x_wide.transpose(0, 2, 1)))
    t_wide = np.kron(basis(NT, MT), np.eye(own))
    t_in, t_out = jnp.asarray(narrow(t_wide.T)), jnp.asarray(narrow(t_wide))
    norm_scale = float(BATCH * NX * NT * NY * NZ) ** (-0.5)

    field = features.reshape(rows, cells)
    cot = cotangent.reshape(rows, cells)
    pick = np.tile(np.eye(CHANS, dtype=np.float32), (group // CHANS, 1))
    same = np.kron(np.eye(group // CHANS, dtype=np.float32), np.ones((CHANS, CHANS), np.float32))
    picked = jnp.asarray(narrow(pick))
    spread_point = matmul(matmul(picked, point_weight).astype(BF16), picked.T)
    spread_back = matmul(matmul(picked, point_weight.T).astype(BF16), picked.T)
    mixer = (spread_point * jnp.asarray(same)).astype(BF16)
    mixer_back = (spread_back * jnp.asarray(same)).astype(BF16)
    bias = jnp.dot(
        jnp.asarray(pick),
        jnp.broadcast_to(bias_vector[:, None], (CHANS, LANES)),
        precision=lax.Precision.HIGHEST,
    )
    spread_shape = (gx, ta, xl * CHANS, LANES)
    block_shape = (devices, xl * CHANS, LANES)
    packed_weight = pack_weight(spec_weight)
    tables = (x_in, t_in, x_out, t_out)

    spread_in = swap(analyse(field, table, xl, tl, devices)).reshape(spread_shape)
    spectrum, mixed = mix([spread_in], packed_weight, (mixer, mixer_back, bias), tables, False)
    returned = swap(mixed.reshape(block_shape))
    mixed_field = point_field(field, mixer, bias)
    output, grad, sent = middle(returned, cot, mixed_field, table, xl, tl)
    spread_grad = swap(sent).reshape(spread_shape)
    summed = sum_everywhere(own_sums(field, grad, group), devices)
    grad_modes, mixed_back = mix([spread_grad], packed_weight, (summed,), tables, True)
    grad_back = swap(mixed_back.reshape(block_shape))
    grad_spec = outer(spectrum, grad_modes, own)
    grad_field = last(grad_back, point_grad(grad, mixer_back), table, xl, tl)
    summed = summed * norm_scale
    return (
        output.reshape(features.shape),
        grad_field.reshape(features.shape),
        grad_spec,
        summed[:, :CHANS],
        summed[:, CHANS],
    )


def analyse_yz(spatial, yz_table):
    return jnp.einsum(
        "qp,bxtcp->bxtcq", yz_table, spatial.astype(F32), precision=lax.Precision.HIGHEST
    )


def build_yz(modes_in, yz_table):
    return jnp.einsum(
        "qp,bxtcq->bxtcp", yz_table, modes_in.astype(F32), precision=lax.Precision.HIGHEST
    )


def analyse_xt(spread, table):
    sizes = spread.shape
    flattened = spread.reshape(sizes[0], sizes[1] * sizes[2], sizes[3] * sizes[4]).astype(F32)
    spectral = jnp.einsum("mp,bpr->bmr", table, flattened, precision=lax.Precision.HIGHEST)
    return spectral.reshape(sizes[0], KX, KT, sizes[3], sizes[4])


def synthesise_xt(modes_in, table):
    sizes = modes_in.shape
    flattened = modes_in.reshape(sizes[0], sizes[1] * sizes[2], sizes[3] * sizes[4])
    spatial = jnp.einsum("mp,bmr->bpr", table, flattened, precision=lax.Precision.HIGHEST)
    return spatial.reshape(sizes[0], NX, NT, sizes[3], sizes[4])


def to_owners(modes_in):
    first = lax.all_to_all(modes_in, "gx", split_axis=4, concat_axis=1, tiled=True)
    return lax.all_to_all(first, "ta", split_axis=4, concat_axis=2, tiled=True)


def to_cells(spread, shape):
    first = lax.all_to_all(
        spread[:, :, :, :, None, None, :], "gx", split_axis=1, concat_axis=4, tiled=True
    )
    second = lax.all_to_all(first, "ta", split_axis=2, concat_axis=5, tiled=True)
    return second.reshape(shape[:4] + (-1,))


def general_body(features, cotangent, spec_weight, point_weight, bias_vector):
    shape = features.shape
    yz_table = jnp.asarray(
        np.kron(narrow(basis(NY, MY)).astype(np.float32), narrow(basis(NZ, MZ)).astype(np.float32))
    )
    xt_table = jnp.asarray(np.kron(basis(NX, MX), basis(NT, MT)))
    norm_scale = float(BATCH * NX * NT * NY * NZ) ** (-0.5)
    highest = lax.Precision.HIGHEST
    spectrum = analyse_xt(to_owners(analyse_yz(features, yz_table).astype(BF16)), xt_table)
    mixed = jnp.einsum("bklip,kliop->bklop", spectrum, spec_weight, precision=highest)
    returned = to_cells(synthesise_xt(mixed, xt_table).astype(BF16), shape)
    pointwise = jnp.einsum("oi,bxtip->bxtop", point_weight, features, preferred_element_type=F32)
    pre = build_yz(returned, yz_table) + pointwise + bias_vector[:, None]
    integral = 0.5 * (1.0 + jax.scipy.special.erf(pre * 0.7071067811865476))
    output = (pre * integral).astype(BF16)
    slope = integral + pre * jnp.exp(-0.5 * pre * pre) * 0.3989422804014327
    grad_pre = (cotangent.astype(F32) * slope).astype(BF16)
    local_point = jnp.einsum("bxtop,bxtip->oi", grad_pre, features, preferred_element_type=F32)
    local_bias = jnp.sum(grad_pre.astype(F32), axis=(0, 1, 2, 4))
    total_point, total_bias = lax.psum((local_point, local_bias), ("gx", "ta"))
    grad_modes = analyse_xt(to_owners(analyse_yz(grad_pre, yz_table).astype(BF16)), xt_table)
    grad_spec = jnp.einsum("bklip,bklop->kliop", spectrum, grad_modes, precision=highest)
    grad_in = jnp.einsum("kliop,bklop->bklip", spec_weight, grad_modes, precision=highest)
    grad_back = to_cells(synthesise_xt(grad_in, xt_table).astype(BF16), shape)
    point_term = jnp.einsum("oi,bxtop->bxtip", point_weight, grad_pre, preferred_element_type=F32)
    grad_field = (build_yz(grad_back, yz_table) + point_term).astype(BF16)
    return (output, grad_field, grad_spec, total_point * norm_scale, total_bias * norm_scale)


def solution(mesh):
    split_field = P(None, "gx", "ta", None, None)
    split_weight = P(None, None, None, None, ("gx", "ta"))
    in_specs = (split_field, split_field, split_weight, P(), P())
    out_specs = (split_field, split_field, split_weight, P(), P())
    gx, ta = mesh.shape["gx"], mesh.shape["ta"]
    own, xl, tl = KQ // (gx * ta), NX // gx, NT // ta
    if own == 32 and xl * CHANS == LANES and tl == 4:
        body = functools.partial(fast_body, gx, ta)
    else:
        body = general_body
    return jax.shard_map(body, mesh=mesh, in_specs=in_specs, out_specs=out_specs, check_vma=False)
```

```python
import functools
import math

import jax
import jax.numpy as jnp
import ml_dtypes
import numpy as np
from jax import lax
from jax.experimental import pallas as pl
from jax.experimental.pallas import tpu as pltpu
from jax.sharding import PartitionSpec as P

NX = 128
NY = 128
NZ = 32
NT = 16
MX = 16
MY = 16
MZ = 16
MT = 8
BATCH = 1
KX = 32
KT = 16
CHANS = 8
CELLS = NY * NZ
KQ = 1024
LANES = 128
PARTS = 2
WIDTH = 512
DENSITY = 1.0 / math.sqrt(2.0 * math.pi)
F32 = jnp.float32
BF16 = jnp.bfloat16


def basis(length, modes):
    frequency = np.concatenate([np.arange(modes + 1), np.arange(1, modes)])
    samples_at = np.arange(length)
    phases = (2.0 * math.pi / length) * (frequency[:, None] * samples_at[None, :] % length)
    cosine_row = np.arange(2 * modes) <= modes
    waves = np.where(cosine_row[:, None], np.cos(phases), np.sin(phases))
    at_edge = cosine_row & ((frequency == 0) | (2 * frequency == length))
    scales = np.where(at_edge, math.sqrt(1.0 / length), math.sqrt(2.0 / length))
    return (waves * scales[:, None]).astype(np.float32)


def narrow(table):
    return np.asarray(table, np.float32).astype(ml_dtypes.bfloat16)


def vmem_params(mebibytes):
    return pltpu.CompilerParams(vmem_limit_bytes=mebibytes * 1024 * 1024)


def matmul(left, right):
    return jnp.dot(left, right, preferred_element_type=F32)


def matmul_turned(left, right):
    return lax.dot_general(
        left, right, (((1,), (1,)), ((), ())), preferred_element_type=F32
    )


def swap_groups(tiles):
    rows = tiles[0].shape[0]
    lane = lax.broadcasted_iota(jnp.int32, (rows, LANES), 1)
    low_half = lane < 64
    even = (lane // 32) % 2 == 0
    first, second, third, fourth = tiles
    b0 = jnp.where(low_half, first, pltpu.roll(third, 64, 1))
    b2 = jnp.where(low_half, pltpu.roll(first, 64, 1), third)
    b1 = jnp.where(low_half, second, pltpu.roll(fourth, 64, 1))
    b3 = jnp.where(low_half, pltpu.roll(second, 64, 1), fourth)
    return (
        jnp.where(even, b0, pltpu.roll(b1, 32, 1)),
        jnp.where(even, pltpu.roll(b0, 96, 1), b1),
        jnp.where(even, b2, pltpu.roll(b3, 32, 1)),
        jnp.where(even, pltpu.roll(b2, 96, 1), b3),
    )


def pack_modes(modes_ref, held_ref, packed_ref, sems, xl, tl):
    sends = []
    for tile in range(KQ // LANES):
        modes = modes_ref[tile * LANES : (tile + 1) * LANES, :].T
        split = modes.reshape(xl, tl, CHANS, LANES)
        tiles = [split[:, step].reshape(xl * CHANS, LANES) for step in range(tl)]
        owners = slice(tile * tl, (tile + 1) * tl)
        held_ref[owners] = jnp.stack([block.astype(BF16) for block in swap_groups(tiles)])
        send = pltpu.make_async_copy(held_ref.at[owners], packed_ref.at[owners], sems.at[tile])
        send.start()
        sends.append(send)
    for send in sends:
        send.wait()


def unpack_modes(packed_ref, wide_ref, xl, tl):
    for tile in range(KQ // LANES):
        tiles = [packed_ref[tile * tl + owner].astype(F32) for owner in range(tl)]
        for step, block in enumerate(swap_groups(tiles)):
            wide_ref[:, step, :, tile * LANES : (tile + 1) * LANES] = block.reshape(
                xl, CHANS, LANES
            )


def analyse_kernel(
    xl, tl, field_ref, table_ref, packed_ref, field, table, total, held, field_sems, table_sems, sems
):
    chunks = table.shape[0]
    ahead = 4
    fetches = []
    for at in range(chunks):
        lanes = slice(at * WIDTH, (at + 1) * WIDTH)
        fetches.append(
            (
                pltpu.make_async_copy(field_ref.at[:, lanes], field.at[at], field_sems.at[at]),
                pltpu.make_async_copy(table_ref.at[at], table.at[at], table_sems.at[at]),
            )
        )

    def start(at):
        for fetch in fetches[at]:
            fetch.start()

    for at in range(ahead):
        start(at)
    for at in range(0, chunks, 2):
        for now in (at, at + 1):
            for fetch in fetches[now]:
                fetch.wait()
            if now + ahead < chunks:
                start(now + ahead)
        part = matmul_turned(
            jnp.concatenate([table[at], table[at + 1]], axis=1),
            jnp.concatenate([field[at], field[at + 1]], axis=1),
        )
        total[...] = part if at == 0 else total[...] + part
    pack_modes(total, held, packed_ref, sems, xl, tl)


def analyse(field, table, xl, tl, devices):
    rows = xl * tl * CHANS
    chunks = CELLS // WIDTH
    packed = (devices, xl * CHANS, LANES)
    return pl.pallas_call(
        functools.partial(analyse_kernel, xl, tl),
        in_specs=[pl.BlockSpec(memory_space=pltpu.HBM)] * 2,
        out_specs=pl.BlockSpec(memory_space=pl.ANY),
        out_shape=jax.ShapeDtypeStruct(packed, BF16),
        scratch_shapes=[
            pltpu.VMEM((chunks, rows, WIDTH), BF16),
            pltpu.VMEM((chunks, KQ, WIDTH), BF16),
            pltpu.VMEM((KQ, rows), F32),
            pltpu.VMEM(packed, BF16),
            pltpu.SemaphoreType.DMA((chunks,)),
            pltpu.SemaphoreType.DMA((chunks,)),
            pltpu.SemaphoreType.DMA((KQ // LANES,)),
        ],
        compiler_params=vmem_params(60),
        cost_estimate=pl.CostEstimate(
            flops=2 * rows * CELLS * KQ, bytes_accessed=13 << 20, transcendentals=0
        ),
        name="analyse",
    )(field, table)


def weight_kernel(weight_ref, packed_ref):
    for kx in range(weight_ref.shape[0]):
        for group in range(KT // 4):
            parts = [weight_ref[kx, 4 * group + k] for k in range(4)]
            joined = jnp.concatenate(parts, axis=-1).reshape(CHANS * CHANS, LANES)
            packed_ref[kx, :, group * LANES : (group + 1) * LANES] = joined.astype(BF16)


def pack_weight(weight):
    per = 4
    own = weight.shape[4]
    return pl.pallas_call(
        weight_kernel,
        grid=(KX // per,),
        in_specs=[pl.BlockSpec((per, KT, CHANS, CHANS, own), lambda n: (n, 0, 0, 0, 0))],
        out_specs=pl.BlockSpec((per, CHANS * CHANS, KT * own), lambda n: (n, 0, 0)),
        out_shape=jax.ShapeDtypeStruct((KX, CHANS * CHANS, KT * own), BF16),
        compiler_params=vmem_params(60),
        cost_estimate=pl.CostEstimate(flops=1 << 20, bytes_accessed=20 << 20, transcendentals=0),
        name="pack_weight",
    )(weight)


def to_modes(spread_refs, x_table_ref, t_table_ref):
    total = 0.0
    for part, spread_ref in enumerate(spread_refs):
        gx, ta, rows, _ = spread_ref.shape
        beside = jnp.concatenate(
            [spread_ref[:, at].reshape(gx * rows, LANES) for at in range(ta)], axis=1
        )
        total = total + matmul(x_table_ref[part], beside)
    return matmul(total.astype(BF16), t_table_ref[...])


def from_modes(modes, x_table_ref, t_table_ref, held_ref, back_refs, sems):
    parts, gx, ta, rows, _ = held_ref.shape
    half = matmul(modes.astype(BF16), t_table_ref[...]).astype(BF16)
    pieces = sems.shape[1]
    per = gx // pieces
    sends = []
    for part in range(parts):
        for piece in range(pieces):
            table = x_table_ref[part, piece * per * rows : (piece + 1) * per * rows, :]
            full = matmul(table, half).astype(BF16)
            owners = slice(piece * per, (piece + 1) * per)
            for at in range(ta):
                held_ref[part, owners, at] = full[:, at * LANES : (at + 1) * LANES].reshape(
                    per, rows, LANES
                )
            send = pltpu.make_async_copy(
                held_ref.at[part, owners], back_refs[part].at[owners], sems.at[part, piece]
            )
            send.start()
            sends.append(send)
    for send in sends:
        send.wait()


def mix_kernel(
    backward,
    afters,
    weight_ref,
    *refs,
):
    x_in_ref, t_in_ref, x_out_ref, t_out_ref = refs[afters : afters + 4]
    refs = refs[afters + 4 :]
    ins, outs = x_in_ref.shape[0], x_out_ref.shape[0]
    spread_refs, modes_ref, back_refs = refs[:ins], refs[ins], refs[ins + 1 : ins + 1 + outs]
    scratch = refs[ins + 1 + outs :]
    weight, modes, mixed, held, x_in, t_in, x_out, t_out = scratch[:8]
    spreads, (sems, weight_sems, spread_sems, back_sems) = scratch[8:-4], scratch[-4:]
    arrivals = [
        pltpu.make_async_copy(source, target, spread_sems.at[at])
        for at, (source, target) in enumerate(zip(spread_refs, spreads))
    ]
    pieces = weight_sems.shape[0]
    per = KX // pieces
    sources = (x_in_ref, t_in_ref, t_out_ref, x_out_ref)
    tables = [
        pltpu.make_async_copy(source, target, sems.at[at])
        for at, (source, target) in enumerate(zip(sources, (x_in, t_in, t_out, x_out)))
    ]
    fetches = []
    for at in range(pieces):
        part = slice(at * per, (at + 1) * per)
        fetches.append(
            pltpu.make_async_copy(weight_ref.at[part], weight.at[part], weight_sems.at[at])
        )
    for copy in arrivals + tables[:2] + fetches + tables[2:]:
        copy.start()
    for copy in arrivals + tables[:2]:
        copy.wait()
    modes[...] = to_modes(spreads, x_in, t_in)
    keep = pltpu.make_async_copy(modes, modes_ref, sems.at[4])
    keep.start()
    for fetch in fetches:
        fetch.wait()
    for kx in range(KX):
        rows = slice(kx * CHANS, (kx + 1) * CHANS)
        own = modes[rows, :]
        weights = weight[kx].astype(F32).reshape(CHANS, CHANS, own.shape[1])
        if backward:
            sums = [jnp.sum(own * weights[i], axis=0, keepdims=True) for i in range(CHANS)]
            mixed[rows, :] = jnp.concatenate(sums, axis=0)
        else:
            total = own[0:1, :] * weights[0]
            for i in range(1, CHANS):
                total = total + own[i : i + 1, :] * weights[i]
            mixed[rows, :] = total
    tables[2].wait()
    tables[3].wait()
    from_modes(mixed[...], x_out, t_out, held, back_refs, back_sems)
    keep.wait()


def mix(spreads, weight, after, tables, backward):
    modes = (KX * CHANS, weight.shape[2])
    gx, ta, _, lanes = spreads[0].shape
    outs = tables[2].shape[0]
    back = (gx, ta, tables[2].shape[1] // gx, lanes)
    anywhere = pl.BlockSpec(memory_space=pl.ANY)
    apart = pl.BlockSpec(memory_space=pltpu.HBM)
    return pl.pallas_call(
        functools.partial(mix_kernel, backward, len(after)),
        out_shape=[jax.ShapeDtypeStruct(modes, F32)] + [jax.ShapeDtypeStruct(back, BF16)] * outs,
        in_specs=[apart] + [anywhere] * len(after) + [apart] * 4 + [anywhere] * len(spreads),
        out_specs=[apart] + [anywhere] * outs,
        scratch_shapes=[
            pltpu.VMEM(weight.shape, BF16),
            pltpu.VMEM(modes, F32),
            pltpu.VMEM(modes, F32),
            pltpu.VMEM((outs,) + back, BF16),
            *[pltpu.VMEM(table.shape, BF16) for table in tables],
            *[pltpu.VMEM(spread.shape, BF16) for spread in spreads],
            pltpu.SemaphoreType.DMA((5,)),
            pltpu.SemaphoreType.DMA((8,)),
            pltpu.SemaphoreType.DMA((len(spreads),)),
            pltpu.SemaphoreType.DMA((outs, 4 // outs)),
        ],
        compiler_params=vmem_params(60),
        cost_estimate=pl.CostEstimate(flops=1 << 30, bytes_accessed=9 << 20, transcendentals=0),
        name="mix_back" if backward else "mix",
    )(weight, *after, *tables, *spreads)


def outer_kernel(spectrum_ref, grad_ref, result_ref):
    own = result_ref.shape[4]
    for kx in range(result_ref.shape[0]):
        rows = slice(kx * CHANS, (kx + 1) * CHANS)
        for group in range(KT // 4):
            at = slice(group * LANES, (group + 1) * LANES)
            inputs = spectrum_ref[rows, at]
            grads = grad_ref[rows, at]
            for i in range(CHANS):
                product = inputs[i : i + 1, :] * grads
                for k in range(4):
                    result_ref[kx, 4 * group + k, i] = product[:, k * own : (k + 1) * own]


def outer(spectrum, grad, own):
    per = 4
    width = KT * own
    return pl.pallas_call(
        outer_kernel,
        grid=(KX // per,),
        in_specs=[pl.BlockSpec((per * CHANS, width), lambda n: (n, 0))] * 2,
        out_specs=pl.BlockSpec((per, KT, CHANS, CHANS, own), lambda n: (n, 0, 0, 0, 0)),
        out_shape=jax.ShapeDtypeStruct((KX, KT, CHANS, CHANS, own), F32),
        compiler_params=vmem_params(60),
        cost_estimate=pl.CostEstimate(flops=1 << 20, bytes_accessed=17 << 20, transcendentals=0),
        name="outer",
    )(spectrum, grad)


def normal_parts(values):
    scaled = 1.0 + 0.2316419 * jnp.abs(values)
    guess = pl.reciprocal(scaled, approx=True)
    t = guess * (2.0 - scaled * guess)
    decay = jnp.exp(values * values * -0.5)
    series = (1.330274429 * DENSITY) * t - 1.821255978 * DENSITY
    series = series * t + 1.781477937 * DENSITY
    series = series * t - 0.356563782 * DENSITY
    series = series * t + 0.319381530 * DENSITY
    tail = decay * (series * t)
    return jnp.where(values >= 0.0, 1.0 - tail, tail), decay


def point_field_kernel(mixer_ref, bias_ref, field_ref, mixed_ref):
    rows = mixer_ref.shape[0]
    bias = jnp.concatenate([bias_ref[...]] * (WIDTH // LANES), axis=1)
    for at in range(mixed_ref.shape[0]):
        for first in range(0, field_ref.shape[0], rows):
            part = slice(first, first + rows)
            field = field_ref[part, at * WIDTH : (at + 1) * WIDTH]
            mixed_ref[at, part, :] = (matmul(mixer_ref[...], field) + bias).astype(BF16)


def point_field(field, mixer, bias):
    rows = field.shape[0]
    group = mixer.shape[0]
    per = 2
    return pl.pallas_call(
        point_field_kernel,
        grid=(CELLS // (per * WIDTH),),
        in_specs=[
            pl.BlockSpec((group, group), lambda n: (0, 0)),
            pl.BlockSpec((group, LANES), lambda n: (0, 0)),
            pl.BlockSpec((rows, per * WIDTH), lambda n: (0, n)),
        ],
        out_specs=pl.BlockSpec((per, rows, WIDTH), lambda n: (n, 0, 0)),
        out_shape=jax.ShapeDtypeStruct((CELLS // WIDTH, rows, WIDTH), BF16),
        compiler_params=vmem_params(60),
        cost_estimate=pl.CostEstimate(
            flops=2 * rows * CELLS * group, bytes_accessed=8 << 20, transcendentals=0
        ),
        name="point_field",
    )(mixer, bias, field)


def point_grad_kernel(mixer_ref, grad_ref, _, mixed_ref):
    rows = mixer_ref.shape[0]
    for at in range(mixed_ref.shape[0]):
        for first in range(0, grad_ref.shape[1], rows):
            part = slice(first, first + rows)
            mixed_ref[at, part, :] = matmul(mixer_ref[...], grad_ref[at, part, :]).astype(BF16)


def point_grad(grad, mixer, after):
    chunks, rows, _ = grad.shape
    group = mixer.shape[0]
    per = 2
    blocks = pl.BlockSpec((per, rows, WIDTH), lambda n: (n, 0, 0))
    return pl.pallas_call(
        point_grad_kernel,
        grid=(chunks // per,),
        in_specs=[
            pl.BlockSpec((group, group), lambda n: (0, 0)),
            blocks,
            pl.BlockSpec(memory_space=pltpu.HBM),
        ],
        out_specs=blocks,
        out_shape=jax.ShapeDtypeStruct(grad.shape, BF16),
        compiler_params=vmem_params(16),
        cost_estimate=pl.CostEstimate(
            flops=2 * rows * CELLS * group, bytes_accessed=8 << 20, transcendentals=0
        ),
        name="point_grad",
    )(mixer, grad, after)


def sums_kernel(group, field_ref, grad_ref, sums_ref, total):
    step = pl.program_id(0)
    rows, width = field_ref.shape
    blocks = grad_ref.shape[0]
    ones = jnp.ones((16, width), BF16)
    part = 0.0
    for first in range(0, rows, group):
        at = slice(first, first + group)
        passing = jnp.concatenate([field_ref[at, :], ones], axis=0)
        grads = jnp.concatenate([grad_ref[block, at, :] for block in range(blocks)], axis=1)
        part = part + matmul_turned(passing, grads)

    @pl.when(step == 0)
    def _():
        total[...] = part

    @pl.when(step > 0)
    def _():
        total[...] += part

    @pl.when(step == pl.num_programs(0) - 1)
    def _():
        row = lax.broadcasted_iota(jnp.int32, (group, group), 0)
        column = lax.broadcasted_iota(jnp.int32, (group, group), 1)
        gram = total[:group, :].T
        bias = total[group : group + CHANS, :]
        same = jnp.where(row // CHANS == column // CHANS, gram, 0.0)
        folded = jnp.sum(same.reshape(group // CHANS, CHANS, group), axis=0)
        source = lax.broadcasted_iota(jnp.int32, (group, LANES), 0)
        target = lax.broadcasted_iota(jnp.int32, (group, LANES), 1)
        select = jnp.where(source % CHANS == target, 1.0, 0.0)
        chan = lax.broadcasted_iota(jnp.int32, (CHANS, group), 0)
        place = lax.broadcasted_iota(jnp.int32, (CHANS, group), 1)
        own_bias = jnp.sum(
            jnp.where(place % CHANS == chan, bias, 0.0), axis=1, keepdims=True
        )
        point = jnp.dot(
            folded, select, precision=lax.Precision.HIGHEST, preferred_element_type=F32
        )
        lane = lax.broadcasted_iota(jnp.int32, (CHANS, LANES), 1)
        sums_ref[...] = jnp.where(lane == CHANS, own_bias, point)


def own_sums(field, grad, group):
    chunks, rows, _ = grad.shape
    per = 2
    return pl.pallas_call(
        functools.partial(sums_kernel, group),
        grid=(chunks // per,),
        in_specs=[
            pl.BlockSpec((rows, per * WIDTH), lambda n: (0, n)),
            pl.BlockSpec((per, rows, WIDTH), lambda n: (n, 0, 0)),
        ],
        out_specs=pl.BlockSpec((CHANS, LANES), lambda n: (0, 0)),
        out_shape=jax.ShapeDtypeStruct((CHANS, LANES), F32),
        scratch_shapes=[pltpu.VMEM((group + 16, group), F32)],
        compiler_params=vmem_params(60),
        cost_estimate=pl.CostEstimate(
            flops=2 * rows * CELLS * group, bytes_accessed=8 << 20, transcendentals=0
        ),
        name="own_sums",
    )(field, grad)


def middle_kernel(
    xl,
    tl,
    packed_ref,
    cotangent_ref,
    mixed_ref,
    table_ref,
    output_ref,
    grad_ref,
    sent_ref,
    wide,
    modes,
    total,
    held,
    sems,
):
    step = pl.program_id(0)
    rows, width = cotangent_ref.shape
    tile = 256
    chunk = 32

    @pl.when(step == 0)
    def _():
        unpack_modes(packed_ref, wide, xl, tl)
        modes[...] = wide[...].reshape(rows, KQ).astype(BF16)
        total[...] = jnp.zeros_like(total)

    def build(at):
        block, first = divmod(at, WIDTH)
        return matmul(modes[...], table_ref[block, :, first : first + tile])

    def pointwise(pre, at):
        block, first = divmod(at, WIDTH)
        for top in range(0, rows, chunk):
            part = slice(top, top + chunk)
            inner, outer = slice(first, first + tile), slice(at, at + tile)
            values = pre[part, :] + mixed_ref[block, part, inner].astype(F32)
            integral, decay = normal_parts(values)
            output_ref[part, outer] = (values * integral).astype(BF16)
            slope = integral + (values * DENSITY) * decay
            grad = (cotangent_ref[part, outer].astype(F32) * slope).astype(BF16)
            grad_ref[block, part, inner] = grad

    firsts = range(0, width, tile)
    ready = build(0)
    for at in firsts:
        pre = ready
        if at + tile < width:
            ready = build(at + tile)
        pointwise(pre, at)
        block, first = divmod(at + tile, WIDTH)
        if first == 0:
            total[...] += matmul_turned(table_ref[block - 1], grad_ref[block - 1])

    @pl.when(step == pl.num_programs(0) - 1)
    def _():
        pack_modes(total, held, sent_ref, sems, xl, tl)


def middle(packed, cotangent, mixed, table, xl, tl):
    rows = xl * tl * CHANS
    chunks = CELLS // WIDTH
    per = 2
    tile = pl.BlockSpec((rows, per * WIDTH), lambda n: (0, n))
    block = pl.BlockSpec((per, rows, WIDTH), lambda n: (n, 0, 0))
    return pl.pallas_call(
        functools.partial(middle_kernel, xl, tl),
        grid=(chunks // per,),
        in_specs=[
            pl.BlockSpec(packed.shape, lambda n: (0, 0, 0)),
            tile,
            block,
            pl.BlockSpec((per, KQ, WIDTH), lambda n: (n, 0, 0)),
        ],
        out_specs=[tile, block, pl.BlockSpec(memory_space=pl.ANY)],
        out_shape=(
            jax.ShapeDtypeStruct((rows, CELLS), BF16),
            jax.ShapeDtypeStruct((chunks, rows, WIDTH), BF16),
            jax.ShapeDtypeStruct(packed.shape, BF16),
        ),
        scratch_shapes=[
            pltpu.VMEM((xl, tl, CHANS, KQ), F32),
            pltpu.VMEM((rows, KQ), BF16),
            pltpu.VMEM((KQ, rows), F32),
            pltpu.VMEM(packed.shape, BF16),
            pltpu.SemaphoreType.DMA((KQ // LANES,)),
        ],
        compiler_params=vmem_params(60),
        cost_estimate=pl.CostEstimate(
            flops=4 * rows * CELLS * KQ, bytes_accessed=26 << 20, transcendentals=rows * CELLS
        ),
        name="middle",
    )(packed, cotangent, mixed, table)


def last_kernel(xl, tl, packed_ref, table_ref, mixed_ref, field_ref, *scratch):
    wide, modes, table, mixed, field, table_sems, mixed_sems, field_sems = scratch
    chunks = table.shape[0]
    ahead = 4
    fetches, sends = [], []
    for at in range(chunks):
        lanes = slice(at * WIDTH, (at + 1) * WIDTH)
        fetches.append(
            (
                pltpu.make_async_copy(table_ref.at[at], table.at[at], table_sems.at[at]),
                pltpu.make_async_copy(mixed_ref.at[at], mixed.at[at], mixed_sems.at[at]),
            )
        )
        sends.append(
            pltpu.make_async_copy(field.at[at], field_ref.at[:, lanes], field_sems.at[at])
        )

    def start(at):
        for fetch in fetches[at]:
            fetch.start()

    for at in range(ahead):
        start(at)
    unpack_modes(packed_ref, wide, xl, tl)
    modes[...] = wide[...].reshape(modes.shape).astype(BF16)
    for at in range(chunks):
        for fetch in fetches[at]:
            fetch.wait()
        if at + ahead < chunks:
            start(at + ahead)
        field[at] = (matmul(modes[...], table[at]) + mixed[at].astype(F32)).astype(BF16)
        sends[at].start()
    for send in sends:
        send.wait()


def last(packed, mixed, table, xl, tl):
    rows = xl * tl * CHANS
    chunks = CELLS // WIDTH
    apart = pl.BlockSpec(memory_space=pltpu.HBM)
    return pl.pallas_call(
        functools.partial(last_kernel, xl, tl),
        in_specs=[pl.BlockSpec(memory_space=pltpu.VMEM), apart, apart],
        out_specs=apart,
        out_shape=jax.ShapeDtypeStruct((rows, CELLS), BF16),
        scratch_shapes=[
            pltpu.VMEM((xl, tl, CHANS, KQ), F32),
            pltpu.VMEM((rows, KQ), BF16),
            pltpu.VMEM((chunks, KQ, WIDTH), BF16),
            pltpu.VMEM((chunks, rows, WIDTH), BF16),
            pltpu.VMEM((chunks, rows, WIDTH), BF16),
            pltpu.SemaphoreType.DMA((chunks,)),
            pltpu.SemaphoreType.DMA((chunks,)),
            pltpu.SemaphoreType.DMA((chunks,)),
        ],
        compiler_params=vmem_params(44),
        cost_estimate=pl.CostEstimate(
            flops=2 * rows * CELLS * KQ, bytes_accessed=18 << 20, transcendentals=0
        ),
        name="last",
    )(packed, table, mixed)


def swap(blocks):
    return lax.all_to_all(blocks, ("gx", "ta"), split_axis=0, concat_axis=0, tiled=True)


def sum_everywhere(values, devices):
    step = 1
    while step < devices:
        pairs = [(at, at ^ step) for at in range(devices)]
        values = values + lax.ppermute(values, ("gx", "ta"), pairs)
        step *= 2
    return values


def fast_body(gx, ta, features, cotangent, spec_weight, point_weight, bias_vector):
    _, xl, tl, _, cells = features.shape
    own = spec_weight.shape[4]
    devices = gx * ta
    rows = xl * tl * CHANS
    group = rows // PARTS
    yz = np.kron(
        narrow(basis(NY, MY)).astype(np.float32), narrow(basis(NZ, MZ)).astype(np.float32)
    )
    blocks = yz.reshape(KQ, CELLS // WIDTH, WIDTH).transpose(1, 0, 2)
    table = jnp.asarray(narrow(blocks))
    x_wide = np.kron(basis(NX, MX), np.eye(CHANS))[None]
    x_in, x_out = jnp.asarray(narrow(x_wide)), jnp.asarray(narrow(x_wide.transpose(0, 2, 1)))
    t_wide = np.kron(basis(NT, MT), np.eye(own))
    t_in, t_out = jnp.asarray(narrow(t_wide.T)), jnp.asarray(narrow(t_wide))
    norm_scale = float(BATCH * NX * NT * NY * NZ) ** (-0.5)

    field = features.reshape(rows, cells)
    cot = cotangent.reshape(rows, cells)
    pick = np.tile(np.eye(CHANS, dtype=np.float32), (group // CHANS, 1))
    same = np.kron(np.eye(group // CHANS, dtype=np.float32), np.ones((CHANS, CHANS), np.float32))
    picked = jnp.asarray(narrow(pick))
    spread_point = matmul(matmul(picked, point_weight).astype(BF16), picked.T)
    spread_back = matmul(matmul(picked, point_weight.T).astype(BF16), picked.T)
    mixer = (spread_point * jnp.asarray(same)).astype(BF16)
    mixer_back = (spread_back * jnp.asarray(same)).astype(BF16)
    bias = jnp.dot(
        jnp.asarray(pick),
        jnp.broadcast_to(bias_vector[:, None], (CHANS, LANES)),
        precision=lax.Precision.HIGHEST,
    )
    spread_shape = (gx, ta, xl * CHANS, LANES)
    block_shape = (devices, xl * CHANS, LANES)
    packed_weight = pack_weight(spec_weight)
    tables = (x_in, t_in, x_out, t_out)

    spread_in = swap(analyse(field, table, xl, tl, devices)).reshape(spread_shape)
    spectrum, mixed = mix([spread_in], packed_weight, (mixer, mixer_back, bias), tables, False)
    returned = swap(mixed.reshape(block_shape))
    mixed_field = point_field(field, mixer, bias)
    output, grad, sent = middle(returned, cot, mixed_field, table, xl, tl)
    spread_grad = swap(sent).reshape(spread_shape)
    summed = sum_everywhere(own_sums(field, grad, group), devices)
    grad_modes, mixed_back = mix([spread_grad], packed_weight, (summed,), tables, True)
    grad_back = swap(mixed_back.reshape(block_shape))
    grad_spec = outer(spectrum, grad_modes, own)
    grad_field = last(grad_back, point_grad(grad, mixer_back, grad_spec), table, xl, tl)
    summed = summed * norm_scale
    return (
        output.reshape(features.shape),
        grad_field.reshape(features.shape),
        grad_spec,
        summed[:, :CHANS],
        summed[:, CHANS],
    )


def analyse_yz(spatial, yz_table):
    return jnp.einsum(
        "qp,bxtcp->bxtcq", yz_table, spatial.astype(F32), precision=lax.Precision.HIGHEST
    )


def build_yz(modes_in, yz_table):
    return jnp.einsum(
        "qp,bxtcq->bxtcp", yz_table, modes_in.astype(F32), precision=lax.Precision.HIGHEST
    )


def analyse_xt(spread, table):
    sizes = spread.shape
    flattened = spread.reshape(sizes[0], sizes[1] * sizes[2], sizes[3] * sizes[4]).astype(F32)
    spectral = jnp.einsum("mp,bpr->bmr", table, flattened, precision=lax.Precision.HIGHEST)
    return spectral.reshape(sizes[0], KX, KT, sizes[3], sizes[4])


def synthesise_xt(modes_in, table):
    sizes = modes_in.shape
    flattened = modes_in.reshape(sizes[0], sizes[1] * sizes[2], sizes[3] * sizes[4])
    spatial = jnp.einsum("mp,bmr->bpr", table, flattened, precision=lax.Precision.HIGHEST)
    return spatial.reshape(sizes[0], NX, NT, sizes[3], sizes[4])


def to_owners(modes_in):
    first = lax.all_to_all(modes_in, "gx", split_axis=4, concat_axis=1, tiled=True)
    return lax.all_to_all(first, "ta", split_axis=4, concat_axis=2, tiled=True)


def to_cells(spread, shape):
    first = lax.all_to_all(
        spread[:, :, :, :, None, None, :], "gx", split_axis=1, concat_axis=4, tiled=True
    )
    second = lax.all_to_all(first, "ta", split_axis=2, concat_axis=5, tiled=True)
    return second.reshape(shape[:4] + (-1,))


def general_body(features, cotangent, spec_weight, point_weight, bias_vector):
    shape = features.shape
    yz_table = jnp.asarray(
        np.kron(narrow(basis(NY, MY)).astype(np.float32), narrow(basis(NZ, MZ)).astype(np.float32))
    )
    xt_table = jnp.asarray(np.kron(basis(NX, MX), basis(NT, MT)))
    norm_scale = float(BATCH * NX * NT * NY * NZ) ** (-0.5)
    highest = lax.Precision.HIGHEST
    spectrum = analyse_xt(to_owners(analyse_yz(features, yz_table).astype(BF16)), xt_table)
    mixed = jnp.einsum("bklip,kliop->bklop", spectrum, spec_weight, precision=highest)
    returned = to_cells(synthesise_xt(mixed, xt_table).astype(BF16), shape)
    pointwise = jnp.einsum("oi,bxtip->bxtop", point_weight, features, preferred_element_type=F32)
    pre = build_yz(returned, yz_table) + pointwise + bias_vector[:, None]
    integral = 0.5 * (1.0 + jax.scipy.special.erf(pre * 0.7071067811865476))
    output = (pre * integral).astype(BF16)
    slope = integral + pre * jnp.exp(-0.5 * pre * pre) * 0.3989422804014327
    grad_pre = (cotangent.astype(F32) * slope).astype(BF16)
    local_point = jnp.einsum("bxtop,bxtip->oi", grad_pre, features, preferred_element_type=F32)
    local_bias = jnp.sum(grad_pre.astype(F32), axis=(0, 1, 2, 4))
    total_point, total_bias = lax.psum((local_point, local_bias), ("gx", "ta"))
    grad_modes = analyse_xt(to_owners(analyse_yz(grad_pre, yz_table).astype(BF16)), xt_table)
    grad_spec = jnp.einsum("bklip,bklop->kliop", spectrum, grad_modes, precision=highest)
    grad_in = jnp.einsum("kliop,bklop->bklip", spec_weight, grad_modes, precision=highest)
    grad_back = to_cells(synthesise_xt(grad_in, xt_table).astype(BF16), shape)
    point_term = jnp.einsum("oi,bxtop->bxtip", point_weight, grad_pre, preferred_element_type=F32)
    grad_field = (build_yz(grad_back, yz_table) + point_term).astype(BF16)
    return (output, grad_field, grad_spec, total_point * norm_scale, total_bias * norm_scale)


def solution(mesh):
    split_field = P(None, "gx", "ta", None, None)
    split_weight = P(None, None, None, None, ("gx", "ta"))
    in_specs = (split_field, split_field, split_weight, P(), P())
    out_specs = (split_field, split_field, split_weight, P(), P())
    gx, ta = mesh.shape["gx"], mesh.shape["ta"]
    own, xl, tl = KQ // (gx * ta), NX // gx, NT // ta
    if own == 32 and xl * CHANS == LANES and tl == 4:
        body = functools.partial(fast_body, gx, ta)
    else:
        body = general_body
    return jax.shard_map(body, mesh=mesh, in_specs=in_specs, out_specs=out_specs, check_vma=False)
```

```python
import functools
import math

import jax
import jax.numpy as jnp
import ml_dtypes
import numpy as np
from jax import lax
from jax.experimental import pallas as pl
from jax.experimental.pallas import tpu as pltpu
from jax.sharding import PartitionSpec as P

NX = 128
NY = 128
NZ = 32
NT = 16
MX = 16
MY = 16
MZ = 16
MT = 8
BATCH = 1
KX = 32
KT = 16
CHANS = 8
CELLS = NY * NZ
KQ = 1024
LANES = 128
PARTS = 2
WIDTH = 512
DENSITY = 1.0 / math.sqrt(2.0 * math.pi)
F32 = jnp.float32
BF16 = jnp.bfloat16


def basis(length, modes):
    frequency = np.concatenate([np.arange(modes + 1), np.arange(1, modes)])
    samples_at = np.arange(length)
    phases = (2.0 * math.pi / length) * (frequency[:, None] * samples_at[None, :] % length)
    cosine_row = np.arange(2 * modes) <= modes
    waves = np.where(cosine_row[:, None], np.cos(phases), np.sin(phases))
    at_edge = cosine_row & ((frequency == 0) | (2 * frequency == length))
    scales = np.where(at_edge, math.sqrt(1.0 / length), math.sqrt(2.0 / length))
    return (waves * scales[:, None]).astype(np.float32)


def narrow(table):
    return np.asarray(table, np.float32).astype(ml_dtypes.bfloat16)


def vmem_params(mebibytes):
    return pltpu.CompilerParams(vmem_limit_bytes=mebibytes * 1024 * 1024)


def matmul(left, right):
    return jnp.dot(left, right, preferred_element_type=F32)


def matmul_turned(left, right):
    return lax.dot_general(
        left, right, (((1,), (1,)), ((), ())), preferred_element_type=F32
    )


def swap_groups(tiles):
    rows = tiles[0].shape[0]
    lane = lax.broadcasted_iota(jnp.int32, (rows, LANES), 1)
    low_half = lane < 64
    even = (lane // 32) % 2 == 0
    first, second, third, fourth = tiles
    b0 = jnp.where(low_half, first, pltpu.roll(third, 64, 1))
    b2 = jnp.where(low_half, pltpu.roll(first, 64, 1), third)
    b1 = jnp.where(low_half, second, pltpu.roll(fourth, 64, 1))
    b3 = jnp.where(low_half, pltpu.roll(second, 64, 1), fourth)
    return (
        jnp.where(even, b0, pltpu.roll(b1, 32, 1)),
        jnp.where(even, pltpu.roll(b0, 96, 1), b1),
        jnp.where(even, b2, pltpu.roll(b3, 32, 1)),
        jnp.where(even, pltpu.roll(b2, 96, 1), b3),
    )


def pack_modes(modes_ref, held_ref, packed_ref, sems, xl, tl):
    sends = []
    for tile in range(KQ // LANES):
        modes = modes_ref[tile * LANES : (tile + 1) * LANES, :].T
        split = modes.reshape(xl, tl, CHANS, LANES)
        tiles = [split[:, step].reshape(xl * CHANS, LANES) for step in range(tl)]
        owners = slice(tile * tl, (tile + 1) * tl)
        held_ref[owners] = jnp.stack([block.astype(BF16) for block in swap_groups(tiles)])
        send = pltpu.make_async_copy(held_ref.at[owners], packed_ref.at[owners], sems.at[tile])
        send.start()
        sends.append(send)
    for send in sends:
        send.wait()


def unpack_modes(packed_ref, wide_ref, xl, tl):
    for tile in range(KQ // LANES):
        tiles = [packed_ref[tile * tl + owner].astype(F32) for owner in range(tl)]
        for step, block in enumerate(swap_groups(tiles)):
            wide_ref[:, step, :, tile * LANES : (tile + 1) * LANES] = block.reshape(
                xl, CHANS, LANES
            )


def analyse_kernel(
    xl, tl, field_ref, table_ref, packed_ref, field, table, total, held, field_sems, table_sems, sems
):
    chunks = table.shape[0]
    ahead = 4
    fetches = []
    for at in range(chunks):
        lanes = slice(at * WIDTH, (at + 1) * WIDTH)
        fetches.append(
            (
                pltpu.make_async_copy(field_ref.at[:, lanes], field.at[at], field_sems.at[at]),
                pltpu.make_async_copy(table_ref.at[at], table.at[at], table_sems.at[at]),
            )
        )

    def start(at):
        for fetch in fetches[at]:
            fetch.start()

    for at in range(ahead):
        start(at)
    for at in range(0, chunks, 2):
        for now in (at, at + 1):
            for fetch in fetches[now]:
                fetch.wait()
            if now + ahead < chunks:
                start(now + ahead)
        part = matmul_turned(
            jnp.concatenate([table[at], table[at + 1]], axis=1),
            jnp.concatenate([field[at], field[at + 1]], axis=1),
        )
        total[...] = part if at == 0 else total[...] + part
    pack_modes(total, held, packed_ref, sems, xl, tl)


def analyse(field, table, xl, tl, devices):
    rows = xl * tl * CHANS
    chunks = CELLS // WIDTH
    packed = (devices, xl * CHANS, LANES)
    return pl.pallas_call(
        functools.partial(analyse_kernel, xl, tl),
        in_specs=[pl.BlockSpec(memory_space=pltpu.HBM)] * 2,
        out_specs=pl.BlockSpec(memory_space=pl.ANY),
        out_shape=jax.ShapeDtypeStruct(packed, BF16),
        scratch_shapes=[
            pltpu.VMEM((chunks, rows, WIDTH), BF16),
            pltpu.VMEM((chunks, KQ, WIDTH), BF16),
            pltpu.VMEM((KQ, rows), F32),
            pltpu.VMEM(packed, BF16),
            pltpu.SemaphoreType.DMA((chunks,)),
            pltpu.SemaphoreType.DMA((chunks,)),
            pltpu.SemaphoreType.DMA((KQ // LANES,)),
        ],
        compiler_params=vmem_params(60),
        cost_estimate=pl.CostEstimate(
            flops=2 * rows * CELLS * KQ, bytes_accessed=13 << 20, transcendentals=0
        ),
        name="analyse",
    )(field, table)


def weight_kernel(weight_ref, packed_ref):
    for kx in range(weight_ref.shape[0]):
        for group in range(KT // 4):
            parts = [weight_ref[kx, 4 * group + k] for k in range(4)]
            joined = jnp.concatenate(parts, axis=-1).reshape(CHANS * CHANS, LANES)
            packed_ref[kx, :, group * LANES : (group + 1) * LANES] = joined.astype(BF16)


def pack_weight(weight):
    per = 4
    own = weight.shape[4]
    return pl.pallas_call(
        weight_kernel,
        grid=(KX // per,),
        in_specs=[pl.BlockSpec((per, KT, CHANS, CHANS, own), lambda n: (n, 0, 0, 0, 0))],
        out_specs=pl.BlockSpec((per, CHANS * CHANS, KT * own), lambda n: (n, 0, 0)),
        out_shape=jax.ShapeDtypeStruct((KX, CHANS * CHANS, KT * own), BF16),
        compiler_params=vmem_params(60),
        cost_estimate=pl.CostEstimate(flops=1 << 20, bytes_accessed=20 << 20, transcendentals=0),
        name="pack_weight",
    )(weight)


def to_modes(spread_refs, x_table_ref, t_table_ref):
    total = 0.0
    for part, spread_ref in enumerate(spread_refs):
        gx, ta, rows, _ = spread_ref.shape
        beside = jnp.concatenate(
            [spread_ref[:, at].reshape(gx * rows, LANES) for at in range(ta)], axis=1
        )
        total = total + matmul(x_table_ref[part], beside)
    return matmul(total.astype(BF16), t_table_ref[...])


def from_modes(modes, x_table_ref, t_table_ref, held_ref, back_refs, sems):
    parts, gx, ta, rows, _ = held_ref.shape
    half = matmul(modes.astype(BF16), t_table_ref[...]).astype(BF16)
    pieces = sems.shape[1]
    per = gx // pieces
    sends = []
    for part in range(parts):
        for piece in range(pieces):
            table = x_table_ref[part, piece * per * rows : (piece + 1) * per * rows, :]
            full = matmul(table, half).astype(BF16)
            owners = slice(piece * per, (piece + 1) * per)
            for at in range(ta):
                held_ref[part, owners, at] = full[:, at * LANES : (at + 1) * LANES].reshape(
                    per, rows, LANES
                )
            send = pltpu.make_async_copy(
                held_ref.at[part, owners], back_refs[part].at[owners], sems.at[part, piece]
            )
            send.start()
            sends.append(send)
    for send in sends:
        send.wait()


def mix_kernel(
    backward,
    afters,
    weight_ref,
    *refs,
):
    x_in_ref, t_in_ref, x_out_ref, t_out_ref = refs[afters : afters + 4]
    refs = refs[afters + 4 :]
    ins, outs = x_in_ref.shape[0], x_out_ref.shape[0]
    spread_refs, modes_ref, back_refs = refs[:ins], refs[ins], refs[ins + 1 : ins + 1 + outs]
    scratch = refs[ins + 1 + outs :]
    weight, modes, mixed, held, x_in, t_in, x_out, t_out = scratch[:8]
    spreads, (sems, weight_sems, spread_sems, back_sems) = scratch[8:-4], scratch[-4:]
    arrivals = [
        pltpu.make_async_copy(source, target, spread_sems.at[at])
        for at, (source, target) in enumerate(zip(spread_refs, spreads))
    ]
    pieces = weight_sems.shape[0]
    per = KX // pieces
    sources = (x_in_ref, t_in_ref, t_out_ref, x_out_ref)
    tables = [
        pltpu.make_async_copy(source, target, sems.at[at])
        for at, (source, target) in enumerate(zip(sources, (x_in, t_in, t_out, x_out)))
    ]
    fetches = []
    for at in range(pieces):
        part = slice(at * per, (at + 1) * per)
        fetches.append(
            pltpu.make_async_copy(weight_ref.at[part], weight.at[part], weight_sems.at[at])
        )
    for copy in arrivals + tables[:2] + fetches + tables[2:]:
        copy.start()
    for copy in arrivals + tables[:2]:
        copy.wait()
    modes[...] = to_modes(spreads, x_in, t_in)
    keep = pltpu.make_async_copy(modes, modes_ref, sems.at[4])
    keep.start()
    for fetch in fetches:
        fetch.wait()
    for kx in range(KX):
        rows = slice(kx * CHANS, (kx + 1) * CHANS)
        own = modes[rows, :]
        weights = weight[kx].astype(F32).reshape(CHANS, CHANS, own.shape[1])
        if backward:
            sums = [jnp.sum(own * weights[i], axis=0, keepdims=True) for i in range(CHANS)]
            mixed[rows, :] = jnp.concatenate(sums, axis=0)
        else:
            total = own[0:1, :] * weights[0]
            for i in range(1, CHANS):
                total = total + own[i : i + 1, :] * weights[i]
            mixed[rows, :] = total
    tables[2].wait()
    tables[3].wait()
    from_modes(mixed[...], x_out, t_out, held, back_refs, back_sems)
    keep.wait()


def mix(spreads, weight, after, tables, backward):
    modes = (KX * CHANS, weight.shape[2])
    gx, ta, _, lanes = spreads[0].shape
    outs = tables[2].shape[0]
    back = (gx, ta, tables[2].shape[1] // gx, lanes)
    anywhere = pl.BlockSpec(memory_space=pl.ANY)
    apart = pl.BlockSpec(memory_space=pltpu.HBM)
    return pl.pallas_call(
        functools.partial(mix_kernel, backward, len(after)),
        out_shape=[jax.ShapeDtypeStruct(modes, F32)] + [jax.ShapeDtypeStruct(back, BF16)] * outs,
        in_specs=[apart] + [anywhere] * len(after) + [apart] * 4 + [anywhere] * len(spreads),
        out_specs=[apart] + [anywhere] * outs,
        scratch_shapes=[
            pltpu.VMEM(weight.shape, BF16),
            pltpu.VMEM(modes, F32),
            pltpu.VMEM(modes, F32),
            pltpu.VMEM((outs,) + back, BF16),
            *[pltpu.VMEM(table.shape, BF16) for table in tables],
            *[pltpu.VMEM(spread.shape, BF16) for spread in spreads],
            pltpu.SemaphoreType.DMA((5,)),
            pltpu.SemaphoreType.DMA((8,)),
            pltpu.SemaphoreType.DMA((len(spreads),)),
            pltpu.SemaphoreType.DMA((outs, 4 // outs)),
        ],
        compiler_params=vmem_params(60),
        cost_estimate=pl.CostEstimate(flops=1 << 30, bytes_accessed=9 << 20, transcendentals=0),
        name="mix_back" if backward else "mix",
    )(weight, *after, *tables, *spreads)


def outer_kernel(spectrum_ref, grad_ref, result_ref):
    own = result_ref.shape[4]
    for kx in range(result_ref.shape[0]):
        rows = slice(kx * CHANS, (kx + 1) * CHANS)
        for group in range(KT // 4):
            at = slice(group * LANES, (group + 1) * LANES)
            inputs = spectrum_ref[rows, at]
            grads = grad_ref[rows, at]
            for i in range(CHANS):
                product = inputs[i : i + 1, :] * grads
                for k in range(4):
                    result_ref[kx, 4 * group + k, i] = product[:, k * own : (k + 1) * own]


def outer(spectrum, grad, own):
    per = 4
    width = KT * own
    return pl.pallas_call(
        outer_kernel,
        grid=(KX // per,),
        in_specs=[pl.BlockSpec((per * CHANS, width), lambda n: (n, 0))] * 2,
        out_specs=pl.BlockSpec((per, KT, CHANS, CHANS, own), lambda n: (n, 0, 0, 0, 0)),
        out_shape=jax.ShapeDtypeStruct((KX, KT, CHANS, CHANS, own), F32),
        compiler_params=vmem_params(60),
        cost_estimate=pl.CostEstimate(flops=1 << 20, bytes_accessed=17 << 20, transcendentals=0),
        name="outer",
    )(spectrum, grad)


def normal_parts(values):
    scaled = 1.0 + 0.2316419 * jnp.abs(values)
    guess = pl.reciprocal(scaled, approx=True)
    t = guess * (2.0 - scaled * guess)
    decay = jnp.exp(values * values * -0.5)
    series = (1.330274429 * DENSITY) * t - 1.821255978 * DENSITY
    series = series * t + 1.781477937 * DENSITY
    series = series * t - 0.356563782 * DENSITY
    series = series * t + 0.319381530 * DENSITY
    tail = decay * (series * t)
    return jnp.where(values >= 0.0, 1.0 - tail, tail), decay


def point_field_kernel(mixer_ref, bias_ref, field_ref, mixed_ref):
    rows = mixer_ref.shape[0]
    bias = jnp.concatenate([bias_ref[...]] * (WIDTH // LANES), axis=1)
    for at in range(mixed_ref.shape[0]):
        for first in range(0, field_ref.shape[0], rows):
            part = slice(first, first + rows)
            field = field_ref[part, at * WIDTH : (at + 1) * WIDTH]
            mixed_ref[at, part, :] = (matmul(mixer_ref[...], field) + bias).astype(BF16)


def point_field(field, mixer, bias):
    rows = field.shape[0]
    group = mixer.shape[0]
    per = 2
    return pl.pallas_call(
        point_field_kernel,
        grid=(CELLS // (per * WIDTH),),
        in_specs=[
            pl.BlockSpec((group, group), lambda n: (0, 0)),
            pl.BlockSpec((group, LANES), lambda n: (0, 0)),
            pl.BlockSpec((rows, per * WIDTH), lambda n: (0, n)),
        ],
        out_specs=pl.BlockSpec((per, rows, WIDTH), lambda n: (n, 0, 0)),
        out_shape=jax.ShapeDtypeStruct((CELLS // WIDTH, rows, WIDTH), BF16),
        compiler_params=vmem_params(60),
        cost_estimate=pl.CostEstimate(
            flops=2 * rows * CELLS * group, bytes_accessed=8 << 20, transcendentals=0
        ),
        name="point_field",
    )(mixer, bias, field)


def point_grad_kernel(mixer_ref, grad_ref, mixed_ref):
    rows = mixer_ref.shape[0]
    for at in range(mixed_ref.shape[0]):
        for first in range(0, grad_ref.shape[1], rows):
            part = slice(first, first + rows)
            mixed_ref[at, part, :] = matmul(mixer_ref[...], grad_ref[at, part, :]).astype(BF16)


def point_grad(grad, mixer):
    chunks, rows, _ = grad.shape
    group = mixer.shape[0]
    per = 2
    blocks = pl.BlockSpec((per, rows, WIDTH), lambda n: (n, 0, 0))
    return pl.pallas_call(
        point_grad_kernel,
        grid=(chunks // per,),
        in_specs=[pl.BlockSpec((group, group), lambda n: (0, 0)), blocks],
        out_specs=blocks,
        out_shape=jax.ShapeDtypeStruct(grad.shape, BF16),
        compiler_params=vmem_params(60),
        cost_estimate=pl.CostEstimate(
            flops=2 * rows * CELLS * group, bytes_accessed=8 << 20, transcendentals=0
        ),
        name="point_grad",
    )(mixer, grad)


def sums_kernel(group, field_ref, grad_ref, sums_ref, total):
    step = pl.program_id(0)
    rows, width = field_ref.shape
    blocks = grad_ref.shape[0]
    ones = jnp.ones((16, width), BF16)
    part = 0.0
    for first in range(0, rows, group):
        at = slice(first, first + group)
        passing = jnp.concatenate([field_ref[at, :], ones], axis=0)
        grads = jnp.concatenate([grad_ref[block, at, :] for block in range(blocks)], axis=1)
        part = part + matmul_turned(passing, grads)

    @pl.when(step == 0)
    def _():
        total[...] = part

    @pl.when(step > 0)
    def _():
        total[...] += part

    @pl.when(step == pl.num_programs(0) - 1)
    def _():
        row = lax.broadcasted_iota(jnp.int32, (group, group), 0)
        column = lax.broadcasted_iota(jnp.int32, (group, group), 1)
        gram = total[:group, :].T
        bias = total[group : group + CHANS, :]
        same = jnp.where(row // CHANS == column // CHANS, gram, 0.0)
        folded = jnp.sum(same.reshape(group // CHANS, CHANS, group), axis=0)
        source = lax.broadcasted_iota(jnp.int32, (group, LANES), 0)
        target = lax.broadcasted_iota(jnp.int32, (group, LANES), 1)
        select = jnp.where(source % CHANS == target, 1.0, 0.0)
        chan = lax.broadcasted_iota(jnp.int32, (CHANS, group), 0)
        place = lax.broadcasted_iota(jnp.int32, (CHANS, group), 1)
        own_bias = jnp.sum(
            jnp.where(place % CHANS == chan, bias, 0.0), axis=1, keepdims=True
        )
        point = jnp.dot(
            folded, select, precision=lax.Precision.HIGHEST, preferred_element_type=F32
        )
        lane = lax.broadcasted_iota(jnp.int32, (CHANS, LANES), 1)
        sums_ref[...] = jnp.where(lane == CHANS, own_bias, point)


def own_sums(field, grad, group):
    chunks, rows, _ = grad.shape
    per = 2
    return pl.pallas_call(
        functools.partial(sums_kernel, group),
        grid=(chunks // per,),
        in_specs=[
            pl.BlockSpec((rows, per * WIDTH), lambda n: (0, n)),
            pl.BlockSpec((per, rows, WIDTH), lambda n: (n, 0, 0)),
        ],
        out_specs=pl.BlockSpec((CHANS, LANES), lambda n: (0, 0)),
        out_shape=jax.ShapeDtypeStruct((CHANS, LANES), F32),
        scratch_shapes=[pltpu.VMEM((group + 16, group), F32)],
        compiler_params=vmem_params(60),
        cost_estimate=pl.CostEstimate(
            flops=2 * rows * CELLS * group, bytes_accessed=8 << 20, transcendentals=0
        ),
        name="own_sums",
    )(field, grad)


def middle_kernel(
    xl,
    tl,
    packed_ref,
    cotangent_ref,
    mixed_ref,
    table_ref,
    output_ref,
    grad_ref,
    sent_ref,
    wide,
    modes,
    total,
    held,
    sems,
):
    step = pl.program_id(0)
    rows, width = cotangent_ref.shape
    tile = 256
    chunk = 32

    @pl.when(step == 0)
    def _():
        unpack_modes(packed_ref, wide, xl, tl)
        modes[...] = wide[...].reshape(rows, KQ).astype(BF16)
        total[...] = jnp.zeros_like(total)

    def build(at):
        block, first = divmod(at, WIDTH)
        return matmul(modes[...], table_ref[block, :, first : first + tile])

    def pointwise(pre, at):
        block, first = divmod(at, WIDTH)
        for top in range(0, rows, chunk):
            part = slice(top, top + chunk)
            inner, outer = slice(first, first + tile), slice(at, at + tile)
            values = pre[part, :] + mixed_ref[block, part, inner].astype(F32)
            integral, decay = normal_parts(values)
            output_ref[part, outer] = (values * integral).astype(BF16)
            slope = integral + (values * DENSITY) * decay
            grad = (cotangent_ref[part, outer].astype(F32) * slope).astype(BF16)
            grad_ref[block, part, inner] = grad

    firsts = range(0, width, tile)
    ready = build(0)
    for at in firsts:
        pre = ready
        if at + tile < width:
            ready = build(at + tile)
        pointwise(pre, at)
        block, first = divmod(at + tile, WIDTH)
        if first == 0:
            total[...] += matmul_turned(table_ref[block - 1], grad_ref[block - 1])

    @pl.when(step == pl.num_programs(0) - 1)
    def _():
        pack_modes(total, held, sent_ref, sems, xl, tl)


def middle(packed, cotangent, mixed, table, xl, tl):
    rows = xl * tl * CHANS
    chunks = CELLS // WIDTH
    per = 2
    tile = pl.BlockSpec((rows, per * WIDTH), lambda n: (0, n))
    block = pl.BlockSpec((per, rows, WIDTH), lambda n: (n, 0, 0))
    return pl.pallas_call(
        functools.partial(middle_kernel, xl, tl),
        grid=(chunks // per,),
        in_specs=[
            pl.BlockSpec(packed.shape, lambda n: (0, 0, 0)),
            tile,
            block,
            pl.BlockSpec((per, KQ, WIDTH), lambda n: (n, 0, 0)),
        ],
        out_specs=[tile, block, pl.BlockSpec(memory_space=pl.ANY)],
        out_shape=(
            jax.ShapeDtypeStruct((rows, CELLS), BF16),
            jax.ShapeDtypeStruct((chunks, rows, WIDTH), BF16),
            jax.ShapeDtypeStruct(packed.shape, BF16),
        ),
        scratch_shapes=[
            pltpu.VMEM((xl, tl, CHANS, KQ), F32),
            pltpu.VMEM((rows, KQ), BF16),
            pltpu.VMEM((KQ, rows), F32),
            pltpu.VMEM(packed.shape, BF16),
            pltpu.SemaphoreType.DMA((KQ // LANES,)),
        ],
        compiler_params=vmem_params(50),
        cost_estimate=pl.CostEstimate(
            flops=4 * rows * CELLS * KQ, bytes_accessed=26 << 20, transcendentals=rows * CELLS
        ),
        name="middle",
    )(packed, cotangent, mixed, table)


def last_kernel(xl, tl, packed_ref, table_ref, mixed_ref, field_ref, *scratch):
    wide, modes, table, mixed, field, table_sems, mixed_sems, field_sems = scratch
    chunks = table.shape[0]
    ahead = 4
    fetches, sends = [], []
    for at in range(chunks):
        lanes = slice(at * WIDTH, (at + 1) * WIDTH)
        fetches.append(
            (
                pltpu.make_async_copy(table_ref.at[at], table.at[at], table_sems.at[at]),
                pltpu.make_async_copy(mixed_ref.at[at], mixed.at[at], mixed_sems.at[at]),
            )
        )
        sends.append(
            pltpu.make_async_copy(field.at[at], field_ref.at[:, lanes], field_sems.at[at])
        )

    def start(at):
        for fetch in fetches[at]:
            fetch.start()

    for at in range(ahead):
        start(at)
    unpack_modes(packed_ref, wide, xl, tl)
    modes[...] = wide[...].reshape(modes.shape).astype(BF16)
    for at in range(chunks):
        for fetch in fetches[at]:
            fetch.wait()
        if at + ahead < chunks:
            start(at + ahead)
        field[at] = (matmul(modes[...], table[at]) + mixed[at].astype(F32)).astype(BF16)
        sends[at].start()
    for send in sends:
        send.wait()


def last(packed, mixed, table, xl, tl):
    rows = xl * tl * CHANS
    chunks = CELLS // WIDTH
    apart = pl.BlockSpec(memory_space=pltpu.HBM)
    return pl.pallas_call(
        functools.partial(last_kernel, xl, tl),
        in_specs=[pl.BlockSpec(memory_space=pltpu.VMEM), apart, apart],
        out_specs=apart,
        out_shape=jax.ShapeDtypeStruct((rows, CELLS), BF16),
        scratch_shapes=[
            pltpu.VMEM((xl, tl, CHANS, KQ), F32),
            pltpu.VMEM((rows, KQ), BF16),
            pltpu.VMEM((chunks, KQ, WIDTH), BF16),
            pltpu.VMEM((chunks, rows, WIDTH), BF16),
            pltpu.VMEM((chunks, rows, WIDTH), BF16),
            pltpu.SemaphoreType.DMA((chunks,)),
            pltpu.SemaphoreType.DMA((chunks,)),
            pltpu.SemaphoreType.DMA((chunks,)),
        ],
        compiler_params=vmem_params(50),
        cost_estimate=pl.CostEstimate(
            flops=2 * rows * CELLS * KQ, bytes_accessed=18 << 20, transcendentals=0
        ),
        name="last",
    )(packed, table, mixed)


def swap(blocks):
    return lax.all_to_all(blocks, ("gx", "ta"), split_axis=0, concat_axis=0, tiled=True)


def sum_everywhere(values, devices):
    step = 1
    while step < devices:
        pairs = [(at, at ^ step) for at in range(devices)]
        values = values + lax.ppermute(values, ("gx", "ta"), pairs)
        step *= 2
    return values


def fast_body(gx, ta, features, cotangent, spec_weight, point_weight, bias_vector):
    _, xl, tl, _, cells = features.shape
    own = spec_weight.shape[4]
    devices = gx * ta
    rows = xl * tl * CHANS
    group = rows // PARTS
    yz = np.kron(
        narrow(basis(NY, MY)).astype(np.float32), narrow(basis(NZ, MZ)).astype(np.float32)
    )
    blocks = yz.reshape(KQ, CELLS // WIDTH, WIDTH).transpose(1, 0, 2)
    table = jnp.asarray(narrow(blocks))
    x_wide = np.kron(basis(NX, MX), np.eye(CHANS))[None]
    x_in, x_out = jnp.asarray(narrow(x_wide)), jnp.asarray(narrow(x_wide.transpose(0, 2, 1)))
    t_wide = np.kron(basis(NT, MT), np.eye(own))
    t_in, t_out = jnp.asarray(narrow(t_wide.T)), jnp.asarray(narrow(t_wide))
    norm_scale = float(BATCH * NX * NT * NY * NZ) ** (-0.5)

    field = features.reshape(rows, cells)
    cot = cotangent.reshape(rows, cells)
    pick = np.tile(np.eye(CHANS, dtype=np.float32), (group // CHANS, 1))
    same = np.kron(np.eye(group // CHANS, dtype=np.float32), np.ones((CHANS, CHANS), np.float32))
    picked = jnp.asarray(narrow(pick))
    spread_point = matmul(matmul(picked, point_weight).astype(BF16), picked.T)
    spread_back = matmul(matmul(picked, point_weight.T).astype(BF16), picked.T)
    mixer = (spread_point * jnp.asarray(same)).astype(BF16)
    mixer_back = (spread_back * jnp.asarray(same)).astype(BF16)
    bias = jnp.dot(
        jnp.asarray(pick),
        jnp.broadcast_to(bias_vector[:, None], (CHANS, LANES)),
        precision=lax.Precision.HIGHEST,
    )
    spread_shape = (gx, ta, xl * CHANS, LANES)
    block_shape = (devices, xl * CHANS, LANES)
    packed_weight = pack_weight(spec_weight)
    tables = (x_in, t_in, x_out, t_out)

    spread_in = swap(analyse(field, table, xl, tl, devices)).reshape(spread_shape)
    spectrum, mixed = mix([spread_in], packed_weight, (mixer, mixer_back, bias), tables, False)
    returned = swap(mixed.reshape(block_shape))
    mixed_field = point_field(field, mixer, bias)
    output, grad, sent = middle(returned, cot, mixed_field, table, xl, tl)
    spread_grad = swap(sent).reshape(spread_shape)
    summed = sum_everywhere(own_sums(field, grad, group), devices)
    grad_modes, mixed_back = mix([spread_grad], packed_weight, (summed,), tables, True)
    grad_back = swap(mixed_back.reshape(block_shape))
    grad_spec = outer(spectrum, grad_modes, own)
    grad_field = last(grad_back, point_grad(grad, mixer_back), table, xl, tl)
    summed = summed * norm_scale
    return (
        output.reshape(features.shape),
        grad_field.reshape(features.shape),
        grad_spec,
        summed[:, :CHANS],
        summed[:, CHANS],
    )


def analyse_yz(spatial, yz_table):
    return jnp.einsum(
        "qp,bxtcp->bxtcq", yz_table, spatial.astype(F32), precision=lax.Precision.HIGHEST
    )


def build_yz(modes_in, yz_table):
    return jnp.einsum(
        "qp,bxtcq->bxtcp", yz_table, modes_in.astype(F32), precision=lax.Precision.HIGHEST
    )


def analyse_xt(spread, table):
    sizes = spread.shape
    flattened = spread.reshape(sizes[0], sizes[1] * sizes[2], sizes[3] * sizes[4]).astype(F32)
    spectral = jnp.einsum("mp,bpr->bmr", table, flattened, precision=lax.Precision.HIGHEST)
    return spectral.reshape(sizes[0], KX, KT, sizes[3], sizes[4])


def synthesise_xt(modes_in, table):
    sizes = modes_in.shape
    flattened = modes_in.reshape(sizes[0], sizes[1] * sizes[2], sizes[3] * sizes[4])
    spatial = jnp.einsum("mp,bmr->bpr", table, flattened, precision=lax.Precision.HIGHEST)
    return spatial.reshape(sizes[0], NX, NT, sizes[3], sizes[4])


def to_owners(modes_in):
    first = lax.all_to_all(modes_in, "gx", split_axis=4, concat_axis=1, tiled=True)
    return lax.all_to_all(first, "ta", split_axis=4, concat_axis=2, tiled=True)


def to_cells(spread, shape):
    first = lax.all_to_all(
        spread[:, :, :, :, None, None, :], "gx", split_axis=1, concat_axis=4, tiled=True
    )
    second = lax.all_to_all(first, "ta", split_axis=2, concat_axis=5, tiled=True)
    return second.reshape(shape[:4] + (-1,))


def general_body(features, cotangent, spec_weight, point_weight, bias_vector):
    shape = features.shape
    yz_table = jnp.asarray(
        np.kron(narrow(basis(NY, MY)).astype(np.float32), narrow(basis(NZ, MZ)).astype(np.float32))
    )
    xt_table = jnp.asarray(np.kron(basis(NX, MX), basis(NT, MT)))
    norm_scale = float(BATCH * NX * NT * NY * NZ) ** (-0.5)
    highest = lax.Precision.HIGHEST
    spectrum = analyse_xt(to_owners(analyse_yz(features, yz_table).astype(BF16)), xt_table)
    mixed = jnp.einsum("bklip,kliop->bklop", spectrum, spec_weight, precision=highest)
    returned = to_cells(synthesise_xt(mixed, xt_table).astype(BF16), shape)
    pointwise = jnp.einsum("oi,bxtip->bxtop", point_weight, features, preferred_element_type=F32)
    pre = build_yz(returned, yz_table) + pointwise + bias_vector[:, None]
    integral = 0.5 * (1.0 + jax.scipy.special.erf(pre * 0.7071067811865476))
    output = (pre * integral).astype(BF16)
    slope = integral + pre * jnp.exp(-0.5 * pre * pre) * 0.3989422804014327
    grad_pre = (cotangent.astype(F32) * slope).astype(BF16)
    local_point = jnp.einsum("bxtop,bxtip->oi", grad_pre, features, preferred_element_type=F32)
    local_bias = jnp.sum(grad_pre.astype(F32), axis=(0, 1, 2, 4))
    total_point, total_bias = lax.psum((local_point, local_bias), ("gx", "ta"))
    grad_modes = analyse_xt(to_owners(analyse_yz(grad_pre, yz_table).astype(BF16)), xt_table)
    grad_spec = jnp.einsum("bklip,bklop->kliop", spectrum, grad_modes, precision=highest)
    grad_in = jnp.einsum("kliop,bklop->bklip", spec_weight, grad_modes, precision=highest)
    grad_back = to_cells(synthesise_xt(grad_in, xt_table).astype(BF16), shape)
    point_term = jnp.einsum("oi,bxtop->bxtip", point_weight, grad_pre, preferred_element_type=F32)
    grad_field = (build_yz(grad_back, yz_table) + point_term).astype(BF16)
    return (output, grad_field, grad_spec, total_point * norm_scale, total_bias * norm_scale)


def solution(mesh):
    split_field = P(None, "gx", "ta", None, None)
    split_weight = P(None, None, None, None, ("gx", "ta"))
    in_specs = (split_field, split_field, split_weight, P(), P())
    out_specs = (split_field, split_field, split_weight, P(), P())
    gx, ta = mesh.shape["gx"], mesh.shape["ta"]
    own, xl, tl = KQ // (gx * ta), NX // gx, NT // ta
    if own == 32 and xl * CHANS == LANES and tl == 4:
        body = functools.partial(fast_body, gx, ta)
    else:
        body = general_body
    return jax.shard_map(body, mesh=mesh, in_specs=in_specs, out_specs=out_specs, check_vma=False)
```

```python
import functools
import math

import jax
import jax.numpy as jnp
import ml_dtypes
import numpy as np
from jax import lax
from jax.experimental import pallas as pl
from jax.experimental.pallas import tpu as pltpu
from jax.sharding import PartitionSpec as P

NX = 128
NY = 128
NZ = 32
NT = 16
MX = 16
MY = 16
MZ = 16
MT = 8
BATCH = 1
KX = 32
KT = 16
CHANS = 8
CELLS = NY * NZ
KQ = 1024
LANES = 128
PARTS = 2
WIDTH = 512
DENSITY = 1.0 / math.sqrt(2.0 * math.pi)
F32 = jnp.float32
BF16 = jnp.bfloat16


def basis(length, modes):
    frequency = np.concatenate([np.arange(modes + 1), np.arange(1, modes)])
    samples_at = np.arange(length)
    phases = (2.0 * math.pi / length) * (frequency[:, None] * samples_at[None, :] % length)
    cosine_row = np.arange(2 * modes) <= modes
    waves = np.where(cosine_row[:, None], np.cos(phases), np.sin(phases))
    at_edge = cosine_row & ((frequency == 0) | (2 * frequency == length))
    scales = np.where(at_edge, math.sqrt(1.0 / length), math.sqrt(2.0 / length))
    return (waves * scales[:, None]).astype(np.float32)


def narrow(table):
    return np.asarray(table, np.float32).astype(ml_dtypes.bfloat16)


def vmem_params(mebibytes):
    return pltpu.CompilerParams(vmem_limit_bytes=mebibytes * 1024 * 1024)


def matmul(left, right):
    return jnp.dot(left, right, preferred_element_type=F32)


def matmul_turned(left, right):
    return lax.dot_general(
        left, right, (((1,), (1,)), ((), ())), preferred_element_type=F32
    )


def swap_groups(tiles):
    rows = tiles[0].shape[0]
    lane = lax.broadcasted_iota(jnp.int32, (rows, LANES), 1)
    low_half = lane < 64
    even = (lane // 32) % 2 == 0
    first, second, third, fourth = tiles
    b0 = jnp.where(low_half, first, pltpu.roll(third, 64, 1))
    b2 = jnp.where(low_half, pltpu.roll(first, 64, 1), third)
    b1 = jnp.where(low_half, second, pltpu.roll(fourth, 64, 1))
    b3 = jnp.where(low_half, pltpu.roll(second, 64, 1), fourth)
    return (
        jnp.where(even, b0, pltpu.roll(b1, 32, 1)),
        jnp.where(even, pltpu.roll(b0, 96, 1), b1),
        jnp.where(even, b2, pltpu.roll(b3, 32, 1)),
        jnp.where(even, pltpu.roll(b2, 96, 1), b3),
    )


def pack_modes(modes_ref, held_ref, packed_ref, sems, xl, tl):
    sends = []
    for tile in range(KQ // LANES):
        modes = modes_ref[tile * LANES : (tile + 1) * LANES, :].T
        split = modes.reshape(xl, tl, CHANS, LANES)
        tiles = [split[:, step].reshape(xl * CHANS, LANES) for step in range(tl)]
        owners = slice(tile * tl, (tile + 1) * tl)
        held_ref[owners] = jnp.stack([block.astype(BF16) for block in swap_groups(tiles)])
        send = pltpu.make_async_copy(held_ref.at[owners], packed_ref.at[owners], sems.at[tile])
        send.start()
        sends.append(send)
    for send in sends:
        send.wait()


def unpack_modes(packed_ref, wide_ref, xl, tl):
    for tile in range(KQ // LANES):
        tiles = [packed_ref[tile * tl + owner].astype(F32) for owner in range(tl)]
        for step, block in enumerate(swap_groups(tiles)):
            wide_ref[:, step, :, tile * LANES : (tile + 1) * LANES] = block.reshape(
                xl, CHANS, LANES
            )


def analyse_kernel(
    xl, tl, field_ref, table_ref, packed_ref, field, table, total, held, field_sems, table_sems, sems
):
    chunks = table.shape[0]
    ahead = 4
    fetches = []
    for at in range(chunks):
        lanes = slice(at * WIDTH, (at + 1) * WIDTH)
        fetches.append(
            (
                pltpu.make_async_copy(field_ref.at[:, lanes], field.at[at], field_sems.at[at]),
                pltpu.make_async_copy(table_ref.at[at], table.at[at], table_sems.at[at]),
            )
        )

    def start(at):
        for fetch in fetches[at]:
            fetch.start()

    for at in range(ahead):
        start(at)
    for at in range(0, chunks, 2):
        for now in (at, at + 1):
            for fetch in fetches[now]:
                fetch.wait()
            if now + ahead < chunks:
                start(now + ahead)
        part = matmul_turned(
            jnp.concatenate([table[at], table[at + 1]], axis=1),
            jnp.concatenate([field[at], field[at + 1]], axis=1),
        )
        total[...] = part if at == 0 else total[...] + part
    pack_modes(total, held, packed_ref, sems, xl, tl)


def analyse(field, table, xl, tl, devices):
    rows = xl * tl * CHANS
    chunks = CELLS // WIDTH
    packed = (devices, xl * CHANS, LANES)
    return pl.pallas_call(
        functools.partial(analyse_kernel, xl, tl),
        in_specs=[pl.BlockSpec(memory_space=pltpu.HBM)] * 2,
        out_specs=pl.BlockSpec(memory_space=pl.ANY),
        out_shape=jax.ShapeDtypeStruct(packed, BF16),
        scratch_shapes=[
            pltpu.VMEM((chunks, rows, WIDTH), BF16),
            pltpu.VMEM((chunks, KQ, WIDTH), BF16),
            pltpu.VMEM((KQ, rows), F32),
            pltpu.VMEM(packed, BF16),
            pltpu.SemaphoreType.DMA((chunks,)),
            pltpu.SemaphoreType.DMA((chunks,)),
            pltpu.SemaphoreType.DMA((KQ // LANES,)),
        ],
        compiler_params=vmem_params(60),
        cost_estimate=pl.CostEstimate(
            flops=2 * rows * CELLS * KQ, bytes_accessed=13 << 20, transcendentals=0
        ),
        name="analyse",
    )(field, table)


def weight_kernel(weight_ref, packed_ref):
    for kx in range(weight_ref.shape[0]):
        for group in range(KT // 4):
            parts = [weight_ref[kx, 4 * group + k] for k in range(4)]
            joined = jnp.concatenate(parts, axis=-1).reshape(CHANS * CHANS, LANES)
            packed_ref[kx, :, group * LANES : (group + 1) * LANES] = joined.astype(BF16)


def pack_weight(weight):
    per = 4
    own = weight.shape[4]
    return pl.pallas_call(
        weight_kernel,
        grid=(KX // per,),
        in_specs=[pl.BlockSpec((per, KT, CHANS, CHANS, own), lambda n: (n, 0, 0, 0, 0))],
        out_specs=pl.BlockSpec((per, CHANS * CHANS, KT * own), lambda n: (n, 0, 0)),
        out_shape=jax.ShapeDtypeStruct((KX, CHANS * CHANS, KT * own), BF16),
        compiler_params=vmem_params(60),
        cost_estimate=pl.CostEstimate(flops=1 << 20, bytes_accessed=20 << 20, transcendentals=0),
        name="pack_weight",
    )(weight)


def to_modes(spread_refs, x_table_ref, t_table_ref):
    total = 0.0
    for part, spread_ref in enumerate(spread_refs):
        gx, ta, rows, _ = spread_ref.shape
        beside = jnp.concatenate(
            [spread_ref[:, at].reshape(gx * rows, LANES) for at in range(ta)], axis=1
        )
        total = total + matmul(x_table_ref[part], beside)
    return matmul(total.astype(BF16), t_table_ref[...])


def from_modes(modes, x_table_ref, t_table_ref, held_ref, back_refs, sems):
    parts, gx, ta, rows, _ = held_ref.shape
    half = matmul(modes.astype(BF16), t_table_ref[...]).astype(BF16)
    pieces = sems.shape[1]
    per = gx // pieces
    sends = []
    for part in range(parts):
        for piece in range(pieces):
            table = x_table_ref[part, piece * per * rows : (piece + 1) * per * rows, :]
            full = matmul(table, half).astype(BF16)
            owners = slice(piece * per, (piece + 1) * per)
            for at in range(ta):
                held_ref[part, owners, at] = full[:, at * LANES : (at + 1) * LANES].reshape(
                    per, rows, LANES
                )
            send = pltpu.make_async_copy(
                held_ref.at[part, owners], back_refs[part].at[owners], sems.at[part, piece]
            )
            send.start()
            sends.append(send)
    for send in sends:
        send.wait()


def mix_kernel(
    backward,
    afters,
    weight_ref,
    *refs,
):
    x_in_ref, t_in_ref, x_out_ref, t_out_ref = refs[afters : afters + 4]
    refs = refs[afters + 4 :]
    ins, outs = x_in_ref.shape[0], x_out_ref.shape[0]
    spread_refs, modes_ref, back_refs = refs[:ins], refs[ins], refs[ins + 1 : ins + 1 + outs]
    scratch = refs[ins + 1 + outs :]
    weight, modes, mixed, held, x_in, t_in, x_out, t_out = scratch[:8]
    spreads, (sems, weight_sems, spread_sems, back_sems) = scratch[8:-4], scratch[-4:]
    arrivals = [
        pltpu.make_async_copy(source, target, spread_sems.at[at])
        for at, (source, target) in enumerate(zip(spread_refs, spreads))
    ]
    pieces = weight_sems.shape[0]
    per = KX // pieces
    sources = (x_in_ref, t_in_ref, t_out_ref, x_out_ref)
    tables = [
        pltpu.make_async_copy(source, target, sems.at[at])
        for at, (source, target) in enumerate(zip(sources, (x_in, t_in, t_out, x_out)))
    ]
    fetches = []
    for at in range(pieces):
        part = slice(at * per, (at + 1) * per)
        fetches.append(
            pltpu.make_async_copy(weight_ref.at[part], weight.at[part], weight_sems.at[at])
        )
    for copy in arrivals + tables[:2] + fetches + tables[2:]:
        copy.start()
    for copy in arrivals + tables[:2]:
        copy.wait()
    modes[...] = to_modes(spreads, x_in, t_in)
    keep = pltpu.make_async_copy(modes, modes_ref, sems.at[4])
    keep.start()
    for fetch in fetches:
        fetch.wait()
    for kx in range(KX):
        rows = slice(kx * CHANS, (kx + 1) * CHANS)
        own = modes[rows, :]
        weights = weight[kx].astype(F32).reshape(CHANS, CHANS, own.shape[1])
        if backward:
            sums = [jnp.sum(own * weights[i], axis=0, keepdims=True) for i in range(CHANS)]
            mixed[rows, :] = jnp.concatenate(sums, axis=0)
        else:
            total = own[0:1, :] * weights[0]
            for i in range(1, CHANS):
                total = total + own[i : i + 1, :] * weights[i]
            mixed[rows, :] = total
    tables[2].wait()
    tables[3].wait()
    from_modes(mixed[...], x_out, t_out, held, back_refs, back_sems)
    keep.wait()


def mix(spreads, weight, after, tables, backward):
    modes = (KX * CHANS, weight.shape[2])
    gx, ta, _, lanes = spreads[0].shape
    outs = tables[2].shape[0]
    back = (gx, ta, tables[2].shape[1] // gx, lanes)
    anywhere = pl.BlockSpec(memory_space=pl.ANY)
    apart = pl.BlockSpec(memory_space=pltpu.HBM)
    return pl.pallas_call(
        functools.partial(mix_kernel, backward, len(after)),
        out_shape=[jax.ShapeDtypeStruct(modes, F32)] + [jax.ShapeDtypeStruct(back, BF16)] * outs,
        in_specs=[apart] + [anywhere] * len(after) + [apart] * 4 + [anywhere] * len(spreads),
        out_specs=[apart] + [anywhere] * outs,
        scratch_shapes=[
            pltpu.VMEM(weight.shape, BF16),
            pltpu.VMEM(modes, F32),
            pltpu.VMEM(modes, F32),
            pltpu.VMEM((outs,) + back, BF16),
            *[pltpu.VMEM(table.shape, BF16) for table in tables],
            *[pltpu.VMEM(spread.shape, BF16) for spread in spreads],
            pltpu.SemaphoreType.DMA((5,)),
            pltpu.SemaphoreType.DMA((8,)),
            pltpu.SemaphoreType.DMA((len(spreads),)),
            pltpu.SemaphoreType.DMA((outs, 4 // outs)),
        ],
        compiler_params=vmem_params(50),
        cost_estimate=pl.CostEstimate(flops=1 << 30, bytes_accessed=9 << 20, transcendentals=0),
        name="mix_back" if backward else "mix",
    )(weight, *after, *tables, *spreads)


def outer_kernel(spectrum_ref, grad_ref, result_ref):
    own = result_ref.shape[4]
    for kx in range(result_ref.shape[0]):
        rows = slice(kx * CHANS, (kx + 1) * CHANS)
        for group in range(KT // 4):
            at = slice(group * LANES, (group + 1) * LANES)
            inputs = spectrum_ref[rows, at]
            grads = grad_ref[rows, at]
            for i in range(CHANS):
                product = inputs[i : i + 1, :] * grads
                for k in range(4):
                    result_ref[kx, 4 * group + k, i] = product[:, k * own : (k + 1) * own]


def outer(spectrum, grad, own):
    per = 4
    width = KT * own
    return pl.pallas_call(
        outer_kernel,
        grid=(KX // per,),
        in_specs=[pl.BlockSpec((per * CHANS, width), lambda n: (n, 0))] * 2,
        out_specs=pl.BlockSpec((per, KT, CHANS, CHANS, own), lambda n: (n, 0, 0, 0, 0)),
        out_shape=jax.ShapeDtypeStruct((KX, KT, CHANS, CHANS, own), F32),
        compiler_params=vmem_params(60),
        cost_estimate=pl.CostEstimate(flops=1 << 20, bytes_accessed=17 << 20, transcendentals=0),
        name="outer",
    )(spectrum, grad)


def normal_parts(values):
    scaled = 1.0 + 0.2316419 * jnp.abs(values)
    guess = pl.reciprocal(scaled, approx=True)
    t = guess * (2.0 - scaled * guess)
    decay = jnp.exp(values * values * -0.5)
    series = (1.330274429 * DENSITY) * t - 1.821255978 * DENSITY
    series = series * t + 1.781477937 * DENSITY
    series = series * t - 0.356563782 * DENSITY
    series = series * t + 0.319381530 * DENSITY
    tail = decay * (series * t)
    return jnp.where(values >= 0.0, 1.0 - tail, tail), decay


def point_field_kernel(mixer_ref, bias_ref, field_ref, mixed_ref):
    rows = mixer_ref.shape[0]
    bias = jnp.concatenate([bias_ref[...]] * (WIDTH // LANES), axis=1)
    for at in range(mixed_ref.shape[0]):
        for first in range(0, field_ref.shape[0], rows):
            part = slice(first, first + rows)
            field = field_ref[part, at * WIDTH : (at + 1) * WIDTH]
            mixed_ref[at, part, :] = (matmul(mixer_ref[...], field) + bias).astype(BF16)


def point_field(field, mixer, bias):
    rows = field.shape[0]
    group = mixer.shape[0]
    per = 2
    return pl.pallas_call(
        point_field_kernel,
        grid=(CELLS // (per * WIDTH),),
        in_specs=[
            pl.BlockSpec((group, group), lambda n: (0, 0)),
            pl.BlockSpec((group, LANES), lambda n: (0, 0)),
            pl.BlockSpec((rows, per * WIDTH), lambda n: (0, n)),
        ],
        out_specs=pl.BlockSpec((per, rows, WIDTH), lambda n: (n, 0, 0)),
        out_shape=jax.ShapeDtypeStruct((CELLS // WIDTH, rows, WIDTH), BF16),
        compiler_params=vmem_params(60),
        cost_estimate=pl.CostEstimate(
            flops=2 * rows * CELLS * group, bytes_accessed=8 << 20, transcendentals=0
        ),
        name="point_field",
    )(mixer, bias, field)


def point_grad_kernel(mixer_ref, grad_ref, mixed_ref):
    rows = mixer_ref.shape[0]
    for at in range(mixed_ref.shape[0]):
        for first in range(0, grad_ref.shape[1], rows):
            part = slice(first, first + rows)
            mixed_ref[at, part, :] = matmul(mixer_ref[...], grad_ref[at, part, :]).astype(BF16)


def point_grad(grad, mixer):
    chunks, rows, _ = grad.shape
    group = mixer.shape[0]
    per = 2
    blocks = pl.BlockSpec((per, rows, WIDTH), lambda n: (n, 0, 0))
    return pl.pallas_call(
        point_grad_kernel,
        grid=(chunks // per,),
        in_specs=[pl.BlockSpec((group, group), lambda n: (0, 0)), blocks],
        out_specs=blocks,
        out_shape=jax.ShapeDtypeStruct(grad.shape, BF16),
        compiler_params=vmem_params(60),
        cost_estimate=pl.CostEstimate(
            flops=2 * rows * CELLS * group, bytes_accessed=8 << 20, transcendentals=0
        ),
        name="point_grad",
    )(mixer, grad)


def sums_kernel(group, field_ref, grad_ref, sums_ref, total):
    step = pl.program_id(0)
    rows, width = field_ref.shape
    blocks = grad_ref.shape[0]
    ones = jnp.ones((16, width), BF16)
    part = 0.0
    for first in range(0, rows, group):
        at = slice(first, first + group)
        passing = jnp.concatenate([field_ref[at, :], ones], axis=0)
        grads = jnp.concatenate([grad_ref[block, at, :] for block in range(blocks)], axis=1)
        part = part + matmul_turned(passing, grads)

    @pl.when(step == 0)
    def _():
        total[...] = part

    @pl.when(step > 0)
    def _():
        total[...] += part

    @pl.when(step == pl.num_programs(0) - 1)
    def _():
        row = lax.broadcasted_iota(jnp.int32, (group, group), 0)
        column = lax.broadcasted_iota(jnp.int32, (group, group), 1)
        gram = total[:group, :].T
        bias = total[group : group + CHANS, :]
        same = jnp.where(row // CHANS == column // CHANS, gram, 0.0)
        folded = jnp.sum(same.reshape(group // CHANS, CHANS, group), axis=0)
        source = lax.broadcasted_iota(jnp.int32, (group, LANES), 0)
        target = lax.broadcasted_iota(jnp.int32, (group, LANES), 1)
        select = jnp.where(source % CHANS == target, 1.0, 0.0)
        chan = lax.broadcasted_iota(jnp.int32, (CHANS, group), 0)
        place = lax.broadcasted_iota(jnp.int32, (CHANS, group), 1)
        own_bias = jnp.sum(
            jnp.where(place % CHANS == chan, bias, 0.0), axis=1, keepdims=True
        )
        point = jnp.dot(
            folded, select, precision=lax.Precision.HIGHEST, preferred_element_type=F32
        )
        lane = lax.broadcasted_iota(jnp.int32, (CHANS, LANES), 1)
        sums_ref[...] = jnp.where(lane == CHANS, own_bias, point)


def own_sums(field, grad, group):
    chunks, rows, _ = grad.shape
    per = 2
    return pl.pallas_call(
        functools.partial(sums_kernel, group),
        grid=(chunks // per,),
        in_specs=[
            pl.BlockSpec((rows, per * WIDTH), lambda n: (0, n)),
            pl.BlockSpec((per, rows, WIDTH), lambda n: (n, 0, 0)),
        ],
        out_specs=pl.BlockSpec((CHANS, LANES), lambda n: (0, 0)),
        out_shape=jax.ShapeDtypeStruct((CHANS, LANES), F32),
        scratch_shapes=[pltpu.VMEM((group + 16, group), F32)],
        compiler_params=vmem_params(60),
        cost_estimate=pl.CostEstimate(
            flops=2 * rows * CELLS * group, bytes_accessed=8 << 20, transcendentals=0
        ),
        name="own_sums",
    )(field, grad)


def middle_kernel(
    xl,
    tl,
    packed_ref,
    cotangent_ref,
    mixed_ref,
    table_ref,
    output_ref,
    grad_ref,
    sent_ref,
    wide,
    modes,
    total,
    held,
    sems,
):
    step = pl.program_id(0)
    rows, width = cotangent_ref.shape
    tile = 256
    chunk = 32

    @pl.when(step == 0)
    def _():
        unpack_modes(packed_ref, wide, xl, tl)
        modes[...] = wide[...].reshape(rows, KQ).astype(BF16)
        total[...] = jnp.zeros_like(total)

    def build(at):
        block, first = divmod(at, WIDTH)
        return matmul(modes[...], table_ref[block, :, first : first + tile])

    def pointwise(pre, at):
        block, first = divmod(at, WIDTH)
        for top in range(0, rows, chunk):
            part = slice(top, top + chunk)
            inner, outer = slice(first, first + tile), slice(at, at + tile)
            values = pre[part, :] + mixed_ref[block, part, inner].astype(F32)
            integral, decay = normal_parts(values)
            output_ref[part, outer] = (values * integral).astype(BF16)
            slope = integral + (values * DENSITY) * decay
            grad = (cotangent_ref[part, outer].astype(F32) * slope).astype(BF16)
            grad_ref[block, part, inner] = grad

    firsts = range(0, width, tile)
    ready = build(0)
    for at in firsts:
        pre = ready
        if at + tile < width:
            ready = build(at + tile)
        pointwise(pre, at)
        block, first = divmod(at + tile, WIDTH)
        if first == 0:
            total[...] += matmul_turned(table_ref[block - 1], grad_ref[block - 1])

    @pl.when(step == pl.num_programs(0) - 1)
    def _():
        pack_modes(total, held, sent_ref, sems, xl, tl)


def middle(packed, cotangent, mixed, table, xl, tl):
    rows = xl * tl * CHANS
    chunks = CELLS // WIDTH
    per = 2
    tile = pl.BlockSpec((rows, per * WIDTH), lambda n: (0, n))
    block = pl.BlockSpec((per, rows, WIDTH), lambda n: (n, 0, 0))
    return pl.pallas_call(
        functools.partial(middle_kernel, xl, tl),
        grid=(chunks // per,),
        in_specs=[
            pl.BlockSpec(packed.shape, lambda n: (0, 0, 0)),
            tile,
            block,
            pl.BlockSpec((per, KQ, WIDTH), lambda n: (n, 0, 0)),
        ],
        out_specs=[tile, block, pl.BlockSpec(memory_space=pl.ANY)],
        out_shape=(
            jax.ShapeDtypeStruct((rows, CELLS), BF16),
            jax.ShapeDtypeStruct((chunks, rows, WIDTH), BF16),
            jax.ShapeDtypeStruct(packed.shape, BF16),
        ),
        scratch_shapes=[
            pltpu.VMEM((xl, tl, CHANS, KQ), F32),
            pltpu.VMEM((rows, KQ), BF16),
            pltpu.VMEM((KQ, rows), F32),
            pltpu.VMEM(packed.shape, BF16),
            pltpu.SemaphoreType.DMA((KQ // LANES,)),
        ],
        compiler_params=vmem_params(50),
        cost_estimate=pl.CostEstimate(
            flops=4 * rows * CELLS * KQ, bytes_accessed=26 << 20, transcendentals=rows * CELLS
        ),
        name="middle",
    )(packed, cotangent, mixed, table)


def last_kernel(xl, tl, packed_ref, table_ref, mixed_ref, field_ref, *scratch):
    wide, modes, table, mixed, field, table_sems, mixed_sems, field_sems = scratch
    chunks = table.shape[0]
    ahead = 4
    fetches, sends = [], []
    for at in range(chunks):
        lanes = slice(at * WIDTH, (at + 1) * WIDTH)
        fetches.append(
            (
                pltpu.make_async_copy(table_ref.at[at], table.at[at], table_sems.at[at]),
                pltpu.make_async_copy(mixed_ref.at[at], mixed.at[at], mixed_sems.at[at]),
            )
        )
        sends.append(
            pltpu.make_async_copy(field.at[at], field_ref.at[:, lanes], field_sems.at[at])
        )

    def start(at):
        for fetch in fetches[at]:
            fetch.start()

    for at in range(ahead):
        start(at)
    unpack_modes(packed_ref, wide, xl, tl)
    modes[...] = wide[...].reshape(modes.shape).astype(BF16)
    for at in range(chunks):
        for fetch in fetches[at]:
            fetch.wait()
        if at + ahead < chunks:
            start(at + ahead)
        field[at] = (matmul(modes[...], table[at]) + mixed[at].astype(F32)).astype(BF16)
        sends[at].start()
    for send in sends:
        send.wait()


def last(packed, mixed, table, xl, tl):
    rows = xl * tl * CHANS
    chunks = CELLS // WIDTH
    apart = pl.BlockSpec(memory_space=pltpu.HBM)
    return pl.pallas_call(
        functools.partial(last_kernel, xl, tl),
        in_specs=[pl.BlockSpec(memory_space=pltpu.VMEM), apart, apart],
        out_specs=apart,
        out_shape=jax.ShapeDtypeStruct((rows, CELLS), BF16),
        scratch_shapes=[
            pltpu.VMEM((xl, tl, CHANS, KQ), F32),
            pltpu.VMEM((rows, KQ), BF16),
            pltpu.VMEM((chunks, KQ, WIDTH), BF16),
            pltpu.VMEM((chunks, rows, WIDTH), BF16),
            pltpu.VMEM((chunks, rows, WIDTH), BF16),
            pltpu.SemaphoreType.DMA((chunks,)),
            pltpu.SemaphoreType.DMA((chunks,)),
            pltpu.SemaphoreType.DMA((chunks,)),
        ],
        compiler_params=vmem_params(50),
        cost_estimate=pl.CostEstimate(
            flops=2 * rows * CELLS * KQ, bytes_accessed=18 << 20, transcendentals=0
        ),
        name="last",
    )(packed, table, mixed)


def swap(blocks):
    return lax.all_to_all(blocks, ("gx", "ta"), split_axis=0, concat_axis=0, tiled=True)


def sum_everywhere(values, devices):
    step = 1
    while step < devices:
        pairs = [(at, at ^ step) for at in range(devices)]
        values = values + lax.ppermute(values, ("gx", "ta"), pairs)
        step *= 2
    return values


def fast_body(gx, ta, features, cotangent, spec_weight, point_weight, bias_vector):
    _, xl, tl, _, cells = features.shape
    own = spec_weight.shape[4]
    devices = gx * ta
    rows = xl * tl * CHANS
    group = rows // PARTS
    yz = np.kron(
        narrow(basis(NY, MY)).astype(np.float32), narrow(basis(NZ, MZ)).astype(np.float32)
    )
    blocks = yz.reshape(KQ, CELLS // WIDTH, WIDTH).transpose(1, 0, 2)
    table = jnp.asarray(narrow(blocks))
    x_wide = np.kron(basis(NX, MX), np.eye(CHANS))[None]
    x_in, x_out = jnp.asarray(narrow(x_wide)), jnp.asarray(narrow(x_wide.transpose(0, 2, 1)))
    t_wide = np.kron(basis(NT, MT), np.eye(own))
    t_in, t_out = jnp.asarray(narrow(t_wide.T)), jnp.asarray(narrow(t_wide))
    norm_scale = float(BATCH * NX * NT * NY * NZ) ** (-0.5)

    field = features.reshape(rows, cells)
    cot = cotangent.reshape(rows, cells)
    pick = np.tile(np.eye(CHANS, dtype=np.float32), (group // CHANS, 1))
    same = np.kron(np.eye(group // CHANS, dtype=np.float32), np.ones((CHANS, CHANS), np.float32))
    picked = jnp.asarray(narrow(pick))
    spread_point = matmul(matmul(picked, point_weight).astype(BF16), picked.T)
    spread_back = matmul(matmul(picked, point_weight.T).astype(BF16), picked.T)
    mixer = (spread_point * jnp.asarray(same)).astype(BF16)
    mixer_back = (spread_back * jnp.asarray(same)).astype(BF16)
    bias = jnp.dot(
        jnp.asarray(pick),
        jnp.broadcast_to(bias_vector[:, None], (CHANS, LANES)),
        precision=lax.Precision.HIGHEST,
    )
    spread_shape = (gx, ta, xl * CHANS, LANES)
    block_shape = (devices, xl * CHANS, LANES)
    packed_weight = pack_weight(spec_weight)
    tables = (x_in, t_in, x_out, t_out)

    spread_in = swap(analyse(field, table, xl, tl, devices)).reshape(spread_shape)
    spectrum, mixed = mix([spread_in], packed_weight, (mixer, mixer_back, bias), tables, False)
    returned = swap(mixed.reshape(block_shape))
    mixed_field = point_field(field, mixer, bias)
    output, grad, sent = middle(returned, cot, mixed_field, table, xl, tl)
    spread_grad = swap(sent).reshape(spread_shape)
    summed = sum_everywhere(own_sums(field, grad, group), devices)
    grad_modes, mixed_back = mix([spread_grad], packed_weight, (summed,), tables, True)
    grad_back = swap(mixed_back.reshape(block_shape))
    grad_spec = outer(spectrum, grad_modes, own)
    grad_field = last(grad_back, point_grad(grad, mixer_back), table, xl, tl)
    summed = summed * norm_scale
    return (
        output.reshape(features.shape),
        grad_field.reshape(features.shape),
        grad_spec,
        summed[:, :CHANS],
        summed[:, CHANS],
    )


def analyse_yz(spatial, yz_table):
    return jnp.einsum(
        "qp,bxtcp->bxtcq", yz_table, spatial.astype(F32), precision=lax.Precision.HIGHEST
    )


def build_yz(modes_in, yz_table):
    return jnp.einsum(
        "qp,bxtcq->bxtcp", yz_table, modes_in.astype(F32), precision=lax.Precision.HIGHEST
    )


def analyse_xt(spread, table):
    sizes = spread.shape
    flattened = spread.reshape(sizes[0], sizes[1] * sizes[2], sizes[3] * sizes[4]).astype(F32)
    spectral = jnp.einsum("mp,bpr->bmr", table, flattened, precision=lax.Precision.HIGHEST)
    return spectral.reshape(sizes[0], KX, KT, sizes[3], sizes[4])


def synthesise_xt(modes_in, table):
    sizes = modes_in.shape
    flattened = modes_in.reshape(sizes[0], sizes[1] * sizes[2], sizes[3] * sizes[4])
    spatial = jnp.einsum("mp,bmr->bpr", table, flattened, precision=lax.Precision.HIGHEST)
    return spatial.reshape(sizes[0], NX, NT, sizes[3], sizes[4])


def to_owners(modes_in):
    first = lax.all_to_all(modes_in, "gx", split_axis=4, concat_axis=1, tiled=True)
    return lax.all_to_all(first, "ta", split_axis=4, concat_axis=2, tiled=True)


def to_cells(spread, shape):
    first = lax.all_to_all(
        spread[:, :, :, :, None, None, :], "gx", split_axis=1, concat_axis=4, tiled=True
    )
    second = lax.all_to_all(first, "ta", split_axis=2, concat_axis=5, tiled=True)
    return second.reshape(shape[:4] + (-1,))


def general_body(features, cotangent, spec_weight, point_weight, bias_vector):
    shape = features.shape
    yz_table = jnp.asarray(
        np.kron(narrow(basis(NY, MY)).astype(np.float32), narrow(basis(NZ, MZ)).astype(np.float32))
    )
    xt_table = jnp.asarray(np.kron(basis(NX, MX), basis(NT, MT)))
    norm_scale = float(BATCH * NX * NT * NY * NZ) ** (-0.5)
    highest = lax.Precision.HIGHEST
    spectrum = analyse_xt(to_owners(analyse_yz(features, yz_table).astype(BF16)), xt_table)
    mixed = jnp.einsum("bklip,kliop->bklop", spectrum, spec_weight, precision=highest)
    returned = to_cells(synthesise_xt(mixed, xt_table).astype(BF16), shape)
    pointwise = jnp.einsum("oi,bxtip->bxtop", point_weight, features, preferred_element_type=F32)
    pre = build_yz(returned, yz_table) + pointwise + bias_vector[:, None]
    integral = 0.5 * (1.0 + jax.scipy.special.erf(pre * 0.7071067811865476))
    output = (pre * integral).astype(BF16)
    slope = integral + pre * jnp.exp(-0.5 * pre * pre) * 0.3989422804014327
    grad_pre = (cotangent.astype(F32) * slope).astype(BF16)
    local_point = jnp.einsum("bxtop,bxtip->oi", grad_pre, features, preferred_element_type=F32)
    local_bias = jnp.sum(grad_pre.astype(F32), axis=(0, 1, 2, 4))
    total_point, total_bias = lax.psum((local_point, local_bias), ("gx", "ta"))
    grad_modes = analyse_xt(to_owners(analyse_yz(grad_pre, yz_table).astype(BF16)), xt_table)
    grad_spec = jnp.einsum("bklip,bklop->kliop", spectrum, grad_modes, precision=highest)
    grad_in = jnp.einsum("kliop,bklop->bklip", spec_weight, grad_modes, precision=highest)
    grad_back = to_cells(synthesise_xt(grad_in, xt_table).astype(BF16), shape)
    point_term = jnp.einsum("oi,bxtop->bxtip", point_weight, grad_pre, preferred_element_type=F32)
    grad_field = (build_yz(grad_back, yz_table) + point_term).astype(BF16)
    return (output, grad_field, grad_spec, total_point * norm_scale, total_bias * norm_scale)


def solution(mesh):
    split_field = P(None, "gx", "ta", None, None)
    split_weight = P(None, None, None, None, ("gx", "ta"))
    in_specs = (split_field, split_field, split_weight, P(), P())
    out_specs = (split_field, split_field, split_weight, P(), P())
    gx, ta = mesh.shape["gx"], mesh.shape["ta"]
    own, xl, tl = KQ // (gx * ta), NX // gx, NT // ta
    if own == 32 and xl * CHANS == LANES and tl == 4:
        body = functools.partial(fast_body, gx, ta)
    else:
        body = general_body
    return jax.shard_map(body, mesh=mesh, in_specs=in_specs, out_specs=out_specs, check_vma=False)
```

```python
import functools
import math

import jax
import jax.numpy as jnp
import ml_dtypes
import numpy as np
from jax import lax
from jax.experimental import pallas as pl
from jax.experimental.pallas import tpu as pltpu
from jax.sharding import PartitionSpec as P

NX = 128
NY = 128
NZ = 32
NT = 16
MX = 16
MY = 16
MZ = 16
MT = 8
BATCH = 1
KX = 32
KT = 16
CHANS = 8
CELLS = NY * NZ
KQ = 1024
LANES = 128
PARTS = 2
WIDTH = 512
DENSITY = 1.0 / math.sqrt(2.0 * math.pi)
F32 = jnp.float32
BF16 = jnp.bfloat16


def basis(length, modes):
    frequency = np.concatenate([np.arange(modes + 1), np.arange(1, modes)])
    samples_at = np.arange(length)
    phases = (2.0 * math.pi / length) * (frequency[:, None] * samples_at[None, :] % length)
    cosine_row = np.arange(2 * modes) <= modes
    waves = np.where(cosine_row[:, None], np.cos(phases), np.sin(phases))
    at_edge = cosine_row & ((frequency == 0) | (2 * frequency == length))
    scales = np.where(at_edge, math.sqrt(1.0 / length), math.sqrt(2.0 / length))
    return (waves * scales[:, None]).astype(np.float32)


def narrow(table):
    return np.asarray(table, np.float32).astype(ml_dtypes.bfloat16)


def vmem_params(mebibytes):
    return pltpu.CompilerParams(vmem_limit_bytes=mebibytes * 1024 * 1024)


def matmul(left, right):
    return jnp.dot(left, right, preferred_element_type=F32)


def matmul_turned(left, right):
    return lax.dot_general(
        left, right, (((1,), (1,)), ((), ())), preferred_element_type=F32
    )


def swap_groups(tiles):
    rows = tiles[0].shape[0]
    lane = lax.broadcasted_iota(jnp.int32, (rows, LANES), 1)
    low_half = lane < 64
    even = (lane // 32) % 2 == 0
    first, second, third, fourth = tiles
    b0 = jnp.where(low_half, first, pltpu.roll(third, 64, 1))
    b2 = jnp.where(low_half, pltpu.roll(first, 64, 1), third)
    b1 = jnp.where(low_half, second, pltpu.roll(fourth, 64, 1))
    b3 = jnp.where(low_half, pltpu.roll(second, 64, 1), fourth)
    return (
        jnp.where(even, b0, pltpu.roll(b1, 32, 1)),
        jnp.where(even, pltpu.roll(b0, 96, 1), b1),
        jnp.where(even, b2, pltpu.roll(b3, 32, 1)),
        jnp.where(even, pltpu.roll(b2, 96, 1), b3),
    )


def pack_modes(modes_ref, held_ref, packed_ref, sems, xl, tl):
    sends = []
    for tile in range(KQ // LANES):
        modes = modes_ref[tile * LANES : (tile + 1) * LANES, :].T
        split = modes.reshape(xl, tl, CHANS, LANES)
        tiles = [split[:, step].reshape(xl * CHANS, LANES) for step in range(tl)]
        owners = slice(tile * tl, (tile + 1) * tl)
        held_ref[owners] = jnp.stack([block.astype(BF16) for block in swap_groups(tiles)])
        send = pltpu.make_async_copy(held_ref.at[owners], packed_ref.at[owners], sems.at[tile])
        send.start()
        sends.append(send)
    for send in sends:
        send.wait()


def unpack_modes(packed_ref, wide_ref, xl, tl):
    for tile in range(KQ // LANES):
        tiles = [packed_ref[tile * tl + owner].astype(F32) for owner in range(tl)]
        for step, block in enumerate(swap_groups(tiles)):
            wide_ref[:, step, :, tile * LANES : (tile + 1) * LANES] = block.reshape(
                xl, CHANS, LANES
            )


def analyse_kernel(
    xl, tl, field_ref, table_ref, packed_ref, field, table, total, held, field_sems, table_sems, sems
):
    chunks = table.shape[0]
    ahead = 8
    fetches = []
    for at in range(chunks):
        lanes = slice(at * WIDTH, (at + 1) * WIDTH)
        fetches.append(
            (
                pltpu.make_async_copy(field_ref.at[:, lanes], field.at[at], field_sems.at[at]),
                pltpu.make_async_copy(table_ref.at[at], table.at[at], table_sems.at[at]),
            )
        )

    def start(at):
        for fetch in fetches[at]:
            fetch.start()

    for at in range(ahead):
        start(at)
    for at in range(0, chunks, 2):
        for now in (at, at + 1):
            for fetch in fetches[now]:
                fetch.wait()
            if now + ahead < chunks:
                start(now + ahead)
        part = matmul_turned(
            jnp.concatenate([table[at], table[at + 1]], axis=1),
            jnp.concatenate([field[at], field[at + 1]], axis=1),
        )
        total[...] = part if at == 0 else total[...] + part
    pack_modes(total, held, packed_ref, sems, xl, tl)


def analyse(field, table, xl, tl, devices):
    rows = xl * tl * CHANS
    chunks = CELLS // WIDTH
    packed = (devices, xl * CHANS, LANES)
    return pl.pallas_call(
        functools.partial(analyse_kernel, xl, tl),
        in_specs=[pl.BlockSpec(memory_space=pltpu.HBM)] * 2,
        out_specs=pl.BlockSpec(memory_space=pl.ANY),
        out_shape=jax.ShapeDtypeStruct(packed, BF16),
        scratch_shapes=[
            pltpu.VMEM((chunks, rows, WIDTH), BF16),
            pltpu.VMEM((chunks, KQ, WIDTH), BF16),
            pltpu.VMEM((KQ, rows), F32),
            pltpu.VMEM(packed, BF16),
            pltpu.SemaphoreType.DMA((chunks,)),
            pltpu.SemaphoreType.DMA((chunks,)),
            pltpu.SemaphoreType.DMA((KQ // LANES,)),
        ],
        compiler_params=vmem_params(60),
        cost_estimate=pl.CostEstimate(
            flops=2 * rows * CELLS * KQ, bytes_accessed=13 << 20, transcendentals=0
        ),
        name="analyse",
    )(field, table)


def weight_kernel(weight_ref, packed_ref):
    for kx in range(weight_ref.shape[0]):
        for group in range(KT // 4):
            parts = [weight_ref[kx, 4 * group + k] for k in range(4)]
            joined = jnp.concatenate(parts, axis=-1).reshape(CHANS * CHANS, LANES)
            packed_ref[kx, :, group * LANES : (group + 1) * LANES] = joined.astype(BF16)


def pack_weight(weight):
    per = 4
    own = weight.shape[4]
    return pl.pallas_call(
        weight_kernel,
        grid=(KX // per,),
        in_specs=[pl.BlockSpec((per, KT, CHANS, CHANS, own), lambda n: (n, 0, 0, 0, 0))],
        out_specs=pl.BlockSpec((per, CHANS * CHANS, KT * own), lambda n: (n, 0, 0)),
        out_shape=jax.ShapeDtypeStruct((KX, CHANS * CHANS, KT * own), BF16),
        compiler_params=vmem_params(60),
        cost_estimate=pl.CostEstimate(flops=1 << 20, bytes_accessed=20 << 20, transcendentals=0),
        name="pack_weight",
    )(weight)


def to_modes(spread_refs, x_table_ref, t_table_ref):
    total = 0.0
    for part, spread_ref in enumerate(spread_refs):
        gx, ta, rows, _ = spread_ref.shape
        beside = jnp.concatenate(
            [spread_ref[:, at].reshape(gx * rows, LANES) for at in range(ta)], axis=1
        )
        total = total + matmul(x_table_ref[part], beside)
    return matmul(total.astype(BF16), t_table_ref[...])


def from_modes(modes, x_table_ref, t_table_ref, held_ref, back_refs, sems):
    parts, gx, ta, rows, _ = held_ref.shape
    half = matmul(modes.astype(BF16), t_table_ref[...]).astype(BF16)
    pieces = sems.shape[1]
    per = gx // pieces
    sends = []
    for part in range(parts):
        for piece in range(pieces):
            table = x_table_ref[part, piece * per * rows : (piece + 1) * per * rows, :]
            full = matmul(table, half).astype(BF16)
            owners = slice(piece * per, (piece + 1) * per)
            for at in range(ta):
                held_ref[part, owners, at] = full[:, at * LANES : (at + 1) * LANES].reshape(
                    per, rows, LANES
                )
            send = pltpu.make_async_copy(
                held_ref.at[part, owners], back_refs[part].at[owners], sems.at[part, piece]
            )
            send.start()
            sends.append(send)
    for send in sends:
        send.wait()


def mix_kernel(
    backward,
    afters,
    weight_ref,
    *refs,
):
    x_in_ref, t_in_ref, x_out_ref, t_out_ref = refs[afters : afters + 4]
    refs = refs[afters + 4 :]
    ins, outs = x_in_ref.shape[0], x_out_ref.shape[0]
    spread_refs, modes_ref, back_refs = refs[:ins], refs[ins], refs[ins + 1 : ins + 1 + outs]
    scratch = refs[ins + 1 + outs :]
    weight, modes, mixed, held, x_in, t_in, x_out, t_out = scratch[:8]
    spreads, (sems, weight_sems, spread_sems, back_sems) = scratch[8:-4], scratch[-4:]
    arrivals = [
        pltpu.make_async_copy(source, target, spread_sems.at[at])
        for at, (source, target) in enumerate(zip(spread_refs, spreads))
    ]
    pieces = weight_sems.shape[0]
    per = KX // pieces
    sources = (x_in_ref, t_in_ref, t_out_ref, x_out_ref)
    tables = [
        pltpu.make_async_copy(source, target, sems.at[at])
        for at, (source, target) in enumerate(zip(sources, (x_in, t_in, t_out, x_out)))
    ]
    fetches = []
    for at in range(pieces):
        part = slice(at * per, (at + 1) * per)
        fetches.append(
            pltpu.make_async_copy(weight_ref.at[part], weight.at[part], weight_sems.at[at])
        )
    for copy in arrivals + tables[:2] + fetches + tables[2:]:
        copy.start()
    for copy in arrivals + tables[:2]:
        copy.wait()
    modes[...] = to_modes(spreads, x_in, t_in)
    keep = pltpu.make_async_copy(modes, modes_ref, sems.at[4])
    keep.start()
    for fetch in fetches:
        fetch.wait()
    for kx in range(KX):
        rows = slice(kx * CHANS, (kx + 1) * CHANS)
        own = modes[rows, :]
        weights = weight[kx].astype(F32).reshape(CHANS, CHANS, own.shape[1])
        if backward:
            sums = [jnp.sum(own * weights[i], axis=0, keepdims=True) for i in range(CHANS)]
            mixed[rows, :] = jnp.concatenate(sums, axis=0)
        else:
            total = own[0:1, :] * weights[0]
            for i in range(1, CHANS):
                total = total + own[i : i + 1, :] * weights[i]
            mixed[rows, :] = total
    tables[2].wait()
    tables[3].wait()
    from_modes(mixed[...], x_out, t_out, held, back_refs, back_sems)
    keep.wait()


def mix(spreads, weight, after, tables, backward):
    modes = (KX * CHANS, weight.shape[2])
    gx, ta, _, lanes = spreads[0].shape
    outs = tables[2].shape[0]
    back = (gx, ta, tables[2].shape[1] // gx, lanes)
    anywhere = pl.BlockSpec(memory_space=pl.ANY)
    apart = pl.BlockSpec(memory_space=pltpu.HBM)
    return pl.pallas_call(
        functools.partial(mix_kernel, backward, len(after)),
        out_shape=[jax.ShapeDtypeStruct(modes, F32)] + [jax.ShapeDtypeStruct(back, BF16)] * outs,
        in_specs=[apart] + [anywhere] * len(after) + [apart] * 4 + [anywhere] * len(spreads),
        out_specs=[apart] + [anywhere] * outs,
        scratch_shapes=[
            pltpu.VMEM(weight.shape, BF16),
            pltpu.VMEM(modes, F32),
            pltpu.VMEM(modes, F32),
            pltpu.VMEM((outs,) + back, BF16),
            *[pltpu.VMEM(table.shape, BF16) for table in tables],
            *[pltpu.VMEM(spread.shape, BF16) for spread in spreads],
            pltpu.SemaphoreType.DMA((5,)),
            pltpu.SemaphoreType.DMA((8,)),
            pltpu.SemaphoreType.DMA((len(spreads),)),
            pltpu.SemaphoreType.DMA((outs, 4 // outs)),
        ],
        compiler_params=vmem_params(60),
        cost_estimate=pl.CostEstimate(flops=1 << 30, bytes_accessed=9 << 20, transcendentals=0),
        name="mix_back" if backward else "mix",
    )(weight, *after, *tables, *spreads)


def outer_kernel(spectrum_ref, grad_ref, result_ref):
    own = result_ref.shape[4]
    for kx in range(result_ref.shape[0]):
        rows = slice(kx * CHANS, (kx + 1) * CHANS)
        for group in range(KT // 4):
            at = slice(group * LANES, (group + 1) * LANES)
            inputs = spectrum_ref[rows, at]
            grads = grad_ref[rows, at]
            for i in range(CHANS):
                product = inputs[i : i + 1, :] * grads
                for k in range(4):
                    result_ref[kx, 4 * group + k, i] = product[:, k * own : (k + 1) * own]


def outer(spectrum, grad, own):
    per = 4
    width = KT * own
    return pl.pallas_call(
        outer_kernel,
        grid=(KX // per,),
        in_specs=[pl.BlockSpec((per * CHANS, width), lambda n: (n, 0))] * 2,
        out_specs=pl.BlockSpec((per, KT, CHANS, CHANS, own), lambda n: (n, 0, 0, 0, 0)),
        out_shape=jax.ShapeDtypeStruct((KX, KT, CHANS, CHANS, own), F32),
        compiler_params=vmem_params(60),
        cost_estimate=pl.CostEstimate(flops=1 << 20, bytes_accessed=17 << 20, transcendentals=0),
        name="outer",
    )(spectrum, grad)


def normal_parts(values):
    scaled = 1.0 + 0.2316419 * jnp.abs(values)
    guess = pl.reciprocal(scaled, approx=True)
    t = guess * (2.0 - scaled * guess)
    decay = jnp.exp(values * values * -0.5)
    series = (1.330274429 * DENSITY) * t - 1.821255978 * DENSITY
    series = series * t + 1.781477937 * DENSITY
    series = series * t - 0.356563782 * DENSITY
    series = series * t + 0.319381530 * DENSITY
    tail = decay * (series * t)
    return jnp.where(values >= 0.0, 1.0 - tail, tail), decay


def point_field_kernel(mixer_ref, bias_ref, field_ref, mixed_ref):
    rows = mixer_ref.shape[0]
    bias = jnp.concatenate([bias_ref[...]] * (WIDTH // LANES), axis=1)
    for at in range(mixed_ref.shape[0]):
        for first in range(0, field_ref.shape[0], rows):
            part = slice(first, first + rows)
            field = field_ref[part, at * WIDTH : (at + 1) * WIDTH]
            mixed_ref[at, part, :] = (matmul(mixer_ref[...], field) + bias).astype(BF16)


def point_field(field, mixer, bias):
    rows = field.shape[0]
    group = mixer.shape[0]
    per = 2
    return pl.pallas_call(
        point_field_kernel,
        grid=(CELLS // (per * WIDTH),),
        in_specs=[
            pl.BlockSpec((group, group), lambda n: (0, 0)),
            pl.BlockSpec((group, LANES), lambda n: (0, 0)),
            pl.BlockSpec((rows, per * WIDTH), lambda n: (0, n)),
        ],
        out_specs=pl.BlockSpec((per, rows, WIDTH), lambda n: (n, 0, 0)),
        out_shape=jax.ShapeDtypeStruct((CELLS // WIDTH, rows, WIDTH), BF16),
        compiler_params=vmem_params(60),
        cost_estimate=pl.CostEstimate(
            flops=2 * rows * CELLS * group, bytes_accessed=8 << 20, transcendentals=0
        ),
        name="point_field",
    )(mixer, bias, field)


def point_grad_kernel(mixer_ref, grad_ref, mixed_ref):
    rows = mixer_ref.shape[0]
    for at in range(mixed_ref.shape[0]):
        for first in range(0, grad_ref.shape[1], rows):
            part = slice(first, first + rows)
            mixed_ref[at, part, :] = matmul(mixer_ref[...], grad_ref[at, part, :]).astype(BF16)


def point_grad(grad, mixer):
    chunks, rows, _ = grad.shape
    group = mixer.shape[0]
    per = 2
    blocks = pl.BlockSpec((per, rows, WIDTH), lambda n: (n, 0, 0))
    return pl.pallas_call(
        point_grad_kernel,
        grid=(chunks // per,),
        in_specs=[pl.BlockSpec((group, group), lambda n: (0, 0)), blocks],
        out_specs=blocks,
        out_shape=jax.ShapeDtypeStruct(grad.shape, BF16),
        compiler_params=vmem_params(60),
        cost_estimate=pl.CostEstimate(
            flops=2 * rows * CELLS * group, bytes_accessed=8 << 20, transcendentals=0
        ),
        name="point_grad",
    )(mixer, grad)


def sums_kernel(group, field_ref, grad_ref, sums_ref, total):
    step = pl.program_id(0)
    rows, width = field_ref.shape
    blocks = grad_ref.shape[0]
    ones = jnp.ones((16, width), BF16)
    part = 0.0
    for first in range(0, rows, group):
        at = slice(first, first + group)
        passing = jnp.concatenate([field_ref[at, :], ones], axis=0)
        grads = jnp.concatenate([grad_ref[block, at, :] for block in range(blocks)], axis=1)
        part = part + matmul_turned(passing, grads)

    @pl.when(step == 0)
    def _():
        total[...] = part

    @pl.when(step > 0)
    def _():
        total[...] += part

    @pl.when(step == pl.num_programs(0) - 1)
    def _():
        row = lax.broadcasted_iota(jnp.int32, (group, group), 0)
        column = lax.broadcasted_iota(jnp.int32, (group, group), 1)
        gram = total[:group, :].T
        bias = total[group : group + CHANS, :]
        same = jnp.where(row // CHANS == column // CHANS, gram, 0.0)
        folded = jnp.sum(same.reshape(group // CHANS, CHANS, group), axis=0)
        source = lax.broadcasted_iota(jnp.int32, (group, LANES), 0)
        target = lax.broadcasted_iota(jnp.int32, (group, LANES), 1)
        select = jnp.where(source % CHANS == target, 1.0, 0.0)
        chan = lax.broadcasted_iota(jnp.int32, (CHANS, group), 0)
        place = lax.broadcasted_iota(jnp.int32, (CHANS, group), 1)
        own_bias = jnp.sum(
            jnp.where(place % CHANS == chan, bias, 0.0), axis=1, keepdims=True
        )
        point = jnp.dot(
            folded, select, precision=lax.Precision.HIGHEST, preferred_element_type=F32
        )
        lane = lax.broadcasted_iota(jnp.int32, (CHANS, LANES), 1)
        sums_ref[...] = jnp.where(lane == CHANS, own_bias, point)


def own_sums(field, grad, group):
    chunks, rows, _ = grad.shape
    per = 2
    return pl.pallas_call(
        functools.partial(sums_kernel, group),
        grid=(chunks // per,),
        in_specs=[
            pl.BlockSpec((rows, per * WIDTH), lambda n: (0, n)),
            pl.BlockSpec((per, rows, WIDTH), lambda n: (n, 0, 0)),
        ],
        out_specs=pl.BlockSpec((CHANS, LANES), lambda n: (0, 0)),
        out_shape=jax.ShapeDtypeStruct((CHANS, LANES), F32),
        scratch_shapes=[pltpu.VMEM((group + 16, group), F32)],
        compiler_params=vmem_params(60),
        cost_estimate=pl.CostEstimate(
            flops=2 * rows * CELLS * group, bytes_accessed=8 << 20, transcendentals=0
        ),
        name="own_sums",
    )(field, grad)


def middle_kernel(
    xl,
    tl,
    packed_ref,
    cotangent_ref,
    mixed_ref,
    table_ref,
    output_ref,
    grad_ref,
    sent_ref,
    wide,
    modes,
    total,
    held,
    sems,
):
    step = pl.program_id(0)
    rows, width = cotangent_ref.shape
    tile = 256
    chunk = 32

    @pl.when(step == 0)
    def _():
        unpack_modes(packed_ref, wide, xl, tl)
        modes[...] = wide[...].reshape(rows, KQ).astype(BF16)
        total[...] = jnp.zeros_like(total)

    def build(at):
        block, first = divmod(at, WIDTH)
        return matmul(modes[...], table_ref[block, :, first : first + tile])

    def pointwise(pre, at):
        block, first = divmod(at, WIDTH)
        for top in range(0, rows, chunk):
            part = slice(top, top + chunk)
            inner, outer = slice(first, first + tile), slice(at, at + tile)
            values = pre[part, :] + mixed_ref[block, part, inner].astype(F32)
            integral, decay = normal_parts(values)
            output_ref[part, outer] = (values * integral).astype(BF16)
            slope = integral + (values * DENSITY) * decay
            grad = (cotangent_ref[part, outer].astype(F32) * slope).astype(BF16)
            grad_ref[block, part, inner] = grad

    firsts = range(0, width, tile)
    ready = build(0)
    for at in firsts:
        pre = ready
        if at + tile < width:
            ready = build(at + tile)
        pointwise(pre, at)
        block, first = divmod(at + tile, WIDTH)
        if first == 0:
            total[...] += matmul_turned(table_ref[block - 1], grad_ref[block - 1])

    @pl.when(step == pl.num_programs(0) - 1)
    def _():
        pack_modes(total, held, sent_ref, sems, xl, tl)


def middle(packed, cotangent, mixed, table, xl, tl):
    rows = xl * tl * CHANS
    chunks = CELLS // WIDTH
    per = 2
    tile = pl.BlockSpec((rows, per * WIDTH), lambda n: (0, n))
    block = pl.BlockSpec((per, rows, WIDTH), lambda n: (n, 0, 0))
    return pl.pallas_call(
        functools.partial(middle_kernel, xl, tl),
        grid=(chunks // per,),
        in_specs=[
            pl.BlockSpec(packed.shape, lambda n: (0, 0, 0)),
            tile,
            block,
            pl.BlockSpec((per, KQ, WIDTH), lambda n: (n, 0, 0)),
        ],
        out_specs=[tile, block, pl.BlockSpec(memory_space=pl.ANY)],
        out_shape=(
            jax.ShapeDtypeStruct((rows, CELLS), BF16),
            jax.ShapeDtypeStruct((chunks, rows, WIDTH), BF16),
            jax.ShapeDtypeStruct(packed.shape, BF16),
        ),
        scratch_shapes=[
            pltpu.VMEM((xl, tl, CHANS, KQ), F32),
            pltpu.VMEM((rows, KQ), BF16),
            pltpu.VMEM((KQ, rows), F32),
            pltpu.VMEM(packed.shape, BF16),
            pltpu.SemaphoreType.DMA((KQ // LANES,)),
        ],
        compiler_params=vmem_params(50),
        cost_estimate=pl.CostEstimate(
            flops=4 * rows * CELLS * KQ, bytes_accessed=26 << 20, transcendentals=rows * CELLS
        ),
        name="middle",
    )(packed, cotangent, mixed, table)


def last_kernel(xl, tl, packed_ref, table_ref, mixed_ref, field_ref, *scratch):
    wide, modes, table, mixed, field, table_sems, mixed_sems, field_sems = scratch
    chunks = table.shape[0]
    ahead = 8
    fetches, sends = [], []
    for at in range(chunks):
        lanes = slice(at * WIDTH, (at + 1) * WIDTH)
        fetches.append(
            (
                pltpu.make_async_copy(table_ref.at[at], table.at[at], table_sems.at[at]),
                pltpu.make_async_copy(mixed_ref.at[at], mixed.at[at], mixed_sems.at[at]),
            )
        )
        sends.append(
            pltpu.make_async_copy(field.at[at], field_ref.at[:, lanes], field_sems.at[at])
        )

    def start(at):
        for fetch in fetches[at]:
            fetch.start()

    for at in range(ahead):
        start(at)
    unpack_modes(packed_ref, wide, xl, tl)
    modes[...] = wide[...].reshape(modes.shape).astype(BF16)
    for at in range(chunks):
        for fetch in fetches[at]:
            fetch.wait()
        if at + ahead < chunks:
            start(at + ahead)
        field[at] = (matmul(modes[...], table[at]) + mixed[at].astype(F32)).astype(BF16)
        sends[at].start()
    for send in sends:
        send.wait()


def last(packed, mixed, table, xl, tl):
    rows = xl * tl * CHANS
    chunks = CELLS // WIDTH
    apart = pl.BlockSpec(memory_space=pltpu.HBM)
    return pl.pallas_call(
        functools.partial(last_kernel, xl, tl),
        in_specs=[pl.BlockSpec(memory_space=pltpu.VMEM), apart, apart],
        out_specs=apart,
        out_shape=jax.ShapeDtypeStruct((rows, CELLS), BF16),
        scratch_shapes=[
            pltpu.VMEM((xl, tl, CHANS, KQ), F32),
            pltpu.VMEM((rows, KQ), BF16),
            pltpu.VMEM((chunks, KQ, WIDTH), BF16),
            pltpu.VMEM((chunks, rows, WIDTH), BF16),
            pltpu.VMEM((chunks, rows, WIDTH), BF16),
            pltpu.SemaphoreType.DMA((chunks,)),
            pltpu.SemaphoreType.DMA((chunks,)),
            pltpu.SemaphoreType.DMA((chunks,)),
        ],
        compiler_params=vmem_params(50),
        cost_estimate=pl.CostEstimate(
            flops=2 * rows * CELLS * KQ, bytes_accessed=18 << 20, transcendentals=0
        ),
        name="last",
    )(packed, table, mixed)


def swap(blocks):
    return lax.all_to_all(blocks, ("gx", "ta"), split_axis=0, concat_axis=0, tiled=True)


def sum_everywhere(values, devices):
    step = 1
    while step < devices:
        pairs = [(at, at ^ step) for at in range(devices)]
        values = values + lax.ppermute(values, ("gx", "ta"), pairs)
        step *= 2
    return values


def fast_body(gx, ta, features, cotangent, spec_weight, point_weight, bias_vector):
    _, xl, tl, _, cells = features.shape
    own = spec_weight.shape[4]
    devices = gx * ta
    rows = xl * tl * CHANS
    group = rows // PARTS
    yz = np.kron(
        narrow(basis(NY, MY)).astype(np.float32), narrow(basis(NZ, MZ)).astype(np.float32)
    )
    blocks = yz.reshape(KQ, CELLS // WIDTH, WIDTH).transpose(1, 0, 2)
    table = jnp.asarray(narrow(blocks))
    x_wide = np.kron(basis(NX, MX), np.eye(CHANS))[None]
    x_in, x_out = jnp.asarray(narrow(x_wide)), jnp.asarray(narrow(x_wide.transpose(0, 2, 1)))
    t_wide = np.kron(basis(NT, MT), np.eye(own))
    t_in, t_out = jnp.asarray(narrow(t_wide.T)), jnp.asarray(narrow(t_wide))
    norm_scale = float(BATCH * NX * NT * NY * NZ) ** (-0.5)

    field = features.reshape(rows, cells)
    cot = cotangent.reshape(rows, cells)
    pick = np.tile(np.eye(CHANS, dtype=np.float32), (group // CHANS, 1))
    same = np.kron(np.eye(group // CHANS, dtype=np.float32), np.ones((CHANS, CHANS), np.float32))
    picked = jnp.asarray(narrow(pick))
    spread_point = matmul(matmul(picked, point_weight).astype(BF16), picked.T)
    spread_back = matmul(matmul(picked, point_weight.T).astype(BF16), picked.T)
    mixer = (spread_point * jnp.asarray(same)).astype(BF16)
    mixer_back = (spread_back * jnp.asarray(same)).astype(BF16)
    bias = jnp.dot(
        jnp.asarray(pick),
        jnp.broadcast_to(bias_vector[:, None], (CHANS, LANES)),
        precision=lax.Precision.HIGHEST,
    )
    spread_shape = (gx, ta, xl * CHANS, LANES)
    block_shape = (devices, xl * CHANS, LANES)
    packed_weight = pack_weight(spec_weight)
    tables = (x_in, t_in, x_out, t_out)

    spread_in = swap(analyse(field, table, xl, tl, devices)).reshape(spread_shape)
    spectrum, mixed = mix([spread_in], packed_weight, (mixer, mixer_back, bias), tables, False)
    returned = swap(mixed.reshape(block_shape))
    mixed_field = point_field(field, mixer, bias)
    output, grad, sent = middle(returned, cot, mixed_field, table, xl, tl)
    spread_grad = swap(sent).reshape(spread_shape)
    summed = sum_everywhere(own_sums(field, grad, group), devices)
    grad_modes, mixed_back = mix([spread_grad], packed_weight, (summed,), tables, True)
    grad_back = swap(mixed_back.reshape(block_shape))
    grad_spec = outer(spectrum, grad_modes, own)
    grad_field = last(grad_back, point_grad(grad, mixer_back), table, xl, tl)
    summed = summed * norm_scale
    return (
        output.reshape(features.shape),
        grad_field.reshape(features.shape),
        grad_spec,
        summed[:, :CHANS],
        summed[:, CHANS],
    )


def analyse_yz(spatial, yz_table):
    return jnp.einsum(
        "qp,bxtcp->bxtcq", yz_table, spatial.astype(F32), precision=lax.Precision.HIGHEST
    )


def build_yz(modes_in, yz_table):
    return jnp.einsum(
        "qp,bxtcq->bxtcp", yz_table, modes_in.astype(F32), precision=lax.Precision.HIGHEST
    )


def analyse_xt(spread, table):
    sizes = spread.shape
    flattened = spread.reshape(sizes[0], sizes[1] * sizes[2], sizes[3] * sizes[4]).astype(F32)
    spectral = jnp.einsum("mp,bpr->bmr", table, flattened, precision=lax.Precision.HIGHEST)
    return spectral.reshape(sizes[0], KX, KT, sizes[3], sizes[4])


def synthesise_xt(modes_in, table):
    sizes = modes_in.shape
    flattened = modes_in.reshape(sizes[0], sizes[1] * sizes[2], sizes[3] * sizes[4])
    spatial = jnp.einsum("mp,bmr->bpr", table, flattened, precision=lax.Precision.HIGHEST)
    return spatial.reshape(sizes[0], NX, NT, sizes[3], sizes[4])


def to_owners(modes_in):
    first = lax.all_to_all(modes_in, "gx", split_axis=4, concat_axis=1, tiled=True)
    return lax.all_to_all(first, "ta", split_axis=4, concat_axis=2, tiled=True)


def to_cells(spread, shape):
    first = lax.all_to_all(
        spread[:, :, :, :, None, None, :], "gx", split_axis=1, concat_axis=4, tiled=True
    )
    second = lax.all_to_all(first, "ta", split_axis=2, concat_axis=5, tiled=True)
    return second.reshape(shape[:4] + (-1,))


def general_body(features, cotangent, spec_weight, point_weight, bias_vector):
    shape = features.shape
    yz_table = jnp.asarray(
        np.kron(narrow(basis(NY, MY)).astype(np.float32), narrow(basis(NZ, MZ)).astype(np.float32))
    )
    xt_table = jnp.asarray(np.kron(basis(NX, MX), basis(NT, MT)))
    norm_scale = float(BATCH * NX * NT * NY * NZ) ** (-0.5)
    highest = lax.Precision.HIGHEST
    spectrum = analyse_xt(to_owners(analyse_yz(features, yz_table).astype(BF16)), xt_table)
    mixed = jnp.einsum("bklip,kliop->bklop", spectrum, spec_weight, precision=highest)
    returned = to_cells(synthesise_xt(mixed, xt_table).astype(BF16), shape)
    pointwise = jnp.einsum("oi,bxtip->bxtop", point_weight, features, preferred_element_type=F32)
    pre = build_yz(returned, yz_table) + pointwise + bias_vector[:, None]
    integral = 0.5 * (1.0 + jax.scipy.special.erf(pre * 0.7071067811865476))
    output = (pre * integral).astype(BF16)
    slope = integral + pre * jnp.exp(-0.5 * pre * pre) * 0.3989422804014327
    grad_pre = (cotangent.astype(F32) * slope).astype(BF16)
    local_point = jnp.einsum("bxtop,bxtip->oi", grad_pre, features, preferred_element_type=F32)
    local_bias = jnp.sum(grad_pre.astype(F32), axis=(0, 1, 2, 4))
    total_point, total_bias = lax.psum((local_point, local_bias), ("gx", "ta"))
    grad_modes = analyse_xt(to_owners(analyse_yz(grad_pre, yz_table).astype(BF16)), xt_table)
    grad_spec = jnp.einsum("bklip,bklop->kliop", spectrum, grad_modes, precision=highest)
    grad_in = jnp.einsum("kliop,bklop->bklip", spec_weight, grad_modes, precision=highest)
    grad_back = to_cells(synthesise_xt(grad_in, xt_table).astype(BF16), shape)
    point_term = jnp.einsum("oi,bxtop->bxtip", point_weight, grad_pre, preferred_element_type=F32)
    grad_field = (build_yz(grad_back, yz_table) + point_term).astype(BF16)
    return (output, grad_field, grad_spec, total_point * norm_scale, total_bias * norm_scale)


def solution(mesh):
    split_field = P(None, "gx", "ta", None, None)
    split_weight = P(None, None, None, None, ("gx", "ta"))
    in_specs = (split_field, split_field, split_weight, P(), P())
    out_specs = (split_field, split_field, split_weight, P(), P())
    gx, ta = mesh.shape["gx"], mesh.shape["ta"]
    own, xl, tl = KQ // (gx * ta), NX // gx, NT // ta
    if own == 32 and xl * CHANS == LANES and tl == 4:
        body = functools.partial(fast_body, gx, ta)
    else:
        body = general_body
    return jax.shard_map(body, mesh=mesh, in_specs=in_specs, out_specs=out_specs, check_vma=False)
```
